32 devices in a mesh: gx: 4 (over z), gy: 8 (over y, x, core).
Axes of the slice: x: 2, y: 2, z: 4, core: 2. Of those that a mesh axis runs over, the one named last changes fastest.
Arguments:
- velocity: float32 [3, 32, 64, 128], P(None, 'gx', 'gy'), may hold values from -1 to 1
- wall_cells: int32 [32, 64, 128], P('gx', 'gy'), may hold values 0 or 1
- tile_counts: int32 [4, 8, 8], P('gx', 'gy'), may hold values from 32 to 256, as said below
- helper_tile: int32 [4, 8], P('gx'), may hold values from 0 to 63, as said below
- base_fields: float32 [4, 8, 8, 3, 32, 1024], P('gx', 'gy'), may hold values from -2.5 to 2.5
- extra_fields: float32 [4, 8, 3, 224, 1024], P('gx', 'gy'), may hold values from -6.1 to 6.1
- base_noise: bfloat16 [4, 8, 8, 2, 3, 32, 1024], P('gx', 'gy'), may hold values from -2.5 to 2.5
- extra_noise: bfloat16 [4, 8, 2, 3, 224, 1024], P('gx', 'gy'), may hold values from -2.5 to 2.5
Outputs:
- new_base_fields: float32 [4, 8, 8, 3, 32, 1024], P('gx', 'gy')
- new_extra_fields: float32 [4, 8, 3, 224, 1024], P('gx', 'gy')
- polymer_stress: float32 [4, 8, 8, 6, 1024], P('gx', 'gy')
The draws below stay inside these ranges and needn't reach their ends.
Inputs may be any that keep to these rules, and one draw needn't show every extreme that they name: `tile_counts`: each entry is 32 or 256. In each row of tiles exactly 8 tiles have 256, these are the tiles that helper_tile names, one column of tiles holds at most 4 of them and in every row some column holds exactly 4. `helper_tile`: entry [i, h] = o * 8 + t names tile t of column o in row i; the entries of a row are distinct and name exactly the row's tiles with 256 fields.
All inputs are finite; a program needn't handle non-finite values. No bound on the sum of `wall_cells` on one device may be relied on, other than what follows from the above.
Results may differ from the reference program's by a relative error of at most 0.0003.
Values sent between devices are 32-bit elements; how exact they have to be, the bound alone decides.
No kernel may reach another device: no remote copies, remote signals or barrier semaphores. Data moves between devices by JAX's collectives and lax.ppermute only.
A program may use at most 128 MiB of HBM per device.

```python
import math
import jax
import jax.numpy as jnp

CELL_X = 8
CELL_Y = 8
CELL_Z = 16
T_DEV = 8
BASE_FIELDS = 32
ALL_FIELDS = 256
STEPS = 2
EXTRA_FIELDS = 224
TILE_CELLS = 1024
HEAVY_MOST = 4
TILES_X = 4
TILES_Y = 8
NX = 32
NY = 64
NZ = 128


def heavy_row(row_key, special):
    slot_total = TILES_Y * HEAVY_MOST
    key_score, key_owner, key_tiles, key_helpers = jax.random.split(row_key, 4)
    slot_index = jnp.arange(slot_total, dtype=jnp.int32)
    slot_owner = slot_index // HEAVY_MOST
    slot_local = slot_index % HEAVY_MOST
    scores = jax.random.randint(key_score, (slot_total,), 0, 1048576, dtype=jnp.int32) * slot_total + slot_index
    forced = jax.random.randint(key_owner, (), 0, TILES_Y, dtype=jnp.int32)
    scores = jnp.where(slot_owner == forced, -1 - slot_index, scores)
    edge_slot = (slot_index == 0) | (slot_index == (TILES_Y - 1) * HEAVY_MOST)
    scores = jnp.where(special & edge_slot, -1 - slot_total - slot_index, scores)
    ranking = jnp.argsort(scores)
    chosen = ranking[:TILES_Y]
    tile_scores = jax.random.randint(key_tiles, (TILES_Y, T_DEV), 0, 1048576, dtype=jnp.int32) * T_DEV
    tile_scores = tile_scores + jnp.arange(T_DEV, dtype=jnp.int32)[None, :]
    owner_grid = jnp.arange(TILES_Y, dtype=jnp.int32)[:, None]
    tile_grid = jnp.arange(T_DEV, dtype=jnp.int32)[None, :]
    edge_tile = (owner_grid == 0) & (tile_grid == 0) | (owner_grid == TILES_Y - 1) & (tile_grid == T_DEV - 1)
    tile_scores = jnp.where(special & edge_tile, -1, tile_scores)
    tile_ranking = jnp.argsort(tile_scores, axis=1).astype(jnp.int32)
    chosen_owner = slot_owner[chosen]
    chosen_tile = tile_ranking[chosen_owner, slot_local[chosen]]
    global_ids = chosen_owner * T_DEV + chosen_tile
    helper_order = jax.random.permutation(key_helpers, TILES_Y)
    helper_ids = global_ids[helper_order].astype(jnp.int32)
    heavy_flag = jnp.any(global_ids[:, None] == jnp.arange(TILES_Y * T_DEV, dtype=jnp.int32)[None, :], axis=0)
    counts = jnp.where(heavy_flag, ALL_FIELDS, BASE_FIELDS).astype(jnp.int32).reshape(TILES_Y, T_DEV)
    return (counts, helper_ids)


def heavy_layout(key):
    base_key = jax.random.fold_in(key, 31)
    special_row = jax.random.randint(jax.random.fold_in(key, 77), (), 0, TILES_X, dtype=jnp.int32)
    row_numbers = jnp.arange(TILES_X, dtype=jnp.int32)
    row_keys = jax.vmap(lambda row_number: jax.random.fold_in(base_key, row_number))(row_numbers)
    return jax.vmap(heavy_row)(row_keys, row_numbers == special_row)


def draw_tile_counts(key, part):
    return heavy_layout(key)[0]


def draw_helper_tile(key, part):
    return heavy_layout(key)[1]


def draw_base_fields(key, part):
    key_scale, key_values = jax.random.split(jax.random.fold_in(key, 101))
    low_scale, high_scale = (0.5, 2.0)
    log_scale = jax.random.uniform(key_scale, (TILES_X, TILES_Y, T_DEV, 1, 1, TILE_CELLS), jnp.float32, math.log(low_scale), math.log(high_scale))
    values = jax.random.uniform(key_values, (TILES_X, TILES_Y, T_DEV, 3, BASE_FIELDS, TILE_CELLS), jnp.float32, -1.0, 1.0)
    return jnp.exp(log_scale) * values


def draw_extra_fields(key, part):
    key_stretch, key_radius, key_direction = jax.random.split(jax.random.fold_in(key, 202), 3)
    low_square, low_radius = (12.0, 0.8)
    log_square = jax.random.uniform(key_stretch, (TILES_X, TILES_Y, 1, 1, TILE_CELLS), jnp.float32, math.log(low_square), math.log(30.0))
    radius = jax.random.uniform(key_radius, (TILES_X, TILES_Y, 1, EXTRA_FIELDS, TILE_CELLS), jnp.float32, low_radius, 1.1)
    direction = jax.random.normal(key_direction, (TILES_X, TILES_Y, 3, EXTRA_FIELDS, TILE_CELLS), jnp.float32)
    length = jnp.sqrt(jnp.sum(direction * direction, axis=2, keepdims=True) + 1e-12)
    return jnp.exp(0.5 * log_square) * radius * (direction / length)


def plant(entries, own_key, smallest, high):
    longest = entries.shape.index(max(entries.shape))
    spots = []
    for shift in (0, 1):
        where = [jax.random.randint(jax.random.fold_in(own_key, axis), (), 0, length) for axis, length in enumerate(entries.shape)]
        where[longest] = (where[longest] + shift) % entries.shape[longest]
        spots.append(tuple(where))
    return entries.at[spots[0]].set(smallest).at[spots[1]].set(high)


def level_of(own_key, extent, cuts, smallest, high):
    gain, own = 1.0, jax.random.fold_in(own_key, 6)
    for axis_at, shards_of in cuts:
        steps = jnp.exp(jax.random.uniform(jax.random.fold_in(own, axis_at), (shards_of,), jnp.float32, smallest / len(cuts), high / len(cuts)))
        gain = gain * jnp.repeat(steps, extent[axis_at] // shards_of).reshape([-1 if axis == axis_at else 1 for axis in range(len(extent))])
    return gain


def scatter_about(stream_key, extent, spread, reach, shards=(), held_as=jnp.bfloat16):
    result = spread * jax.random.normal(stream_key, extent, jnp.float32)
    if shards:
        result = result * level_of(stream_key, extent, shards, -0.22, 0.18)
    return jnp.clip(result, -reach, reach).astype(held_as)


def setup_inputs(seed: int = 0) -> dict:
    arg_keys = jax.random.split(jax.random.key(seed), 9)
    velocity = jnp.clip(jax.random.uniform(arg_keys[0], (3, NX, NY, NZ), jnp.float32, -1.0, 1.0) * level_of(arg_keys[0], (3, NX, NY, NZ), ((1, 4), (2, 8)), -0.4, 0.0), -1.0, 1.0)
    wall_cells = plant((jax.random.randint(arg_keys[1], (NX, NY, NZ), 0, 8) < 1).astype(jnp.int32), jax.random.fold_in(arg_keys[1], 1), 0, 1)
    tile_counts = draw_tile_counts(jax.random.fold_in(arg_keys[8], 71), 0)
    helper_tile = draw_helper_tile(jax.random.fold_in(arg_keys[8], 71), 0)
    base_fields = draw_base_fields(jax.random.fold_in(arg_keys[8], 71), 0)
    extra_fields = draw_extra_fields(jax.random.fold_in(arg_keys[8], 71), 0)
    base_noise = scatter_about(arg_keys[6], (TILES_X, TILES_Y, T_DEV, STEPS, 3, BASE_FIELDS, TILE_CELLS), 1.0, 2.5, ((0, 4), (1, 8)))
    extra_noise = scatter_about(arg_keys[7], (TILES_X, TILES_Y, STEPS, 3, EXTRA_FIELDS, TILE_CELLS), 1.0, 2.5, ((0, 4), (1, 8)))
    return {"velocity": velocity, "wall_cells": wall_cells, "tile_counts": tile_counts, "helper_tile": helper_tile, "base_fields": base_fields, "extra_fields": extra_fields, "base_noise": base_noise, "extra_noise": extra_noise}


time_step = 0.05
weissenberg = 0.25
max_extension = 50.0
noise_scale = (time_step / weissenberg) ** 0.5
component_pairs = ((0, 0), (1, 1), (2, 2), (0, 1), (0, 2), (1, 2))


def velocity_gradient(padded, wall_cells):
    along_x = (padded[:, 2:, 1:-1, 1:-1] - padded[:, :-2, 1:-1, 1:-1]) * 0.5
    along_y = (padded[:, 1:-1, 2:, 1:-1] - padded[:, 1:-1, :-2, 1:-1]) * 0.5
    along_z = (padded[:, 1:-1, 1:-1, 2:] - padded[:, 1:-1, 1:-1, :-2]) * 0.5
    fluid = (wall_cells == 0).astype(jnp.float32)
    stacked = jnp.stack([along_x, along_y, along_z], axis=1) * fluid
    return stacked.reshape((9,) + wall_cells.shape)


def spring_factor(total, count):
    return 1.0 / (1.0 - (total / count) / max_extension)


def advance(state, grad, factor, noise):
    relax = factor[..., None, :] * (0.5 / weissenberg)
    parts = []
    for component in range(3):
        drift = grad[..., 3 * component, None, :] * state[..., 0, :, :]
        drift = drift + grad[..., 3 * component + 1, None, :] * state[..., 1, :, :]
        drift = drift + grad[..., 3 * component + 2, None, :] * state[..., 2, :, :]
        current = state[..., component, :, :]
        parts.append(current + time_step * (drift - relax * current)
                     + noise_scale * noise[..., component, :, :].astype(jnp.float32))
    return jnp.stack(parts, axis=-3)


def moments(state):
    return jnp.stack([jnp.sum(state[..., first_axis, :, :] * state[..., second_axis, :, :], axis=-2)
                      for first_axis, second_axis in component_pairs], axis=-2)


def polymer_stress(total, count):
    second = total / count
    trace = second[..., 0, :] + second[..., 1, :] + second[..., 2, :]
    stretch = 1.0 / (1.0 - trace / max_extension)
    unit = jnp.array([1.0, 1.0, 1.0, 0.0, 0.0, 0.0], jnp.float32)[:, None]
    return (stretch[..., None, :] * second - unit) / weissenberg


def add_helpers(own_rows, extra_rows, helper_tile):
    row_index = jnp.arange(TILES_X, dtype=jnp.int32)[:, None]
    flat = own_rows.reshape((TILES_X, TILES_Y * T_DEV) + own_rows.shape[3:])
    flat = flat.at[row_index, helper_tile].add(extra_rows)
    return flat.reshape(own_rows.shape)


def reference(velocity, wall_cells, tile_counts, helper_tile, base_fields, extra_fields, base_noise, extra_noise):
    padded = jnp.pad(velocity, ((0, 0), (1, 1), (1, 1), (1, 1)))
    grad_grid = velocity_gradient(padded, wall_cells)
    tile_grad = grad_grid.reshape(9, TILES_X, CELL_X, TILES_Y, CELL_Y, T_DEV, CELL_Z)
    tile_grad = tile_grad.transpose(1, 3, 5, 0, 2, 4, 6).reshape(TILES_X, TILES_Y, T_DEV, 9, TILE_CELLS)
    row_index = jnp.arange(TILES_X, dtype=jnp.int32)[:, None]
    helper_grad = tile_grad.reshape(TILES_X, TILES_Y * T_DEV, 9, TILE_CELLS)[row_index, helper_tile]
    counts = tile_counts.astype(jnp.float32)
    base_state = base_fields
    extra_state = extra_fields
    for step_index in range(STEPS):
        base_square = jnp.sum(base_state * base_state, axis=(3, 4))
        extra_square = jnp.sum(extra_state * extra_state, axis=(2, 3))
        tile_total = add_helpers(base_square, extra_square, helper_tile)
        factor = spring_factor(tile_total, counts[..., None])
        helper_factor = factor.reshape(TILES_X, TILES_Y * T_DEV, TILE_CELLS)[row_index, helper_tile]
        base_state = advance(base_state, tile_grad, factor, base_noise[:, :, :, step_index])
        extra_state = advance(extra_state, helper_grad, helper_factor, extra_noise[:, :, step_index])
    moment_total = add_helpers(moments(base_state), moments(extra_state), helper_tile)
    stress = polymer_stress(moment_total, counts[..., None, None])
    return base_state, extra_state, stress
```

```python
import functools

import jax
import jax.numpy as jnp
from jax import lax
from jax.experimental import pallas as pl
from jax.experimental.pallas import tpu as pltpu
from jax.sharding import PartitionSpec as P

ALL_FIELDS = 256
HEAVY_MOST = 4
LANES = 128
SUB = 8

time_step = 0.05
weissenberg = 0.25
max_extension = 50.0
noise_scale = (time_step / weissenberg) ** 0.5
component_pairs = ((0, 0), (1, 1), (2, 2), (0, 1), (0, 2), (1, 2))
moment_of = {(0, 0): 0, (1, 1): 1, (2, 2): 2, (0, 1): 3, (1, 0): 3, (0, 2): 4, (2, 0): 4, (1, 2): 5, (2, 1): 5}
f32 = jnp.float32

smem = pl.BlockSpec(memory_space=pltpu.SMEM)
vmem = pl.BlockSpec(memory_space=pltpu.VMEM)
anywhere = pl.BlockSpec(memory_space=pl.ANY)


def column_sum(value):
    return jnp.sum(value, axis=0, keepdims=True)


def wide(row):
    return jnp.broadcast_to(row, (SUB, LANES))


def turned(value, cell_z):
    sub = lax.broadcasted_iota(jnp.int32, value.shape, 0)
    group = lax.broadcasted_iota(jnp.int32, value.shape, 1) // cell_z
    bit = 1
    while bit < SUB:
        low, high = (sub & bit) != 0, (group & bit) != 0
        up = pltpu.roll(pltpu.roll(value, SUB - bit, 0), cell_z * bit, 1)
        down = pltpu.roll(pltpu.roll(value, bit, 0), LANES - cell_z * bit, 1)
        value = jnp.where(low == high, value, jnp.where(low, down, up))
        bit *= 2
    return value


def relax_of(total, count):
    factor = 1.0 / (1.0 - total / count / max_extension)
    return 1.0 - (time_step * 0.5 / weissenberg) * factor


def stepped(vectors, noise, matrix):
    return [
        matrix[3 * a] * vectors[0]
        + matrix[3 * a + 1] * vectors[1]
        + matrix[3 * a + 2] * vectors[2]
        + noise_scale * noise[a]
        for a in range(3)
    ]


def with_diagonal(grad, relax):
    return [g + relax if i % 4 == 0 else g for i, g in enumerate(grad)]


def noise_rows(ref, start):
    both = [ref(a, pl.ds(start, 2 * SUB)).astype(f32) for a in range(3)]
    return [[w[:SUB] for w in both], [w[SUB:] for w in both]]


def load_heavy(tiles, me, helper, copies):
    slots = helper.shape[1]
    rank = jnp.int32(0)
    found = []
    for h in range(slots):
        tile = helper[0, h] - me * tiles
        owned = (tile >= 0) & (tile < tiles)
        found.append((owned, tile, rank))

        @pl.when(owned)
        def _(tile=tile, rank=rank):
            for copy in copies(tile, rank):
                copy.start()

        rank = rank + owned.astype(jnp.int32)
    return found


def heavy_moments(helper, base, noise, out, fields, shocks, sems):
    tiles = base.shape[2]
    me = lax.axis_index("gy")
    groups = fields.shape[2] // (2 * SUB)

    def copies(tile, rank):
        return (
            pltpu.make_async_copy(base.at[0, 0, tile], fields.at[rank], sems.at[0, rank]),
            pltpu.make_async_copy(noise.at[0, 0, tile, 0], shocks.at[rank], sems.at[1, rank]),
        )

    for h, (owned, tile, rank) in enumerate(load_heavy(tiles, me, helper, copies)):

        @pl.when(owned)
        def _(h=h, tile=tile, rank=rank):
            for copy in copies(tile, rank):
                copy.wait()

            @pl.loop(0, fields.shape[3] // LANES)
            def _(x):
                lanes = pl.ds(pl.multiple_of(x * LANES, LANES), LANES)
                sums = [jnp.zeros((SUB, LANES), f32)] * 16
                for group in range(groups):
                    pair = noise_rows(lambda a, rows: shocks[rank, a, rows, lanes], group * 2 * SUB)
                    for half in range(2):
                        rows = pl.ds((2 * group + half) * SUB, SUB)
                        q = [fields[rank, a, rows, lanes] for a in range(3)]
                        w = pair[half]
                        terms = [q[a] * q[b] for a, b in component_pairs]
                        terms += [q[a] * w[b] for a in range(3) for b in range(3)]
                        terms += [w[0] * w[0] + w[1] * w[1] + w[2] * w[2]]
                        sums = [s + t for s, t in zip(sums, terms)]
                for i, s in enumerate(sums):
                    out[h, i, pl.ds(x, 1), :] = column_sum(s)


def call_heavy_moments(helper_tile, base_fields, base_noise):
    slots = helper_tile.shape[1]
    _, _, _, _, count, cells = base_fields.shape
    return pl.pallas_call(
        heavy_moments,
        out_shape=jax.ShapeDtypeStruct((slots, 16, cells // LANES, LANES), f32),
        in_specs=[smem, anywhere, anywhere],
        out_specs=vmem,
        scratch_shapes=[
            pltpu.VMEM((HEAVY_MOST, 3, count, cells), f32),
            pltpu.VMEM((HEAVY_MOST, 3, count, cells), jnp.bfloat16),
            pltpu.SemaphoreType.DMA((2, HEAVY_MOST)),
        ],
        compiler_params=pltpu.CompilerParams(vmem_limit_bytes=16 << 20),
        cost_estimate=pl.CostEstimate(flops=8 << 20, bytes_accessed=2 << 20, transcendentals=0),
        name="heavy_moments",
    )(helper_tile, base_fields, base_noise)


def gradients(tiles, helper, velocity, x_low, x_high, y_low, y_high, wall, moments, grad, message):
    me = lax.axis_index("gy")
    depth = velocity.shape[1]
    cell_z = velocity.shape[3] // tiles
    sub = lax.broadcasted_iota(jnp.int32, (SUB, LANES), 0)
    lane = lax.broadcasted_iota(jnp.int32, (SUB, LANES), 1)
    z = lane % cell_z
    scales = [
        turned(jnp.where(wall[x] == 0, 0.5 * time_step, 0.0).astype(f32), cell_z) for x in range(depth)
    ]
    for a in range(3):
        rows = [x_low[a]] + [velocity[a, x] for x in range(depth)] + [x_high[a]]
        rows = [turned(row, cell_z) for row in rows]
        for x in range(depth):
            edge = jnp.where(sub == 0, y_low[a, pl.ds(x, 1), :], y_high[a, pl.ds(x, 1), :])
            edge = turned(edge, cell_z)
            here = rows[x + 1]
            y_up = jnp.where(lane < LANES - cell_z, pltpu.roll(here, LANES - cell_z, 1), edge)
            y_down = jnp.where(lane >= cell_z, pltpu.roll(here, cell_z, 1), edge)
            next_tile = pltpu.roll(pltpu.roll(here, cell_z - 1, 1), SUB - 1, 0)
            last_tile = pltpu.roll(pltpu.roll(here, LANES - cell_z + 1, 1), 1, 0)
            next_tile = jnp.where(sub == SUB - 1, 0.0, next_tile)
            last_tile = jnp.where(sub == 0, 0.0, last_tile)
            z_up = jnp.where(z == cell_z - 1, next_tile, pltpu.roll(here, LANES - 1, 1))
            z_down = jnp.where(z == 0, last_tile, pltpu.roll(here, 1, 1))
            for b, difference in enumerate((rows[x + 2] - rows[x], y_up - y_down, z_up - z_down)):
                grad[pl.ds(((3 * a + b) * depth + x) * SUB, SUB), :] = difference * scales[x]
    for h in range(helper.shape[1]):
        tile = helper[0, h] - me * tiles

        @pl.when((tile >= 0) & (tile < tiles))
        def _(h=h, tile=tile):
            g = [grad[pl.ds(i * depth * SUB + tile, depth, stride=SUB), :] for i in range(9)]
            m = [moments[h, i] for i in range(16)]
            cross = lambda a, b: m[6 + 3 * a + b]
            square = lambda a, b: m[moment_of[a, b]]
            once, twice, kick = 0.0, 0.0, 0.0
            for a in range(3):
                for b in range(3):
                    once += g[3 * a + b] * square(a, b)
                    kick += g[3 * a + b] * cross(b, a)
                    inner = 0.0
                    for c in range(3):
                        inner += g[3 * a + c] * square(b, c)
                    twice += g[3 * a + b] * inner
            for i in range(9):
                message[h, i] = g[i]
            message[h, 9] = twice + (2 * noise_scale) * kick + noise_scale**2 * m[15]
            message[h, 10] = 2.0 * once + (2 * noise_scale) * (cross(0, 0) + cross(1, 1) + cross(2, 2))
            message[h, 11] = m[0] + m[1] + m[2]


def call_gradients(tiles, helper_tile, velocity, halos, wall_cells, moments):
    slots = helper_tile.shape[1]
    depth = velocity.shape[1]
    return pl.pallas_call(
        functools.partial(gradients, tiles),
        out_shape=(
            jax.ShapeDtypeStruct((9 * depth * SUB, LANES), f32),
            jax.ShapeDtypeStruct((slots, 12, depth, LANES), f32),
        ),
        in_specs=[smem] + [vmem] * 7,
        out_specs=(vmem, vmem),
        compiler_params=pltpu.CompilerParams(vmem_limit_bytes=8 << 20),
        cost_estimate=pl.CostEstimate(flops=4 << 20, bytes_accessed=1 << 20, transcendentals=0),
        name="gradients",
    )(helper_tile, velocity, *halos, wall_cells, moments)


def stress_rows(sums, count):
    second = [s / count for s in sums]
    stretch = 1.0 / (1.0 - (second[0] + second[1] + second[2]) / max_extension)
    return [(stretch * s - (1.0 if i < 3 else 0.0)) / weissenberg for i, s in enumerate(second)]


def tile_grad(grad, depth, tile, x):
    return [wide(grad[pl.ds((i * depth + x) * SUB + tile, 1), :]) for i in range(9)]


def ordinary(counts, base, noise, grad, new_base, stress, totals, relaxes):
    tile = pl.program_id(0)
    count = counts[0, 0, tile]
    cells = base.shape[-1]
    depth = cells // LANES
    groups = base.shape[4] // (2 * SUB)

    @pl.when(count != ALL_FIELDS)
    def _():
        scale = count.astype(f32)
        for x in range(depth):
            lanes = pl.ds(x * LANES, LANES)
            total = jnp.zeros((SUB, LANES), f32)
            for group in range(2 * groups):
                for a in range(3):
                    q = base[0, 0, 0, a, pl.ds(group * SUB, SUB), lanes]
                    total = total + q * q
            totals[pl.ds(x, 1), :] = column_sum(total)
        for step in range(2):
            relaxes[...] = relax_of(totals[...], scale)
            source = base if step == 0 else new_base
            for x in range(depth):
                lanes = pl.ds(x * LANES, LANES)
                matrix = with_diagonal(tile_grad(grad, depth, tile, x), wide(relaxes[pl.ds(x, 1), :]))
                sums = [jnp.zeros((SUB, LANES), f32)] * (1 if step == 0 else 6)
                for group in range(groups):
                    pair = noise_rows(lambda a, rows: noise[0, 0, 0, step, a, rows, lanes], group * 2 * SUB)
                    for half in range(2):
                        rows = pl.ds((2 * group + half) * SUB, SUB)
                        q = [source[0, 0, 0, a, rows, lanes] for a in range(3)]
                        q = stepped(q, pair[half], matrix)
                        for a in range(3):
                            new_base[0, 0, 0, a, rows, lanes] = q[a]
                        if step == 0:
                            sums[0] = sums[0] + (q[0] * q[0] + q[1] * q[1] + q[2] * q[2])
                        else:
                            sums = [s + q[a] * q[b] for s, (a, b) in zip(sums, component_pairs)]
                if step == 0:
                    totals[pl.ds(x, 1), :] = column_sum(sums[0])
                else:
                    for i, row in enumerate(stress_rows([column_sum(s) for s in sums], scale)):
                        stress[0, 0, 0, pl.ds(i, 1), lanes] = row


def call_ordinary(tile_counts, base_fields, base_noise, grad):
    _, _, tiles, _, count, cells = base_fields.shape
    steps = base_noise.shape[3]
    depth = cells // LANES
    return pl.pallas_call(
        ordinary,
        grid=(tiles,),
        out_shape=(
            jax.ShapeDtypeStruct(base_fields.shape, f32),
            jax.ShapeDtypeStruct((1, 1, tiles, 6, cells), f32),
        ),
        in_specs=[
            smem,
            pl.BlockSpec((1, 1, 1, 3, count, cells), lambda t: (0, 0, t, 0, 0, 0)),
            pl.BlockSpec((1, 1, 1, steps, 3, count, cells), lambda t: (0, 0, t, 0, 0, 0, 0)),
            vmem,
        ],
        out_specs=(
            pl.BlockSpec((1, 1, 1, 3, count, cells), lambda t: (0, 0, t, 0, 0, 0)),
            pl.BlockSpec((1, 1, 1, 6, cells), lambda t: (0, 0, t, 0, 0)),
        ),
        scratch_shapes=[pltpu.VMEM((depth, LANES), f32), pltpu.VMEM((depth, LANES), f32)],
        compiler_params=pltpu.CompilerParams(vmem_limit_bytes=12 << 20),
        cost_estimate=pl.CostEstimate(flops=32 << 20, bytes_accessed=10 << 20, transcendentals=0),
        name="ordinary_tiles",
    )(tile_counts, base_fields, base_noise, grad)


def extra(tiles, helper, fields, noise, message, new_fields, reply):
    me = lax.axis_index("gy")
    owner = helper[0, me] // tiles
    x = pl.program_id(0)
    groups = fields.shape[3] // (2 * SUB)
    row = lambda i: wide(message[owner, i, pl.ds(x, 1), :])
    grad = [row(i) for i in range(9)]

    def squares(i, total):
        for half in range(2):
            rows = pl.ds(pl.multiple_of((2 * i + half) * SUB, SUB), SUB)
            for a in range(3):
                q = fields[0, 0, a, rows, :]
                total = total + q * q
        return total

    zero = jnp.zeros((SUB, LANES), f32)
    total = column_sum(lax.fori_loop(0, groups, squares, zero, unroll=True))
    first = relax_of(total + row(11), float(ALL_FIELDS))

    def advance(step, source, matrix, i, sums):
        pair = noise_rows(lambda a, rows: noise[0, 0, step, a, rows, :], pl.multiple_of(i * 2 * SUB, 2 * SUB))
        for half in range(2):
            rows = pl.ds(pl.multiple_of((2 * i + half) * SUB, SUB), SUB)
            q = stepped([source[0, 0, a, rows, :] for a in range(3)], pair[half], matrix)
            for a in range(3):
                new_fields[0, 0, a, rows, :] = q[a]
            if step == 0:
                sums = [sums[0] + (q[0] * q[0] + q[1] * q[1] + q[2] * q[2])]
            else:
                sums = [s + q[a] * q[b] for s, (a, b) in zip(sums, component_pairs)]
        return sums

    matrix = with_diagonal(grad, first)
    sums = lax.fori_loop(0, groups, functools.partial(advance, 0, fields, matrix), [zero], unroll=True)
    total = column_sum(sums[0]) + (row(9) + first * row(10) + first * first * row(11))
    second = relax_of(total, float(ALL_FIELDS))
    matrix = with_diagonal(grad, second)
    sums = lax.fori_loop(0, groups, functools.partial(advance, 1, new_fields, matrix), [zero] * 6, unroll=True)
    reply[0, pl.ds(x, 1), :] = first[:1]
    reply[1, pl.ds(x, 1), :] = second[:1]
    for i, s in enumerate(sums):
        reply[2 + i, pl.ds(x, 1), :] = column_sum(s)


def call_extra(tiles, helper_tile, extra_fields, extra_noise, message):
    _, _, _, count, cells = extra_fields.shape
    steps = extra_noise.shape[2]
    depth = cells // LANES
    return pl.pallas_call(
        functools.partial(extra, tiles),
        grid=(depth,),
        out_shape=(
            jax.ShapeDtypeStruct(extra_fields.shape, f32),
            jax.ShapeDtypeStruct((8, depth, LANES), f32),
        ),
        in_specs=[
            smem,
            pl.BlockSpec((1, 1, 3, count, LANES), lambda x: (0, 0, 0, 0, x)),
            pl.BlockSpec((1, 1, steps, 3, count, LANES), lambda x: (0, 0, 0, 0, 0, x)),
            vmem,
        ],
        out_specs=(
            pl.BlockSpec((1, 1, 3, count, LANES), lambda x: (0, 0, 0, 0, x)),
            pl.BlockSpec((8, depth, LANES), lambda x: (0, 0, 0)),
        ),
        compiler_params=pltpu.CompilerParams(vmem_limit_bytes=12 << 20),
        cost_estimate=pl.CostEstimate(flops=32 << 20, bytes_accessed=9 << 20, transcendentals=0),
        name="extra_fields",
    )(helper_tile, extra_fields, extra_noise, message)


def heavy(helper, base, noise, grad, replies, old_base, old_stress, new_base, stress, fields, shocks, rows_out, sems):
    tiles = base.shape[2]
    me = lax.axis_index("gy")
    cells = base.shape[-1]
    depth = cells // LANES
    groups = base.shape[4] // (2 * SUB)

    def copies(tile, rank):
        return (
            pltpu.make_async_copy(base.at[0, 0, tile], fields.at[rank], sems.at[0, rank]),
            pltpu.make_async_copy(noise.at[0, 0, tile], shocks.at[rank], sems.at[1, rank]),
        )

    def results(tile, rank):
        return (
            pltpu.make_async_copy(fields.at[rank], new_base.at[0, 0, tile], sems.at[2, rank]),
            pltpu.make_async_copy(rows_out.at[rank], stress.at[0, 0, tile], sems.at[3, rank]),
        )

    found = load_heavy(tiles, me, helper, copies)
    for h, (owned, tile, rank) in enumerate(found):

        @pl.when(owned)
        def _(h=h, tile=tile, rank=rank):
            for copy in copies(tile, rank):
                copy.wait()

            @pl.loop(0, depth)
            def _(x):
                lanes = pl.ds(pl.multiple_of(x * LANES, LANES), LANES)
                g = tile_grad(grad, depth, tile, x)
                matrices = [with_diagonal(g, wide(replies[h, s, pl.ds(x, 1), :])) for s in range(2)]
                sums = [jnp.zeros((SUB, LANES), f32)] * 6
                for group in range(groups):
                    pairs = [
                        noise_rows(lambda a, rows: shocks[rank, s, a, rows, lanes], group * 2 * SUB) for s in range(2)
                    ]
                    for half in range(2):
                        rows = pl.ds((2 * group + half) * SUB, SUB)
                        q = [fields[rank, a, rows, lanes] for a in range(3)]
                        for s in range(2):
                            q = stepped(q, pairs[s][half], matrices[s])
                        for a in range(3):
                            fields[rank, a, rows, lanes] = q[a]
                        sums = [s + q[a] * q[b] for s, (a, b) in zip(sums, component_pairs)]
                sums = [column_sum(s) + replies[h, 2 + i, pl.ds(x, 1), :] for i, s in enumerate(sums)]
                for i, row in enumerate(stress_rows(sums, float(ALL_FIELDS))):
                    rows_out[rank, pl.ds(i, 1), lanes] = row

            for copy in results(tile, rank):
                copy.start()

    for owned, tile, rank in found:

        @pl.when(owned)
        def _(tile=tile, rank=rank):
            for copy in results(tile, rank):
                copy.wait()


def call_heavy(helper_tile, base_fields, base_noise, grad, replies, new_base, stress):
    _, _, _, _, count, cells = base_fields.shape
    steps = base_noise.shape[3]
    return pl.pallas_call(
        heavy,
        out_shape=(
            jax.ShapeDtypeStruct(new_base.shape, f32),
            jax.ShapeDtypeStruct(stress.shape, f32),
        ),
        in_specs=[smem, anywhere, anywhere, vmem, vmem, anywhere, anywhere],
        out_specs=(anywhere, anywhere),
        input_output_aliases={5: 0, 6: 1},
        scratch_shapes=[
            pltpu.VMEM((HEAVY_MOST, 3, count, cells), f32),
            pltpu.VMEM((HEAVY_MOST, steps, 3, count, cells), jnp.bfloat16),
            pltpu.VMEM((HEAVY_MOST, 6, cells), f32),
            pltpu.SemaphoreType.DMA((4, HEAVY_MOST)),
        ],
        compiler_params=pltpu.CompilerParams(vmem_limit_bytes=16 << 20),
        cost_estimate=pl.CostEstimate(flops=8 << 20, bytes_accessed=4 << 20, transcendentals=0),
        name="heavy_tiles",
    )(helper_tile, base_fields, base_noise, grad, replies, new_base, stress)


def neighbours(block, axis, dim):
    size, length = lax.axis_size(axis), block.shape[dim]
    up = [(i, i + 1) for i in range(size - 1)]
    down = [(i + 1, i) for i in range(size - 1)]
    last = lax.index_in_dim(block, length - 1, dim, keepdims=False)
    first = lax.index_in_dim(block, 0, dim, keepdims=False)
    return lax.ppermute(last, axis, up), lax.ppermute(first, axis, down)


def per_device(
    velocity, wall_cells, tile_counts, helper_tile, base_fields, extra_fields, base_noise, extra_noise
):
    tiles = tile_counts.shape[2]
    halos = neighbours(velocity, "gx", 1) + neighbours(velocity, "gy", 2)
    moments = call_heavy_moments(helper_tile, base_fields, base_noise)
    grad, message = call_gradients(tiles, helper_tile, velocity, halos, wall_cells, moments)
    message = lax.all_to_all(message, "gy", 0, 0, tiled=True)
    new_base, stress = call_ordinary(tile_counts, base_fields, base_noise, grad)
    new_extra, reply = call_extra(tiles, helper_tile, extra_fields, extra_noise, message)
    replies = lax.all_gather(reply, "gy", axis=0)
    new_base, stress = call_heavy(helper_tile, base_fields, base_noise, grad, replies, new_base, stress)
    return new_base, new_extra, stress


def solution(mesh):
    in_specs = (
        P(None, "gx", "gy", None),
        P("gx", "gy", None),
        P("gx", "gy", None),
        P("gx", None),
        P("gx", "gy", None, None, None, None),
        P("gx", "gy", None, None, None),
        P("gx", "gy", None, None, None, None, None),
        P("gx", "gy", None, None, None, None),
    )
    out_specs = (
        P("gx", "gy", None, None, None, None),
        P("gx", "gy", None, None, None),
        P("gx", "gy", None, None, None),
    )
    return jax.shard_map(
        per_device, mesh=mesh, in_specs=in_specs, out_specs=out_specs, check_vma=False
    )
```

```python
import functools

import jax
import jax.numpy as jnp
from jax import lax
from jax.experimental import pallas as pl
from jax.experimental.pallas import tpu as pltpu
from jax.sharding import PartitionSpec as P

ALL_FIELDS = 256
HEAVY_MOST = 4
LANES = 128
SUB = 8
LARGE = 16 << 20

time_step = 0.05
weissenberg = 0.25
max_extension = 50.0
noise_scale = (time_step / weissenberg) ** 0.5
component_pairs = ((0, 0), (1, 1), (2, 2), (0, 1), (0, 2), (1, 2))
moment_of = {(0, 0): 0, (1, 1): 1, (2, 2): 2, (0, 1): 3, (1, 0): 3, (0, 2): 4, (2, 0): 4, (1, 2): 5, (2, 1): 5}
f32 = jnp.float32

smem = pl.BlockSpec(memory_space=pltpu.SMEM)
vmem = pl.BlockSpec(memory_space=pltpu.VMEM)
hbm = pl.BlockSpec(memory_space=pltpu.HBM)


def far_memory(*arrays):
    return [pltpu.with_memory_space_constraint(array, pltpu.HBM) for array in arrays]


def column_sum(value):
    return jnp.sum(value, axis=0, keepdims=True)


def wide(row):
    return jnp.broadcast_to(row, (SUB, LANES))


def turned(value, cell_z):
    sub = lax.broadcasted_iota(jnp.int32, value.shape, 0)
    group = lax.broadcasted_iota(jnp.int32, value.shape, 1) // cell_z
    skewed = pltpu.roll(value, cell_z, 1, stride=cell_z, stride_axis=0)
    mixed = jnp.take_along_axis(skewed, (group + sub) & (SUB - 1), axis=0, mode="promise_in_bounds")
    return pltpu.roll(mixed, 0, 1, stride=cell_z, stride_axis=0)


def relax_of(total, inverse):
    factor = 1.0 / (1.0 - total * inverse / max_extension)
    return 1.0 - (time_step * 0.5 / weissenberg) * factor


def stepped(vectors, noise, matrix):
    return [
        matrix[3 * a] * vectors[0]
        + matrix[3 * a + 1] * vectors[1]
        + matrix[3 * a + 2] * vectors[2]
        + noise_scale * noise[a]
        for a in range(3)
    ]


def with_diagonal(grad, relax):
    return [g + relax if i % 4 == 0 else g for i, g in enumerate(grad)]


def noise_rows(ref, start):
    both = [ref(a, pl.ds(start, 2 * SUB)).astype(f32) for a in range(3)]
    return [[w[:SUB] for w in both], [w[SUB:] for w in both]]


def add_moments(sums, q):
    return [s + q[a] * q[b] for s, (a, b) in zip(sums, component_pairs)]


def owned_slots(tiles, me, helper):
    rank = jnp.int32(0)
    found = []
    for h in range(helper.shape[1]):
        tile = helper[0, h] - me * tiles
        owned = (tile >= 0) & (tile < tiles)
        found.append((h, owned, tile, rank))
        rank = rank + owned.astype(jnp.int32)
    return found


def small(flops, traffic):
    return pl.CostEstimate(flops=flops, bytes_accessed=traffic, transcendentals=0)


def edges(velocity, x_last, x_first, y_last, y_first):
    depth, width = velocity.shape[1:3]
    for a in range(3):
        x_last[a] = velocity[a, depth - 1]
        x_first[a] = velocity[a, 0]
        for x in range(depth):
            y_last[a, pl.ds(x, 1), :] = velocity[a, x, pl.ds(width - 1, 1), :]
            y_first[a, pl.ds(x, 1), :] = velocity[a, x, pl.ds(0, 1), :]


def call_edges(velocity):
    _, depth, width, length = velocity.shape
    along_x = jax.ShapeDtypeStruct((3, width, length), f32)
    along_y = jax.ShapeDtypeStruct((3, depth, length), f32)
    return pl.pallas_call(
        edges,
        out_shape=(along_x, along_x, along_y, along_y),
        in_specs=[vmem],
        out_specs=(vmem,) * 4,
        compiler_params=pltpu.CompilerParams(vmem_limit_bytes=4 << 20),
        cost_estimate=small(1 << 10, 1 << 17),
        name="edges",
    )(velocity)


def heavy_moments(helper, base, noise, out, fields, shocks, sems):
    tiles = base.shape[2]
    me = lax.axis_index("gy")
    groups = fields.shape[2] // (2 * SUB)

    def copies(tile, rank):
        return (
            pltpu.make_async_copy(base.at[0, 0, tile], fields.at[rank], sems.at[0, rank]),
            pltpu.make_async_copy(noise.at[0, 0, tile, 0], shocks.at[rank, 0], sems.at[1, rank]),
        )

    def later(tile, rank):
        return pltpu.make_async_copy(noise.at[0, 0, tile, 1], shocks.at[rank, 1], sems.at[2, rank])

    found = owned_slots(tiles, me, helper)
    for _, owned, tile, rank in found:

        @pl.when(owned)
        def _(tile=tile, rank=rank):
            for copy in copies(tile, rank):
                copy.start()
            later(tile, rank).start()

    for h, owned, tile, rank in found:

        @pl.when(owned)
        def _(h=h, tile=tile, rank=rank):
            for copy in copies(tile, rank):
                copy.wait()

            @pl.loop(0, fields.shape[3] // LANES)
            def _(x):
                lanes = pl.ds(pl.multiple_of(x * LANES, LANES), LANES)
                sums = [jnp.zeros((SUB, LANES), f32)] * 16
                for group in range(groups):
                    pair = noise_rows(lambda a, rows: shocks[rank, 0, a, rows, lanes], group * 2 * SUB)
                    for half in range(2):
                        rows = pl.ds((2 * group + half) * SUB, SUB)
                        q = [fields[rank, a, rows, lanes] for a in range(3)]
                        w = pair[half]
                        terms = [q[a] * q[b] for a, b in component_pairs]
                        terms += [q[a] * w[b] for a in range(3) for b in range(3)]
                        terms += [w[0] * w[0] + w[1] * w[1] + w[2] * w[2]]
                        sums = [s + t for s, t in zip(sums, terms)]
                for i, s in enumerate(sums):
                    out[h, i, pl.ds(x, 1), :] = column_sum(s)

    for _, owned, tile, rank in found:

        @pl.when(owned)
        def _(tile=tile, rank=rank):
            later(tile, rank).wait()


def call_heavy_moments(helper_tile, base_fields, base_noise):
    slots = helper_tile.shape[1]
    _, _, _, _, count, cells = base_fields.shape
    steps = base_noise.shape[3]
    return pl.pallas_call(
        heavy_moments,
        out_shape=(
            jax.ShapeDtypeStruct((slots, 16, cells // LANES, LANES), f32),
            jax.ShapeDtypeStruct((HEAVY_MOST, 3, count, cells), f32),
            jax.ShapeDtypeStruct((HEAVY_MOST, steps, 3, count, cells), jnp.bfloat16),
        ),
        in_specs=[smem, hbm, hbm],
        out_specs=(vmem, vmem, vmem),
        scratch_shapes=[pltpu.SemaphoreType.DMA((3, HEAVY_MOST))],
        compiler_params=pltpu.CompilerParams(vmem_limit_bytes=LARGE),
        cost_estimate=small(8 << 20, 3 << 20),
        name="heavy_moments",
    )(helper_tile, *far_memory(base_fields, base_noise))


def gradients(tiles, helper, velocity, x_low, x_high, y_low, y_high, wall, moments, grad, keep, send):
    me = lax.axis_index("gy")
    depth = velocity.shape[1]
    cell_z = velocity.shape[3] // tiles
    sub = lax.broadcasted_iota(jnp.int32, (SUB, LANES), 0)
    lane = lax.broadcasted_iota(jnp.int32, (SUB, LANES), 1)
    z = lane % cell_z
    scales = [turned(jnp.where(wall[x] == 0, 0.5 * time_step, 0.0).astype(f32), cell_z) for x in range(depth)]
    for a in range(3):
        rows = [x_low[a]] + [velocity[a, x] for x in range(depth)] + [x_high[a]]
        rows = [turned(row, cell_z) for row in rows]
        low, high = turned(y_low[a], cell_z), turned(y_high[a], cell_z)
        for x in range(depth):
            here = rows[x + 1]
            above = high if x == depth - 1 else pltpu.roll(high, LANES - cell_z * (x + 1), 1)
            below = low if x == 0 else pltpu.roll(low, LANES - cell_z * x, 1)
            y_up = jnp.where(lane < LANES - cell_z, pltpu.roll(here, LANES - cell_z, 1), above)
            y_down = jnp.where(lane >= cell_z, pltpu.roll(here, cell_z, 1), below)
            next_tile = pltpu.roll(pltpu.roll(here, cell_z - 1, 1), 1, 0)
            last_tile = pltpu.roll(pltpu.roll(here, LANES - cell_z + 1, 1), SUB - 1, 0)
            next_tile = jnp.where(sub == 0, 0.0, next_tile)
            last_tile = jnp.where(sub == SUB - 1, 0.0, last_tile)
            z_up = jnp.where(z == cell_z - 1, next_tile, pltpu.roll(here, LANES - 1, 1))
            z_down = jnp.where(z == 0, last_tile, pltpu.roll(here, 1, 1))
            for b, difference in enumerate((rows[x + 2] - rows[x], y_up - y_down, z_up - z_down)):
                grad[pl.ds(((3 * a + b) * depth + x) * SUB, SUB), :] = difference * scales[x]
    for h, owned, tile, _ in owned_slots(tiles, me, helper):

        @pl.when(owned)
        def _(h=h, tile=tile):
            g = [grad[pl.ds(i * depth * SUB + SUB - 1 - tile, depth, stride=SUB), :] for i in range(9)]
            m = [moments[h, i] for i in range(16)]
            cross = lambda a, b: m[6 + 3 * a + b]
            square = lambda a, b: m[moment_of[a, b]]
            once, twice, kick = 0.0, 0.0, 0.0
            for a in range(3):
                for b in range(3):
                    once += g[3 * a + b] * square(a, b)
                    kick += g[3 * a + b] * cross(b, a)
                    inner = 0.0
                    for c in range(3):
                        inner += g[3 * a + c] * square(b, c)
                    twice += g[3 * a + b] * inner
            rows = g + [
                twice + (2 * noise_scale) * kick + noise_scale**2 * m[15],
                2.0 * once + (2 * noise_scale) * (cross(0, 0) + cross(1, 1) + cross(2, 2)),
                m[0] + m[1] + m[2],
            ]
            stays = (me & 1) == (h & 1)

            @pl.when(stays)
            def _():
                for i, row in enumerate(rows):
                    keep[h >> 1, i] = row

            @pl.when(jnp.logical_not(stays))
            def _():
                for i, row in enumerate(rows):
                    send[h >> 1, i] = row


def call_gradients(tiles, helper_tile, velocity, halos, wall_cells, moments):
    slots = helper_tile.shape[1]
    depth = velocity.shape[1]
    half = jax.ShapeDtypeStruct((slots // 2, 12, depth, LANES), f32)
    return pl.pallas_call(
        functools.partial(gradients, tiles),
        out_shape=(jax.ShapeDtypeStruct((9 * depth * SUB, LANES), f32), half, half),
        in_specs=[smem] + [vmem] * 7,
        out_specs=(vmem,) * 3,
        compiler_params=pltpu.CompilerParams(vmem_limit_bytes=8 << 20),
        cost_estimate=small(4 << 20, 1 << 20),
        name="gradients",
    )(helper_tile, velocity, *halos, wall_cells, moments)


def swapped(block, bit):
    size = lax.axis_size("gy")
    return lax.ppermute(block, "gy", [(i, i ^ (1 << bit)) for i in range(size)])


def arrived(tiles, me, helper, slot, bit):
    owner = helper[0, slot] // tiles
    return (((owner ^ me) >> bit) & 1) == 1


def merge(tiles, bit, helper, kept, received, keep, send):
    me = lax.axis_index("gy")
    below = me & ((2 << bit) - 1)
    mine = (me >> (bit + 1)) & 1
    for j in range(kept.shape[0]):
        pick = arrived(tiles, me, helper, (j << (bit + 1)) | below, bit)
        stays = mine == (j & 1)
        for source, chosen in ((received, pick), (kept, jnp.logical_not(pick))):
            for out, there in ((keep, stays), (send, jnp.logical_not(stays))):

                @pl.when(chosen & there)
                def _(j=j, source=source, out=out):
                    for i in range(kept.shape[1]):
                        out[j >> 1, i] = source[j, i]


def call_merge(tiles, bit, helper_tile, kept, received):
    half = jax.ShapeDtypeStruct((kept.shape[0] // 2,) + kept.shape[1:], f32)
    return pl.pallas_call(
        functools.partial(merge, tiles, bit),
        out_shape=(half, half),
        in_specs=[smem, vmem, vmem],
        out_specs=(vmem, vmem),
        compiler_params=pltpu.CompilerParams(vmem_limit_bytes=4 << 20),
        cost_estimate=small(1 << 10, 1 << 18),
        name="merge",
    )(helper_tile, kept, received)


def call_join(first, second):
    def join(first, second, out):
        out[: first.shape[0]] = first[...]
        out[first.shape[0] :] = second[...]

    return pl.pallas_call(
        join,
        out_shape=jax.ShapeDtypeStruct((2 * first.shape[0],) + first.shape[1:], f32),
        in_specs=[vmem, vmem],
        out_specs=vmem,
        compiler_params=pltpu.CompilerParams(vmem_limit_bytes=4 << 20),
        cost_estimate=small(1 << 10, 1 << 18),
        name="join",
    )(first, second)


def stress_rows(sums, inverse):
    second = [s * inverse for s in sums]
    stretch = 1.0 / (1.0 - (second[0] + second[1] + second[2]) / max_extension)
    return [(stretch * s - (1.0 if i < 3 else 0.0)) * (1.0 / weissenberg) for i, s in enumerate(second)]


def tile_grad(grad, depth, tile, x):
    return [wide(grad[pl.ds((i * depth + x + 1) * SUB - 1 - tile, 1), :]) for i in range(9)]


def ordinary(counts, base, noise, grad, new_base, stress, fields, shocks, totals, relaxes, sems):
    tiles, _, count, cells = fields.shape
    depth = cells // LANES
    groups = count // (2 * SUB)

    def loads(tile):
        return (
            pltpu.make_async_copy(base.at[0, 0, tile], fields.at[tile], sems.at[0, tile]),
            pltpu.make_async_copy(noise.at[0, 0, tile], shocks.at[tile], sems.at[1, tile]),
        )

    def store(tile):
        return pltpu.make_async_copy(fields.at[tile], new_base.at[0, 0, tile], sems.at[0, tile])

    for tile in range(tiles):

        @pl.when(counts[0, 0, tile] != ALL_FIELDS)
        def _(tile=tile):
            for copy in loads(tile):
                copy.start()

    @pl.loop(0, tiles)
    def _(tile):
        tile_count = counts[0, 0, tile]

        @pl.when(tile_count != ALL_FIELDS)
        def _():
            for copy in loads(tile):
                copy.wait()
            inverse = 1.0 / jnp.full((1, LANES), tile_count.astype(f32))
            for x in range(depth):
                lanes = pl.ds(x * LANES, LANES)
                total = jnp.zeros((SUB, LANES), f32)
                for group in range(2 * groups):
                    for a in range(3):
                        q = fields[tile, a, pl.ds(group * SUB, SUB), lanes]
                        total = total + q * q
                totals[pl.ds(x, 1), :] = column_sum(total)
            for step in range(2):
                relaxes[...] = relax_of(totals[...], inverse)
                for x in range(depth):
                    lanes = pl.ds(x * LANES, LANES)
                    matrix = with_diagonal(tile_grad(grad, depth, tile, x), wide(relaxes[pl.ds(x, 1), :]))
                    sums = [jnp.zeros((SUB, LANES), f32)] * (1 if step == 0 else 6)
                    for group in range(groups):
                        pair = noise_rows(lambda a, rows: shocks[tile, step, a, rows, lanes], group * 2 * SUB)
                        for half in range(2):
                            rows = pl.ds((2 * group + half) * SUB, SUB)
                            q = stepped([fields[tile, a, rows, lanes] for a in range(3)], pair[half], matrix)
                            for a in range(3):
                                fields[tile, a, rows, lanes] = q[a]
                            if step == 0:
                                sums[0] = sums[0] + (q[0] * q[0] + q[1] * q[1] + q[2] * q[2])
                            else:
                                sums = add_moments(sums, q)
                    if step == 0:
                        totals[pl.ds(x, 1), :] = column_sum(sums[0])
                    else:
                        for i, row in enumerate(stress_rows([column_sum(s) for s in sums], inverse)):
                            stress[x, i, pl.ds(tile, 1), :] = row
            store(tile).start()

    for tile in range(tiles):

        @pl.when(counts[0, 0, tile] != ALL_FIELDS)
        def _(tile=tile):
            store(tile).wait()


def call_ordinary(tile_counts, base_fields, base_noise, grad):
    _, _, tiles, _, count, cells = base_fields.shape
    steps = base_noise.shape[3]
    depth = cells // LANES
    return pl.pallas_call(
        ordinary,
        out_shape=(
            jax.ShapeDtypeStruct(base_fields.shape, f32),
            jax.ShapeDtypeStruct((depth, 6, tiles, LANES), f32),
        ),
        in_specs=[smem, hbm, hbm, vmem],
        out_specs=(hbm, vmem),
        scratch_shapes=[
            pltpu.VMEM((tiles, 3, count, cells), f32),
            pltpu.VMEM((tiles, steps, 3, count, cells), jnp.bfloat16),
            pltpu.VMEM((depth, LANES), f32),
            pltpu.VMEM((depth, LANES), f32),
            pltpu.SemaphoreType.DMA((2, tiles)),
        ],
        compiler_params=pltpu.CompilerParams(vmem_limit_bytes=LARGE),
        cost_estimate=small(32 << 20, 10 << 20),
        name="ordinary_tiles",
    )(tile_counts, *far_memory(base_fields, base_noise), grad)


def extra(tiles, bit, rows_each, helper, base, noise, kept, received, new_fields, reply, fields, shocks, message, sems):
    me = lax.axis_index("gy")
    steps, _, count, cells = shocks.shape
    depth = cells // LANES
    pieces = count // rows_each
    groups = count // (2 * SUB)
    inverse = 1.0 / float(ALL_FIELDS)

    def field_load(r):
        rows = pl.ds(r * rows_each, rows_each)
        return pltpu.make_async_copy(base.at[0, 0, :, rows], fields.at[:, rows], sems.at[r])

    def noise_load(step):
        return pltpu.make_async_copy(noise.at[0, 0, step], shocks.at[step], sems.at[pieces + step])

    def store(x):
        lanes = pl.ds(x * LANES, LANES)
        return pltpu.make_async_copy(
            fields.at[:, :, lanes], new_fields.at[0, 0, :, :, lanes], sems.at[pieces + steps + x]
        )

    for r in range(pieces):
        field_load(r).start()
    for step in range(steps):
        noise_load(step).start()
    pick = arrived(tiles, me, helper, me, bit)
    for i in range(message.shape[0]):
        message[i] = jnp.where(pick, received[0, i], kept[0, i])

    def squares(r, totals):
        field_load(r).wait()
        totals = list(totals)
        for x in range(depth):
            for group in range(rows_each // SUB):
                rows = pl.ds(pl.multiple_of(r * rows_each + group * SUB, SUB), SUB)
                for a in range(3):
                    q = fields[a, rows, pl.ds(x * LANES, LANES)]
                    totals[x] = totals[x] + q * q
        return totals

    zero = jnp.zeros((SUB, LANES), f32)
    totals = lax.fori_loop(0, pieces, squares, [zero] * depth)
    for x in range(depth):
        reply[0, pl.ds(x, 1), :] = column_sum(totals[x])
    first = relax_of(reply[0] + message[11], inverse)
    reply[0] = first

    for step in range(2):
        noise_load(step).wait()

        @pl.loop(0, depth)
        def _(x):
            lanes = pl.ds(pl.multiple_of(x * LANES, LANES), LANES)
            grad = [wide(message[i, pl.ds(x, 1), :]) for i in range(9)]
            matrix = with_diagonal(grad, wide(reply[step, pl.ds(x, 1), :]))
            sums = [zero] * (1 if step == 0 else 6)
            for group in range(groups):
                pair = noise_rows(lambda a, rows: shocks[step, a, rows, lanes], group * 2 * SUB)
                for half in range(2):
                    rows = pl.ds((2 * group + half) * SUB, SUB)
                    q = stepped([fields[a, rows, lanes] for a in range(3)], pair[half], matrix)
                    for a in range(3):
                        fields[a, rows, lanes] = q[a]
                    if step == 0:
                        sums[0] = sums[0] + (q[0] * q[0] + q[1] * q[1] + q[2] * q[2])
                    else:
                        sums = add_moments(sums, q)
            if step == 0:
                reply[1, pl.ds(x, 1), :] = column_sum(sums[0])
            else:
                for i, s in enumerate(sums):
                    reply[2 + i, pl.ds(x, 1), :] = column_sum(s)
                store(x).start()

        if step == 0:
            total = reply[1] + (message[9] + first * message[10] + first * first * message[11])
            reply[1] = relax_of(total, inverse)

    for x in range(depth):
        store(x).wait()


def call_extra(tiles, bit, helper_tile, extra_fields, extra_noise, kept, received):
    _, _, _, count, cells = extra_fields.shape
    steps = extra_noise.shape[2]
    depth = cells // LANES
    rows_each = 32
    return pl.pallas_call(
        functools.partial(extra, tiles, bit, rows_each),
        out_shape=(
            jax.ShapeDtypeStruct(extra_fields.shape, f32),
            jax.ShapeDtypeStruct((8, depth, LANES), f32),
        ),
        in_specs=[smem, hbm, hbm, vmem, vmem],
        out_specs=(hbm, vmem),
        scratch_shapes=[
            pltpu.VMEM((3, count, cells), f32),
            pltpu.VMEM((steps, 3, count, cells), jnp.bfloat16),
            pltpu.VMEM(kept.shape[1:], f32),
            pltpu.SemaphoreType.DMA((count // rows_each + steps + depth,)),
        ],
        compiler_params=pltpu.CompilerParams(vmem_limit_bytes=LARGE),
        cost_estimate=small(32 << 20, 9 << 20),
        name="extra_fields",
    )(helper_tile, *far_memory(extra_fields, extra_noise), kept, received)


def heavy(bits, helper, base, noise, grad, near, far, old_base, old_stress, new_base, stress, fields, rows, answer, sems):
    slots = helper.shape[1]
    tiles = old_stress.shape[2]
    me = lax.axis_index("gy")
    _, _, count, cells = base.shape
    depth = cells // LANES
    groups = count // (2 * SUB)

    def store(tile, rank):
        return pltpu.make_async_copy(fields.at[rank], new_base.at[0, 0, tile], sems.at[rank])

    rows[...] = old_stress[...]
    found = owned_slots(tiles, me, helper)
    for h, owned, tile, rank in found:

        @pl.when(owned)
        def _(h=h, tile=tile, rank=rank):
            flips = me ^ h
            place = sum(((flips >> (bits - 1 - i)) & 1) << i for i in range(bits))
            is_far = place >= slots // 2
            place = place & (slots // 2 - 1)
            for i in range(near.shape[1]):
                answer[i] = jnp.where(is_far, far[place, i], near[place, i])

            @pl.loop(0, depth)
            def _(x):
                lanes = pl.ds(pl.multiple_of(x * LANES, LANES), LANES)
                g = tile_grad(grad, depth, tile, x)
                matrices = [with_diagonal(g, wide(answer[s, pl.ds(x, 1), :])) for s in range(2)]
                sums = [jnp.zeros((SUB, LANES), f32)] * 6
                for group in range(groups):
                    pairs = [
                        noise_rows(lambda a, r: noise[rank, s, a, r, lanes], group * 2 * SUB) for s in range(2)
                    ]
                    for half in range(2):
                        part = pl.ds((2 * group + half) * SUB, SUB)
                        q = [base[rank, a, part, lanes] for a in range(3)]
                        for s in range(2):
                            q = stepped(q, pairs[s][half], matrices[s])
                        for a in range(3):
                            fields[rank, a, part, lanes] = q[a]
                        sums = add_moments(sums, q)
                sums = [column_sum(s) + answer[2 + i, pl.ds(x, 1), :] for i, s in enumerate(sums)]
                for i, row in enumerate(stress_rows(sums, 1.0 / float(ALL_FIELDS))):
                    rows[x, i, pl.ds(tile, 1), :] = row

            store(tile, rank).start()

    def result(x):
        target = stress.at[0, 0, :, :, pl.ds(x * LANES, LANES)]
        return pltpu.make_async_copy(rows.at[x], target, sems.at[HEAVY_MOST + x])

    for x in range(depth):
        result(x).start()
    for _, owned, tile, rank in found:

        @pl.when(owned)
        def _(tile=tile, rank=rank):
            store(tile, rank).wait()

    for x in range(depth):
        result(x).wait()


def call_heavy(bits, helper_tile, held, held_noise, grad, near, far, new_base, stress):
    depth, _, tiles, _ = stress.shape
    return pl.pallas_call(
        functools.partial(heavy, bits),
        out_shape=(
            jax.ShapeDtypeStruct(new_base.shape, f32),
            jax.ShapeDtypeStruct((1, 1, 6, tiles, depth * LANES), f32),
        ),
        in_specs=[smem, vmem, vmem, vmem, vmem, vmem, hbm, vmem],
        out_specs=(hbm, hbm),
        input_output_aliases={6: 0},
        scratch_shapes=[
            pltpu.VMEM(held.shape, f32),
            pltpu.VMEM(stress.shape, f32),
            pltpu.VMEM(near.shape[1:], f32),
            pltpu.SemaphoreType.DMA((HEAVY_MOST + depth,)),
        ],
        compiler_params=pltpu.CompilerParams(vmem_limit_bytes=LARGE),
        cost_estimate=small(8 << 20, 4 << 20),
        name="heavy_tiles",
    )(helper_tile, held, held_noise, grad, near, far, new_base, stress)


def both_ways(last, first, axis):
    size = lax.axis_size(axis)
    up = [(i, i + 1) for i in range(size - 1)]
    down = [(i + 1, i) for i in range(size - 1)]
    return lax.ppermute(last, axis, up), lax.ppermute(first, axis, down)


def per_device(
    velocity, wall_cells, tile_counts, helper_tile, base_fields, extra_fields, base_noise, extra_noise
):
    tiles = tile_counts.shape[2]
    bits = lax.axis_size("gy").bit_length() - 1
    x_last, x_first, y_last, y_first = call_edges(velocity)
    halos = both_ways(x_last, x_first, "gx") + both_ways(y_last, y_first, "gy")
    moments, held, held_noise = call_heavy_moments(helper_tile, base_fields, base_noise)
    grad, keep, send = call_gradients(tiles, helper_tile, velocity, halos, wall_cells, moments)
    received = swapped(send, 0)
    for bit in range(bits - 1):
        keep, send = call_merge(tiles, bit, helper_tile, keep, received)
        received = swapped(send, bit + 1)
    new_base, stress = call_ordinary(tile_counts, base_fields, base_noise, grad)
    new_extra, reply = call_extra(tiles, bits - 1, helper_tile, extra_fields, extra_noise, keep, received)
    near = reply[None]
    for bit in range(bits - 1, 0, -1):
        near = call_join(near, swapped(near, bit))
    far = swapped(near, 0)
    new_base, stress = call_heavy(bits, helper_tile, held, held_noise, grad, near, far, new_base, stress)
    return new_base, new_extra, jnp.swapaxes(stress, 2, 3)


def solution(mesh):
    in_specs = (
        P(None, "gx", "gy", None),
        P("gx", "gy", None),
        P("gx", "gy", None),
        P("gx", None),
        P("gx", "gy", None, None, None, None),
        P("gx", "gy", None, None, None),
        P("gx", "gy", None, None, None, None, None),
        P("gx", "gy", None, None, None, None),
    )
    out_specs = (
        P("gx", "gy", None, None, None, None),
        P("gx", "gy", None, None, None),
        P("gx", "gy", None, None, None),
    )
    return jax.shard_map(
        per_device, mesh=mesh, in_specs=in_specs, out_specs=out_specs, check_vma=False
    )
```

```python
import functools

import jax
import jax.numpy as jnp
from jax import lax
from jax.experimental import pallas as pl
from jax.experimental.pallas import tpu as pltpu
from jax.sharding import PartitionSpec as P

ALL_FIELDS = 256
LANES = 128
SUB = 8
SMALL = 10 << 20
LARGE = 14 << 20

time_step = 0.05
weissenberg = 0.25
max_extension = 50.0
noise_scale = (time_step / weissenberg) ** 0.5
component_pairs = ((0, 0), (1, 1), (2, 2), (0, 1), (0, 2), (1, 2))
moment_of = {(0, 0): 0, (1, 1): 1, (2, 2): 2, (0, 1): 3, (1, 0): 3, (0, 2): 4, (2, 0): 4, (1, 2): 5, (2, 1): 5}
f32 = jnp.float32

smem = pl.BlockSpec(memory_space=pltpu.SMEM)
vmem = pl.BlockSpec(memory_space=pltpu.VMEM)
hbm = pl.BlockSpec(memory_space=pltpu.HBM)
anywhere = pl.BlockSpec(memory_space=pl.ANY)


def far_memory(*arrays):
    return [pltpu.with_memory_space_constraint(array, pltpu.HBM) for array in arrays]


def near_memory(*arrays):
    return [pltpu.with_memory_space_constraint(array, pltpu.VMEM) for array in arrays]


def column_sum(value):
    return jnp.sum(value, axis=0, keepdims=True)


def wide(row):
    return jnp.broadcast_to(row, (SUB, LANES))


def turned(value, cell_z):
    sub = lax.broadcasted_iota(jnp.int32, value.shape, 0)
    group = lax.broadcasted_iota(jnp.int32, value.shape, 1) // cell_z
    skewed = pltpu.roll(value, cell_z, 1, stride=cell_z, stride_axis=0)
    mixed = jnp.take_along_axis(skewed, (group + sub) & (SUB - 1), axis=0, mode="promise_in_bounds")
    return pltpu.roll(mixed, 0, 1, stride=cell_z, stride_axis=0)


def relax_of(total, inverse):
    factor = 1.0 / (1.0 - total * inverse / max_extension)
    return 1.0 - (time_step * 0.5 / weissenberg) * factor


def stepped(vectors, noise, matrix):
    return [
        matrix[3 * a] * vectors[0]
        + matrix[3 * a + 1] * vectors[1]
        + matrix[3 * a + 2] * vectors[2]
        + noise_scale * noise[a]
        for a in range(3)
    ]


def with_diagonal(grad, relax):
    return [g + relax if i % 4 == 0 else g for i, g in enumerate(grad)]


def noise_rows(ref, start):
    both = [ref(a, pl.ds(start, 2 * SUB)).astype(f32) for a in range(3)]
    return [[w[:SUB] for w in both], [w[SUB:] for w in both]]


def add_moments(sums, q):
    return [s + q[a] * q[b] for s, (a, b) in zip(sums, component_pairs)]


def product_sums(sums, q, w):
    terms = [q[a] * q[b] for a, b in component_pairs]
    terms += [q[a] * w[b] for a in range(3) for b in range(3)]
    terms += [w[0] * w[0] + w[1] * w[1] + w[2] * w[2]]
    return [s + t for s, t in zip(sums, terms)]


def coefficients(g, m):
    cross = lambda a, b: m[6 + 3 * a + b]
    square = lambda a, b: m[moment_of[a, b]]
    once, twice, kick = 0.0, 0.0, 0.0
    for a in range(3):
        for b in range(3):
            once += g[3 * a + b] * square(a, b)
            kick += g[3 * a + b] * cross(b, a)
            inner = 0.0
            for c in range(3):
                inner += g[3 * a + c] * square(b, c)
            twice += g[3 * a + b] * inner
    return [
        twice + (2 * noise_scale) * kick + noise_scale**2 * m[15],
        2.0 * once + (2 * noise_scale) * (cross(0, 0) + cross(1, 1) + cross(2, 2)),
        m[0] + m[1] + m[2],
    ]


def owned_slots(tiles, me, helper):
    found = []
    for h in range(helper.shape[1]):
        tile = helper[0, h] - me * tiles
        found.append((h, (tile >= 0) & (tile < tiles), tile))
    return found


def small(flops, traffic):
    return pl.CostEstimate(flops=flops, bytes_accessed=traffic, transcendentals=0)


def edges(helper, velocity, x_last, x_first, y_last, y_first):
    depth, width = velocity.shape[1:3]
    for a in range(3):
        x_last[a] = velocity[a, depth - 1]
        x_first[a] = velocity[a, 0]
        for x in range(depth):
            y_last[a, pl.ds(x, 1), :] = velocity[a, x, pl.ds(width - 1, 1), :]
            y_first[a, pl.ds(x, 1), :] = velocity[a, x, pl.ds(0, 1), :]


def call_edges(helper_tile, velocity):
    _, depth, width, length = velocity.shape
    along_x = jax.ShapeDtypeStruct((3, width, length), f32)
    along_y = jax.ShapeDtypeStruct((3, depth, length), f32)
    return pl.pallas_call(
        edges,
        out_shape=(along_x, along_x, along_y, along_y),
        in_specs=[smem, vmem],
        out_specs=(vmem,) * 4,
        compiler_params=pltpu.CompilerParams(vmem_limit_bytes=4 << 20),
        cost_estimate=small(1 << 10, 1 << 17),
        name="edges",
    )(helper_tile, velocity)


def heavy_moments(helper, base, noise, out, fields, shocks, sems):
    slots, _, count, cells = fields.shape
    tiles = base.shape[2]
    me = lax.axis_index("gy")

    def loads(h, tile):
        return (
            pltpu.make_async_copy(base.at[0, 0, tile], fields.at[h], sems.at[0, h]),
            pltpu.make_async_copy(noise.at[0, 0, tile, 0], shocks.at[h], sems.at[1, h]),
        )

    found = owned_slots(tiles, me, helper)
    for h, owned, tile in found:

        @pl.when(owned)
        def _(h=h, tile=tile):
            for copy in loads(h, tile):
                copy.start()

    for h, owned, tile in found:

        @pl.when(owned)
        def _(h=h, tile=tile):
            for copy in loads(h, tile):
                copy.wait()

            @pl.loop(0, cells // LANES)
            def _(x):
                lanes = pl.ds(pl.multiple_of(x * LANES, LANES), LANES)
                sums = [jnp.zeros((SUB, LANES), f32)] * 16
                for group in range(count // (2 * SUB)):
                    pair = noise_rows(lambda a, rows: shocks[h, a, rows, lanes], group * 2 * SUB)
                    for half in range(2):
                        rows = pl.ds((2 * group + half) * SUB, SUB)
                        sums = product_sums(sums, [fields[h, a, rows, lanes] for a in range(3)], pair[half])
                for i, s in enumerate(sums):
                    out[h, i, pl.ds(x, 1), :] = column_sum(s)


def call_heavy_moments(helper_tile, base_fields, base_noise):
    slots = helper_tile.shape[1]
    count, cells = base_fields.shape[-2:]
    return pl.pallas_call(
        heavy_moments,
        out_shape=jax.ShapeDtypeStruct((slots, 16, cells // LANES, LANES), f32),
        in_specs=[smem, hbm, hbm],
        out_specs=vmem,
        scratch_shapes=[
            pltpu.VMEM((slots, 3, count, cells), f32),
            pltpu.VMEM((slots, 3, count, cells), jnp.bfloat16),
            pltpu.SemaphoreType.DMA((2, slots)),
        ],
        compiler_params=pltpu.CompilerParams(vmem_limit_bytes=LARGE),
        cost_estimate=small(8 << 20, 3 << 20),
        name="heavy_moments",
    )(helper_tile, *far_memory(base_fields, base_noise))


def extra_moments(unroll, before, base, noise, out):
    _, _, _, count, cells = base.shape
    zero = jnp.zeros((SUB, LANES), f32)

    @pl.loop(0, cells // LANES)
    def _(x):
        lanes = pl.ds(pl.multiple_of(x * LANES, LANES), LANES)

        def body(i, sums):
            start = pl.multiple_of(i * 2 * SUB, 2 * SUB)
            pair = noise_rows(lambda a, rows: noise[0, 0, 0, a, rows, lanes], start)
            for half in range(2):
                rows = pl.ds(start + half * SUB, SUB)
                sums = product_sums(sums, [base[0, 0, a, rows, lanes] for a in range(3)], pair[half])
            return sums

        for i, s in enumerate(lax.fori_loop(0, count // (2 * SUB), body, [zero] * 16, unroll=unroll)):
            out[i, pl.ds(x, 1), :] = column_sum(s)


def call_extra_moments(before, extra_fields, extra_noise):
    cells = extra_fields.shape[-1]
    return pl.pallas_call(
        functools.partial(extra_moments, 7),
        out_shape=jax.ShapeDtypeStruct((16, cells // LANES, LANES), f32),
        in_specs=[anywhere, vmem, vmem],
        out_specs=vmem,
        compiler_params=pltpu.CompilerParams(vmem_limit_bytes=SMALL),
        cost_estimate=small(8 << 20, 5 << 20),
        name="extra_moments",
    )(before, *near_memory(extra_fields, extra_noise))


def gradients(tiles, helper, velocity, x_low, x_high, y_low, y_high, wall, moments, grad, keep, send):
    me = lax.axis_index("gy")
    depth = velocity.shape[1]
    cell_z = velocity.shape[3] // tiles
    sub = lax.broadcasted_iota(jnp.int32, (SUB, LANES), 0)
    lane = lax.broadcasted_iota(jnp.int32, (SUB, LANES), 1)
    z = lane % cell_z
    scales = [turned(jnp.where(wall[x] == 0, 0.5 * time_step, 0.0).astype(f32), cell_z) for x in range(depth)]
    for a in range(3):
        rows = [x_low[a]] + [velocity[a, x] for x in range(depth)] + [x_high[a]]
        rows = [turned(row, cell_z) for row in rows]
        low, high = turned(y_low[a], cell_z), turned(y_high[a], cell_z)
        for x in range(depth):
            here = rows[x + 1]
            above = high if x == depth - 1 else pltpu.roll(high, LANES - cell_z * (x + 1), 1)
            below = low if x == 0 else pltpu.roll(low, LANES - cell_z * x, 1)
            y_up = jnp.where(lane < LANES - cell_z, pltpu.roll(here, LANES - cell_z, 1), above)
            y_down = jnp.where(lane >= cell_z, pltpu.roll(here, cell_z, 1), below)
            next_tile = pltpu.roll(pltpu.roll(here, cell_z - 1, 1), 1, 0)
            last_tile = pltpu.roll(pltpu.roll(here, LANES - cell_z + 1, 1), SUB - 1, 0)
            next_tile = jnp.where(sub == 0, 0.0, next_tile)
            last_tile = jnp.where(sub == SUB - 1, 0.0, last_tile)
            z_up = jnp.where(z == cell_z - 1, next_tile, pltpu.roll(here, LANES - 1, 1))
            z_down = jnp.where(z == 0, last_tile, pltpu.roll(here, 1, 1))
            for b, difference in enumerate((rows[x + 2] - rows[x], y_up - y_down, z_up - z_down)):
                grad[pl.ds(((3 * a + b) * depth + x) * SUB, SUB), :] = difference * scales[x]
    for h, owned, tile in owned_slots(tiles, me, helper):

        @pl.when(owned)
        def _(h=h, tile=tile):
            g = [grad[pl.ds(i * depth * SUB + SUB - 1 - tile, depth, stride=SUB), :] for i in range(9)]
            rows = g + coefficients(g, [moments[h, i] for i in range(16)])
            stays = (me & 1) == (h & 1)

            @pl.when(stays)
            def _():
                for i, row in enumerate(rows):
                    keep[h >> 1, i] = row

            @pl.when(jnp.logical_not(stays))
            def _():
                for i, row in enumerate(rows):
                    send[h >> 1, i] = row


def call_gradients(tiles, helper_tile, velocity, halos, wall_cells, moments):
    slots = helper_tile.shape[1]
    depth = velocity.shape[1]
    half = jax.ShapeDtypeStruct((slots // 2, 12, depth, LANES), f32)
    return pl.pallas_call(
        functools.partial(gradients, tiles),
        out_shape=(jax.ShapeDtypeStruct((9 * depth * SUB, LANES), f32), half, half),
        in_specs=[smem] + [vmem] * 7,
        out_specs=(vmem,) * 3,
        compiler_params=pltpu.CompilerParams(vmem_limit_bytes=8 << 20),
        cost_estimate=small(4 << 20, 1 << 20),
        name="gradients",
    )(helper_tile, velocity, *halos, wall_cells, moments)


def swapped(block, bit):
    size = lax.axis_size("gy")
    return lax.ppermute(block, "gy", [(i, i ^ (1 << bit)) for i in range(size)])


def arrived(tiles, me, helper, slot, bit):
    owner = helper[0, slot] // tiles
    return (((owner ^ me) >> bit) & 1) == 1


def merge(tiles, bit, helper, before, kept, received, keep, send):
    me = lax.axis_index("gy")
    below = me & ((2 << bit) - 1)
    mine = (me >> (bit + 1)) & 1
    for j in range(kept.shape[0]):
        pick = arrived(tiles, me, helper, (j << (bit + 1)) | below, bit)
        stays = mine == (j & 1)
        for source, chosen in ((received, pick), (kept, jnp.logical_not(pick))):
            for out, there in ((keep, stays), (send, jnp.logical_not(stays))):

                @pl.when(chosen & there)
                def _(j=j, source=source, out=out):
                    for i in range(kept.shape[1]):
                        out[j >> 1, i] = source[j, i]


def call_merge(tiles, bit, helper_tile, before, kept, received):
    half = jax.ShapeDtypeStruct((kept.shape[0] // 2,) + kept.shape[1:], f32)
    return pl.pallas_call(
        functools.partial(merge, tiles, bit),
        out_shape=(half, half),
        in_specs=[smem, anywhere, vmem, vmem],
        out_specs=(vmem, vmem),
        compiler_params=pltpu.CompilerParams(vmem_limit_bytes=4 << 20),
        cost_estimate=small(1 << 10, 1 << 18),
        name="merge",
    )(helper_tile, before, kept, received)


def call_join(before, first, second):
    def join(before, first, second, out):
        out[: first.shape[0]] = first[...]
        out[first.shape[0] :] = second[...]

    return pl.pallas_call(
        join,
        out_shape=jax.ShapeDtypeStruct((2 * first.shape[0],) + first.shape[1:], f32),
        in_specs=[anywhere, vmem, vmem],
        out_specs=vmem,
        compiler_params=pltpu.CompilerParams(vmem_limit_bytes=4 << 20),
        cost_estimate=small(1 << 10, 1 << 18),
        name="join",
    )(before, first, second)


def stress_rows(sums, inverse):
    second = [s * inverse for s in sums]
    stretch = 1.0 / (1.0 - (second[0] + second[1] + second[2]) / max_extension)
    return [(stretch * s - (1.0 if i < 3 else 0.0)) * (1.0 / weissenberg) for i, s in enumerate(second)]


def tile_grad(grad, depth, tile, x):
    return [wide(grad[pl.ds((i * depth + x + 1) * SUB - 1 - tile, 1), :]) for i in range(9)]


def ordinary(first, counts, before, base, noise, grad, old_base, new_base, stress, halfway, fields, totals, relaxes, sems):
    here, _, count, cells = fields.shape
    depth = cells // LANES
    groups = count // (2 * SUB)
    zero = jnp.zeros((SUB, LANES), f32)

    def store(place):
        return pltpu.make_async_copy(fields.at[place], new_base.at[0, 0, first + place], sems.at[place])

    for place in range(here):
        tile = first + place
        tile_count = counts[0, 0, tile]

        @pl.when(tile_count != ALL_FIELDS)
        def _(place=place, tile=tile, tile_count=tile_count):
            inverse = 1.0 / jnp.full((1, LANES), tile_count.astype(f32))
            for x in range(depth):
                total = zero
                for group in range(2 * groups):
                    for a in range(3):
                        q = base[0, 0, tile, a, pl.ds(group * SUB, SUB), pl.ds(x * LANES, LANES)]
                        total = total + q * q
                totals[pl.ds(x, 1), :] = column_sum(total)
            for step in range(2):
                relaxes[...] = relax_of(totals[...], inverse)

                def body(x, step=step):
                    lanes = pl.ds(pl.multiple_of(x * LANES, LANES), LANES)
                    matrix = with_diagonal(tile_grad(grad, depth, tile, x), wide(relaxes[pl.ds(x, 1), :]))
                    sums = [zero] * (1 if step == 0 else 6)
                    for group in range(groups):
                        pair = noise_rows(lambda a, rows: noise[0, 0, tile, step, a, rows, lanes], group * 2 * SUB)
                        for half in range(2):
                            rows = pl.ds((2 * group + half) * SUB, SUB)
                            if step == 0:
                                q = [base[0, 0, tile, a, rows, lanes] for a in range(3)]
                            else:
                                q = [halfway[a, rows, lanes] for a in range(3)]
                            q = stepped(q, pair[half], matrix)
                            for a in range(3):
                                if step == 0:
                                    halfway[a, rows, lanes] = q[a]
                                else:
                                    fields[place, a, rows, lanes] = q[a]
                            if step == 0:
                                sums[0] = sums[0] + (q[0] * q[0] + q[1] * q[1] + q[2] * q[2])
                            else:
                                sums = add_moments(sums, q)
                    if step == 0:
                        totals[pl.ds(x, 1), :] = column_sum(sums[0])
                    else:
                        for i, row in enumerate(stress_rows([column_sum(s) for s in sums], inverse)):
                            stress[x, i, pl.ds(place, 1), :] = row

                @pl.loop(0, depth // 2)
                def _(x):
                    body(2 * x)
                    body(2 * x + 1)

            store(place).start()

    for place in range(here):

        @pl.when(counts[0, 0, first + place] != ALL_FIELDS)
        def _(place=place):
            store(place).wait()


def call_ordinary(first, here, tile_counts, before, base_fields, base_noise, grad, new_base):
    count, cells = base_fields.shape[-2:]
    depth = cells // LANES
    body = functools.partial(ordinary, first)
    if new_base is None:
        body = lambda *refs: ordinary(first, *refs[:5], None, *refs[5:])
    return pl.pallas_call(
        body,
        out_shape=(
            jax.ShapeDtypeStruct(base_fields.shape, f32),
            jax.ShapeDtypeStruct((depth, 6, here, LANES), f32),
        ),
        in_specs=[smem, anywhere, vmem, vmem, vmem] + [hbm] * (new_base is not None),
        out_specs=(hbm, vmem),
        input_output_aliases={} if new_base is None else {5: 0},
        scratch_shapes=[
            pltpu.VMEM((3, count, cells), f32),
            pltpu.VMEM((here, 3, count, cells), f32),
            pltpu.VMEM((depth, LANES), f32),
            pltpu.VMEM((depth, LANES), f32),
            pltpu.SemaphoreType.DMA((here,)),
        ],
        compiler_params=pltpu.CompilerParams(vmem_limit_bytes=SMALL),
        cost_estimate=small(8 << 20, 3 << 20),
        name="ordinary_tiles",
    )(tile_counts, before, *near_memory(base_fields, base_noise), grad, *([] if new_base is None else [new_base]))


def extra(tiles, bit, unroll, helper, base, noise, moments, kept, received, new_fields, reply, message):
    me = lax.axis_index("gy")
    _, _, _, count, cells = base.shape
    inverse = 1.0 / float(ALL_FIELDS)
    zero = jnp.zeros((SUB, LANES), f32)
    pick = arrived(tiles, me, helper, me, bit)
    for i in range(message.shape[0]):
        message[i] = jnp.where(pick, received[0, i], kept[0, i])
    own = coefficients([message[i] for i in range(9)], [moments[i] for i in range(16)])
    both = [message[9 + i] + own[i] for i in range(3)]
    first = relax_of(both[2], inverse)
    second = relax_of(both[0] + first * (both[1] + first * both[2]), inverse)
    reply[0], reply[1] = first, second

    @pl.loop(0, cells // LANES)
    def _(x):
        lanes = pl.ds(pl.multiple_of(x * LANES, LANES), LANES)
        grad = [wide(message[i, pl.ds(x, 1), :]) for i in range(9)]
        matrices = [with_diagonal(grad, wide(reply[step, pl.ds(x, 1), :])) for step in range(2)]

        def body(i, sums):
            start = pl.multiple_of(i * 2 * SUB, 2 * SUB)
            pairs = [noise_rows(lambda a, rows: noise[0, 0, step, a, rows, lanes], start) for step in range(2)]
            for half in range(2):
                rows = pl.ds(start + half * SUB, SUB)
                q = [base[0, 0, a, rows, lanes] for a in range(3)]
                for step in range(2):
                    q = stepped(q, pairs[step][half], matrices[step])
                for a in range(3):
                    new_fields[0, 0, a, rows, lanes] = q[a]
                sums = add_moments(sums, q)
            return sums

        for i, s in enumerate(lax.fori_loop(0, count // (2 * SUB), body, [zero] * 6, unroll=unroll)):
            reply[2 + i, pl.ds(x, 1), :] = column_sum(s)


def call_extra(tiles, bit, helper_tile, extra_fields, extra_noise, moments, kept, received):
    depth = extra_fields.shape[-1] // LANES
    return pl.pallas_call(
        functools.partial(extra, tiles, bit, 7),
        out_shape=(
            pltpu.VMEM(extra_fields.shape, f32),
            jax.ShapeDtypeStruct((8, depth, LANES), f32),
        ),
        in_specs=[smem, vmem, vmem, vmem, vmem, vmem],
        out_specs=(vmem, vmem),
        scratch_shapes=[pltpu.VMEM(kept.shape[1:], f32)],
        compiler_params=pltpu.CompilerParams(vmem_limit_bytes=SMALL),
        cost_estimate=small(32 << 20, 9 << 20),
        name="extra_fields",
    )(helper_tile, *near_memory(extra_fields, extra_noise), moments, kept, received)


def heavy(bits, piece_count, helper, base, noise, grad, near, far, *refs):
    pieces, (_, new_base, stress, fields, rows, answer, sems) = refs[:piece_count], refs[piece_count:]
    _, _, tiles, _, count, cells = base.shape
    slots = helper.shape[1]
    me = lax.axis_index("gy")
    depth = cells // LANES
    groups = count // (2 * SUB)

    def store(h, tile):
        return pltpu.make_async_copy(fields.at[h], new_base.at[0, 0, tile], sems.at[h])

    def result(x):
        target = stress.at[0, 0, :, :, pl.ds(x * LANES, LANES)]
        return pltpu.make_async_copy(rows.at[x], target, sems.at[slots + x])

    at = 0
    for piece in pieces:
        rows[:, :, at : at + piece.shape[2], :] = piece[...]
        at += piece.shape[2]
    found = owned_slots(tiles, me, helper)
    for h, owned, tile in found:

        @pl.when(owned)
        def _(h=h, tile=tile):
            flips = me ^ h
            place = sum(((flips >> (bits - 1 - i)) & 1) << i for i in range(bits))
            is_far = place >= slots // 2
            place = place & (slots // 2 - 1)
            for i in range(near.shape[1]):
                answer[i] = jnp.where(is_far, far[place, i], near[place, i])

            def body(x):
                lanes = pl.ds(pl.multiple_of(x * LANES, LANES), LANES)
                g = tile_grad(grad, depth, tile, x)
                matrices = [with_diagonal(g, wide(answer[s, pl.ds(x, 1), :])) for s in range(2)]
                sums = [jnp.zeros((SUB, LANES), f32)] * 6
                for group in range(groups):
                    pairs = [
                        noise_rows(lambda a, r: noise[0, 0, tile, s, a, r, lanes], group * 2 * SUB) for s in range(2)
                    ]
                    for half in range(2):
                        part = pl.ds((2 * group + half) * SUB, SUB)
                        q = [base[0, 0, tile, a, part, lanes] for a in range(3)]
                        for s in range(2):
                            q = stepped(q, pairs[s][half], matrices[s])
                        for a in range(3):
                            fields[h, a, part, lanes] = q[a]
                        sums = add_moments(sums, q)
                sums = [column_sum(s) + answer[2 + i, pl.ds(x, 1), :] for i, s in enumerate(sums)]
                for i, row in enumerate(stress_rows(sums, 1.0 / float(ALL_FIELDS))):
                    rows[x, i, pl.ds(tile, 1), :] = row

            @pl.loop(0, depth // 2)
            def _(x):
                body(2 * x)
                body(2 * x + 1)

            store(h, tile).start()

    for x in range(depth):
        result(x).start()
    for h, owned, tile in found:

        @pl.when(owned)
        def _(h=h, tile=tile):
            store(h, tile).wait()

    for x in range(depth):
        result(x).wait()


def call_heavy(bits, helper_tile, base_fields, base_noise, grad, near, far, pieces, new_base):
    _, _, tiles, _, count, cells = base_fields.shape
    depth = cells // LANES
    slots = helper_tile.shape[1]
    return pl.pallas_call(
        functools.partial(heavy, bits, len(pieces)),
        out_shape=(
            jax.ShapeDtypeStruct(new_base.shape, f32),
            jax.ShapeDtypeStruct((1, 1, 6, tiles, cells), f32),
        ),
        in_specs=[smem] + [vmem] * (5 + len(pieces)) + [hbm],
        out_specs=(hbm, hbm),
        input_output_aliases={6 + len(pieces): 0},
        scratch_shapes=[
            pltpu.VMEM((slots, 3, count, cells), f32),
            pltpu.VMEM((depth, 6, tiles, LANES), f32),
            pltpu.VMEM(near.shape[1:], f32),
            pltpu.SemaphoreType.DMA((slots + depth,)),
        ],
        compiler_params=pltpu.CompilerParams(vmem_limit_bytes=SMALL),
        cost_estimate=small(8 << 20, 4 << 20),
        name="heavy_tiles",
    )(helper_tile, *near_memory(base_fields, base_noise), grad, near, far, *pieces, new_base)


def both_ways(last, first, axis):
    size = lax.axis_size(axis)
    up = [(i, i + 1) for i in range(size - 1)]
    down = [(i + 1, i) for i in range(size - 1)]
    return lax.ppermute(last, axis, up), lax.ppermute(first, axis, down)


def per_device(
    velocity, wall_cells, tile_counts, helper_tile, base_fields, extra_fields, base_noise, extra_noise
):
    tiles = tile_counts.shape[2]
    bits = lax.axis_size("gy").bit_length() - 1
    x_last, x_first, y_last, y_first = call_edges(helper_tile, velocity)
    halos = both_ways(x_last, x_first, "gx") + both_ways(y_last, y_first, "gy")
    moments = call_heavy_moments(helper_tile, base_fields, base_noise)
    grad, keep, send = call_gradients(tiles, helper_tile, velocity, halos, wall_cells, moments)
    gaps = 2 * bits - 2
    new_base, pieces, done = None, [], 0

    def fill(before):
        nonlocal new_base, done
        here = (tiles - done) // (gaps - len(pieces))
        new_base, piece = call_ordinary(done, here, tile_counts, before, base_fields, base_noise, grad, new_base)
        pieces.append(piece)
        done += here
        return piece

    for bit in range(bits):
        received = swapped(send, bit)
        if bit == 1:
            before = extra_sums = call_extra_moments(send, extra_fields, extra_noise)
        else:
            before = fill(send)
        if bit < bits - 1:
            keep, send = call_merge(tiles, bit, helper_tile, before, keep, received)
    new_extra, reply = call_extra(tiles, bits - 1, helper_tile, extra_fields, extra_noise, extra_sums, keep, received)
    near = reply[None]
    for bit in range(bits - 1, 0, -1):
        received = swapped(near, bit)
        near = call_join(fill(near), near, received)
    far = swapped(near, 0)
    new_base, stress = call_heavy(bits, helper_tile, base_fields, base_noise, grad, near, far, pieces, new_base)
    return new_base, new_extra, jnp.swapaxes(stress, 2, 3)


def solution(mesh):
    in_specs = (
        P(None, "gx", "gy", None),
        P("gx", "gy", None),
        P("gx", "gy", None),
        P("gx", None),
        P("gx", "gy", None, None, None, None),
        P("gx", "gy", None, None, None),
        P("gx", "gy", None, None, None, None, None),
        P("gx", "gy", None, None, None, None),
    )
    out_specs = (
        P("gx", "gy", None, None, None, None),
        P("gx", "gy", None, None, None),
        P("gx", "gy", None, None, None),
    )
    return jax.shard_map(
        per_device, mesh=mesh, in_specs=in_specs, out_specs=out_specs, check_vma=False
    )
```

```python
import functools

import jax
import jax.numpy as jnp
from jax import lax
from jax.experimental import pallas as pl
from jax.experimental.pallas import tpu as pltpu
from jax.sharding import PartitionSpec as P

ALL_FIELDS = 256
LANES = 128
SUB = 8
SMALL = 10 << 20
LARGE = 14 << 20

time_step = 0.05
weissenberg = 0.25
max_extension = 50.0
noise_scale = (time_step / weissenberg) ** 0.5
component_pairs = ((0, 0), (1, 1), (2, 2), (0, 1), (0, 2), (1, 2))
moment_of = {(0, 0): 0, (1, 1): 1, (2, 2): 2, (0, 1): 3, (1, 0): 3, (0, 2): 4, (2, 0): 4, (1, 2): 5, (2, 1): 5}
f32 = jnp.float32

smem = pl.BlockSpec(memory_space=pltpu.SMEM)
vmem = pl.BlockSpec(memory_space=pltpu.VMEM)
hbm = pl.BlockSpec(memory_space=pltpu.HBM)
anywhere = pl.BlockSpec(memory_space=pl.ANY)


def far_memory(*arrays):
    return [pltpu.with_memory_space_constraint(array, pltpu.HBM) for array in arrays]


def near_memory(*arrays):
    return [pltpu.with_memory_space_constraint(array, pltpu.VMEM) for array in arrays]


def column_sum(value):
    return jnp.sum(value, axis=0, keepdims=True)


def packed_sum(values):
    sub = lax.broadcasted_iota(jnp.int32, (SUB, LANES), 0)
    bit = 1
    while len(values) > 1:
        low = (sub & bit) == 0
        values = [
            jnp.where(low, a, b) + pltpu.roll(jnp.where(low, b, a), bit, 0)
            for a, b in zip(values[0::2], values[1::2])
        ]
        bit *= 2
    return values[0]


def wide(row):
    return jnp.broadcast_to(row, (SUB, LANES))


def turned(value, cell_z):
    sub = lax.broadcasted_iota(jnp.int32, value.shape, 0)
    group = lax.broadcasted_iota(jnp.int32, value.shape, 1) // cell_z
    skewed = pltpu.roll(value, cell_z, 1, stride=cell_z, stride_axis=0)
    mixed = jnp.take_along_axis(skewed, (group + sub) & (SUB - 1), axis=0, mode="promise_in_bounds")
    return pltpu.roll(mixed, 0, 1, stride=cell_z, stride_axis=0)


def relax_of(total, inverse):
    factor = 1.0 / (1.0 - total * inverse / max_extension)
    return 1.0 - (time_step * 0.5 / weissenberg) * factor


def stepped(vectors, noise, matrix):
    return [
        matrix[3 * a] * vectors[0]
        + matrix[3 * a + 1] * vectors[1]
        + matrix[3 * a + 2] * vectors[2]
        + noise_scale * noise[a]
        for a in range(3)
    ]


def with_diagonal(grad, relax):
    return [g + relax if i % 4 == 0 else g for i, g in enumerate(grad)]


def noise_rows(ref, start):
    both = [ref(a, pl.ds(start, 2 * SUB)).astype(f32) for a in range(3)]
    return [[w[:SUB] for w in both], [w[SUB:] for w in both]]


def add_moments(sums, q):
    return [s + q[a] * q[b] for s, (a, b) in zip(sums, component_pairs)]


def product_sums(sums, q, w):
    terms = [q[a] * q[b] for a, b in component_pairs]
    terms += [q[a] * w[b] for a in range(3) for b in range(3)]
    terms += [w[0] * w[0] + w[1] * w[1] + w[2] * w[2]]
    return [s + t for s, t in zip(sums, terms)]


def coefficients(g, m):
    cross = lambda a, b: m[6 + 3 * a + b]
    square = lambda a, b: m[moment_of[a, b]]
    once, twice, kick = 0.0, 0.0, 0.0
    for a in range(3):
        for b in range(3):
            once += g[3 * a + b] * square(a, b)
            kick += g[3 * a + b] * cross(b, a)
            inner = 0.0
            for c in range(3):
                inner += g[3 * a + c] * square(b, c)
            twice += g[3 * a + b] * inner
    return [
        twice + (2 * noise_scale) * kick + noise_scale**2 * m[15],
        2.0 * once + (2 * noise_scale) * (cross(0, 0) + cross(1, 1) + cross(2, 2)),
        m[0] + m[1] + m[2],
    ]


def owned_slots(tiles, me, helper):
    found = []
    for h in range(helper.shape[1]):
        tile = helper[0, h] - me * tiles
        found.append((h, (tile >= 0) & (tile < tiles), tile))
    return found


def small(flops, traffic):
    return pl.CostEstimate(flops=flops, bytes_accessed=traffic, transcendentals=0)


def is_even(axis):
    return (lax.axis_index(axis) & 1) == 0


def edges(velocity, x_one, x_two, y_one, y_two):
    depth, width = velocity.shape[1:3]
    even = is_even("gx")
    for a in range(3):
        first, last = velocity[a, 0], velocity[a, depth - 1]
        x_one[a] = jnp.where(even, last, first)
        x_two[a] = jnp.where(even, first, last)
    even = is_even("gy")
    for a in range(3):
        for x in range(depth):
            first, last = velocity[a, x, pl.ds(0, 1), :], velocity[a, x, pl.ds(width - 1, 1), :]
            y_one[a, pl.ds(x, 1), :] = jnp.where(even, last, first)
            y_two[a, pl.ds(x, 1), :] = jnp.where(even, first, last)


def call_edges(velocity):
    _, depth, width, length = velocity.shape
    along_x = jax.ShapeDtypeStruct((3, width, length), f32)
    along_y = jax.ShapeDtypeStruct((3, depth, length), f32)
    return pl.pallas_call(
        edges,
        out_shape=(along_x, along_x, along_y, along_y),
        in_specs=[vmem],
        out_specs=(vmem,) * 4,
        compiler_params=pltpu.CompilerParams(vmem_limit_bytes=4 << 20),
        cost_estimate=small(1 << 10, 1 << 17),
        name="edges",
    )(velocity)


def two_swaps(one, two, axis):
    size = lax.axis_size(axis)
    within = [(i, i ^ 1) for i in range(size)]
    across = [(i, min(max(i - 1 + 2 * (i & 1), 0), size - 1)) for i in range(size)]
    return lax.ppermute(one, axis, within), lax.ppermute(two, axis, across)


def low_and_high(axis, one, two, a):
    even, place = is_even(axis), lax.axis_index(axis)
    low = jnp.where(even, two[a], one[a])
    high = jnp.where(even, one[a], two[a])
    return jnp.where(place == 0, 0.0, low), jnp.where(place == lax.axis_size(axis) - 1, 0.0, high)


def heavy_moments(helper, base, noise, out, fields, shocks, sems):
    slots, _, count, cells = fields.shape
    tiles = base.shape[2]
    me = lax.axis_index("gy")

    def loads(h, tile):
        return (
            pltpu.make_async_copy(base.at[0, 0, tile], fields.at[h], sems.at[0, h]),
            pltpu.make_async_copy(noise.at[0, 0, tile, 0], shocks.at[h], sems.at[1, h]),
        )

    found = owned_slots(tiles, me, helper)
    for h, owned, tile in found:

        @pl.when(owned)
        def _(h=h, tile=tile):
            for copy in loads(h, tile):
                copy.start()

    for h, owned, tile in found:

        @pl.when(owned)
        def _(h=h, tile=tile):
            for copy in loads(h, tile):
                copy.wait()

            @pl.loop(0, cells // LANES)
            def _(x):
                lanes = pl.ds(pl.multiple_of(x * LANES, LANES), LANES)
                sums = [jnp.zeros((SUB, LANES), f32)] * 16
                for group in range(count // (2 * SUB)):
                    pair = noise_rows(lambda a, rows: shocks[h, a, rows, lanes], group * 2 * SUB)
                    for half in range(2):
                        rows = pl.ds((2 * group + half) * SUB, SUB)
                        sums = product_sums(sums, [fields[h, a, rows, lanes] for a in range(3)], pair[half])
                for i, s in enumerate(sums):
                    out[h, i, pl.ds(x, 1), :] = column_sum(s)


def call_heavy_moments(helper_tile, base_fields, base_noise):
    slots = helper_tile.shape[1]
    count, cells = base_fields.shape[-2:]
    return pl.pallas_call(
        heavy_moments,
        out_shape=jax.ShapeDtypeStruct((slots, 16, cells // LANES, LANES), f32),
        in_specs=[smem, hbm, hbm],
        out_specs=vmem,
        scratch_shapes=[
            pltpu.VMEM((slots, 3, count, cells), f32),
            pltpu.VMEM((slots, 3, count, cells), jnp.bfloat16),
            pltpu.SemaphoreType.DMA((2, slots)),
        ],
        compiler_params=pltpu.CompilerParams(vmem_limit_bytes=LARGE),
        cost_estimate=small(8 << 20, 3 << 20),
        name="heavy_moments",
    )(helper_tile, *far_memory(base_fields, base_noise))


def extra_moments(unroll, before, base, noise, out):
    _, _, _, count, cells = base.shape
    zero = jnp.zeros((SUB, LANES), f32)

    @pl.loop(0, cells // LANES)
    def _(x):
        lanes = pl.ds(pl.multiple_of(x * LANES, LANES), LANES)

        def body(i, sums):
            start = pl.multiple_of(i * 2 * SUB, 2 * SUB)
            pair = noise_rows(lambda a, rows: noise[0, 0, 0, a, rows, lanes], start)
            for half in range(2):
                rows = pl.ds(start + half * SUB, SUB)
                sums = product_sums(sums, [base[0, 0, a, rows, lanes] for a in range(3)], pair[half])
            return sums

        for i, s in enumerate(lax.fori_loop(0, count // (2 * SUB), body, [zero] * 16, unroll=unroll)):
            out[i, pl.ds(x, 1), :] = column_sum(s)


def call_extra_moments(before, extra_fields, extra_noise):
    cells = extra_fields.shape[-1]
    return pl.pallas_call(
        functools.partial(extra_moments, 7),
        out_shape=jax.ShapeDtypeStruct((16, cells // LANES, LANES), f32),
        in_specs=[anywhere, vmem, vmem],
        out_specs=vmem,
        compiler_params=pltpu.CompilerParams(vmem_limit_bytes=SMALL),
        cost_estimate=small(8 << 20, 5 << 20),
        name="extra_moments",
    )(before, *near_memory(extra_fields, extra_noise))


def gradients(tiles, helper, velocity, x_one, x_two, y_one, y_two, wall, moments, grad, keep, send):
    me = lax.axis_index("gy")
    depth = velocity.shape[1]
    cell_z = velocity.shape[3] // tiles
    sub = lax.broadcasted_iota(jnp.int32, (SUB, LANES), 0)
    lane = lax.broadcasted_iota(jnp.int32, (SUB, LANES), 1)
    z = lane % cell_z
    scales = [turned(jnp.where(wall[x] == 0, 0.5 * time_step, 0.0).astype(f32), cell_z) for x in range(depth)]
    for a in range(3):
        x_low, x_high = low_and_high("gx", x_one, x_two, a)
        y_low, y_high = low_and_high("gy", y_one, y_two, a)
        rows = [x_low] + [velocity[a, x] for x in range(depth)] + [x_high]
        rows = [turned(row, cell_z) for row in rows]
        low, high = turned(y_low, cell_z), turned(y_high, cell_z)
        for x in range(depth):
            here = rows[x + 1]
            above = high if x == depth - 1 else pltpu.roll(high, LANES - cell_z * (x + 1), 1)
            below = low if x == 0 else pltpu.roll(low, LANES - cell_z * x, 1)
            y_up = jnp.where(lane < LANES - cell_z, pltpu.roll(here, LANES - cell_z, 1), above)
            y_down = jnp.where(lane >= cell_z, pltpu.roll(here, cell_z, 1), below)
            next_tile = pltpu.roll(pltpu.roll(here, cell_z - 1, 1), 1, 0)
            last_tile = pltpu.roll(pltpu.roll(here, LANES - cell_z + 1, 1), SUB - 1, 0)
            next_tile = jnp.where(sub == 0, 0.0, next_tile)
            last_tile = jnp.where(sub == SUB - 1, 0.0, last_tile)
            z_up = jnp.where(z == cell_z - 1, next_tile, pltpu.roll(here, LANES - 1, 1))
            z_down = jnp.where(z == 0, last_tile, pltpu.roll(here, 1, 1))
            for b, difference in enumerate((rows[x + 2] - rows[x], y_up - y_down, z_up - z_down)):
                grad[pl.ds(((3 * a + b) * depth + x) * SUB, SUB), :] = difference * scales[x]
    keep[...] = jnp.zeros(keep.shape, f32)
    send[...] = jnp.zeros(send.shape, f32)
    for h, owned, tile in owned_slots(tiles, me, helper):

        @pl.when(owned)
        def _(h=h, tile=tile):
            g = [grad[pl.ds(i * depth * SUB + SUB - 1 - tile, depth, stride=SUB), :] for i in range(9)]
            rows = g + coefficients(g, [moments[h, i] for i in range(16)])
            stays = (me & 1) == (h & 1)

            @pl.when(stays)
            def _():
                for i, row in enumerate(rows):
                    keep[h >> 1, i] = row

            @pl.when(jnp.logical_not(stays))
            def _():
                for i, row in enumerate(rows):
                    send[h >> 1, i] = row


def call_gradients(tiles, helper_tile, velocity, halos, wall_cells, moments):
    slots = helper_tile.shape[1]
    depth = velocity.shape[1]
    half = jax.ShapeDtypeStruct((slots // 2, 12, depth, LANES), f32)
    return pl.pallas_call(
        functools.partial(gradients, tiles),
        out_shape=(jax.ShapeDtypeStruct((9 * depth * SUB, LANES), f32), half, half),
        in_specs=[smem] + [vmem] * 7,
        out_specs=(vmem,) * 3,
        compiler_params=pltpu.CompilerParams(vmem_limit_bytes=8 << 20),
        cost_estimate=small(4 << 20, 1 << 20),
        name="gradients",
    )(helper_tile, velocity, *halos, wall_cells, moments)


def swapped(block, bit):
    size = lax.axis_size("gy")
    return lax.ppermute(block, "gy", [(i, i ^ (1 << bit)) for i in range(size)])


def merge(bit, before, kept, received, keep, send):
    mine = (lax.axis_index("gy") >> (bit + 1)) & 1
    for j in range(0, kept.shape[0], 2):
        for i in range(kept.shape[1]):
            even, odd = [kept[k, i] + received[k, i] for k in (j, j + 1)]
            keep[j // 2, i] = jnp.where(mine == 0, even, odd)
            send[j // 2, i] = jnp.where(mine == 0, odd, even)


def call_merge(bit, before, kept, received):
    half = jax.ShapeDtypeStruct((kept.shape[0] // 2,) + kept.shape[1:], f32)
    return pl.pallas_call(
        functools.partial(merge, bit),
        out_shape=(half, half),
        in_specs=[anywhere, vmem, vmem],
        out_specs=(vmem, vmem),
        compiler_params=pltpu.CompilerParams(vmem_limit_bytes=4 << 20),
        cost_estimate=small(1 << 10, 1 << 18),
        name="merge",
    )(before, kept, received)


def call_join(before, first, second):
    def join(before, first, second, out):
        out[: first.shape[0]] = first[...]
        out[first.shape[0] :] = second[...]

    return pl.pallas_call(
        join,
        out_shape=jax.ShapeDtypeStruct((2 * first.shape[0],) + first.shape[1:], f32),
        in_specs=[anywhere, vmem, vmem],
        out_specs=vmem,
        compiler_params=pltpu.CompilerParams(vmem_limit_bytes=4 << 20),
        cost_estimate=small(1 << 10, 1 << 18),
        name="join",
    )(before, first, second)


def stress_rows(sums, inverse):
    second = [s * inverse for s in sums]
    stretch = 1.0 / (1.0 - (second[0] + second[1] + second[2]) / max_extension)
    return [(stretch * s - (1.0 if i < 3 else 0.0)) * (1.0 / weissenberg) for i, s in enumerate(second)]


def tile_grad(grad, depth, tile, x):
    return [wide(grad[pl.ds((i * depth + x + 1) * SUB - 1 - tile, 1), :]) for i in range(9)]


def tile_sums(read, write, noise, matrices, count, add, many):
    sums = [jnp.zeros((SUB, LANES), f32)] * many
    for group in range(count // (2 * SUB)):
        pairs = [noise_rows(functools.partial(noise, step), group * 2 * SUB) for step in range(len(matrices))]
        for half in range(2):
            rows = pl.ds((2 * group + half) * SUB, SUB)
            q = [read(a, rows) for a in range(3)]
            for step, matrix in enumerate(matrices):
                q = stepped(q, pairs[step][half], matrix)
            for a in range(3):
                write(a, rows, q[a])
            sums = add(sums, q)
    return sums


def add_square(sums, q):
    return [sums[0] + (q[0] * q[0] + q[1] * q[1] + q[2] * q[2])]


def ordinary(first, has_block, has_base, has_extra, *refs):
    refs = list(refs)
    before, base, noise, grad = refs[:4]
    del refs[:4]
    block = refs.pop(0) if has_block else None
    if has_base:
        refs.pop(0)
    extra_near = refs.pop(0) if has_extra else None
    new_base = refs.pop(0) if has_block else None
    new_extra = refs.pop(0) if has_extra else None
    fields, stress, halfway, relaxes, sems = refs
    here, _, count, cells = fields.shape
    depth = cells // LANES
    inverse = 1.0 / count
    copies = []
    if has_block:
        last = block.shape[0]
        copies += [
            pltpu.make_async_copy(block.at[i], new_base.at[0, 0, first - last + i], sems.at[i]) for i in range(last)
        ]
    if has_extra:
        copies += [
            pltpu.make_async_copy(extra_near.at[0, 0, a], new_extra.at[0, 0, a], sems.at[len(copies) + a])
            for a in range(3)
        ]
    for copy in copies:
        copy.start()
    for place in range(here):
        tile = first + place
        totals = []
        for x in range(depth):
            total = jnp.zeros((SUB, LANES), f32)
            for group in range(count // SUB):
                for a in range(3):
                    q = base[0, 0, tile, a, pl.ds(group * SUB, SUB), pl.ds(x * LANES, LANES)]
                    total = total + q * q
            totals.append(total)
        for step in range(2):
            relaxes[place, step] = relax_of(packed_sum(totals), inverse)
            totals = []
            for x in range(depth):
                lanes = pl.ds(x * LANES, LANES)
                matrix = with_diagonal(tile_grad(grad, depth, tile, x), wide(relaxes[place, step, pl.ds(x, 1), :]))

                def read(a, rows):
                    return base[0, 0, tile, a, rows, lanes] if step == 0 else halfway[place, a, rows, lanes]

                def write(a, rows, value):
                    if step == 0:
                        halfway[place, a, rows, lanes] = value
                    else:
                        fields[place, a, rows, lanes] = value

                def shock(_, a, rows):
                    return noise[0, 0, tile, step, a, rows, lanes]

                if step == 0:
                    totals += tile_sums(read, write, shock, [matrix], count, add_square, 1)
                else:
                    totals.append(tile_sums(read, write, shock, [matrix], count, add_moments, 6))
        for i, row in enumerate(stress_rows([packed_sum(list(same)) for same in zip(*totals)], inverse)):
            stress[i, place] = row
    for copy in copies:
        copy.wait()


def call_ordinary(first, here, before, base_fields, base_noise, grad, block, new_base, new_extra):
    count, cells = base_fields.shape[-2:]
    depth = cells // LANES
    has_block, has_base, has_extra = block is not None, new_base is not None, new_extra is not None
    operands = [before, *near_memory(base_fields, base_noise), grad]
    specs = [anywhere, vmem, vmem, vmem]
    shapes, out_specs, aliases = [], [], {}
    copies = 0
    if has_block:
        operands += near_memory(block)
        specs.append(vmem)
        shapes.append(jax.ShapeDtypeStruct(base_fields.shape, f32))
        out_specs.append(hbm)
        copies += block.shape[0]
    if has_base:
        aliases[len(operands)] = 0
        operands.append(new_base)
        specs.append(hbm)
    if has_extra:
        operands += near_memory(new_extra)
        specs.append(vmem)
        shapes.append(jax.ShapeDtypeStruct(new_extra.shape, f32))
        out_specs.append(hbm)
        copies += 3
    shapes += [
        pltpu.VMEM((here, 3, count, cells), f32),
        jax.ShapeDtypeStruct((6, here, depth, LANES), f32),
    ]
    out_specs += [vmem, vmem]
    results = pl.pallas_call(
        functools.partial(ordinary, first, has_block, has_base, has_extra),
        out_shape=tuple(shapes),
        in_specs=specs,
        out_specs=tuple(out_specs),
        input_output_aliases=aliases,
        scratch_shapes=[
            pltpu.VMEM((here, 3, count, cells), f32),
            pltpu.VMEM((here, 2, depth, LANES), f32),
            pltpu.SemaphoreType.DMA((max(copies, 1),)),
        ],
        compiler_params=pltpu.CompilerParams(vmem_limit_bytes=SMALL),
        cost_estimate=small(8 << 20, 3 << 20),
        name="ordinary_tiles",
    )(*operands)
    results = list(results)
    piece, block = results.pop(), results.pop()
    new_base = results.pop(0) if has_block else None
    return new_base, block, piece, (results[0] if has_extra else None)


def extra(unroll, before, base, noise, moments, kept, received, new_fields, reply, message):
    _, _, _, count, cells = base.shape
    inverse = 1.0 / float(ALL_FIELDS)
    zero = jnp.zeros((SUB, LANES), f32)
    message[...] = kept[0] + received[0]
    own = coefficients([message[i] for i in range(9)], [moments[i] for i in range(16)])
    both = [message[9 + i] + own[i] for i in range(3)]
    first = relax_of(both[2], inverse)
    second = relax_of(both[0] + first * (both[1] + first * both[2]), inverse)
    reply[0], reply[1] = first, second

    @pl.loop(0, cells // LANES)
    def _(x):
        lanes = pl.ds(pl.multiple_of(x * LANES, LANES), LANES)
        grad = [wide(message[i, pl.ds(x, 1), :]) for i in range(9)]
        matrices = [with_diagonal(grad, wide(reply[step, pl.ds(x, 1), :])) for step in range(2)]

        def body(i, sums):
            start = pl.multiple_of(i * 2 * SUB, 2 * SUB)
            pairs = [noise_rows(lambda a, rows: noise[0, 0, step, a, rows, lanes], start) for step in range(2)]
            for half in range(2):
                rows = pl.ds(start + half * SUB, SUB)
                q = [base[0, 0, a, rows, lanes] for a in range(3)]
                for step in range(2):
                    q = stepped(q, pairs[step][half], matrices[step])
                for a in range(3):
                    new_fields[0, 0, a, rows, lanes] = q[a]
                sums = add_moments(sums, q)
            return sums

        for i, s in enumerate(lax.fori_loop(0, count // (2 * SUB), body, [zero] * 6, unroll=unroll)):
            reply[2 + i, pl.ds(x, 1), :] = column_sum(s)


def call_extra(before, extra_fields, extra_noise, moments, kept, received):
    depth = extra_fields.shape[-1] // LANES
    return pl.pallas_call(
        functools.partial(extra, 7),
        out_shape=(
            pltpu.VMEM(extra_fields.shape, f32),
            jax.ShapeDtypeStruct((8, depth, LANES), f32),
        ),
        in_specs=[anywhere, vmem, vmem, vmem, vmem, vmem],
        out_specs=(vmem, vmem),
        scratch_shapes=[pltpu.VMEM(kept.shape[1:], f32)],
        compiler_params=pltpu.CompilerParams(vmem_limit_bytes=SMALL),
        cost_estimate=small(32 << 20, 9 << 20),
        name="extra_fields",
    )(before, *near_memory(extra_fields, extra_noise), moments, kept, received)


def heavy(bits, piece_count, helper, base, noise, grad, near, far, block, *refs):
    pieces, (_, new_base, stress, fields, rows, answer, sems) = refs[:piece_count], refs[piece_count:]
    _, _, tiles, _, count, cells = base.shape
    slots = helper.shape[1]
    me = lax.axis_index("gy")
    depth = cells // LANES
    last = block.shape[0]
    flat = rows.reshape(6 * depth * tiles, LANES)

    def put_stress(tile, packed):
        for i, value in enumerate(packed):
            flat[pl.ds(i * depth * tiles + tile, depth, stride=tiles), :] = value

    def leave(i):
        return pltpu.make_async_copy(block.at[i], new_base.at[0, 0, tiles - last + i], sems.at[slots + depth + i])

    def store(h, tile):
        return pltpu.make_async_copy(fields.at[h], new_base.at[0, 0, tile], sems.at[h])

    def result(x):
        target = stress.at[0, 0, :, :, pl.ds(x * LANES, LANES)]
        return pltpu.make_async_copy(rows.at[:, x], target, sems.at[slots + x])

    for i in range(last):
        leave(i).start()
    tile = 0
    for piece in pieces:
        for place in range(piece.shape[1]):
            put_stress(tile, [piece[i, place] for i in range(6)])
            tile += 1

    @pl.loop(0, slots)
    def _(h):
        tile = helper[0, h] - me * tiles

        @pl.when((tile >= 0) & (tile < tiles))
        def _():
            flips = me ^ h
            place = sum(((flips >> (bits - 1 - i)) & 1) << i for i in range(bits))
            is_far = place >= slots // 2
            place = place & (slots // 2 - 1)
            for i in range(near.shape[1]):
                answer[i] = jnp.where(is_far, far[place, i], near[place, i])
            totals = []
            for x in range(depth):
                lanes = pl.ds(x * LANES, LANES)
                g = tile_grad(grad, depth, tile, x)
                matrices = [with_diagonal(g, wide(answer[step, pl.ds(x, 1), :])) for step in range(2)]

                def read(a, part):
                    return base[0, 0, tile, a, part, lanes]

                def write(a, part, value):
                    fields[h, a, part, lanes] = value

                def shock(step, a, part):
                    return noise[0, 0, tile, step, a, part, lanes]

                totals.append(tile_sums(read, write, shock, matrices, count, add_moments, 6))
            sums = [packed_sum(list(same)) + answer[2 + i] for i, same in enumerate(zip(*totals))]
            put_stress(tile, stress_rows(sums, 1.0 / ALL_FIELDS))

    for x in range(depth):
        result(x).start()
    for i in range(last):
        leave(i).wait()

    def each_owned(act):
        @pl.loop(0, slots)
        def _(h):
            tile = helper[0, h] - me * tiles

            @pl.when((tile >= 0) & (tile < tiles))
            def _():
                act(store(h, tile))

    each_owned(lambda copy: copy.start())
    for x in range(depth):
        result(x).wait()
    each_owned(lambda copy: copy.wait())


def call_heavy(bits, helper_tile, base_fields, base_noise, grad, near, far, block, pieces, new_base):
    _, _, tiles, _, count, cells = base_fields.shape
    depth = cells // LANES
    slots = helper_tile.shape[1]
    return pl.pallas_call(
        functools.partial(heavy, bits, len(pieces)),
        out_shape=(
            jax.ShapeDtypeStruct(new_base.shape, f32),
            jax.ShapeDtypeStruct((1, 1, 6, tiles, cells), f32),
        ),
        in_specs=[smem] + [vmem] * (6 + len(pieces)) + [hbm],
        out_specs=(hbm, hbm),
        input_output_aliases={7 + len(pieces): 0},
        scratch_shapes=[
            pltpu.VMEM((slots, 3, count, cells), f32),
            pltpu.VMEM((6, depth, tiles, LANES), f32),
            pltpu.VMEM(near.shape[1:], f32),
            pltpu.SemaphoreType.DMA((slots + depth + block.shape[0],)),
        ],
        compiler_params=pltpu.CompilerParams(vmem_limit_bytes=SMALL),
        cost_estimate=small(8 << 20, 4 << 20),
        name="heavy_tiles",
    )(helper_tile, *near_memory(base_fields, base_noise), grad, near, far, *near_memory(block), *pieces, new_base)


def per_device(
    velocity, wall_cells, tile_counts, helper_tile, base_fields, extra_fields, base_noise, extra_noise
):
    tiles = tile_counts.shape[2]
    bits = lax.axis_size("gy").bit_length() - 1
    x_one, x_two, y_one, y_two = call_edges(velocity)
    halos = two_swaps(x_one, x_two, "gx") + two_swaps(y_one, y_two, "gy")
    moments = call_heavy_moments(helper_tile, base_fields, base_noise)
    grad, keep, send = call_gradients(tiles, helper_tile, velocity, halos, wall_cells, moments)
    gaps = 2 * bits - 2
    new_base, block, pieces, done = None, None, [], 0

    def fill(before, extra_near=None):
        nonlocal new_base, block, done
        here = (tiles - done) // (gaps - len(pieces))
        new_base, block, piece, extra_far = call_ordinary(
            done, here, before, base_fields, base_noise, grad, block, new_base, extra_near
        )
        pieces.append(piece)
        done += here
        return piece, extra_far

    for bit in range(bits):
        received = swapped(send, bit)
        if bit == 1:
            before = extra_sums = call_extra_moments(send, extra_fields, extra_noise)
        else:
            before, _ = fill(send)
        if bit < bits - 1:
            keep, send = call_merge(bit, before, keep, received)
    extra_near, reply = call_extra(before, extra_fields, extra_noise, extra_sums, keep, received)
    near = reply[None]
    for bit in range(bits - 1, 0, -1):
        received = swapped(near, bit)
        if bit == bits - 1:
            before, new_extra = fill(near, extra_near)
        else:
            before, _ = fill(near)
        near = call_join(before, near, received)
    far = swapped(near, 0)
    new_base, stress = call_heavy(
        bits, helper_tile, base_fields, base_noise, grad, near, far, block, pieces, new_base
    )
    return new_base, new_extra, jnp.swapaxes(stress, 2, 3)


def solution(mesh):
    in_specs = (
        P(None, "gx", "gy", None),
        P("gx", "gy", None),
        P("gx", "gy", None),
        P("gx", None),
        P("gx", "gy", None, None, None, None),
        P("gx", "gy", None, None, None),
        P("gx", "gy", None, None, None, None, None),
        P("gx", "gy", None, None, None, None),
    )
    out_specs = (
        P("gx", "gy", None, None, None, None),
        P("gx", "gy", None, None, None),
        P("gx", "gy", None, None, None),
    )
    return jax.shard_map(
        per_device, mesh=mesh, in_specs=in_specs, out_specs=out_specs, check_vma=False
    )
```

```python
import functools

import jax
import jax.numpy as jnp
from jax import lax
from jax.experimental import pallas as pl
from jax.experimental.pallas import tpu as pltpu
from jax.sharding import PartitionSpec as P

ALL_FIELDS = 256
HEAVY_MOST = 4
LANES = 128
SUB = 8
SMALL = 10 << 20
LARGE = 14 << 20

time_step = 0.05
weissenberg = 0.25
max_extension = 50.0
noise_scale = (time_step / weissenberg) ** 0.5
component_pairs = ((0, 0), (1, 1), (2, 2), (0, 1), (0, 2), (1, 2))
moment_of = {(0, 0): 0, (1, 1): 1, (2, 2): 2, (0, 1): 3, (1, 0): 3, (0, 2): 4, (2, 0): 4, (1, 2): 5, (2, 1): 5}
f32 = jnp.float32

vmem = pl.BlockSpec(memory_space=pltpu.VMEM)
hbm = pl.BlockSpec(memory_space=pltpu.HBM)
anywhere = pl.BlockSpec(memory_space=pl.ANY)


def far_memory(*arrays):
    return [pltpu.with_memory_space_constraint(array, pltpu.HBM) for array in arrays]


def near_memory(*arrays):
    return [pltpu.with_memory_space_constraint(array, pltpu.VMEM) for array in arrays]


def column_sum(value):
    return jnp.sum(value, axis=0, keepdims=True)


def packed_sum(values):
    sub = lax.broadcasted_iota(jnp.int32, (SUB, LANES), 0)
    bit = 1
    while len(values) > 1:
        low = (sub & bit) == 0
        values = [
            jnp.where(low, a, b) + pltpu.roll(jnp.where(low, b, a), bit, 0)
            for a, b in zip(values[0::2], values[1::2])
        ]
        bit *= 2
    return values[0]


def wide(row):
    return jnp.broadcast_to(row, (SUB, LANES))


def turned(value, cell_z):
    sub = lax.broadcasted_iota(jnp.int32, value.shape, 0)
    group = lax.broadcasted_iota(jnp.int32, value.shape, 1) // cell_z
    skewed = pltpu.roll(value, cell_z, 1, stride=cell_z, stride_axis=0)
    mixed = jnp.take_along_axis(skewed, (group + sub) & (SUB - 1), axis=0, mode="promise_in_bounds")
    return pltpu.roll(mixed, 0, 1, stride=cell_z, stride_axis=0)


def relax_of(total, inverse):
    factor = 1.0 / (1.0 - total * inverse / max_extension)
    return 1.0 - (time_step * 0.5 / weissenberg) * factor


def stepped(vectors, noise, matrix):
    return [
        matrix[3 * a] * vectors[0]
        + matrix[3 * a + 1] * vectors[1]
        + matrix[3 * a + 2] * vectors[2]
        + noise_scale * noise[a]
        for a in range(3)
    ]


def with_diagonal(grad, relax):
    return [g + relax if i % 4 == 0 else g for i, g in enumerate(grad)]


def noise_rows(ref, start):
    both = [ref(a, pl.ds(start, 2 * SUB)).astype(f32) for a in range(3)]
    return [[w[:SUB] for w in both], [w[SUB:] for w in both]]


def add_moments(sums, q):
    return [s + q[a] * q[b] for s, (a, b) in zip(sums, component_pairs)]


def product_sums(sums, q, w):
    terms = [q[a] * q[b] for a, b in component_pairs]
    terms += [q[a] * w[b] for a in range(3) for b in range(3)]
    terms += [w[0] * w[0] + w[1] * w[1] + w[2] * w[2]]
    return [s + t for s, t in zip(sums, terms)]


def coefficients(g, m):
    cross = lambda a, b: m[6 + 3 * a + b]
    square = lambda a, b: m[moment_of[a, b]]
    once, twice, kick = 0.0, 0.0, 0.0
    for a in range(3):
        for b in range(3):
            once += g[3 * a + b] * square(a, b)
            kick += g[3 * a + b] * cross(b, a)
            inner = 0.0
            for c in range(3):
                inner += g[3 * a + c] * square(b, c)
            twice += g[3 * a + b] * inner
    return [
        twice + (2 * noise_scale) * kick + noise_scale**2 * m[15],
        2.0 * once + (2 * noise_scale) * (cross(0, 0) + cross(1, 1) + cross(2, 2)),
        m[0] + m[1] + m[2],
    ]


def owned_slots(tiles, me, helper):
    found = []
    row = helper[...]
    for h in range(helper.shape[1]):
        tile = row[0, h] - me * tiles
        found.append((h, (tile >= 0) & (tile < tiles), tile))
    return found


def small(flops, traffic):
    return pl.CostEstimate(flops=flops, bytes_accessed=traffic, transcendentals=0)


def is_even(axis):
    return (lax.axis_index(axis) & 1) == 0


def edges(helper, velocity, helper_near, x_one, x_two, y_one, y_two):
    depth, width = velocity.shape[1:3]
    helper_near[...] = helper[...]
    even = is_even("gx")
    for a in range(3):
        first, last = velocity[a, 0], velocity[a, depth - 1]
        x_one[a] = jnp.where(even, last, first)
        x_two[a] = jnp.where(even, first, last)
    even = is_even("gy")
    for a in range(3):
        for x in range(depth):
            first, last = velocity[a, x, pl.ds(0, 1), :], velocity[a, x, pl.ds(width - 1, 1), :]
            y_one[a, pl.ds(x, 1), :] = jnp.where(even, last, first)
            y_two[a, pl.ds(x, 1), :] = jnp.where(even, first, last)


def call_edges(helper_tile, velocity):
    _, depth, width, length = velocity.shape
    along_x = jax.ShapeDtypeStruct((3, width, length), f32)
    along_y = jax.ShapeDtypeStruct((3, depth, length), f32)
    return pl.pallas_call(
        edges,
        out_shape=(jax.ShapeDtypeStruct(helper_tile.shape, jnp.int32), along_x, along_x, along_y, along_y),
        in_specs=[vmem, vmem],
        out_specs=(vmem,) * 5,
        compiler_params=pltpu.CompilerParams(vmem_limit_bytes=4 << 20),
        cost_estimate=small(1 << 10, 1 << 17),
        name="edges",
    )(*far_memory(helper_tile, velocity))


def two_swaps(one, two, axis):
    size = lax.axis_size(axis)
    within = [(i, i ^ 1) for i in range(size)]
    across = [(i, (i - 1 + 2 * (i & 1)) % size) for i in range(size)]
    return lax.ppermute(one, axis, within), lax.ppermute(two, axis, across)


def low_and_high(axis, one, two, a):
    even, place = is_even(axis), lax.axis_index(axis)
    low = jnp.where(even, two[a], one[a])
    high = jnp.where(even, one[a], two[a])
    return jnp.where(place == 0, 0.0, low), jnp.where(place == lax.axis_size(axis) - 1, 0.0, high)


def heavy_moments(helper, base, noise, out, fields, shocks, sems):
    slots, _, count, cells = fields.shape
    tiles = base.shape[2]
    me = lax.axis_index("gy")

    def loads(h, tile):
        return (
            pltpu.make_async_copy(base.at[0, 0, tile], fields.at[h], sems.at[0, h]),
            pltpu.make_async_copy(noise.at[0, 0, tile, 0], shocks.at[h], sems.at[1, h]),
        )

    found = owned_slots(tiles, me, helper)
    for h, owned, tile in found:

        @pl.when(owned)
        def _(h=h, tile=tile):
            for copy in loads(h, tile):
                copy.start()

    for h, owned, tile in found:

        @pl.when(owned)
        def _(h=h, tile=tile):
            for copy in loads(h, tile):
                copy.wait()

            @pl.loop(0, cells // LANES)
            def _(x):
                lanes = pl.ds(pl.multiple_of(x * LANES, LANES), LANES)
                sums = [jnp.zeros((SUB, LANES), f32)] * 16
                for group in range(count // (2 * SUB)):
                    pair = noise_rows(lambda a, rows: shocks[h, a, rows, lanes], group * 2 * SUB)
                    for half in range(2):
                        rows = pl.ds((2 * group + half) * SUB, SUB)
                        sums = product_sums(sums, [fields[h, a, rows, lanes] for a in range(3)], pair[half])
                for i, s in enumerate(sums):
                    out[h, i, pl.ds(x, 1), :] = column_sum(s)


def call_heavy_moments(helper_tile, base_fields, base_noise):
    slots = helper_tile.shape[1]
    count, cells = base_fields.shape[-2:]
    return pl.pallas_call(
        heavy_moments,
        out_shape=jax.ShapeDtypeStruct((slots, 16, cells // LANES, LANES), f32),
        in_specs=[vmem, hbm, hbm],
        out_specs=vmem,
        scratch_shapes=[
            pltpu.VMEM((slots, 3, count, cells), f32),
            pltpu.VMEM((slots, 3, count, cells), jnp.bfloat16),
            pltpu.SemaphoreType.DMA((2, slots)),
        ],
        compiler_params=pltpu.CompilerParams(vmem_limit_bytes=LARGE),
        cost_estimate=small(8 << 20, 3 << 20),
        name="heavy_moments",
    )(helper_tile, *far_memory(base_fields, base_noise))


def extra_moments(unroll, before, base, noise, out):
    _, _, _, count, cells = base.shape
    zero = jnp.zeros((SUB, LANES), f32)

    @pl.loop(0, cells // LANES)
    def _(x):
        lanes = pl.ds(pl.multiple_of(x * LANES, LANES), LANES)

        def body(i, sums):
            start = pl.multiple_of(i * 2 * SUB, 2 * SUB)
            pair = noise_rows(lambda a, rows: noise[0, 0, 0, a, rows, lanes], start)
            for half in range(2):
                rows = pl.ds(start + half * SUB, SUB)
                sums = product_sums(sums, [base[0, 0, a, rows, lanes] for a in range(3)], pair[half])
            return sums

        for i, s in enumerate(lax.fori_loop(0, count // (2 * SUB), body, [zero] * 16, unroll=unroll)):
            out[i, pl.ds(x, 1), :] = column_sum(s)


def call_extra_moments(before, extra_fields, extra_noise):
    cells = extra_fields.shape[-1]
    return pl.pallas_call(
        functools.partial(extra_moments, 7),
        out_shape=jax.ShapeDtypeStruct((16, cells // LANES, LANES), f32),
        in_specs=[anywhere, vmem, vmem],
        out_specs=vmem,
        compiler_params=pltpu.CompilerParams(vmem_limit_bytes=SMALL),
        cost_estimate=small(8 << 20, 5 << 20),
        name="extra_moments",
    )(before, *near_memory(extra_fields, extra_noise))


def gradients(tiles, helper, velocity, x_one, x_two, y_one, y_two, wall, moments, grad, keep, send):
    me = lax.axis_index("gy")
    depth = velocity.shape[1]
    cell_z = velocity.shape[3] // tiles
    sub = lax.broadcasted_iota(jnp.int32, (SUB, LANES), 0)
    lane = lax.broadcasted_iota(jnp.int32, (SUB, LANES), 1)
    z = lane % cell_z
    scales = [turned(jnp.where(wall[x] == 0, 0.5 * time_step, 0.0).astype(f32), cell_z) for x in range(depth)]
    for a in range(3):
        x_low, x_high = low_and_high("gx", x_one, x_two, a)
        y_low, y_high = low_and_high("gy", y_one, y_two, a)
        rows = [x_low] + [velocity[a, x] for x in range(depth)] + [x_high]
        rows = [turned(row, cell_z) for row in rows]
        low, high = turned(y_low, cell_z), turned(y_high, cell_z)
        for x in range(depth):
            here = rows[x + 1]
            above = high if x == depth - 1 else pltpu.roll(high, LANES - cell_z * (x + 1), 1)
            below = low if x == 0 else pltpu.roll(low, LANES - cell_z * x, 1)
            y_up = jnp.where(lane < LANES - cell_z, pltpu.roll(here, LANES - cell_z, 1), above)
            y_down = jnp.where(lane >= cell_z, pltpu.roll(here, cell_z, 1), below)
            next_tile = pltpu.roll(pltpu.roll(here, cell_z - 1, 1), 1, 0)
            last_tile = pltpu.roll(pltpu.roll(here, LANES - cell_z + 1, 1), SUB - 1, 0)
            next_tile = jnp.where(sub == 0, 0.0, next_tile)
            last_tile = jnp.where(sub == SUB - 1, 0.0, last_tile)
            z_up = jnp.where(z == cell_z - 1, next_tile, pltpu.roll(here, LANES - 1, 1))
            z_down = jnp.where(z == 0, last_tile, pltpu.roll(here, 1, 1))
            for b, difference in enumerate((rows[x + 2] - rows[x], y_up - y_down, z_up - z_down)):
                grad[pl.ds(((3 * a + b) * depth + x) * SUB, SUB), :] = difference * scales[x]
    keep[...] = jnp.zeros(keep.shape, f32)
    send[...] = jnp.zeros(send.shape, f32)
    for h, owned, tile in owned_slots(tiles, me, helper):

        @pl.when(owned)
        def _(h=h, tile=tile):
            g = [grad[pl.ds(i * depth * SUB + SUB - 1 - tile, depth, stride=SUB), :] for i in range(9)]
            rows = g + coefficients(g, [moments[h, i] for i in range(16)])
            stays = (me & 1) == (h & 1)

            @pl.when(stays)
            def _():
                for i, row in enumerate(rows):
                    keep[h >> 1, i] = row

            @pl.when(jnp.logical_not(stays))
            def _():
                for i, row in enumerate(rows):
                    send[h >> 1, i] = row


def call_gradients(tiles, helper_tile, velocity, halos, wall_cells, moments):
    slots = helper_tile.shape[1]
    depth = velocity.shape[1]
    half = jax.ShapeDtypeStruct((slots // 2, 12, depth, LANES), f32)
    return pl.pallas_call(
        functools.partial(gradients, tiles),
        out_shape=(jax.ShapeDtypeStruct((9 * depth * SUB, LANES), f32), half, half),
        in_specs=[vmem] * 8,
        out_specs=(vmem,) * 3,
        compiler_params=pltpu.CompilerParams(vmem_limit_bytes=8 << 20),
        cost_estimate=small(4 << 20, 1 << 20),
        name="gradients",
    )(helper_tile, velocity, *halos, wall_cells, moments)


def swapped(block, bit):
    size = lax.axis_size("gy")
    return lax.ppermute(block, "gy", [(i, i ^ (1 << bit)) for i in range(size)])


def merge(bit, before, kept, received, keep, send):
    mine = (lax.axis_index("gy") >> (bit + 1)) & 1
    for j in range(0, kept.shape[0], 2):
        for i in range(kept.shape[1]):
            even, odd = [kept[k, i] + received[k, i] for k in (j, j + 1)]
            keep[j // 2, i] = jnp.where(mine == 0, even, odd)
            send[j // 2, i] = jnp.where(mine == 0, odd, even)


def call_merge(bit, before, kept, received):
    half = jax.ShapeDtypeStruct((kept.shape[0] // 2,) + kept.shape[1:], f32)
    return pl.pallas_call(
        functools.partial(merge, bit),
        out_shape=(half, half),
        in_specs=[anywhere, vmem, vmem],
        out_specs=(vmem, vmem),
        compiler_params=pltpu.CompilerParams(vmem_limit_bytes=4 << 20),
        cost_estimate=small(1 << 10, 1 << 18),
        name="merge",
    )(before, kept, received)


def call_join(before, first, second):
    def join(before, first, second, out):
        out[: first.shape[0]] = first[...]
        out[first.shape[0] :] = second[...]

    return pl.pallas_call(
        join,
        out_shape=jax.ShapeDtypeStruct((2 * first.shape[0],) + first.shape[1:], f32),
        in_specs=[anywhere, vmem, vmem],
        out_specs=vmem,
        compiler_params=pltpu.CompilerParams(vmem_limit_bytes=4 << 20),
        cost_estimate=small(1 << 10, 1 << 18),
        name="join",
    )(before, first, second)


def stress_rows(sums, inverse):
    second = [s * inverse for s in sums]
    stretch = 1.0 / (1.0 - (second[0] + second[1] + second[2]) / max_extension)
    return [(stretch * s - (1.0 if i < 3 else 0.0)) * (1.0 / weissenberg) for i, s in enumerate(second)]


def tile_grad(grad, depth, tile, x):
    return [wide(grad[pl.ds((i * depth + x + 1) * SUB - 1 - tile, 1), :]) for i in range(9)]


def tile_sums(read, write, noise, matrices, count, add, many):
    sums = [jnp.zeros((SUB, LANES), f32)] * many
    for group in range(count // (2 * SUB)):
        pairs = [noise_rows(functools.partial(noise, step), group * 2 * SUB) for step in range(len(matrices))]
        for half in range(2):
            rows = pl.ds((2 * group + half) * SUB, SUB)
            q = [read(a, rows) for a in range(3)]
            for step, matrix in enumerate(matrices):
                q = stepped(q, pairs[step][half], matrix)
            for a in range(3):
                write(a, rows, q[a])
            sums = add(sums, q)
    return sums


def add_square(sums, q):
    return [sums[0] + (q[0] * q[0] + q[1] * q[1] + q[2] * q[2])]


def ordinary(first, has_block, has_base, has_extra, *refs):
    refs = list(refs)
    before, base, noise, grad = refs[:4]
    del refs[:4]
    block = refs.pop(0) if has_block else None
    if has_base:
        refs.pop(0)
    extra_near = refs.pop(0) if has_extra else None
    new_base = refs.pop(0) if has_block else None
    new_extra = refs.pop(0) if has_extra else None
    fields, stress, halfway, relaxes, sems = refs
    here, _, count, cells = fields.shape
    depth = cells // LANES
    inverse = 1.0 / count
    copies = []
    if has_block:
        last = block.shape[0]
        copies += [
            pltpu.make_async_copy(block.at[i], new_base.at[0, 0, first - last + i], sems.at[i]) for i in range(last)
        ]
    if has_extra:
        copies += [
            pltpu.make_async_copy(extra_near.at[0, 0, a], new_extra.at[0, 0, a], sems.at[len(copies) + a])
            for a in range(3)
        ]
    for copy in copies:
        copy.start()
    for place in range(here):
        tile = first + place
        totals = []
        for x in range(depth):
            total = jnp.zeros((SUB, LANES), f32)
            for group in range(count // SUB):
                for a in range(3):
                    q = base[0, 0, tile, a, pl.ds(group * SUB, SUB), pl.ds(x * LANES, LANES)]
                    total = total + q * q
            totals.append(total)
        for step in range(2):
            relaxes[place, step] = relax_of(packed_sum(totals), inverse)
            totals = []
            for x in range(depth):
                lanes = pl.ds(x * LANES, LANES)
                matrix = with_diagonal(tile_grad(grad, depth, tile, x), wide(relaxes[place, step, pl.ds(x, 1), :]))

                def read(a, rows):
                    return base[0, 0, tile, a, rows, lanes] if step == 0 else halfway[place, a, rows, lanes]

                def write(a, rows, value):
                    if step == 0:
                        halfway[place, a, rows, lanes] = value
                    else:
                        fields[place, a, rows, lanes] = value

                def shock(_, a, rows):
                    return noise[0, 0, tile, step, a, rows, lanes]

                if step == 0:
                    totals += tile_sums(read, write, shock, [matrix], count, add_square, 1)
                else:
                    totals.append(tile_sums(read, write, shock, [matrix], count, add_moments, 6))
        for i, row in enumerate(stress_rows([packed_sum(list(same)) for same in zip(*totals)], inverse)):
            stress[i, place] = row
    for copy in copies:
        copy.wait()


def call_ordinary(first, here, before, base_fields, base_noise, grad, block, new_base, new_extra):
    count, cells = base_fields.shape[-2:]
    depth = cells // LANES
    has_block, has_base, has_extra = block is not None, new_base is not None, new_extra is not None
    operands = [before, *near_memory(base_fields, base_noise), grad]
    specs = [anywhere, vmem, vmem, vmem]
    shapes, out_specs, aliases = [], [], {}
    copies = 0
    if has_block:
        operands += near_memory(block)
        specs.append(vmem)
        shapes.append(jax.ShapeDtypeStruct(base_fields.shape, f32))
        out_specs.append(hbm)
        copies += block.shape[0]
    if has_base:
        aliases[len(operands)] = 0
        operands.append(new_base)
        specs.append(hbm)
    if has_extra:
        operands += near_memory(new_extra)
        specs.append(vmem)
        shapes.append(jax.ShapeDtypeStruct(new_extra.shape, f32))
        out_specs.append(hbm)
        copies += 3
    shapes += [
        pltpu.VMEM((here, 3, count, cells), f32),
        jax.ShapeDtypeStruct((6, here, depth, LANES), f32),
    ]
    out_specs += [vmem, vmem]
    results = pl.pallas_call(
        functools.partial(ordinary, first, has_block, has_base, has_extra),
        out_shape=tuple(shapes),
        in_specs=specs,
        out_specs=tuple(out_specs),
        input_output_aliases=aliases,
        scratch_shapes=[
            pltpu.VMEM((here, 3, count, cells), f32),
            pltpu.VMEM((here, 2, depth, LANES), f32),
            pltpu.SemaphoreType.DMA((max(copies, 1),)),
        ],
        compiler_params=pltpu.CompilerParams(vmem_limit_bytes=SMALL),
        cost_estimate=small(8 << 20, 3 << 20),
        name="ordinary_tiles",
    )(*operands)
    results = list(results)
    piece, block = results.pop(), results.pop()
    new_base = results.pop(0) if has_block else None
    return new_base, block, piece, (results[0] if has_extra else None)


def extra(unroll, before, base, noise, moments, kept, received, new_fields, reply, message):
    _, _, _, count, cells = base.shape
    inverse = 1.0 / float(ALL_FIELDS)
    zero = jnp.zeros((SUB, LANES), f32)
    message[...] = kept[0] + received[0]
    own = coefficients([message[i] for i in range(9)], [moments[i] for i in range(16)])
    both = [message[9 + i] + own[i] for i in range(3)]
    first = relax_of(both[2], inverse)
    second = relax_of(both[0] + first * (both[1] + first * both[2]), inverse)
    reply[0], reply[1] = first, second

    @pl.loop(0, cells // LANES)
    def _(x):
        lanes = pl.ds(pl.multiple_of(x * LANES, LANES), LANES)
        grad = [wide(message[i, pl.ds(x, 1), :]) for i in range(9)]
        matrices = [with_diagonal(grad, wide(reply[step, pl.ds(x, 1), :])) for step in range(2)]

        def body(i, sums):
            start = pl.multiple_of(i * 2 * SUB, 2 * SUB)
            pairs = [noise_rows(lambda a, rows: noise[0, 0, step, a, rows, lanes], start) for step in range(2)]
            for half in range(2):
                rows = pl.ds(start + half * SUB, SUB)
                q = [base[0, 0, a, rows, lanes] for a in range(3)]
                for step in range(2):
                    q = stepped(q, pairs[step][half], matrices[step])
                for a in range(3):
                    new_fields[0, 0, a, rows, lanes] = q[a]
                sums = add_moments(sums, q)
            return sums

        for i, s in enumerate(lax.fori_loop(0, count // (2 * SUB), body, [zero] * 6, unroll=unroll)):
            reply[2 + i, pl.ds(x, 1), :] = column_sum(s)


def call_extra(before, extra_fields, extra_noise, moments, kept, received):
    depth = extra_fields.shape[-1] // LANES
    return pl.pallas_call(
        functools.partial(extra, 7),
        out_shape=(
            pltpu.VMEM(extra_fields.shape, f32),
            jax.ShapeDtypeStruct((8, depth, LANES), f32),
        ),
        in_specs=[anywhere, vmem, vmem, vmem, vmem, vmem],
        out_specs=(vmem, vmem),
        scratch_shapes=[pltpu.VMEM(kept.shape[1:], f32)],
        compiler_params=pltpu.CompilerParams(vmem_limit_bytes=SMALL),
        cost_estimate=small(32 << 20, 9 << 20),
        name="extra_fields",
    )(before, *near_memory(extra_fields, extra_noise), moments, kept, received)


def finish(piece_count, before, block, *refs):
    pieces, (_, new_base, rows, sems) = refs[:piece_count], refs[piece_count:]
    _, depth, tiles, _ = rows.shape
    last = block.shape[0]
    flat = rows.reshape(6 * depth * tiles, LANES)
    copies = [pltpu.make_async_copy(block.at[i], new_base.at[0, 0, tiles - last + i], sems.at[i]) for i in range(last)]
    for copy in copies:
        copy.start()
    tile = 0
    for piece in pieces:
        for place in range(piece.shape[1]):
            for i in range(6):
                flat[pl.ds(i * depth * tiles + tile, depth, stride=tiles), :] = piece[i, place]
            tile += 1
    for copy in copies:
        copy.wait()


def call_finish(before, block, pieces, new_base):
    tiles, cells = new_base.shape[2], new_base.shape[-1]
    return pl.pallas_call(
        functools.partial(finish, len(pieces)),
        out_shape=(
            jax.ShapeDtypeStruct(new_base.shape, f32),
            jax.ShapeDtypeStruct((6, cells // LANES, tiles, LANES), f32),
        ),
        in_specs=[anywhere, vmem] + [vmem] * len(pieces) + [hbm],
        out_specs=(hbm, vmem),
        input_output_aliases={2 + len(pieces): 0},
        scratch_shapes=[pltpu.SemaphoreType.DMA((block.shape[0],))],
        compiler_params=pltpu.CompilerParams(vmem_limit_bytes=4 << 20),
        cost_estimate=small(1 << 10, 1 << 20),
        name="finish",
    )(before, *near_memory(block), *pieces, new_base)


def heavy(bits, helper, base, noise, grad, near, far, ready, old_base, new_base, stress, fields, rows, answer, sems):
    _, _, tiles, _, count, cells = base.shape
    slots = helper.shape[1]
    me = lax.axis_index("gy")
    depth = cells // LANES
    flat = rows.reshape(6 * depth * tiles, LANES)

    def store(h, tile):
        return pltpu.make_async_copy(fields.at[h], new_base.at[0, 0, tile], sems.at[h])

    def result(x):
        target = stress.at[0, 0, :, :, pl.ds(x * LANES, LANES)]
        return pltpu.make_async_copy(rows.at[:, x], target, sems.at[slots + x])

    rows[...] = ready[...]
    found = owned_slots(tiles, me, helper)
    places = jnp.int32(0)
    order = [jnp.int32(0)] * HEAVY_MOST
    for h, owned, tile in found:
        entry = h * tiles + tile
        order = [jnp.where(owned & (places == k), entry, kept) for k, kept in enumerate(order)]
        places = places + owned.astype(jnp.int32)

    for k, entry in enumerate(order):

        @pl.when(k < places)
        def _(entry=entry):
            h, tile = entry // tiles, entry % tiles
            flips = me ^ h
            place = sum(((flips >> (bits - 1 - i)) & 1) << i for i in range(bits))
            is_far = place >= slots // 2
            place = place & (slots // 2 - 1)
            for i in range(near.shape[1]):
                answer[i] = jnp.where(is_far, far[place, i], near[place, i])
            totals = []
            for x in range(depth):
                lanes = pl.ds(x * LANES, LANES)
                g = tile_grad(grad, depth, tile, x)
                matrices = [with_diagonal(g, wide(answer[step, pl.ds(x, 1), :])) for step in range(2)]

                def read(a, part):
                    return base[0, 0, tile, a, part, lanes]

                def write(a, part, value):
                    fields[h, a, part, lanes] = value

                def shock(step, a, part):
                    return noise[0, 0, tile, step, a, part, lanes]

                totals.append(tile_sums(read, write, shock, matrices, count, add_moments, 6))
            store(h, tile).start()
            sums = [packed_sum(list(same)) + answer[2 + i] for i, same in enumerate(zip(*totals))]
            for i, value in enumerate(stress_rows(sums, 1.0 / ALL_FIELDS)):
                flat[pl.ds(i * depth * tiles + tile, depth, stride=tiles), :] = value

    for x in range(depth):
        result(x).start()
    for k, entry in enumerate(order):

        @pl.when(k < places)
        def _(entry=entry):
            store(entry // tiles, entry % tiles).wait()

    for x in range(depth):
        result(x).wait()


def call_heavy(bits, helper_tile, base_fields, base_noise, grad, near, far, ready, new_base):
    _, _, tiles, _, count, cells = base_fields.shape
    depth = cells // LANES
    slots = helper_tile.shape[1]
    return pl.pallas_call(
        functools.partial(heavy, bits),
        out_shape=(
            jax.ShapeDtypeStruct(new_base.shape, f32),
            jax.ShapeDtypeStruct((1, 1, 6, tiles, cells), f32),
        ),
        in_specs=[vmem] * 7 + [hbm],
        out_specs=(hbm, hbm),
        input_output_aliases={7: 0},
        scratch_shapes=[
            pltpu.VMEM((slots, 3, count, cells), f32),
            pltpu.VMEM((6, depth, tiles, LANES), f32),
            pltpu.VMEM(near.shape[1:], f32),
            pltpu.SemaphoreType.DMA((slots + depth,)),
        ],
        compiler_params=pltpu.CompilerParams(vmem_limit_bytes=SMALL),
        cost_estimate=small(8 << 20, 4 << 20),
        name="heavy_tiles",
    )(helper_tile, *near_memory(base_fields, base_noise), grad, near, far, ready, new_base)


def per_device(
    velocity, wall_cells, tile_counts, helper_tile, base_fields, extra_fields, base_noise, extra_noise
):
    tiles = tile_counts.shape[2]
    bits = lax.axis_size("gy").bit_length() - 1
    helper_tile, x_one, x_two, y_one, y_two = call_edges(helper_tile, velocity)
    halos = two_swaps(x_one, x_two, "gx") + two_swaps(y_one, y_two, "gy")
    moments = call_heavy_moments(helper_tile, base_fields, base_noise)
    grad, keep, send = call_gradients(tiles, helper_tile, velocity, halos, wall_cells, moments)
    gaps = 2 * bits - 2
    new_base, block, pieces, done = None, None, [], 0

    def fill(before, extra_near=None):
        nonlocal new_base, block, done
        here = (tiles - done) // (gaps - len(pieces))
        new_base, block, piece, extra_far = call_ordinary(
            done, here, before, base_fields, base_noise, grad, block, new_base, extra_near
        )
        pieces.append(piece)
        done += here
        return piece, extra_far

    for bit in range(bits):
        received = swapped(send, bit)
        if bit == 1:
            before = extra_sums = call_extra_moments(send, extra_fields, extra_noise)
        else:
            before, _ = fill(send)
        if bit < bits - 1:
            keep, send = call_merge(bit, before, keep, received)
    extra_near, reply = call_extra(before, extra_fields, extra_noise, extra_sums, keep, received)
    near = reply[None]
    for bit in range(bits - 1, 0, -1):
        received = swapped(near, bit)
        if bit == bits - 1:
            before, new_extra = fill(near, extra_near)
        else:
            before, _ = fill(near)
        near = call_join(before, near, received)
    far = swapped(near, 0)
    new_base, ready = call_finish(near, block, pieces, new_base)
    new_base, stress = call_heavy(bits, helper_tile, base_fields, base_noise, grad, near, far, ready, new_base)
    return new_base, new_extra, jnp.swapaxes(stress, 2, 3)


def solution(mesh):
    in_specs = (
        P(None, "gx", "gy", None),
        P("gx", "gy", None),
        P("gx", "gy", None),
        P("gx", None),
        P("gx", "gy", None, None, None, None),
        P("gx", "gy", None, None, None),
        P("gx", "gy", None, None, None, None, None),
        P("gx", "gy", None, None, None, None),
    )
    out_specs = (
        P("gx", "gy", None, None, None, None),
        P("gx", "gy", None, None, None),
        P("gx", "gy", None, None, None),
    )
    return jax.shard_map(
        per_device, mesh=mesh, in_specs=in_specs, out_specs=out_specs, check_vma=False
    )
```

```python
import functools

import jax
import jax.numpy as jnp
from jax import lax
from jax.experimental import pallas as pl
from jax.experimental.pallas import tpu as pltpu
from jax.sharding import PartitionSpec as P

ALL_FIELDS = 256
HEAVY_MOST = 4
LANES = 128
SUB = 8
SMALL = 10 << 20

time_step = 0.05
weissenberg = 0.25
max_extension = 50.0
noise_scale = (time_step / weissenberg) ** 0.5
component_pairs = ((0, 0), (1, 1), (2, 2), (0, 1), (0, 2), (1, 2))
moment_of = {(0, 0): 0, (1, 1): 1, (2, 2): 2, (0, 1): 3, (1, 0): 3, (0, 2): 4, (2, 0): 4, (1, 2): 5, (2, 1): 5}
f32 = jnp.float32

vmem = pl.BlockSpec(memory_space=pltpu.VMEM)
hbm = pl.BlockSpec(memory_space=pltpu.HBM)
anywhere = pl.BlockSpec(memory_space=pl.ANY)


def far_memory(*arrays):
    return [pltpu.with_memory_space_constraint(array, pltpu.HBM) for array in arrays]


def near_memory(*arrays):
    return [pltpu.with_memory_space_constraint(array, pltpu.VMEM) for array in arrays]


def column_sum(value):
    return jnp.sum(value, axis=0, keepdims=True)


def interleaved(a, b, bit):
    low = (lax.broadcasted_iota(jnp.int32, (SUB, LANES), 0) & bit) == 0
    return jnp.where(low, a, b) + pltpu.roll(jnp.where(low, b, a), bit, 0)


def packed_sums(values_of, count):
    stack = []
    for x in range(count):
        bit, values = 1, values_of(x)
        while stack and stack[-1][0] == bit:
            values = [interleaved(a, b, bit) for a, b in zip(stack.pop()[1], values)]
            bit *= 2
        stack.append((bit, values))
    return stack[0][1]


def wide(row):
    return jnp.broadcast_to(row, (SUB, LANES))


def turned(value, cell_z):
    sub = lax.broadcasted_iota(jnp.int32, value.shape, 0)
    group = lax.broadcasted_iota(jnp.int32, value.shape, 1) // cell_z
    skewed = pltpu.roll(value, cell_z, 1, stride=cell_z, stride_axis=0)
    mixed = jnp.take_along_axis(skewed, (group + sub) & (SUB - 1), axis=0, mode="promise_in_bounds")
    return pltpu.roll(mixed, 0, 1, stride=cell_z, stride_axis=0)


def relax_of(total, inverse):
    factor = 1.0 / (1.0 - total * inverse / max_extension)
    return 1.0 - (time_step * 0.5 / weissenberg) * factor


def stepped(vectors, noise, matrix):
    return [
        matrix[3 * a] * vectors[0]
        + matrix[3 * a + 1] * vectors[1]
        + matrix[3 * a + 2] * vectors[2]
        + noise_scale * noise[a]
        for a in range(3)
    ]


def with_diagonal(grad, relax):
    return [g + relax if i % 4 == 0 else g for i, g in enumerate(grad)]


def noise_rows(ref, start):
    both = [ref(a, pl.ds(start, 2 * SUB)).astype(f32) for a in range(3)]
    return [[w[:SUB] for w in both], [w[SUB:] for w in both]]


def add_moments(sums, q):
    return [s + q[a] * q[b] for s, (a, b) in zip(sums, component_pairs)]


def product_sums(sums, q, w):
    terms = [q[a] * q[b] for a, b in component_pairs]
    terms += [q[a] * w[b] for a in range(3) for b in range(3)]
    terms += [w[0] * w[0] + w[1] * w[1] + w[2] * w[2]]
    return [s + t for s, t in zip(sums, terms)]


def coefficients(g, m):
    cross = lambda a, b: m[6 + 3 * a + b]
    square = lambda a, b: m[moment_of[a, b]]
    once, twice, kick = 0.0, 0.0, 0.0
    for a in range(3):
        for b in range(3):
            once += g[3 * a + b] * square(a, b)
            kick += g[3 * a + b] * cross(b, a)
            inner = 0.0
            for c in range(3):
                inner += g[3 * a + c] * square(b, c)
            twice += g[3 * a + b] * inner
    return [
        twice + (2 * noise_scale) * kick + noise_scale**2 * m[15],
        2.0 * once + (2 * noise_scale) * (cross(0, 0) + cross(1, 1) + cross(2, 2)),
        m[0] + m[1] + m[2],
    ]


def owned_slots(tiles, me, helper):
    found = []
    row = helper[...]
    for h in range(helper.shape[1]):
        tile = row[0, h] - me * tiles
        found.append((h, (tile >= 0) & (tile < tiles), tile))
    return found


def owned_order(tiles, me, helper):
    places = jnp.int32(0)
    order = [jnp.int32(0)] * HEAVY_MOST
    for h, owned, tile in owned_slots(tiles, me, helper):
        entry = h * tiles + tile
        order = [jnp.where(owned & (places == k), entry, kept) for k, kept in enumerate(order)]
        places = places + owned.astype(jnp.int32)
    return places, [(entry // tiles, entry % tiles) for entry in order]


def small(flops, traffic):
    return pl.CostEstimate(flops=flops, bytes_accessed=traffic, transcendentals=0)


def is_even(axis):
    return (lax.axis_index(axis) & 1) == 0


def edges(helper, velocity, helper_near, x_one, x_two, y_one, y_two):
    depth, width = velocity.shape[1:3]
    helper_near[...] = helper[...]
    even = is_even("gx")
    for a in range(3):
        first, last = velocity[a, 0], velocity[a, depth - 1]
        x_one[a] = jnp.where(even, last, first)
        x_two[a] = jnp.where(even, first, last)
    even = is_even("gy")
    for a in range(3):
        for x in range(depth):
            first, last = velocity[a, x, pl.ds(0, 1), :], velocity[a, x, pl.ds(width - 1, 1), :]
            y_one[a, pl.ds(x, 1), :] = jnp.where(even, last, first)
            y_two[a, pl.ds(x, 1), :] = jnp.where(even, first, last)


def call_edges(helper_tile, velocity):
    _, depth, width, length = velocity.shape
    along_x = jax.ShapeDtypeStruct((3, width, length), f32)
    along_y = jax.ShapeDtypeStruct((3, depth, length), f32)
    return pl.pallas_call(
        edges,
        out_shape=(jax.ShapeDtypeStruct(helper_tile.shape, jnp.int32), along_x, along_x, along_y, along_y),
        in_specs=[vmem, vmem],
        out_specs=(vmem,) * 5,
        compiler_params=pltpu.CompilerParams(vmem_limit_bytes=4 << 20),
        cost_estimate=small(1 << 10, 1 << 17),
        name="edges",
    )(*far_memory(helper_tile, velocity))


def two_swaps(one, two, axis):
    size = lax.axis_size(axis)
    within = [(i, i ^ 1) for i in range(size)]
    across = [(i, (i - 1 + 2 * (i & 1)) % size) for i in range(size)]
    return lax.ppermute(one, axis, within), lax.ppermute(two, axis, across)


def low_and_high(axis, one, two, a):
    even, place = is_even(axis), lax.axis_index(axis)
    low = jnp.where(even, two[a], one[a])
    high = jnp.where(even, one[a], two[a])
    return jnp.where(place == 0, 0.0, low), jnp.where(place == lax.axis_size(axis) - 1, 0.0, high)


def heavy_moments(helper, base, noise, out, fields, shocks, sems):
    _, _, count, cells = fields.shape
    tiles = base.shape[2]
    me = lax.axis_index("gy")

    def loads(k, tile):
        return (
            pltpu.make_async_copy(base.at[0, 0, tile], fields.at[k], sems.at[0, k]),
            pltpu.make_async_copy(noise.at[0, 0, tile, 0], shocks.at[k], sems.at[1, k]),
        )

    places, order = owned_order(tiles, me, helper)
    for k, (_, tile) in enumerate(order):

        @pl.when(k < places)
        def _(k=k, tile=tile):
            for copy in loads(k, tile):
                copy.start()

    for k, (h, tile) in enumerate(order):

        @pl.when(k < places)
        def _(k=k, h=h, tile=tile):
            for copy in loads(k, tile):
                copy.wait()

            def sums_of(x):
                lanes = pl.ds(x * LANES, LANES)
                sums = [jnp.zeros((SUB, LANES), f32)] * 16
                for group in range(count // (2 * SUB)):
                    pair = noise_rows(lambda a, rows: shocks[k, a, rows, lanes], group * 2 * SUB)
                    for half in range(2):
                        rows = pl.ds((2 * group + half) * SUB, SUB)
                        sums = product_sums(sums, [fields[k, a, rows, lanes] for a in range(3)], pair[half])
                return sums

            for i, value in enumerate(packed_sums(sums_of, cells // LANES)):
                out[h, i] = value


def call_heavy_moments(helper_tile, base_fields, base_noise):
    slots = helper_tile.shape[1]
    count, cells = base_fields.shape[-2:]
    return pl.pallas_call(
        heavy_moments,
        out_shape=jax.ShapeDtypeStruct((slots, 16, cells // LANES, LANES), f32),
        in_specs=[vmem, hbm, hbm],
        out_specs=vmem,
        scratch_shapes=[
            pltpu.VMEM((HEAVY_MOST, 3, count, cells), f32),
            pltpu.VMEM((HEAVY_MOST, 3, count, cells), jnp.bfloat16),
            pltpu.SemaphoreType.DMA((2, HEAVY_MOST)),
        ],
        compiler_params=pltpu.CompilerParams(vmem_limit_bytes=SMALL),
        cost_estimate=small(8 << 20, 3 << 20),
        name="heavy_moments",
    )(helper_tile, *far_memory(base_fields, base_noise))


def extra_moments(unroll, before, base, noise, out):
    _, _, _, count, cells = base.shape
    zero = jnp.zeros((SUB, LANES), f32)

    @pl.loop(0, cells // LANES)
    def _(x):
        lanes = pl.ds(pl.multiple_of(x * LANES, LANES), LANES)

        def body(i, sums):
            start = pl.multiple_of(i * 2 * SUB, 2 * SUB)
            pair = noise_rows(lambda a, rows: noise[0, 0, 0, a, rows, lanes], start)
            for half in range(2):
                rows = pl.ds(start + half * SUB, SUB)
                sums = product_sums(sums, [base[0, 0, a, rows, lanes] for a in range(3)], pair[half])
            return sums

        for i, s in enumerate(lax.fori_loop(0, count // (2 * SUB), body, [zero] * 16, unroll=unroll)):
            out[i, pl.ds(x, 1), :] = column_sum(s)


def call_extra_moments(before, extra_fields, extra_noise):
    cells = extra_fields.shape[-1]
    return pl.pallas_call(
        functools.partial(extra_moments, 7),
        out_shape=jax.ShapeDtypeStruct((16, cells // LANES, LANES), f32),
        in_specs=[anywhere, vmem, vmem],
        out_specs=vmem,
        compiler_params=pltpu.CompilerParams(vmem_limit_bytes=SMALL),
        cost_estimate=small(8 << 20, 5 << 20),
        name="extra_moments",
    )(before, *near_memory(extra_fields, extra_noise))


def gradients(tiles, helper, velocity, x_one, x_two, y_one, y_two, wall, moments, grad, keep, send):
    me = lax.axis_index("gy")
    depth = velocity.shape[1]
    cell_z = velocity.shape[3] // tiles
    sub = lax.broadcasted_iota(jnp.int32, (SUB, LANES), 0)
    lane = lax.broadcasted_iota(jnp.int32, (SUB, LANES), 1)
    z = lane % cell_z
    scales = [turned(jnp.where(wall[x] == 0, 0.5 * time_step, 0.0).astype(f32), cell_z) for x in range(depth)]
    for a in range(3):
        x_low, x_high = low_and_high("gx", x_one, x_two, a)
        y_low, y_high = low_and_high("gy", y_one, y_two, a)
        rows = [x_low] + [velocity[a, x] for x in range(depth)] + [x_high]
        rows = [turned(row, cell_z) for row in rows]
        low, high = turned(y_low, cell_z), turned(y_high, cell_z)
        for x in range(depth):
            here = rows[x + 1]
            above = high if x == depth - 1 else pltpu.roll(high, LANES - cell_z * (x + 1), 1)
            below = low if x == 0 else pltpu.roll(low, LANES - cell_z * x, 1)
            y_up = jnp.where(lane < LANES - cell_z, pltpu.roll(here, LANES - cell_z, 1), above)
            y_down = jnp.where(lane >= cell_z, pltpu.roll(here, cell_z, 1), below)
            next_tile = pltpu.roll(pltpu.roll(here, cell_z - 1, 1), 1, 0)
            last_tile = pltpu.roll(pltpu.roll(here, LANES - cell_z + 1, 1), SUB - 1, 0)
            next_tile = jnp.where(sub == 0, 0.0, next_tile)
            last_tile = jnp.where(sub == SUB - 1, 0.0, last_tile)
            z_up = jnp.where(z == cell_z - 1, next_tile, pltpu.roll(here, LANES - 1, 1))
            z_down = jnp.where(z == 0, last_tile, pltpu.roll(here, 1, 1))
            for b, difference in enumerate((rows[x + 2] - rows[x], y_up - y_down, z_up - z_down)):
                grad[pl.ds(((3 * a + b) * depth + x) * SUB, SUB), :] = difference * scales[x]
    keep[...] = jnp.zeros(keep.shape, f32)
    send[...] = jnp.zeros(send.shape, f32)
    for h, owned, tile in owned_slots(tiles, me, helper):

        @pl.when(owned)
        def _(h=h, tile=tile):
            g = [grad[pl.ds(i * depth * SUB + SUB - 1 - tile, depth, stride=SUB), :] for i in range(9)]
            rows = g + coefficients(g, [moments[h, i] for i in range(16)])
            stays = (me & 1) == (h & 1)

            @pl.when(stays)
            def _():
                for i, row in enumerate(rows):
                    keep[h >> 1, i] = row

            @pl.when(jnp.logical_not(stays))
            def _():
                for i, row in enumerate(rows):
                    send[h >> 1, i] = row


def call_gradients(tiles, helper_tile, velocity, halos, wall_cells, moments):
    slots = helper_tile.shape[1]
    depth = velocity.shape[1]
    half = jax.ShapeDtypeStruct((slots // 2, 12, depth, LANES), f32)
    return pl.pallas_call(
        functools.partial(gradients, tiles),
        out_shape=(jax.ShapeDtypeStruct((9 * depth * SUB, LANES), f32), half, half),
        in_specs=[vmem] * 8,
        out_specs=(vmem,) * 3,
        compiler_params=pltpu.CompilerParams(vmem_limit_bytes=8 << 20),
        cost_estimate=small(4 << 20, 1 << 20),
        name="gradients",
    )(helper_tile, velocity, *halos, wall_cells, moments)


def swapped(block, flip):
    size = lax.axis_size("gy")
    return lax.ppermute(block, "gy", [(i, i ^ flip) for i in range(size)])


def merge(before, kept, received, keep, *sends):
    pair = lax.axis_index("gy") >> 1
    for flip, out in enumerate((keep,) + sends):
        out[...] = kept[pair ^ flip] + received[pair ^ flip]


def call_merge(before, kept, received):
    one = jax.ShapeDtypeStruct(kept.shape[1:], f32)
    return pl.pallas_call(
        merge,
        out_shape=(one,) * kept.shape[0],
        in_specs=[anywhere, vmem, vmem],
        out_specs=(vmem,) * kept.shape[0],
        compiler_params=pltpu.CompilerParams(vmem_limit_bytes=4 << 20),
        cost_estimate=small(1 << 10, 1 << 18),
        name="merge",
    )(before, kept, received)


def join(before, *refs):
    for i, ref in enumerate(refs[:-1]):
        refs[-1][i] = ref[...]


def call_join(before, blocks):
    return pl.pallas_call(
        join,
        out_shape=jax.ShapeDtypeStruct((len(blocks),) + blocks[0].shape, f32),
        in_specs=[anywhere] + [vmem] * len(blocks),
        out_specs=vmem,
        compiler_params=pltpu.CompilerParams(vmem_limit_bytes=4 << 20),
        cost_estimate=small(1 << 10, 1 << 18),
        name="join",
    )(before, *blocks)


def stress_rows(sums, inverse):
    second = [s * inverse for s in sums]
    stretch = 1.0 / (1.0 - (second[0] + second[1] + second[2]) / max_extension)
    return [(stretch * s - (1.0 if i < 3 else 0.0)) * (1.0 / weissenberg) for i, s in enumerate(second)]


def tile_grad(grad, depth, tile, x):
    return [wide(grad[pl.ds((i * depth + x + 1) * SUB - 1 - tile, 1), :]) for i in range(9)]


def tile_sums(read, write, noise, matrices, count, add, many):
    sums = [jnp.zeros((SUB, LANES), f32)] * many
    for group in range(count // (2 * SUB)):
        pairs = [noise_rows(functools.partial(noise, step), group * 2 * SUB) for step in range(len(matrices))]
        for half in range(2):
            rows = pl.ds((2 * group + half) * SUB, SUB)
            q = [read(a, rows) for a in range(3)]
            for step, matrix in enumerate(matrices):
                q = stepped(q, pairs[step][half], matrix)
            for a in range(3):
                write(a, rows, q[a])
            sums = add(sums, q)
    return sums


def add_square(sums, q):
    return [sums[0] + (q[0] * q[0] + q[1] * q[1] + q[2] * q[2])]


def ordinary(first, has_block, has_base, has_extra, *refs):
    refs = list(refs)
    before, base, noise, grad = refs[:4]
    del refs[:4]
    block = refs.pop(0) if has_block else None
    if has_base:
        refs.pop(0)
    extra_near = refs.pop(0) if has_extra else None
    new_base = refs.pop(0) if has_block else None
    new_extra = refs.pop(0) if has_extra else None
    fields, stress, halfway, relaxes, sems = refs
    here, _, count, cells = fields.shape
    depth = cells // LANES
    inverse = 1.0 / count
    copies = []
    if has_block:
        last = block.shape[0]
        copies += [
            pltpu.make_async_copy(block.at[i], new_base.at[0, 0, first - last + i], sems.at[i]) for i in range(last)
        ]
    if has_extra:
        copies += [
            pltpu.make_async_copy(extra_near.at[0, 0, a], new_extra.at[0, 0, a], sems.at[len(copies) + a])
            for a in range(3)
        ]
    for copy in copies:
        copy.start()
    for place in range(here):
        tile = first + place

        def squares(x):
            total = jnp.zeros((SUB, LANES), f32)
            for group in range(count // SUB):
                for a in range(3):
                    q = base[0, 0, tile, a, pl.ds(group * SUB, SUB), pl.ds(x * LANES, LANES)]
                    total = total + q * q
            return [total]

        sums = packed_sums(squares, depth)
        for step in range(2):
            relaxes[place, step] = relax_of(sums[0], inverse)

            def sums_of(x):
                lanes = pl.ds(x * LANES, LANES)
                matrix = with_diagonal(tile_grad(grad, depth, tile, x), wide(relaxes[place, step, pl.ds(x, 1), :]))

                def read(a, rows):
                    return base[0, 0, tile, a, rows, lanes] if step == 0 else halfway[place, a, rows, lanes]

                def write(a, rows, value):
                    if step == 0:
                        halfway[place, a, rows, lanes] = value
                    else:
                        fields[place, a, rows, lanes] = value

                def shock(_, a, rows):
                    return noise[0, 0, tile, step, a, rows, lanes]

                if step == 0:
                    return tile_sums(read, write, shock, [matrix], count, add_square, 1)
                return tile_sums(read, write, shock, [matrix], count, add_moments, 6)

            sums = packed_sums(sums_of, depth)
        for i, row in enumerate(stress_rows(sums, inverse)):
            stress[i, place] = row
    for copy in copies:
        copy.wait()


def call_ordinary(first, here, before, base_fields, base_noise, grad, block, new_base, new_extra):
    count, cells = base_fields.shape[-2:]
    depth = cells // LANES
    has_block, has_base, has_extra = block is not None, new_base is not None, new_extra is not None
    operands = [before, *near_memory(base_fields, base_noise), grad]
    specs = [anywhere, vmem, vmem, vmem]
    shapes, out_specs, aliases = [], [], {}
    copies = 0
    if has_block:
        operands += near_memory(block)
        specs.append(vmem)
        shapes.append(jax.ShapeDtypeStruct(base_fields.shape, f32))
        out_specs.append(hbm)
        copies += block.shape[0]
    if has_base:
        aliases[len(operands)] = 0
        operands.append(new_base)
        specs.append(hbm)
    if has_extra:
        operands += near_memory(new_extra)
        specs.append(vmem)
        shapes.append(jax.ShapeDtypeStruct(new_extra.shape, f32))
        out_specs.append(hbm)
        copies += 3
    shapes += [
        pltpu.VMEM((here, 3, count, cells), f32),
        jax.ShapeDtypeStruct((6, here, depth, LANES), f32),
    ]
    out_specs += [vmem, vmem]
    results = pl.pallas_call(
        functools.partial(ordinary, first, has_block, has_base, has_extra),
        out_shape=tuple(shapes),
        in_specs=specs,
        out_specs=tuple(out_specs),
        input_output_aliases=aliases,
        scratch_shapes=[
            pltpu.VMEM((here, 3, count, cells), f32),
            pltpu.VMEM((here, 2, depth, LANES), f32),
            pltpu.SemaphoreType.DMA((max(copies, 1),)),
        ],
        compiler_params=pltpu.CompilerParams(vmem_limit_bytes=SMALL),
        cost_estimate=small(8 << 20, 3 << 20),
        name="ordinary_tiles",
    )(*operands)
    results = list(results)
    piece, block = results.pop(), results.pop()
    new_base = results.pop(0) if has_block else None
    return new_base, block, piece, (results[0] if has_extra else None)


def extra(unroll, before, base, noise, moments, *refs):
    *parts, new_fields, reply, message = refs
    _, _, _, count, cells = base.shape
    inverse = 1.0 / float(ALL_FIELDS)
    zero = jnp.zeros((SUB, LANES), f32)
    message[...] = sum(part[...] for part in parts)
    own = coefficients([message[i] for i in range(9)], [moments[i] for i in range(16)])
    both = [message[9 + i] + own[i] for i in range(3)]
    first = relax_of(both[2], inverse)
    second = relax_of(both[0] + first * (both[1] + first * both[2]), inverse)
    reply[0], reply[1] = first, second

    @pl.loop(0, cells // LANES)
    def _(x):
        lanes = pl.ds(pl.multiple_of(x * LANES, LANES), LANES)
        grad = [wide(message[i, pl.ds(x, 1), :]) for i in range(9)]
        matrices = [with_diagonal(grad, wide(reply[step, pl.ds(x, 1), :])) for step in range(2)]

        def body(i, sums):
            start = pl.multiple_of(i * 2 * SUB, 2 * SUB)
            pairs = [noise_rows(lambda a, rows: noise[0, 0, step, a, rows, lanes], start) for step in range(2)]
            for half in range(2):
                rows = pl.ds(start + half * SUB, SUB)
                q = [base[0, 0, a, rows, lanes] for a in range(3)]
                for step in range(2):
                    q = stepped(q, pairs[step][half], matrices[step])
                for a in range(3):
                    new_fields[0, 0, a, rows, lanes] = q[a]
                sums = add_moments(sums, q)
            return sums

        for i, s in enumerate(lax.fori_loop(0, count // (2 * SUB), body, [zero] * 6, unroll=unroll)):
            reply[2 + i, pl.ds(x, 1), :] = column_sum(s)


def call_extra(before, extra_fields, extra_noise, moments, parts):
    depth = extra_fields.shape[-1] // LANES
    return pl.pallas_call(
        functools.partial(extra, 7),
        out_shape=(
            pltpu.VMEM(extra_fields.shape, f32),
            jax.ShapeDtypeStruct((8, depth, LANES), f32),
        ),
        in_specs=[anywhere, vmem, vmem, vmem] + [vmem] * len(parts),
        out_specs=(vmem, vmem),
        scratch_shapes=[pltpu.VMEM(parts[0].shape, f32)],
        compiler_params=pltpu.CompilerParams(vmem_limit_bytes=SMALL),
        cost_estimate=small(32 << 20, 9 << 20),
        name="extra_fields",
    )(before, *near_memory(extra_fields, extra_noise), moments, *parts)


def finish(piece_count, before, block, *refs):
    pieces, (_, new_base, rows, sems) = refs[:piece_count], refs[piece_count:]
    _, depth, tiles, _ = rows.shape
    last = block.shape[0]
    flat = rows.reshape(6 * depth * tiles, LANES)
    copies = [pltpu.make_async_copy(block.at[i], new_base.at[0, 0, tiles - last + i], sems.at[i]) for i in range(last)]
    for copy in copies:
        copy.start()
    tile = 0
    for piece in pieces:
        for place in range(piece.shape[1]):
            for i in range(6):
                flat[pl.ds(i * depth * tiles + tile, depth, stride=tiles), :] = piece[i, place]
            tile += 1
    for copy in copies:
        copy.wait()


def call_finish(before, block, pieces, new_base):
    tiles, cells = new_base.shape[2], new_base.shape[-1]
    return pl.pallas_call(
        functools.partial(finish, len(pieces)),
        out_shape=(
            jax.ShapeDtypeStruct(new_base.shape, f32),
            jax.ShapeDtypeStruct((6, cells // LANES, tiles, LANES), f32),
        ),
        in_specs=[anywhere, vmem] + [vmem] * len(pieces) + [hbm],
        out_specs=(hbm, vmem),
        input_output_aliases={2 + len(pieces): 0},
        scratch_shapes=[pltpu.SemaphoreType.DMA((block.shape[0],))],
        compiler_params=pltpu.CompilerParams(vmem_limit_bytes=4 << 20),
        cost_estimate=small(1 << 10, 1 << 20),
        name="finish",
    )(before, *near_memory(block), *pieces, new_base)


def heavy(helper, base, noise, grad, near, far, ready, old_base, new_base, stress, fields, rows, answer, sems):
    _, _, tiles, _, count, cells = base.shape
    me = lax.axis_index("gy")
    depth = cells // LANES
    flat = rows.reshape(6 * depth * tiles, LANES)

    def store(k, tile):
        return pltpu.make_async_copy(fields.at[k], new_base.at[0, 0, tile], sems.at[k])

    def result(x):
        target = stress.at[0, 0, :, :, pl.ds(x * LANES, LANES)]
        return pltpu.make_async_copy(rows.at[:, x], target, sems.at[HEAVY_MOST + x])

    rows[...] = ready[...]
    places, order = owned_order(tiles, me, helper)
    for k, (h, tile) in enumerate(order):

        @pl.when(k < places)
        def _(k=k, h=h, tile=tile):
            flip = (me ^ h) >> 1
            is_far = ((me ^ h) & 1) == 1
            for i in range(near.shape[1]):
                answer[i] = jnp.where(is_far, far[flip, i], near[flip, i])

            def sums_of(x):
                lanes = pl.ds(x * LANES, LANES)
                g = tile_grad(grad, depth, tile, x)
                matrices = [with_diagonal(g, wide(answer[step, pl.ds(x, 1), :])) for step in range(2)]

                def read(a, part):
                    return base[0, 0, tile, a, part, lanes]

                def write(a, part, value):
                    fields[k, a, part, lanes] = value

                def shock(step, a, part):
                    return noise[0, 0, tile, step, a, part, lanes]

                return tile_sums(read, write, shock, matrices, count, add_moments, 6)

            sums = packed_sums(sums_of, depth)
            store(k, tile).start()
            sums = [s + answer[2 + i] for i, s in enumerate(sums)]
            for i, value in enumerate(stress_rows(sums, 1.0 / ALL_FIELDS)):
                flat[pl.ds(i * depth * tiles + tile, depth, stride=tiles), :] = value

    for x in range(depth):
        result(x).start()
    for k, (_, tile) in enumerate(order):

        @pl.when(k < places)
        def _(k=k, tile=tile):
            store(k, tile).wait()

    for x in range(depth):
        result(x).wait()


def call_heavy(helper_tile, base_fields, base_noise, grad, near, far, ready, new_base):
    _, _, tiles, _, count, cells = base_fields.shape
    depth = cells // LANES
    return pl.pallas_call(
        heavy,
        out_shape=(
            jax.ShapeDtypeStruct(new_base.shape, f32),
            jax.ShapeDtypeStruct((1, 1, 6, tiles, cells), f32),
        ),
        in_specs=[vmem] * 7 + [hbm],
        out_specs=(hbm, hbm),
        input_output_aliases={7: 0},
        scratch_shapes=[
            pltpu.VMEM((HEAVY_MOST, 3, count, cells), f32),
            pltpu.VMEM((6, depth, tiles, LANES), f32),
            pltpu.VMEM(near.shape[1:], f32),
            pltpu.SemaphoreType.DMA((HEAVY_MOST + depth,)),
        ],
        compiler_params=pltpu.CompilerParams(vmem_limit_bytes=SMALL),
        cost_estimate=small(8 << 20, 4 << 20),
        name="heavy_tiles",
    )(helper_tile, *near_memory(base_fields, base_noise), grad, near, far, ready, new_base)


def per_device(
    velocity, wall_cells, tile_counts, helper_tile, base_fields, extra_fields, base_noise, extra_noise
):
    tiles = tile_counts.shape[2]
    pairs = lax.axis_size("gy") // 2
    helper_tile, x_one, x_two, y_one, y_two = call_edges(helper_tile, velocity)
    halos = two_swaps(x_one, x_two, "gx") + two_swaps(y_one, y_two, "gy")
    moments = call_heavy_moments(helper_tile, base_fields, base_noise)
    grad, keep, send = call_gradients(tiles, helper_tile, velocity, halos, wall_cells, moments)
    gaps = 3
    new_base, block, pieces, done = None, None, [], 0

    def fill(before, extra_near=None):
        nonlocal new_base, block, done
        here = (tiles - done) // (gaps - len(pieces))
        new_base, block, piece, extra_far = call_ordinary(
            done, here, before, base_fields, base_noise, grad, block, new_base, extra_near
        )
        pieces.append(piece)
        done += here
        return piece, extra_far

    received = swapped(send, 1)
    before, _ = fill(send)
    keep, *sends = call_merge(before, keep, received)
    parts = [keep] + [swapped(send, 2 * flip) for flip, send in enumerate(sends, 1)]
    before, _ = fill(sends[0])
    extra_sums = call_extra_moments(before, extra_fields, extra_noise)
    extra_near, reply = call_extra(before, extra_fields, extra_noise, extra_sums, parts)
    replies = [reply] + [swapped(reply, 2 * flip) for flip in range(1, pairs)]
    before, new_extra = fill(reply, extra_near)
    near = call_join(before, replies)
    far = swapped(near, 1)
    new_base, ready = call_finish(near, block, pieces, new_base)
    new_base, stress = call_heavy(helper_tile, base_fields, base_noise, grad, near, far, ready, new_base)
    return new_base, new_extra, jnp.swapaxes(stress, 2, 3)


def solution(mesh):
    in_specs = (
        P(None, "gx", "gy", None),
        P("gx", "gy", None),
        P("gx", "gy", None),
        P("gx", None),
        P("gx", "gy", None, None, None, None),
        P("gx", "gy", None, None, None),
        P("gx", "gy", None, None, None, None, None),
        P("gx", "gy", None, None, None, None),
    )
    out_specs = (
        P("gx", "gy", None, None, None, None),
        P("gx", "gy", None, None, None),
        P("gx", "gy", None, None, None),
    )
    return jax.shard_map(
        per_device, mesh=mesh, in_specs=in_specs, out_specs=out_specs, check_vma=False
    )
```

```python
import functools

import jax
import jax.numpy as jnp
from jax import lax
from jax.experimental import pallas as pl
from jax.experimental.pallas import tpu as pltpu
from jax.sharding import PartitionSpec as P

ALL_FIELDS = 256
HEAVY_MOST = 4
LANES = 128
SUB = 8
SMALL = 10 << 20

time_step = 0.05
weissenberg = 0.25
max_extension = 50.0
noise_scale = (time_step / weissenberg) ** 0.5
component_pairs = ((0, 0), (1, 1), (2, 2), (0, 1), (0, 2), (1, 2))
moment_of = {(0, 0): 0, (1, 1): 1, (2, 2): 2, (0, 1): 3, (1, 0): 3, (0, 2): 4, (2, 0): 4, (1, 2): 5, (2, 1): 5}
f32 = jnp.float32

vmem = pl.BlockSpec(memory_space=pltpu.VMEM)
hbm = pl.BlockSpec(memory_space=pltpu.HBM)
anywhere = pl.BlockSpec(memory_space=pl.ANY)


def far_memory(*arrays):
    return [pltpu.with_memory_space_constraint(array, pltpu.HBM) for array in arrays]


def near_memory(*arrays):
    return [pltpu.with_memory_space_constraint(array, pltpu.VMEM) for array in arrays]


def column_sum(value):
    return jnp.sum(value, axis=0, keepdims=True)


def interleaved(a, b, bit):
    low = (lax.broadcasted_iota(jnp.int32, (SUB, LANES), 0) & bit) == 0
    return jnp.where(low, a, b) + pltpu.roll(jnp.where(low, b, a), bit, 0)


def packed_sums(values_of, count):
    stack = []
    for x in range(count):
        bit, values = 1, values_of(x)
        while stack and stack[-1][0] == bit:
            values = [interleaved(a, b, bit) for a, b in zip(stack.pop()[1], values)]
            bit *= 2
        stack.append((bit, values))
    return stack[0][1]


def wide(row):
    return jnp.broadcast_to(row, (SUB, LANES))


def turned(value, cell_z):
    sub = lax.broadcasted_iota(jnp.int32, value.shape, 0)
    group = lax.broadcasted_iota(jnp.int32, value.shape, 1) // cell_z
    skewed = pltpu.roll(value, cell_z, 1, stride=cell_z, stride_axis=0)
    mixed = jnp.take_along_axis(skewed, (group + sub) & (SUB - 1), axis=0, mode="promise_in_bounds")
    return pltpu.roll(mixed, 0, 1, stride=cell_z, stride_axis=0)


def relax_of(total, inverse):
    factor = 1.0 / (1.0 - total * inverse / max_extension)
    return 1.0 - (time_step * 0.5 / weissenberg) * factor


def stepped(vectors, noise, matrix):
    return [
        matrix[3 * a] * vectors[0]
        + matrix[3 * a + 1] * vectors[1]
        + matrix[3 * a + 2] * vectors[2]
        + noise_scale * noise[a]
        for a in range(3)
    ]


def with_diagonal(grad, relax):
    return [g + relax if i % 4 == 0 else g for i, g in enumerate(grad)]


def noise_rows(ref, start):
    both = [ref(a, pl.ds(start, 2 * SUB)).astype(f32) for a in range(3)]
    return [[w[:SUB] for w in both], [w[SUB:] for w in both]]


def add_moments(sums, q):
    return [s + q[a] * q[b] for s, (a, b) in zip(sums, component_pairs)]


def product_sums(sums, q, w):
    terms = [q[a] * q[b] for a, b in component_pairs]
    terms += [q[a] * w[b] for a in range(3) for b in range(3)]
    terms += [w[0] * w[0] + w[1] * w[1] + w[2] * w[2]]
    return [s + t for s, t in zip(sums, terms)]


def coefficients(g, m):
    cross = lambda a, b: m[6 + 3 * a + b]
    square = lambda a, b: m[moment_of[a, b]]
    once, twice, kick = 0.0, 0.0, 0.0
    for a in range(3):
        for b in range(3):
            once += g[3 * a + b] * square(a, b)
            kick += g[3 * a + b] * cross(b, a)
            inner = 0.0
            for c in range(3):
                inner += g[3 * a + c] * square(b, c)
            twice += g[3 * a + b] * inner
    return [
        twice + (2 * noise_scale) * kick + noise_scale**2 * m[15],
        2.0 * once + (2 * noise_scale) * (cross(0, 0) + cross(1, 1) + cross(2, 2)),
        m[0] + m[1] + m[2],
    ]


def owned_slots(tiles, me, helper):
    found = []
    row = helper[...]
    for h in range(helper.shape[1]):
        tile = row[0, h] - me * tiles
        found.append((h, (tile >= 0) & (tile < tiles), tile))
    return found


def owned_order(tiles, me, helper):
    places = jnp.int32(0)
    order = [jnp.int32(0)] * HEAVY_MOST
    for h, owned, tile in owned_slots(tiles, me, helper):
        entry = h * tiles + tile
        order = [jnp.where(owned & (places == k), entry, kept) for k, kept in enumerate(order)]
        places = places + owned.astype(jnp.int32)
    return places, [(entry // tiles, entry % tiles) for entry in order]


def small(flops, traffic):
    return pl.CostEstimate(flops=flops, bytes_accessed=traffic, transcendentals=0)


def is_even(axis):
    return (lax.axis_index(axis) & 1) == 0


def edges(helper, velocity, helper_near, x_one, x_two, y_one, y_two):
    depth, width = velocity.shape[1:3]
    helper_near[...] = helper[...]
    even = is_even("gx")
    for a in range(3):
        first, last = velocity[a, 0], velocity[a, depth - 1]
        x_one[a] = jnp.where(even, last, first)
        x_two[a] = jnp.where(even, first, last)
    even = is_even("gy")
    for a in range(3):
        for x in range(depth):
            first, last = velocity[a, x, pl.ds(0, 1), :], velocity[a, x, pl.ds(width - 1, 1), :]
            y_one[a, pl.ds(x, 1), :] = jnp.where(even, last, first)
            y_two[a, pl.ds(x, 1), :] = jnp.where(even, first, last)


def call_edges(helper_tile, velocity):
    _, depth, width, length = velocity.shape
    along_x = jax.ShapeDtypeStruct((3, width, length), f32)
    along_y = jax.ShapeDtypeStruct((3, depth, length), f32)
    return pl.pallas_call(
        edges,
        out_shape=(jax.ShapeDtypeStruct(helper_tile.shape, jnp.int32), along_x, along_x, along_y, along_y),
        in_specs=[vmem, vmem],
        out_specs=(vmem,) * 5,
        compiler_params=pltpu.CompilerParams(vmem_limit_bytes=4 << 20),
        cost_estimate=small(1 << 10, 1 << 17),
        name="edges",
    )(*far_memory(helper_tile, velocity))


def two_swaps(one, two, axis):
    size = lax.axis_size(axis)
    within = [(i, i ^ 1) for i in range(size)]
    across = [(i, (i - 1 + 2 * (i & 1)) % size) for i in range(size)]
    return lax.ppermute(one, axis, within), lax.ppermute(two, axis, across)


def low_and_high(axis, one, two, a):
    even, place = is_even(axis), lax.axis_index(axis)
    low = jnp.where(even, two[a], one[a])
    high = jnp.where(even, one[a], two[a])
    return jnp.where(place == 0, 0.0, low), jnp.where(place == lax.axis_size(axis) - 1, 0.0, high)


def heavy_moments(helper, base, noise, out, fields, shocks, sems):
    _, _, count, cells = fields.shape
    tiles = base.shape[2]
    me = lax.axis_index("gy")

    def loads(k, tile):
        return (
            pltpu.make_async_copy(base.at[0, 0, tile], fields.at[k], sems.at[0, k]),
            pltpu.make_async_copy(noise.at[0, 0, tile, 0], shocks.at[k], sems.at[1, k]),
        )

    places, order = owned_order(tiles, me, helper)
    for k, (_, tile) in enumerate(order):

        @pl.when(k < places)
        def _(k=k, tile=tile):
            for copy in loads(k, tile):
                copy.start()

    for k, (h, tile) in enumerate(order):

        @pl.when(k < places)
        def _(k=k, h=h, tile=tile):
            for copy in loads(k, tile):
                copy.wait()

            def sums_of(x):
                lanes = pl.ds(x * LANES, LANES)
                sums = [jnp.zeros((SUB, LANES), f32)] * 16
                for group in range(count // (2 * SUB)):
                    pair = noise_rows(lambda a, rows: shocks[k, a, rows, lanes], group * 2 * SUB)
                    for half in range(2):
                        rows = pl.ds((2 * group + half) * SUB, SUB)
                        sums = product_sums(sums, [fields[k, a, rows, lanes] for a in range(3)], pair[half])
                return sums

            for i, value in enumerate(packed_sums(sums_of, cells // LANES)):
                out[h, i] = value


def call_heavy_moments(helper_tile, base_fields, base_noise):
    slots = helper_tile.shape[1]
    count, cells = base_fields.shape[-2:]
    return pl.pallas_call(
        heavy_moments,
        out_shape=jax.ShapeDtypeStruct((slots, 16, cells // LANES, LANES), f32),
        in_specs=[vmem, hbm, hbm],
        out_specs=vmem,
        scratch_shapes=[
            pltpu.VMEM((HEAVY_MOST, 3, count, cells), f32),
            pltpu.VMEM((HEAVY_MOST, 3, count, cells), jnp.bfloat16),
            pltpu.SemaphoreType.DMA((2, HEAVY_MOST)),
        ],
        compiler_params=pltpu.CompilerParams(vmem_limit_bytes=SMALL),
        cost_estimate=small(8 << 20, 3 << 20),
        name="heavy_moments",
    )(helper_tile, *far_memory(base_fields, base_noise))


def extra_moments(unroll, before, base, noise, out):
    _, _, _, count, cells = base.shape
    zero = jnp.zeros((SUB, LANES), f32)

    @pl.loop(0, cells // LANES)
    def _(x):
        lanes = pl.ds(pl.multiple_of(x * LANES, LANES), LANES)

        def body(i, sums):
            start = pl.multiple_of(i * 2 * SUB, 2 * SUB)
            pair = noise_rows(lambda a, rows: noise[0, 0, 0, a, rows, lanes], start)
            for half in range(2):
                rows = pl.ds(start + half * SUB, SUB)
                sums = product_sums(sums, [base[0, 0, a, rows, lanes] for a in range(3)], pair[half])
            return sums

        for i, s in enumerate(lax.fori_loop(0, count // (2 * SUB), body, [zero] * 16, unroll=unroll)):
            out[i, pl.ds(x, 1), :] = column_sum(s)


def call_extra_moments(before, extra_fields, extra_noise):
    cells = extra_fields.shape[-1]
    return pl.pallas_call(
        functools.partial(extra_moments, 7),
        out_shape=jax.ShapeDtypeStruct((16, cells // LANES, LANES), f32),
        in_specs=[anywhere, vmem, vmem],
        out_specs=vmem,
        compiler_params=pltpu.CompilerParams(vmem_limit_bytes=SMALL),
        cost_estimate=small(8 << 20, 5 << 20),
        name="extra_moments",
    )(before, *near_memory(extra_fields, extra_noise))


def gradients(tiles, helper, velocity, x_one, x_two, y_one, y_two, wall, moments, grad, keep, send):
    me = lax.axis_index("gy")
    depth = velocity.shape[1]
    cell_z = velocity.shape[3] // tiles
    sub = lax.broadcasted_iota(jnp.int32, (SUB, LANES), 0)
    lane = lax.broadcasted_iota(jnp.int32, (SUB, LANES), 1)
    z = lane % cell_z
    scales = [turned(jnp.where(wall[x] == 0, 0.5 * time_step, 0.0).astype(f32), cell_z) for x in range(depth)]
    for a in range(3):
        x_low, x_high = low_and_high("gx", x_one, x_two, a)
        y_low, y_high = low_and_high("gy", y_one, y_two, a)
        rows = [x_low] + [velocity[a, x] for x in range(depth)] + [x_high]
        rows = [turned(row, cell_z) for row in rows]
        low, high = turned(y_low, cell_z), turned(y_high, cell_z)
        for x in range(depth):
            here = rows[x + 1]
            above = high if x == depth - 1 else pltpu.roll(high, LANES - cell_z * (x + 1), 1)
            below = low if x == 0 else pltpu.roll(low, LANES - cell_z * x, 1)
            y_up = jnp.where(lane < LANES - cell_z, pltpu.roll(here, LANES - cell_z, 1), above)
            y_down = jnp.where(lane >= cell_z, pltpu.roll(here, cell_z, 1), below)
            next_tile = pltpu.roll(pltpu.roll(here, cell_z - 1, 1), 1, 0)
            last_tile = pltpu.roll(pltpu.roll(here, LANES - cell_z + 1, 1), SUB - 1, 0)
            next_tile = jnp.where(sub == 0, 0.0, next_tile)
            last_tile = jnp.where(sub == SUB - 1, 0.0, last_tile)
            z_up = jnp.where(z == cell_z - 1, next_tile, pltpu.roll(here, LANES - 1, 1))
            z_down = jnp.where(z == 0, last_tile, pltpu.roll(here, 1, 1))
            for b, difference in enumerate((rows[x + 2] - rows[x], y_up - y_down, z_up - z_down)):
                grad[pl.ds(((3 * a + b) * depth + x) * SUB, SUB), :] = difference * scales[x]
    keep[...] = jnp.zeros(keep.shape, f32)
    send[...] = jnp.zeros(send.shape, f32)
    for h, owned, tile in owned_slots(tiles, me, helper):

        @pl.when(owned)
        def _(h=h, tile=tile):
            g = [grad[pl.ds(i * depth * SUB + SUB - 1 - tile, depth, stride=SUB), :] for i in range(9)]
            rows = g + coefficients(g, [moments[h, i] for i in range(16)])
            stays = (me & 1) == (h & 1)

            @pl.when(stays)
            def _():
                for i, row in enumerate(rows):
                    keep[h >> 1, i] = row

            @pl.when(jnp.logical_not(stays))
            def _():
                for i, row in enumerate(rows):
                    send[h >> 1, i] = row


def call_gradients(tiles, helper_tile, velocity, halos, wall_cells, moments):
    slots = helper_tile.shape[1]
    depth = velocity.shape[1]
    half = jax.ShapeDtypeStruct((slots // 2, 12, depth, LANES), f32)
    return pl.pallas_call(
        functools.partial(gradients, tiles),
        out_shape=(jax.ShapeDtypeStruct((9 * depth * SUB, LANES), f32), half, half),
        in_specs=[vmem] * 8,
        out_specs=(vmem,) * 3,
        compiler_params=pltpu.CompilerParams(vmem_limit_bytes=8 << 20),
        cost_estimate=small(4 << 20, 1 << 20),
        name="gradients",
    )(helper_tile, velocity, *halos, wall_cells, moments)


def swapped(block, flip):
    size = lax.axis_size("gy")
    return lax.ppermute(block, "gy", [(i, i ^ flip) for i in range(size)])


def merge(before, kept, received, keep, *sends):
    pair = lax.axis_index("gy") >> 1
    for flip, out in enumerate((keep,) + sends):
        out[...] = kept[pair ^ flip] + received[pair ^ flip]


def call_merge(before, kept, received):
    one = jax.ShapeDtypeStruct(kept.shape[1:], f32)
    return pl.pallas_call(
        merge,
        out_shape=(one,) * kept.shape[0],
        in_specs=[anywhere, vmem, vmem],
        out_specs=(vmem,) * kept.shape[0],
        compiler_params=pltpu.CompilerParams(vmem_limit_bytes=4 << 20),
        cost_estimate=small(1 << 10, 1 << 18),
        name="merge",
    )(before, kept, received)


def join(before, *refs):
    for i, ref in enumerate(refs[:-1]):
        refs[-1][i] = ref[...]


def call_join(before, blocks):
    return pl.pallas_call(
        join,
        out_shape=jax.ShapeDtypeStruct((len(blocks),) + blocks[0].shape, f32),
        in_specs=[anywhere] + [vmem] * len(blocks),
        out_specs=vmem,
        compiler_params=pltpu.CompilerParams(vmem_limit_bytes=4 << 20),
        cost_estimate=small(1 << 10, 1 << 18),
        name="join",
    )(before, *blocks)


def stress_rows(sums, inverse):
    second = [s * inverse for s in sums]
    stretch = 1.0 / (1.0 - (second[0] + second[1] + second[2]) / max_extension)
    return [(stretch * s - (1.0 if i < 3 else 0.0)) * (1.0 / weissenberg) for i, s in enumerate(second)]


def tile_grad(grad, depth, tile, x):
    return [wide(grad[pl.ds((i * depth + x + 1) * SUB - 1 - tile, 1), :]) for i in range(9)]


def tile_sums(read, write, noise, matrices, count, add, many):
    sums = [jnp.zeros((SUB, LANES), f32)] * many
    for group in range(count // (2 * SUB)):
        pairs = [noise_rows(functools.partial(noise, step), group * 2 * SUB) for step in range(len(matrices))]
        for half in range(2):
            rows = pl.ds((2 * group + half) * SUB, SUB)
            q = [read(a, rows) for a in range(3)]
            for step, matrix in enumerate(matrices):
                q = stepped(q, pairs[step][half], matrix)
            for a in range(3):
                write(a, rows, q[a])
            sums = add(sums, q)
    return sums


def add_square(sums, q):
    return [sums[0] + (q[0] * q[0] + q[1] * q[1] + q[2] * q[2])]


def ordinary(first, has_block, has_base, has_extra, *refs):
    refs = list(refs)
    before, base, noise, grad = refs[:4]
    del refs[:4]
    block = refs.pop(0) if has_block else None
    if has_base:
        refs.pop(0)
    extra_near = refs.pop(0) if has_extra else None
    new_base = refs.pop(0) if has_block else None
    new_extra = refs.pop(0) if has_extra else None
    fields, stress, halfway, relaxes, sems = refs
    here, _, count, cells = fields.shape
    depth = cells // LANES
    inverse = 1.0 / count
    copies = []
    if has_block:
        last = block.shape[0]
        copies += [
            pltpu.make_async_copy(block.at[i], new_base.at[0, 0, first - last + i], sems.at[i]) for i in range(last)
        ]
    if has_extra:
        copies += [
            pltpu.make_async_copy(extra_near.at[0, 0, a], new_extra.at[0, 0, a], sems.at[len(copies) + a])
            for a in range(3)
        ]
    for copy in copies:
        copy.start()
    for place in range(here):
        tile = first + place

        def squares(x):
            total = jnp.zeros((SUB, LANES), f32)
            for group in range(count // SUB):
                for a in range(3):
                    q = base[0, 0, tile, a, pl.ds(group * SUB, SUB), pl.ds(x * LANES, LANES)]
                    total = total + q * q
            return [total]

        sums = packed_sums(squares, depth)
        for step in range(2):
            relaxes[place, step] = relax_of(sums[0], inverse)

            def sums_of(x):
                lanes = pl.ds(x * LANES, LANES)
                matrix = with_diagonal(tile_grad(grad, depth, tile, x), wide(relaxes[place, step, pl.ds(x, 1), :]))

                def read(a, rows):
                    return base[0, 0, tile, a, rows, lanes] if step == 0 else halfway[place, a, rows, lanes]

                def write(a, rows, value):
                    if step == 0:
                        halfway[place, a, rows, lanes] = value
                    else:
                        fields[place, a, rows, lanes] = value

                def shock(_, a, rows):
                    return noise[0, 0, tile, step, a, rows, lanes]

                if step == 0:
                    return tile_sums(read, write, shock, [matrix], count, add_square, 1)
                return tile_sums(read, write, shock, [matrix], count, add_moments, 6)

            sums = packed_sums(sums_of, depth)
        for i, row in enumerate(stress_rows(sums, inverse)):
            stress[i, place] = row
    for copy in copies:
        copy.wait()


def call_ordinary(first, here, before, base_fields, base_noise, grad, block, new_base, new_extra):
    count, cells = base_fields.shape[-2:]
    depth = cells // LANES
    has_block, has_base, has_extra = block is not None, new_base is not None, new_extra is not None
    operands = [before, *near_memory(base_fields, base_noise), grad]
    specs = [anywhere, vmem, vmem, vmem]
    shapes, out_specs, aliases = [], [], {}
    copies = 0
    if has_block:
        operands += near_memory(block)
        specs.append(vmem)
        shapes.append(jax.ShapeDtypeStruct(base_fields.shape, f32))
        out_specs.append(hbm)
        copies += block.shape[0]
    if has_base:
        aliases[len(operands)] = 0
        operands.append(new_base)
        specs.append(hbm)
    if has_extra:
        operands += near_memory(new_extra)
        specs.append(vmem)
        shapes.append(jax.ShapeDtypeStruct(new_extra.shape, f32))
        out_specs.append(hbm)
        copies += 3
    shapes += [
        pltpu.VMEM((here, 3, count, cells), f32),
        jax.ShapeDtypeStruct((6, here, depth, LANES), f32),
    ]
    out_specs += [vmem, vmem]
    results = pl.pallas_call(
        functools.partial(ordinary, first, has_block, has_base, has_extra),
        out_shape=tuple(shapes),
        in_specs=specs,
        out_specs=tuple(out_specs),
        input_output_aliases=aliases,
        scratch_shapes=[
            pltpu.VMEM((here, 3, count, cells), f32),
            pltpu.VMEM((here, 2, depth, LANES), f32),
            pltpu.SemaphoreType.DMA((max(copies, 1),)),
        ],
        compiler_params=pltpu.CompilerParams(vmem_limit_bytes=SMALL),
        cost_estimate=small(8 << 20, 3 << 20),
        name="ordinary_tiles",
    )(*operands)
    results = list(results)
    piece, block = results.pop(), results.pop()
    new_base = results.pop(0) if has_block else None
    return new_base, block, piece, (results[0] if has_extra else None)


def extra(unroll, before, base, noise, moments, *refs):
    *parts, new_fields, reply, message = refs
    _, _, _, count, cells = base.shape
    inverse = 1.0 / float(ALL_FIELDS)
    zero = jnp.zeros((SUB, LANES), f32)
    message[...] = sum(part[...] for part in parts)
    own = coefficients([message[i] for i in range(9)], [moments[i] for i in range(16)])
    both = [message[9 + i] + own[i] for i in range(3)]
    first = relax_of(both[2], inverse)
    second = relax_of(both[0] + first * (both[1] + first * both[2]), inverse)
    reply[0], reply[1] = first, second

    @pl.loop(0, cells // LANES)
    def _(x):
        lanes = pl.ds(pl.multiple_of(x * LANES, LANES), LANES)
        grad = [wide(message[i, pl.ds(x, 1), :]) for i in range(9)]
        matrices = [with_diagonal(grad, wide(reply[step, pl.ds(x, 1), :])) for step in range(2)]

        def body(i, sums):
            start = pl.multiple_of(i * 2 * SUB, 2 * SUB)
            pairs = [noise_rows(lambda a, rows: noise[0, 0, step, a, rows, lanes], start) for step in range(2)]
            for half in range(2):
                rows = pl.ds(start + half * SUB, SUB)
                q = [base[0, 0, a, rows, lanes] for a in range(3)]
                for step in range(2):
                    q = stepped(q, pairs[step][half], matrices[step])
                for a in range(3):
                    new_fields[0, 0, a, rows, lanes] = q[a]
                sums = add_moments(sums, q)
            return sums

        for i, s in enumerate(lax.fori_loop(0, count // (2 * SUB), body, [zero] * 6, unroll=unroll)):
            reply[2 + i, pl.ds(x, 1), :] = column_sum(s)


def call_extra(before, extra_fields, extra_noise, moments, parts):
    depth = extra_fields.shape[-1] // LANES
    return pl.pallas_call(
        functools.partial(extra, 7),
        out_shape=(
            pltpu.VMEM(extra_fields.shape, f32),
            jax.ShapeDtypeStruct((8, depth, LANES), f32),
        ),
        in_specs=[anywhere, vmem, vmem, vmem] + [vmem] * len(parts),
        out_specs=(vmem, vmem),
        scratch_shapes=[pltpu.VMEM(parts[0].shape, f32)],
        compiler_params=pltpu.CompilerParams(vmem_limit_bytes=SMALL),
        cost_estimate=small(32 << 20, 9 << 20),
        name="extra_fields",
    )(before, *near_memory(extra_fields, extra_noise), moments, *parts)


def finish(piece_count, before, block, *refs):
    pieces, (_, new_base, rows, sems) = refs[:piece_count], refs[piece_count:]
    _, depth, tiles, _ = rows.shape
    last = block.shape[0]
    flat = rows.reshape(6 * depth * tiles, LANES)
    copies = [pltpu.make_async_copy(block.at[i], new_base.at[0, 0, tiles - last + i], sems.at[i]) for i in range(last)]
    for copy in copies:
        copy.start()
    tile = 0
    for piece in pieces:
        for place in range(piece.shape[1]):
            for i in range(6):
                flat[pl.ds(i * depth * tiles + tile, depth, stride=tiles), :] = piece[i, place]
            tile += 1
    for copy in copies:
        copy.wait()


def call_finish(before, block, pieces, new_base):
    tiles, cells = new_base.shape[2], new_base.shape[-1]
    return pl.pallas_call(
        functools.partial(finish, len(pieces)),
        out_shape=(
            jax.ShapeDtypeStruct(new_base.shape, f32),
            jax.ShapeDtypeStruct((6, cells // LANES, tiles, LANES), f32),
        ),
        in_specs=[anywhere, vmem] + [vmem] * len(pieces) + [hbm],
        out_specs=(hbm, vmem),
        input_output_aliases={2 + len(pieces): 0},
        scratch_shapes=[pltpu.SemaphoreType.DMA((block.shape[0],))],
        compiler_params=pltpu.CompilerParams(vmem_limit_bytes=4 << 20),
        cost_estimate=small(1 << 10, 1 << 20),
        name="finish",
    )(before, *near_memory(block), *pieces, new_base)


def heavy(helper, base, noise, grad, near, far, ready, old_base, new_base, stress, fields, rows, answer, sems):
    _, _, tiles, _, count, cells = base.shape
    me = lax.axis_index("gy")
    depth = cells // LANES
    flat = rows.reshape(6 * depth * tiles, LANES)

    def store(k, tile):
        return pltpu.make_async_copy(fields.at[k], new_base.at[0, 0, tile], sems.at[k])

    def result(x):
        target = stress.at[0, 0, :, :, pl.ds(x * LANES, LANES)]
        return pltpu.make_async_copy(rows.at[:, x], target, sems.at[HEAVY_MOST + x])

    rows[...] = ready[...]
    places, order = owned_order(tiles, me, helper)
    for k, (h, tile) in enumerate(order):

        @pl.when(k < places)
        def _(k=k, h=h, tile=tile):
            flip = (me ^ h) >> 1
            is_far = ((me ^ h) & 1) == 1
            for i in range(near.shape[1]):
                answer[i] = jnp.where(is_far, far[flip, i], near[flip, i])

            def sums_of(x):
                lanes = pl.ds(x * LANES, LANES)
                g = tile_grad(grad, depth, tile, x)
                matrices = [with_diagonal(g, wide(answer[step, pl.ds(x, 1), :])) for step in range(2)]

                def read(a, part):
                    return base[0, 0, tile, a, part, lanes]

                def write(a, part, value):
                    fields[k, a, part, lanes] = value

                def shock(step, a, part):
                    return noise[0, 0, tile, step, a, part, lanes]

                return tile_sums(read, write, shock, matrices, count, add_moments, 6)

            sums = packed_sums(sums_of, depth)
            store(k, tile).start()
            sums = [s + answer[2 + i] for i, s in enumerate(sums)]
            for i, value in enumerate(stress_rows(sums, 1.0 / ALL_FIELDS)):
                flat[pl.ds(i * depth * tiles + tile, depth, stride=tiles), :] = value

    for x in range(depth):
        result(x).start()
    for k, (_, tile) in enumerate(order):

        @pl.when(k < places)
        def _(k=k, tile=tile):
            store(k, tile).wait()

    for x in range(depth):
        result(x).wait()


def call_heavy(helper_tile, base_fields, base_noise, grad, near, far, ready, new_base):
    _, _, tiles, _, count, cells = base_fields.shape
    depth = cells // LANES
    return pl.pallas_call(
        heavy,
        out_shape=(
            jax.ShapeDtypeStruct(new_base.shape, f32),
            jax.ShapeDtypeStruct((1, 1, 6, tiles, cells), f32),
        ),
        in_specs=[vmem] * 7 + [hbm],
        out_specs=(hbm, hbm),
        input_output_aliases={7: 0},
        scratch_shapes=[
            pltpu.VMEM((HEAVY_MOST, 3, count, cells), f32),
            pltpu.VMEM((6, depth, tiles, LANES), f32),
            pltpu.VMEM(near.shape[1:], f32),
            pltpu.SemaphoreType.DMA((HEAVY_MOST + depth,)),
        ],
        compiler_params=pltpu.CompilerParams(vmem_limit_bytes=SMALL),
        cost_estimate=small(8 << 20, 4 << 20),
        name="heavy_tiles",
    )(helper_tile, *near_memory(base_fields, base_noise), grad, near, far, ready, new_base)


def per_device(
    velocity, wall_cells, tile_counts, helper_tile, base_fields, extra_fields, base_noise, extra_noise
):
    tiles = tile_counts.shape[2]
    pairs = lax.axis_size("gy") // 2
    helper_tile, x_one, x_two, y_one, y_two = call_edges(helper_tile, velocity)
    halos = two_swaps(x_one, x_two, "gx") + two_swaps(y_one, y_two, "gy")
    moments = call_heavy_moments(helper_tile, base_fields, base_noise)
    grad, keep, send = call_gradients(tiles, helper_tile, velocity, halos, wall_cells, moments)
    gaps = 3
    new_base, block, pieces, done = None, None, [], 0

    def fill(before, extra_near=None):
        nonlocal new_base, block, done
        here = (tiles - done) // (gaps - len(pieces))
        new_base, block, piece, extra_far = call_ordinary(
            done, here, before, base_fields, base_noise, grad, block, new_base, extra_near
        )
        pieces.append(piece)
        done += here
        return piece, extra_far

    received = swapped(send, 1)
    before, _ = fill(send)
    keep, *sends = call_merge(before, keep, received)
    parts = [keep] + [swapped(send, 2 * flip) for flip, send in enumerate(sends, 1)]
    extra_sums = call_extra_moments(sends[0], extra_fields, extra_noise)
    before, _ = fill(extra_sums)
    extra_near, reply = call_extra(before, extra_fields, extra_noise, extra_sums, parts)
    replies = [reply] + [swapped(reply, 2 * flip) for flip in range(1, pairs)]
    before, new_extra = fill(reply, extra_near)
    near = call_join(before, replies)
    far = swapped(near, 1)
    new_base, ready = call_finish(near, block, pieces, new_base)
    new_base, stress = call_heavy(helper_tile, base_fields, base_noise, grad, near, far, ready, new_base)
    return new_base, new_extra, jnp.swapaxes(stress, 2, 3)


def solution(mesh):
    in_specs = (
        P(None, "gx", "gy", None),
        P("gx", "gy", None),
        P("gx", "gy", None),
        P("gx", None),
        P("gx", "gy", None, None, None, None),
        P("gx", "gy", None, None, None),
        P("gx", "gy", None, None, None, None, None),
        P("gx", "gy", None, None, None, None),
    )
    out_specs = (
        P("gx", "gy", None, None, None, None),
        P("gx", "gy", None, None, None),
        P("gx", "gy", None, None, None),
    )
    return jax.shard_map(
        per_device, mesh=mesh, in_specs=in_specs, out_specs=out_specs, check_vma=False
    )
```

```python
import functools

import jax
import jax.numpy as jnp
from jax import lax
from jax.experimental import pallas as pl
from jax.experimental.pallas import tpu as pltpu
from jax.sharding import PartitionSpec as P

ALL_FIELDS = 256
HEAVY_MOST = 4
LANES = 128
SUB = 8
SMALL = 10 << 20

time_step = 0.05
weissenberg = 0.25
max_extension = 50.0
noise_scale = (time_step / weissenberg) ** 0.5
component_pairs = ((0, 0), (1, 1), (2, 2), (0, 1), (0, 2), (1, 2))
moment_of = {(0, 0): 0, (1, 1): 1, (2, 2): 2, (0, 1): 3, (1, 0): 3, (0, 2): 4, (2, 0): 4, (1, 2): 5, (2, 1): 5}
f32 = jnp.float32

vmem = pl.BlockSpec(memory_space=pltpu.VMEM)
hbm = pl.BlockSpec(memory_space=pltpu.HBM)
anywhere = pl.BlockSpec(memory_space=pl.ANY)


def far_memory(*arrays):
    return [pltpu.with_memory_space_constraint(array, pltpu.HBM) for array in arrays]


def near_memory(*arrays):
    return [pltpu.with_memory_space_constraint(array, pltpu.VMEM) for array in arrays]


def column_sum(value):
    return jnp.sum(value, axis=0, keepdims=True)


def interleaved(a, b, bit):
    low = (lax.broadcasted_iota(jnp.int32, (SUB, LANES), 0) & bit) == 0
    return jnp.where(low, a, b) + pltpu.roll(jnp.where(low, b, a), bit, 0)


def packed_sums(values_of, count):
    stack = []
    for x in range(count):
        bit, values = 1, values_of(x)
        while stack and stack[-1][0] == bit:
            values = [interleaved(a, b, bit) for a, b in zip(stack.pop()[1], values)]
            bit *= 2
        stack.append((bit, values))
    return stack[0][1]


def wide(row):
    return jnp.broadcast_to(row, (SUB, LANES))


def turned(value, cell_z):
    sub = lax.broadcasted_iota(jnp.int32, value.shape, 0)
    group = lax.broadcasted_iota(jnp.int32, value.shape, 1) // cell_z
    skewed = pltpu.roll(value, cell_z, 1, stride=cell_z, stride_axis=0)
    mixed = jnp.take_along_axis(skewed, (group + sub) & (SUB - 1), axis=0, mode="promise_in_bounds")
    return pltpu.roll(mixed, 0, 1, stride=cell_z, stride_axis=0)


def relax_of(total, inverse):
    factor = 1.0 / (1.0 - total * inverse / max_extension)
    return 1.0 - (time_step * 0.5 / weissenberg) * factor


def stepped(vectors, noise, matrix):
    return [
        matrix[3 * a] * vectors[0]
        + matrix[3 * a + 1] * vectors[1]
        + matrix[3 * a + 2] * vectors[2]
        + noise_scale * noise[a]
        for a in range(3)
    ]


def with_diagonal(grad, relax):
    return [g + relax if i % 4 == 0 else g for i, g in enumerate(grad)]


def noise_rows(ref, start):
    both = [ref(a, pl.ds(start, 2 * SUB)).astype(f32) for a in range(3)]
    return [[w[:SUB] for w in both], [w[SUB:] for w in both]]


def add_moments(sums, q):
    return [s + q[a] * q[b] for s, (a, b) in zip(sums, component_pairs)]


def product_sums(sums, q, w):
    terms = [q[a] * q[b] for a, b in component_pairs]
    terms += [q[a] * w[b] for a in range(3) for b in range(3)]
    terms += [w[0] * w[0] + w[1] * w[1] + w[2] * w[2]]
    return [s + t for s, t in zip(sums, terms)]


def coefficients(g, m):
    cross = lambda a, b: m[6 + 3 * a + b]
    square = lambda a, b: m[moment_of[a, b]]
    once, twice, kick = 0.0, 0.0, 0.0
    for a in range(3):
        for b in range(3):
            once += g[3 * a + b] * square(a, b)
            kick += g[3 * a + b] * cross(b, a)
            inner = 0.0
            for c in range(3):
                inner += g[3 * a + c] * square(b, c)
            twice += g[3 * a + b] * inner
    return [
        twice + (2 * noise_scale) * kick + noise_scale**2 * m[15],
        2.0 * once + (2 * noise_scale) * (cross(0, 0) + cross(1, 1) + cross(2, 2)),
        m[0] + m[1] + m[2],
    ]


def owned_slots(tiles, me, helper):
    found = []
    row = helper[...]
    for h in range(helper.shape[1]):
        tile = row[0, h] - me * tiles
        found.append((h, (tile >= 0) & (tile < tiles), tile))
    return found


def owned_order(tiles, me, helper):
    places = jnp.int32(0)
    order = [jnp.int32(0)] * HEAVY_MOST
    for h, owned, tile in owned_slots(tiles, me, helper):
        entry = h * tiles + tile
        order = [jnp.where(owned & (places == k), entry, kept) for k, kept in enumerate(order)]
        places = places + owned.astype(jnp.int32)
    return places, [(entry // tiles, entry % tiles) for entry in order]


def small(flops, traffic):
    return pl.CostEstimate(flops=flops, bytes_accessed=traffic, transcendentals=0)


def is_even(axis):
    return (lax.axis_index(axis) & 1) == 0


def edges(helper, velocity, helper_near, x_one, x_two, y_one, y_two):
    depth, width = velocity.shape[1:3]
    helper_near[...] = helper[...]
    even = is_even("gx")
    for a in range(3):
        first, last = velocity[a, 0], velocity[a, depth - 1]
        x_one[a] = jnp.where(even, last, first)
        x_two[a] = jnp.where(even, first, last)
    even = is_even("gy")
    for a in range(3):
        for x in range(depth):
            first, last = velocity[a, x, pl.ds(0, 1), :], velocity[a, x, pl.ds(width - 1, 1), :]
            y_one[a, pl.ds(x, 1), :] = jnp.where(even, last, first)
            y_two[a, pl.ds(x, 1), :] = jnp.where(even, first, last)


def call_edges(helper_tile, velocity):
    _, depth, width, length = velocity.shape
    along_x = jax.ShapeDtypeStruct((3, width, length), f32)
    along_y = jax.ShapeDtypeStruct((3, depth, length), f32)
    return pl.pallas_call(
        edges,
        out_shape=(jax.ShapeDtypeStruct(helper_tile.shape, jnp.int32), along_x, along_x, along_y, along_y),
        in_specs=[vmem, vmem],
        out_specs=(vmem,) * 5,
        compiler_params=pltpu.CompilerParams(vmem_limit_bytes=4 << 20),
        cost_estimate=small(1 << 10, 1 << 17),
        name="edges",
    )(*far_memory(helper_tile, velocity))


def two_swaps(one, two, axis):
    size = lax.axis_size(axis)
    within = [(i, i ^ 1) for i in range(size)]
    across = [(i, (i - 1 + 2 * (i & 1)) % size) for i in range(size)]
    return lax.ppermute(one, axis, within), lax.ppermute(two, axis, across)


def low_and_high(axis, one, two, a):
    even, place = is_even(axis), lax.axis_index(axis)
    low = jnp.where(even, two[a], one[a])
    high = jnp.where(even, one[a], two[a])
    return jnp.where(place == 0, 0.0, low), jnp.where(place == lax.axis_size(axis) - 1, 0.0, high)


def heavy_moments(helper, base, noise, out, fields, shocks, sems):
    _, _, count, cells = fields.shape
    tiles = base.shape[2]
    me = lax.axis_index("gy")

    def loads(k, tile):
        return (
            pltpu.make_async_copy(base.at[0, 0, tile], fields.at[k], sems.at[0, k]),
            pltpu.make_async_copy(noise.at[0, 0, tile, 0], shocks.at[k], sems.at[1, k]),
        )

    places, order = owned_order(tiles, me, helper)
    for k, (_, tile) in enumerate(order):

        @pl.when(k < places)
        def _(k=k, tile=tile):
            for copy in loads(k, tile):
                copy.start()

    for k, (h, tile) in enumerate(order):

        @pl.when(k < places)
        def _(k=k, h=h, tile=tile):
            for copy in loads(k, tile):
                copy.wait()

            def sums_of(x):
                lanes = pl.ds(x * LANES, LANES)
                sums = [jnp.zeros((SUB, LANES), f32)] * 16
                for group in range(count // (2 * SUB)):
                    pair = noise_rows(lambda a, rows: shocks[k, a, rows, lanes], group * 2 * SUB)
                    for half in range(2):
                        rows = pl.ds((2 * group + half) * SUB, SUB)
                        sums = product_sums(sums, [fields[k, a, rows, lanes] for a in range(3)], pair[half])
                return sums

            for i, value in enumerate(packed_sums(sums_of, cells // LANES)):
                out[h, i] = value


def call_heavy_moments(helper_tile, base_fields, base_noise):
    slots = helper_tile.shape[1]
    count, cells = base_fields.shape[-2:]
    return pl.pallas_call(
        heavy_moments,
        out_shape=jax.ShapeDtypeStruct((slots, 16, cells // LANES, LANES), f32),
        in_specs=[vmem, hbm, hbm],
        out_specs=vmem,
        scratch_shapes=[
            pltpu.VMEM((HEAVY_MOST, 3, count, cells), f32),
            pltpu.VMEM((HEAVY_MOST, 3, count, cells), jnp.bfloat16),
            pltpu.SemaphoreType.DMA((2, HEAVY_MOST)),
        ],
        compiler_params=pltpu.CompilerParams(vmem_limit_bytes=SMALL),
        cost_estimate=small(8 << 20, 3 << 20),
        name="heavy_moments",
    )(helper_tile, *far_memory(base_fields, base_noise))


def extra_moments(unroll, before, base, noise, out):
    _, _, _, count, cells = base.shape
    zero = jnp.zeros((SUB, LANES), f32)

    @pl.loop(0, cells // LANES)
    def _(x):
        lanes = pl.ds(pl.multiple_of(x * LANES, LANES), LANES)

        def body(i, sums):
            start = pl.multiple_of(i * 2 * SUB, 2 * SUB)
            pair = noise_rows(lambda a, rows: noise[0, 0, 0, a, rows, lanes], start)
            for half in range(2):
                rows = pl.ds(start + half * SUB, SUB)
                sums = product_sums(sums, [base[0, 0, a, rows, lanes] for a in range(3)], pair[half])
            return sums

        for i, s in enumerate(lax.fori_loop(0, count // (2 * SUB), body, [zero] * 16, unroll=unroll)):
            out[i, pl.ds(x, 1), :] = column_sum(s)


def call_extra_moments(before, extra_fields, extra_noise):
    cells = extra_fields.shape[-1]
    return pl.pallas_call(
        functools.partial(extra_moments, 7),
        out_shape=jax.ShapeDtypeStruct((16, cells // LANES, LANES), f32),
        in_specs=[anywhere, vmem, vmem],
        out_specs=vmem,
        compiler_params=pltpu.CompilerParams(vmem_limit_bytes=SMALL),
        cost_estimate=small(8 << 20, 5 << 20),
        name="extra_moments",
    )(before, *near_memory(extra_fields, extra_noise))


def gradients(tiles, helper, velocity, x_one, x_two, y_one, y_two, wall, moments, grad, keep, send):
    me = lax.axis_index("gy")
    depth = velocity.shape[1]
    cell_z = velocity.shape[3] // tiles
    sub = lax.broadcasted_iota(jnp.int32, (SUB, LANES), 0)
    lane = lax.broadcasted_iota(jnp.int32, (SUB, LANES), 1)
    z = lane % cell_z
    scales = [turned(jnp.where(wall[x] == 0, 0.5 * time_step, 0.0).astype(f32), cell_z) for x in range(depth)]
    for a in range(3):
        x_low, x_high = low_and_high("gx", x_one, x_two, a)
        y_low, y_high = low_and_high("gy", y_one, y_two, a)
        rows = [x_low] + [velocity[a, x] for x in range(depth)] + [x_high]
        rows = [turned(row, cell_z) for row in rows]
        low, high = turned(y_low, cell_z), turned(y_high, cell_z)
        for x in range(depth):
            here = rows[x + 1]
            above = high if x == depth - 1 else pltpu.roll(high, LANES - cell_z * (x + 1), 1)
            below = low if x == 0 else pltpu.roll(low, LANES - cell_z * x, 1)
            y_up = jnp.where(lane < LANES - cell_z, pltpu.roll(here, LANES - cell_z, 1), above)
            y_down = jnp.where(lane >= cell_z, pltpu.roll(here, cell_z, 1), below)
            next_tile = pltpu.roll(pltpu.roll(here, cell_z - 1, 1), 1, 0)
            last_tile = pltpu.roll(pltpu.roll(here, LANES - cell_z + 1, 1), SUB - 1, 0)
            next_tile = jnp.where(sub == 0, 0.0, next_tile)
            last_tile = jnp.where(sub == SUB - 1, 0.0, last_tile)
            z_up = jnp.where(z == cell_z - 1, next_tile, pltpu.roll(here, LANES - 1, 1))
            z_down = jnp.where(z == 0, last_tile, pltpu.roll(here, 1, 1))
            for b, difference in enumerate((rows[x + 2] - rows[x], y_up - y_down, z_up - z_down)):
                grad[pl.ds(((3 * a + b) * depth + x) * SUB, SUB), :] = difference * scales[x]
    keep[...] = jnp.zeros(keep.shape, f32)
    send[...] = jnp.zeros(send.shape, f32)
    for h, owned, tile in owned_slots(tiles, me, helper):

        @pl.when(owned)
        def _(h=h, tile=tile):
            g = [grad[pl.ds(i * depth * SUB + SUB - 1 - tile, depth, stride=SUB), :] for i in range(9)]
            rows = g + coefficients(g, [moments[h, i] for i in range(16)])
            stays = (me & 1) == (h & 1)

            @pl.when(stays)
            def _():
                for i, row in enumerate(rows):
                    keep[h >> 1, i] = row

            @pl.when(jnp.logical_not(stays))
            def _():
                for i, row in enumerate(rows):
                    send[h >> 1, i] = row


def call_gradients(tiles, helper_tile, velocity, halos, wall_cells, moments):
    slots = helper_tile.shape[1]
    depth = velocity.shape[1]
    half = jax.ShapeDtypeStruct((slots // 2, 12, depth, LANES), f32)
    return pl.pallas_call(
        functools.partial(gradients, tiles),
        out_shape=(jax.ShapeDtypeStruct((9 * depth * SUB, LANES), f32), half, half),
        in_specs=[vmem] * 8,
        out_specs=(vmem,) * 3,
        compiler_params=pltpu.CompilerParams(vmem_limit_bytes=8 << 20),
        cost_estimate=small(4 << 20, 1 << 20),
        name="gradients",
    )(helper_tile, velocity, *halos, wall_cells, moments)


def swapped_within(block):
    size = lax.axis_size("gy")
    return lax.ppermute(block, "gy", [(i, i ^ 1) for i in range(size)])


def swapped_across(block, stage):
    size = lax.axis_size("gy")
    bits = (size // 2).bit_length() - 1
    return lax.ppermute(block, "gy", [(i, i ^ (2 << (bits - 1 - stage if i & 1 else stage))) for i in range(size)])


def by_stage(flip, pairs, odd):
    bits = pairs.bit_length() - 1
    turned_over = sum(((flip >> (bits - 1 - i)) & 1) << i for i in range(bits))
    return jnp.where(odd, turned_over, flip)


def halve(first, before, kept, received, keep, send):
    me = lax.axis_index("gy")
    for k in range(kept.shape[0]):
        slot = (me >> 1) ^ by_stage(k, kept.shape[0], (me & 1) == 1) if first else k
        out = send if k & 1 else keep
        out[k >> 1] = kept[slot] + received[slot]


def call_halve(first, before, kept, received):
    half = jax.ShapeDtypeStruct((kept.shape[0] // 2,) + kept.shape[1:], f32)
    return pl.pallas_call(
        functools.partial(halve, first),
        out_shape=(half, half),
        in_specs=[anywhere, vmem, vmem],
        out_specs=(vmem, vmem),
        compiler_params=pltpu.CompilerParams(vmem_limit_bytes=4 << 20),
        cost_estimate=small(1 << 10, 1 << 18),
        name="halve",
    )(before, kept, received)


def join(before, first, second, out):
    count = first.shape[0]
    out[:count] = first[...]
    out[count:] = second[...]


def call_join(before, first, second):
    return pl.pallas_call(
        join,
        out_shape=jax.ShapeDtypeStruct((2 * first.shape[0],) + first.shape[1:], f32),
        in_specs=[anywhere, vmem, vmem],
        out_specs=vmem,
        compiler_params=pltpu.CompilerParams(vmem_limit_bytes=4 << 20),
        cost_estimate=small(1 << 10, 1 << 18),
        name="join",
    )(before, first, second)


def stress_rows(sums, inverse):
    second = [s * inverse for s in sums]
    stretch = 1.0 / (1.0 - (second[0] + second[1] + second[2]) / max_extension)
    return [(stretch * s - (1.0 if i < 3 else 0.0)) * (1.0 / weissenberg) for i, s in enumerate(second)]


def tile_grad(grad, depth, tile, x):
    return [wide(grad[pl.ds((i * depth + x + 1) * SUB - 1 - tile, 1), :]) for i in range(9)]


def tile_sums(read, write, noise, matrices, count, add, many):
    sums = [jnp.zeros((SUB, LANES), f32)] * many
    for group in range(count // (2 * SUB)):
        pairs = [noise_rows(functools.partial(noise, step), group * 2 * SUB) for step in range(len(matrices))]
        for half in range(2):
            rows = pl.ds((2 * group + half) * SUB, SUB)
            q = [read(a, rows) for a in range(3)]
            for step, matrix in enumerate(matrices):
                q = stepped(q, pairs[step][half], matrix)
            for a in range(3):
                write(a, rows, q[a])
            sums = add(sums, q)
    return sums


def add_square(sums, q):
    return [sums[0] + (q[0] * q[0] + q[1] * q[1] + q[2] * q[2])]


def ordinary(first, has_block, has_base, leaving, has_old, *refs):
    refs = list(refs)
    before, base, noise, grad = refs[:4]
    del refs[:4]
    block = refs.pop(0) if has_block else None
    if has_base:
        refs.pop(0)
    extra_near = refs.pop(0) if leaving else None
    if has_old:
        refs.pop(0)
    new_base = refs.pop(0) if has_block else None
    new_extra = refs.pop(0) if leaving else None
    fields, stress, halfway, relaxes, sems = refs
    here, _, count, cells = fields.shape
    depth = cells // LANES
    inverse = 1.0 / count
    copies = []
    if has_block:
        last = block.shape[0]
        copies += [
            pltpu.make_async_copy(block.at[i], new_base.at[0, 0, first - last + i], sems.at[i]) for i in range(last)
        ]
    copies += [
        pltpu.make_async_copy(extra_near.at[0, 0, a], new_extra.at[0, 0, a], sems.at[len(copies) + i])
        for i, a in enumerate(leaving)
    ]
    for copy in copies:
        copy.start()
    for place in range(here):
        tile = first + place

        def squares(x):
            total = jnp.zeros((SUB, LANES), f32)
            for group in range(count // SUB):
                for a in range(3):
                    q = base[0, 0, tile, a, pl.ds(group * SUB, SUB), pl.ds(x * LANES, LANES)]
                    total = total + q * q
            return [total]

        sums = packed_sums(squares, depth)
        for step in range(2):
            relaxes[place, step] = relax_of(sums[0], inverse)

            def sums_of(x):
                lanes = pl.ds(x * LANES, LANES)
                matrix = with_diagonal(tile_grad(grad, depth, tile, x), wide(relaxes[place, step, pl.ds(x, 1), :]))

                def read(a, rows):
                    return base[0, 0, tile, a, rows, lanes] if step == 0 else halfway[place, a, rows, lanes]

                def write(a, rows, value):
                    if step == 0:
                        halfway[place, a, rows, lanes] = value
                    else:
                        fields[place, a, rows, lanes] = value

                def shock(_, a, rows):
                    return noise[0, 0, tile, step, a, rows, lanes]

                if step == 0:
                    return tile_sums(read, write, shock, [matrix], count, add_square, 1)
                return tile_sums(read, write, shock, [matrix], count, add_moments, 6)

            sums = packed_sums(sums_of, depth)
        for i, row in enumerate(stress_rows(sums, inverse)):
            stress[i, place] = row
    for copy in copies:
        copy.wait()


def call_ordinary(first, here, before, base_fields, base_noise, grad, block, new_base, extra_near, leaving, new_extra):
    count, cells = base_fields.shape[-2:]
    depth = cells // LANES
    has_block, has_base, has_old = block is not None, new_base is not None, bool(leaving) and new_extra is not None
    operands = [before, *near_memory(base_fields, base_noise), grad]
    specs = [anywhere, vmem, vmem, vmem]
    shapes, out_specs, aliases = [], [], {}
    copies = 0
    if has_block:
        operands += near_memory(block)
        specs.append(vmem)
        shapes.append(jax.ShapeDtypeStruct(base_fields.shape, f32))
        out_specs.append(hbm)
        copies += block.shape[0]
    if has_base:
        aliases[len(operands)] = 0
        operands.append(new_base)
        specs.append(hbm)
    if leaving:
        operands += near_memory(extra_near)
        specs.append(vmem)
        if has_old:
            aliases[len(operands)] = len(shapes)
            operands.append(new_extra)
            specs.append(hbm)
        shapes.append(jax.ShapeDtypeStruct(extra_near.shape, f32))
        out_specs.append(hbm)
        copies += len(leaving)
    shapes += [
        pltpu.VMEM((here, 3, count, cells), f32),
        jax.ShapeDtypeStruct((6, here, depth, LANES), f32),
    ]
    out_specs += [vmem, vmem]
    results = pl.pallas_call(
        functools.partial(ordinary, first, has_block, has_base, leaving, has_old),
        out_shape=tuple(shapes),
        in_specs=specs,
        out_specs=tuple(out_specs),
        input_output_aliases=aliases,
        scratch_shapes=[
            pltpu.VMEM((here, 3, count, cells), f32),
            pltpu.VMEM((here, 2, depth, LANES), f32),
            pltpu.SemaphoreType.DMA((max(copies, 1),)),
        ],
        compiler_params=pltpu.CompilerParams(vmem_limit_bytes=SMALL),
        cost_estimate=small(8 << 20, 3 << 20),
        name="ordinary_tiles",
    )(*operands)
    results = list(results)
    piece, block = results.pop(), results.pop()
    new_base = results.pop(0) if has_block else None
    return new_base, block, piece, (results[0] if leaving else None)


def extra(unroll, before, base, noise, moments, *refs):
    *parts, new_fields, reply, message = refs
    _, _, _, count, cells = base.shape
    inverse = 1.0 / float(ALL_FIELDS)
    zero = jnp.zeros((SUB, LANES), f32)
    message[...] = sum(part[0] for part in parts)
    own = coefficients([message[i] for i in range(9)], [moments[i] for i in range(16)])
    both = [message[9 + i] + own[i] for i in range(3)]
    first = relax_of(both[2], inverse)
    second = relax_of(both[0] + first * (both[1] + first * both[2]), inverse)
    reply[0], reply[1] = first, second

    @pl.loop(0, cells // LANES)
    def _(x):
        lanes = pl.ds(pl.multiple_of(x * LANES, LANES), LANES)
        grad = [wide(message[i, pl.ds(x, 1), :]) for i in range(9)]
        matrices = [with_diagonal(grad, wide(reply[step, pl.ds(x, 1), :])) for step in range(2)]

        def body(i, sums):
            start = pl.multiple_of(i * 2 * SUB, 2 * SUB)
            pairs = [noise_rows(lambda a, rows: noise[0, 0, step, a, rows, lanes], start) for step in range(2)]
            for half in range(2):
                rows = pl.ds(start + half * SUB, SUB)
                q = [base[0, 0, a, rows, lanes] for a in range(3)]
                for step in range(2):
                    q = stepped(q, pairs[step][half], matrices[step])
                for a in range(3):
                    new_fields[0, 0, a, rows, lanes] = q[a]
                sums = add_moments(sums, q)
            return sums

        for i, s in enumerate(lax.fori_loop(0, count // (2 * SUB), body, [zero] * 6, unroll=unroll)):
            reply[2 + i, pl.ds(x, 1), :] = column_sum(s)


def call_extra(before, extra_fields, extra_noise, moments, parts):
    depth = extra_fields.shape[-1] // LANES
    return pl.pallas_call(
        functools.partial(extra, 7),
        out_shape=(
            pltpu.VMEM(extra_fields.shape, f32),
            jax.ShapeDtypeStruct((8, depth, LANES), f32),
        ),
        in_specs=[anywhere, vmem, vmem, vmem] + [vmem] * len(parts),
        out_specs=(vmem, vmem),
        scratch_shapes=[pltpu.VMEM(parts[0].shape[1:], f32)],
        compiler_params=pltpu.CompilerParams(vmem_limit_bytes=SMALL),
        cost_estimate=small(32 << 20, 9 << 20),
        name="extra_fields",
    )(before, *near_memory(extra_fields, extra_noise), moments, *parts)


def finish(piece_count, before, block, *refs):
    pieces, (_, new_base, rows, sems) = refs[:piece_count], refs[piece_count:]
    _, depth, tiles, _ = rows.shape
    last = block.shape[0]
    flat = rows.reshape(6 * depth * tiles, LANES)
    copies = [pltpu.make_async_copy(block.at[i], new_base.at[0, 0, tiles - last + i], sems.at[i]) for i in range(last)]
    for copy in copies:
        copy.start()
    tile = 0
    for piece in pieces:
        for place in range(piece.shape[1]):
            for i in range(6):
                flat[pl.ds(i * depth * tiles + tile, depth, stride=tiles), :] = piece[i, place]
            tile += 1
    for copy in copies:
        copy.wait()


def call_finish(before, block, pieces, new_base):
    tiles, cells = new_base.shape[2], new_base.shape[-1]
    return pl.pallas_call(
        functools.partial(finish, len(pieces)),
        out_shape=(
            jax.ShapeDtypeStruct(new_base.shape, f32),
            jax.ShapeDtypeStruct((6, cells // LANES, tiles, LANES), f32),
        ),
        in_specs=[anywhere, vmem] + [vmem] * len(pieces) + [hbm],
        out_specs=(hbm, vmem),
        input_output_aliases={2 + len(pieces): 0},
        scratch_shapes=[pltpu.SemaphoreType.DMA((block.shape[0],))],
        compiler_params=pltpu.CompilerParams(vmem_limit_bytes=4 << 20),
        cost_estimate=small(1 << 10, 1 << 20),
        name="finish",
    )(before, *near_memory(block), *pieces, new_base)


def heavy(helper, base, noise, grad, near, far, ready, old_base, new_base, stress, fields, rows, answer, sems):
    _, _, tiles, _, count, cells = base.shape
    me = lax.axis_index("gy")
    depth = cells // LANES
    flat = rows.reshape(6 * depth * tiles, LANES)

    def store(k, tile):
        return pltpu.make_async_copy(fields.at[k], new_base.at[0, 0, tile], sems.at[k])

    def result(x):
        target = stress.at[0, 0, :, :, pl.ds(x * LANES, LANES)]
        return pltpu.make_async_copy(rows.at[:, x], target, sems.at[HEAVY_MOST + x])

    rows[...] = ready[...]
    places, order = owned_order(tiles, me, helper)
    for k, (h, tile) in enumerate(order):

        @pl.when(k < places)
        def _(k=k, h=h, tile=tile):
            flip = (me ^ h) >> 1
            is_far, odd = ((me ^ h) & 1) == 1, (h & 1) == 1
            place = by_stage(flip, near.shape[0], odd)
            for i in range(near.shape[1]):
                answer[i] = jnp.where(is_far, far[place, i], near[place, i])

            def sums_of(x):
                lanes = pl.ds(x * LANES, LANES)
                g = tile_grad(grad, depth, tile, x)
                matrices = [with_diagonal(g, wide(answer[step, pl.ds(x, 1), :])) for step in range(2)]

                def read(a, part):
                    return base[0, 0, tile, a, part, lanes]

                def write(a, part, value):
                    fields[k, a, part, lanes] = value

                def shock(step, a, part):
                    return noise[0, 0, tile, step, a, part, lanes]

                return tile_sums(read, write, shock, matrices, count, add_moments, 6)

            sums = packed_sums(sums_of, depth)
            store(k, tile).start()
            sums = [s + answer[2 + i] for i, s in enumerate(sums)]
            for i, value in enumerate(stress_rows(sums, 1.0 / ALL_FIELDS)):
                flat[pl.ds(i * depth * tiles + tile, depth, stride=tiles), :] = value

    for x in range(depth):
        result(x).start()
    for k, (_, tile) in enumerate(order):

        @pl.when(k < places)
        def _(k=k, tile=tile):
            store(k, tile).wait()

    for x in range(depth):
        result(x).wait()


def call_heavy(helper_tile, base_fields, base_noise, grad, near, far, ready, new_base):
    _, _, tiles, _, count, cells = base_fields.shape
    depth = cells // LANES
    return pl.pallas_call(
        heavy,
        out_shape=(
            jax.ShapeDtypeStruct(new_base.shape, f32),
            jax.ShapeDtypeStruct((1, 1, 6, tiles, cells), f32),
        ),
        in_specs=[vmem] * 7 + [hbm],
        out_specs=(hbm, hbm),
        input_output_aliases={7: 0},
        scratch_shapes=[
            pltpu.VMEM((HEAVY_MOST, 3, count, cells), f32),
            pltpu.VMEM((6, depth, tiles, LANES), f32),
            pltpu.VMEM(near.shape[1:], f32),
            pltpu.SemaphoreType.DMA((HEAVY_MOST + depth,)),
        ],
        compiler_params=pltpu.CompilerParams(vmem_limit_bytes=SMALL),
        cost_estimate=small(8 << 20, 4 << 20),
        name="heavy_tiles",
    )(helper_tile, *near_memory(base_fields, base_noise), grad, near, far, ready, new_base)


def per_device(
    velocity, wall_cells, tile_counts, helper_tile, base_fields, extra_fields, base_noise, extra_noise
):
    tiles = tile_counts.shape[2]
    stages = (lax.axis_size("gy") // 2).bit_length() - 1
    helper_tile, x_one, x_two, y_one, y_two = call_edges(helper_tile, velocity)
    halos = two_swaps(x_one, x_two, "gx") + two_swaps(y_one, y_two, "gy")
    moments = call_heavy_moments(helper_tile, base_fields, base_noise)
    grad, keep, send = call_gradients(tiles, helper_tile, velocity, halos, wall_cells, moments)
    gaps = 2 * stages
    new_base, block, pieces, done, new_extra = None, None, [], 0, None

    def fill(before, extra_near=None, leaving=()):
        nonlocal new_base, block, done, new_extra
        here = (tiles - done) // (gaps - len(pieces))
        new_base, block, piece, extra_far = call_ordinary(
            done, here, before, base_fields, base_noise, grad, block, new_base, extra_near, leaving, new_extra
        )
        new_extra = extra_far if leaving else new_extra
        pieces.append(piece)
        done += here
        return piece

    received = swapped_within(send)
    before = fill(send)
    for stage in range(stages):
        keep, send = call_halve(stage == 0, before, keep, received)
        received = swapped_across(send, stage)
        if stage == 0:
            before = extra_sums = call_extra_moments(send, extra_fields, extra_noise)
        else:
            before = fill(send)
    extra_near, reply = call_extra(before, extra_fields, extra_noise, extra_sums, [keep, received])
    near = reply[None]
    for stage in range(stages):
        received = swapped_across(near, stage)
        before = fill(near, extra_near, ((0,), (1, 2))[stage] if stage < 2 else ())
        near = call_join(before, near, received)
    far = swapped_within(near)
    new_base, ready = call_finish(near, block, pieces, new_base)
    new_base, stress = call_heavy(helper_tile, base_fields, base_noise, grad, near, far, ready, new_base)
    return new_base, new_extra, jnp.swapaxes(stress, 2, 3)


def solution(mesh):
    in_specs = (
        P(None, "gx", "gy", None),
        P("gx", "gy", None),
        P("gx", "gy", None),
        P("gx", None),
        P("gx", "gy", None, None, None, None),
        P("gx", "gy", None, None, None),
        P("gx", "gy", None, None, None, None, None),
        P("gx", "gy", None, None, None, None),
    )
    out_specs = (
        P("gx", "gy", None, None, None, None),
        P("gx", "gy", None, None, None),
        P("gx", "gy", None, None, None),
    )
    return jax.shard_map(
        per_device, mesh=mesh, in_specs=in_specs, out_specs=out_specs, check_vma=False
    )
```

```python
import functools

import jax
import jax.numpy as jnp
from jax import lax
from jax.experimental import pallas as pl
from jax.experimental.pallas import tpu as pltpu
from jax.sharding import PartitionSpec as P

ALL_FIELDS = 256
HEAVY_MOST = 4
LANES = 128
SUB = 8
SMALL = 10 << 20

time_step = 0.05
weissenberg = 0.25
max_extension = 50.0
noise_scale = (time_step / weissenberg) ** 0.5
component_pairs = ((0, 0), (1, 1), (2, 2), (0, 1), (0, 2), (1, 2))
moment_of = {(0, 0): 0, (1, 1): 1, (2, 2): 2, (0, 1): 3, (1, 0): 3, (0, 2): 4, (2, 0): 4, (1, 2): 5, (2, 1): 5}
f32 = jnp.float32

vmem = pl.BlockSpec(memory_space=pltpu.VMEM)
hbm = pl.BlockSpec(memory_space=pltpu.HBM)
anywhere = pl.BlockSpec(memory_space=pl.ANY)


def far_memory(*arrays):
    return [pltpu.with_memory_space_constraint(array, pltpu.HBM) for array in arrays]


def near_memory(*arrays):
    return [pltpu.with_memory_space_constraint(array, pltpu.VMEM) for array in arrays]


def column_sum(value):
    return jnp.sum(value, axis=0, keepdims=True)


def interleaved(a, b, bit):
    low = (lax.broadcasted_iota(jnp.int32, (SUB, LANES), 0) & bit) == 0
    return jnp.where(low, a, b) + pltpu.roll(jnp.where(low, b, a), bit, 0)


def packed_sums(values_of, count):
    stack = []
    for x in range(count):
        bit, values = 1, values_of(x)
        while stack and stack[-1][0] == bit:
            values = [interleaved(a, b, bit) for a, b in zip(stack.pop()[1], values)]
            bit *= 2
        stack.append((bit, values))
    return stack[0][1]


def wide(row):
    return jnp.broadcast_to(row, (SUB, LANES))


def turned(value, cell_z):
    sub = lax.broadcasted_iota(jnp.int32, value.shape, 0)
    group = lax.broadcasted_iota(jnp.int32, value.shape, 1) // cell_z
    skewed = pltpu.roll(value, cell_z, 1, stride=cell_z, stride_axis=0)
    mixed = jnp.take_along_axis(skewed, (group + sub) & (SUB - 1), axis=0, mode="promise_in_bounds")
    return pltpu.roll(mixed, 0, 1, stride=cell_z, stride_axis=0)


def relax_of(total, inverse):
    factor = 1.0 / (1.0 - total * inverse / max_extension)
    return 1.0 - (time_step * 0.5 / weissenberg) * factor


def stepped(vectors, noise, matrix):
    return [
        matrix[3 * a] * vectors[0]
        + matrix[3 * a + 1] * vectors[1]
        + matrix[3 * a + 2] * vectors[2]
        + noise_scale * noise[a]
        for a in range(3)
    ]


def with_diagonal(grad, relax):
    return [g + relax if i % 4 == 0 else g for i, g in enumerate(grad)]


def noise_rows(ref, start):
    both = [ref(a, pl.ds(start, 2 * SUB)).astype(f32) for a in range(3)]
    return [[w[:SUB] for w in both], [w[SUB:] for w in both]]


def add_moments(sums, q):
    return [s + q[a] * q[b] for s, (a, b) in zip(sums, component_pairs)]


def product_sums(sums, q, w):
    terms = [q[a] * q[b] for a, b in component_pairs]
    terms += [q[a] * w[b] for a in range(3) for b in range(3)]
    terms += [w[0] * w[0] + w[1] * w[1] + w[2] * w[2]]
    return [s + t for s, t in zip(sums, terms)]


def coefficients(g, m):
    cross = lambda a, b: m[6 + 3 * a + b]
    square = lambda a, b: m[moment_of[a, b]]
    once, twice, kick = 0.0, 0.0, 0.0
    for a in range(3):
        for b in range(3):
            once += g[3 * a + b] * square(a, b)
            kick += g[3 * a + b] * cross(b, a)
            inner = 0.0
            for c in range(3):
                inner += g[3 * a + c] * square(b, c)
            twice += g[3 * a + b] * inner
    return [
        twice + (2 * noise_scale) * kick + noise_scale**2 * m[15],
        2.0 * once + (2 * noise_scale) * (cross(0, 0) + cross(1, 1) + cross(2, 2)),
        m[0] + m[1] + m[2],
    ]


def owned_slots(tiles, me, helper):
    found = []
    row = helper[...]
    for h in range(helper.shape[1]):
        tile = row[0, h] - me * tiles
        found.append((h, (tile >= 0) & (tile < tiles), tile))
    return found


def owned_order(tiles, me, helper):
    places = jnp.int32(0)
    order = [jnp.int32(0)] * HEAVY_MOST
    for h, owned, tile in owned_slots(tiles, me, helper):
        entry = h * tiles + tile
        order = [jnp.where(owned & (places == k), entry, kept) for k, kept in enumerate(order)]
        places = places + owned.astype(jnp.int32)
    return places, [(entry // tiles, entry % tiles) for entry in order]


def small(flops, traffic):
    return pl.CostEstimate(flops=flops, bytes_accessed=traffic, transcendentals=0)


def is_even(axis):
    return (lax.axis_index(axis) & 1) == 0


def edges(helper, velocity, helper_near, x_one, x_two, y_one, y_two):
    depth, width = velocity.shape[1:3]
    helper_near[...] = helper[...]
    even = is_even("gx")
    for a in range(3):
        first, last = velocity[a, 0], velocity[a, depth - 1]
        x_one[a] = jnp.where(even, last, first)
        x_two[a] = jnp.where(even, first, last)
    even = is_even("gy")
    for a in range(3):
        for x in range(depth):
            first, last = velocity[a, x, pl.ds(0, 1), :], velocity[a, x, pl.ds(width - 1, 1), :]
            y_one[a, pl.ds(x, 1), :] = jnp.where(even, last, first)
            y_two[a, pl.ds(x, 1), :] = jnp.where(even, first, last)


def call_edges(helper_tile, velocity):
    _, depth, width, length = velocity.shape
    along_x = jax.ShapeDtypeStruct((3, width, length), f32)
    along_y = jax.ShapeDtypeStruct((3, depth, length), f32)
    return pl.pallas_call(
        edges,
        out_shape=(jax.ShapeDtypeStruct(helper_tile.shape, jnp.int32), along_x, along_x, along_y, along_y),
        in_specs=[vmem, vmem],
        out_specs=(vmem,) * 5,
        compiler_params=pltpu.CompilerParams(vmem_limit_bytes=4 << 20),
        cost_estimate=small(1 << 10, 1 << 17),
        name="edges",
    )(*far_memory(helper_tile, velocity))


def swap_within(block, axis):
    return lax.ppermute(block, axis, [(i, i ^ 1) for i in range(lax.axis_size(axis))])


def swap_across(block, axis):
    size = lax.axis_size(axis)
    return lax.ppermute(block, axis, [(i, (i - 1 + 2 * (i & 1)) % size) for i in range(size)])


def low_and_high(axis, one, two, a):
    even, place = is_even(axis), lax.axis_index(axis)
    low = jnp.where(even, two[a], one[a])
    high = jnp.where(even, one[a], two[a])
    return jnp.where(place == 0, 0.0, low), jnp.where(place == lax.axis_size(axis) - 1, 0.0, high)


def heavy_moments(helper, base, noise, out, fields, shocks, sems):
    _, _, count, cells = fields.shape
    tiles = base.shape[2]
    me = lax.axis_index("gy")

    def loads(k, tile):
        return (
            pltpu.make_async_copy(base.at[0, 0, tile], fields.at[k], sems.at[0, k]),
            pltpu.make_async_copy(noise.at[0, 0, tile, 0], shocks.at[k], sems.at[1, k]),
        )

    places, order = owned_order(tiles, me, helper)
    for k, (_, tile) in enumerate(order):

        @pl.when(k < places)
        def _(k=k, tile=tile):
            for copy in loads(k, tile):
                copy.start()

    for k, (h, tile) in enumerate(order):

        @pl.when(k < places)
        def _(k=k, h=h, tile=tile):
            for copy in loads(k, tile):
                copy.wait()

            def sums_of(x):
                lanes = pl.ds(x * LANES, LANES)
                sums = [jnp.zeros((SUB, LANES), f32)] * 16
                for group in range(count // (2 * SUB)):
                    pair = noise_rows(lambda a, rows: shocks[k, a, rows, lanes], group * 2 * SUB)
                    for half in range(2):
                        rows = pl.ds((2 * group + half) * SUB, SUB)
                        sums = product_sums(sums, [fields[k, a, rows, lanes] for a in range(3)], pair[half])
                return sums

            for i, value in enumerate(packed_sums(sums_of, cells // LANES)):
                out[h, i] = value


def call_heavy_moments(helper_tile, base_fields, base_noise):
    slots = helper_tile.shape[1]
    count, cells = base_fields.shape[-2:]
    return pl.pallas_call(
        heavy_moments,
        out_shape=jax.ShapeDtypeStruct((slots, 16, cells // LANES, LANES), f32),
        in_specs=[vmem, hbm, hbm],
        out_specs=vmem,
        scratch_shapes=[
            pltpu.VMEM((HEAVY_MOST, 3, count, cells), f32),
            pltpu.VMEM((HEAVY_MOST, 3, count, cells), jnp.bfloat16),
            pltpu.SemaphoreType.DMA((2, HEAVY_MOST)),
        ],
        compiler_params=pltpu.CompilerParams(vmem_limit_bytes=SMALL),
        cost_estimate=small(8 << 20, 3 << 20),
        name="heavy_moments",
    )(helper_tile, *far_memory(base_fields, base_noise))


def extra_moments(unroll, before, base, noise, out):
    _, _, _, count, cells = base.shape
    zero = jnp.zeros((SUB, LANES), f32)

    @pl.loop(0, cells // LANES)
    def _(x):
        lanes = pl.ds(pl.multiple_of(x * LANES, LANES), LANES)

        def body(i, sums):
            start = pl.multiple_of(i * 2 * SUB, 2 * SUB)
            pair = noise_rows(lambda a, rows: noise[0, 0, 0, a, rows, lanes], start)
            for half in range(2):
                rows = pl.ds(start + half * SUB, SUB)
                sums = product_sums(sums, [base[0, 0, a, rows, lanes] for a in range(3)], pair[half])
            return sums

        for i, s in enumerate(lax.fori_loop(0, count // (2 * SUB), body, [zero] * 16, unroll=unroll)):
            out[i, pl.ds(x, 1), :] = column_sum(s)


def call_extra_moments(before, extra_fields, extra_noise):
    cells = extra_fields.shape[-1]
    return pl.pallas_call(
        functools.partial(extra_moments, 7),
        out_shape=jax.ShapeDtypeStruct((16, cells // LANES, LANES), f32),
        in_specs=[anywhere, vmem, vmem],
        out_specs=vmem,
        compiler_params=pltpu.CompilerParams(vmem_limit_bytes=SMALL),
        cost_estimate=small(8 << 20, 5 << 20),
        name="extra_moments",
    )(before, *near_memory(extra_fields, extra_noise))


def gradients(tiles, helper, velocity, y_two, x_two, x_one, y_one, wall, moments, grad, keep, send):
    me = lax.axis_index("gy")
    depth = velocity.shape[1]
    cell_z = velocity.shape[3] // tiles
    sub = lax.broadcasted_iota(jnp.int32, (SUB, LANES), 0)
    lane = lax.broadcasted_iota(jnp.int32, (SUB, LANES), 1)
    z = lane % cell_z
    scales = [turned(jnp.where(wall[x] == 0, 0.5 * time_step, 0.0).astype(f32), cell_z) for x in range(depth)]
    for a in range(3):
        x_low, x_high = low_and_high("gx", x_one, x_two, a)
        y_low, y_high = low_and_high("gy", y_one, y_two, a)
        rows = [x_low] + [velocity[a, x] for x in range(depth)] + [x_high]
        rows = [turned(row, cell_z) for row in rows]
        low, high = turned(y_low, cell_z), turned(y_high, cell_z)
        for x in range(depth):
            here = rows[x + 1]
            above = high if x == depth - 1 else pltpu.roll(high, LANES - cell_z * (x + 1), 1)
            below = low if x == 0 else pltpu.roll(low, LANES - cell_z * x, 1)
            y_up = jnp.where(lane < LANES - cell_z, pltpu.roll(here, LANES - cell_z, 1), above)
            y_down = jnp.where(lane >= cell_z, pltpu.roll(here, cell_z, 1), below)
            next_tile = pltpu.roll(pltpu.roll(here, cell_z - 1, 1), 1, 0)
            last_tile = pltpu.roll(pltpu.roll(here, LANES - cell_z + 1, 1), SUB - 1, 0)
            next_tile = jnp.where(sub == 0, 0.0, next_tile)
            last_tile = jnp.where(sub == SUB - 1, 0.0, last_tile)
            z_up = jnp.where(z == cell_z - 1, next_tile, pltpu.roll(here, LANES - 1, 1))
            z_down = jnp.where(z == 0, last_tile, pltpu.roll(here, 1, 1))
            for b, difference in enumerate((rows[x + 2] - rows[x], y_up - y_down, z_up - z_down)):
                grad[pl.ds(((3 * a + b) * depth + x) * SUB, SUB), :] = difference * scales[x]
    keep[...] = jnp.zeros(keep.shape, f32)
    send[...] = jnp.zeros(send.shape, f32)
    for h, owned, tile in owned_slots(tiles, me, helper):

        @pl.when(owned)
        def _(h=h, tile=tile):
            g = [grad[pl.ds(i * depth * SUB + SUB - 1 - tile, depth, stride=SUB), :] for i in range(9)]
            rows = g + coefficients(g, [moments[h, i] for i in range(16)])
            stays = (me & 1) == (h & 1)

            @pl.when(stays)
            def _():
                for i, row in enumerate(rows):
                    keep[h >> 1, i] = row

            @pl.when(jnp.logical_not(stays))
            def _():
                for i, row in enumerate(rows):
                    send[h >> 1, i] = row


def call_gradients(tiles, helper_tile, velocity, halos, wall_cells, moments):
    slots = helper_tile.shape[1]
    depth = velocity.shape[1]
    half = jax.ShapeDtypeStruct((slots // 2, 12, depth, LANES), f32)
    return pl.pallas_call(
        functools.partial(gradients, tiles),
        out_shape=(jax.ShapeDtypeStruct((9 * depth * SUB, LANES), f32), half, half),
        in_specs=[vmem] * 8,
        out_specs=(vmem,) * 3,
        compiler_params=pltpu.CompilerParams(vmem_limit_bytes=8 << 20),
        cost_estimate=small(4 << 20, 1 << 20),
        name="gradients",
    )(helper_tile, velocity, *halos, wall_cells, moments)


def swapped(block, flip):
    size = lax.axis_size("gy")
    return lax.ppermute(block, "gy", [(i, i ^ flip) for i in range(size)])


def merge(before, kept, received, keep, *sends):
    pair = lax.axis_index("gy") >> 1
    for flip, out in enumerate((keep,) + sends):
        out[...] = kept[pair ^ flip] + received[pair ^ flip]


def call_merge(before, kept, received):
    one = jax.ShapeDtypeStruct(kept.shape[1:], f32)
    return pl.pallas_call(
        merge,
        out_shape=(one,) * kept.shape[0],
        in_specs=[anywhere, vmem, vmem],
        out_specs=(vmem,) * kept.shape[0],
        compiler_params=pltpu.CompilerParams(vmem_limit_bytes=4 << 20),
        cost_estimate=small(1 << 10, 1 << 18),
        name="merge",
    )(before, kept, received)


def join(before, *refs):
    for i, ref in enumerate(refs[:-1]):
        refs[-1][i] = ref[...]


def call_join(before, blocks):
    return pl.pallas_call(
        join,
        out_shape=jax.ShapeDtypeStruct((len(blocks),) + blocks[0].shape, f32),
        in_specs=[anywhere] + [vmem] * len(blocks),
        out_specs=vmem,
        compiler_params=pltpu.CompilerParams(vmem_limit_bytes=4 << 20),
        cost_estimate=small(1 << 10, 1 << 18),
        name="join",
    )(before, *blocks)


def stress_rows(sums, inverse):
    second = [s * inverse for s in sums]
    stretch = 1.0 / (1.0 - (second[0] + second[1] + second[2]) / max_extension)
    return [(stretch * s - (1.0 if i < 3 else 0.0)) * (1.0 / weissenberg) for i, s in enumerate(second)]


def tile_grad(grad, depth, tile, x):
    return [wide(grad[pl.ds((i * depth + x + 1) * SUB - 1 - tile, 1), :]) for i in range(9)]


def tile_sums(read, write, noise, matrices, count, add, many):
    sums = [jnp.zeros((SUB, LANES), f32)] * many
    for group in range(count // (2 * SUB)):
        pairs = [noise_rows(functools.partial(noise, step), group * 2 * SUB) for step in range(len(matrices))]
        for half in range(2):
            rows = pl.ds((2 * group + half) * SUB, SUB)
            q = [read(a, rows) for a in range(3)]
            for step, matrix in enumerate(matrices):
                q = stepped(q, pairs[step][half], matrix)
            for a in range(3):
                write(a, rows, q[a])
            sums = add(sums, q)
    return sums


def add_square(sums, q):
    return [sums[0] + (q[0] * q[0] + q[1] * q[1] + q[2] * q[2])]


def ordinary(first, has_block, has_base, has_extra, *refs):
    refs = list(refs)
    before, base, noise, grad = refs[:4]
    del refs[:4]
    block = refs.pop(0) if has_block else None
    if has_base:
        refs.pop(0)
    extra_near = refs.pop(0) if has_extra else None
    new_base = refs.pop(0) if has_block else None
    new_extra = refs.pop(0) if has_extra else None
    fields, stress, halfway, relaxes, sems = refs
    here, _, count, cells = fields.shape
    depth = cells // LANES
    inverse = 1.0 / count
    copies = []
    if has_block:
        last = block.shape[0]
        copies += [
            pltpu.make_async_copy(block.at[i], new_base.at[0, 0, first - last + i], sems.at[i]) for i in range(last)
        ]
    if has_extra:
        copies += [
            pltpu.make_async_copy(extra_near.at[0, 0, a], new_extra.at[0, 0, a], sems.at[len(copies) + a])
            for a in range(3)
        ]
    for copy in copies:
        copy.start()
    for place in range(here):
        tile = first + place

        def squares(x):
            total = jnp.zeros((SUB, LANES), f32)
            for group in range(count // SUB):
                for a in range(3):
                    q = base[0, 0, tile, a, pl.ds(group * SUB, SUB), pl.ds(x * LANES, LANES)]
                    total = total + q * q
            return [total]

        sums = packed_sums(squares, depth)
        for step in range(2):
            relaxes[place, step] = relax_of(sums[0], inverse)

            def sums_of(x):
                lanes = pl.ds(x * LANES, LANES)
                matrix = with_diagonal(tile_grad(grad, depth, tile, x), wide(relaxes[place, step, pl.ds(x, 1), :]))

                def read(a, rows):
                    return base[0, 0, tile, a, rows, lanes] if step == 0 else halfway[place, a, rows, lanes]

                def write(a, rows, value):
                    if step == 0:
                        halfway[place, a, rows, lanes] = value
                    else:
                        fields[place, a, rows, lanes] = value

                def shock(_, a, rows):
                    return noise[0, 0, tile, step, a, rows, lanes]

                if step == 0:
                    return tile_sums(read, write, shock, [matrix], count, add_square, 1)
                return tile_sums(read, write, shock, [matrix], count, add_moments, 6)

            sums = packed_sums(sums_of, depth)
        for i, row in enumerate(stress_rows(sums, inverse)):
            stress[i, place] = row
    for copy in copies:
        copy.wait()


def call_ordinary(first, here, before, base_fields, base_noise, grad, block, new_base, new_extra):
    count, cells = base_fields.shape[-2:]
    depth = cells // LANES
    has_block, has_base, has_extra = block is not None, new_base is not None, new_extra is not None
    operands = [before, *near_memory(base_fields, base_noise), grad]
    specs = [anywhere, vmem, vmem, vmem]
    shapes, out_specs, aliases = [], [], {}
    copies = 0
    if has_block:
        operands += near_memory(block)
        specs.append(vmem)
        shapes.append(jax.ShapeDtypeStruct(base_fields.shape, f32))
        out_specs.append(hbm)
        copies += block.shape[0]
    if has_base:
        aliases[len(operands)] = 0
        operands.append(new_base)
        specs.append(hbm)
    if has_extra:
        operands += near_memory(new_extra)
        specs.append(vmem)
        shapes.append(jax.ShapeDtypeStruct(new_extra.shape, f32))
        out_specs.append(hbm)
        copies += 3
    shapes += [
        pltpu.VMEM((here, 3, count, cells), f32),
        jax.ShapeDtypeStruct((6, here, depth, LANES), f32),
    ]
    out_specs += [vmem, vmem]
    results = pl.pallas_call(
        functools.partial(ordinary, first, has_block, has_base, has_extra),
        out_shape=tuple(shapes),
        in_specs=specs,
        out_specs=tuple(out_specs),
        input_output_aliases=aliases,
        scratch_shapes=[
            pltpu.VMEM((here, 3, count, cells), f32),
            pltpu.VMEM((here, 2, depth, LANES), f32),
            pltpu.SemaphoreType.DMA((max(copies, 1),)),
        ],
        compiler_params=pltpu.CompilerParams(vmem_limit_bytes=SMALL),
        cost_estimate=small(8 << 20, 3 << 20),
        name="ordinary_tiles",
    )(*operands)
    results = list(results)
    piece, block = results.pop(), results.pop()
    new_base = results.pop(0) if has_block else None
    return new_base, block, piece, (results[0] if has_extra else None)


def extra(unroll, before, base, noise, moments, *refs):
    *parts, new_fields, reply, message = refs
    _, _, _, count, cells = base.shape
    inverse = 1.0 / float(ALL_FIELDS)
    zero = jnp.zeros((SUB, LANES), f32)
    message[...] = sum(part[...] for part in parts)
    own = coefficients([message[i] for i in range(9)], [moments[i] for i in range(16)])
    both = [message[9 + i] + own[i] for i in range(3)]
    first = relax_of(both[2], inverse)
    second = relax_of(both[0] + first * (both[1] + first * both[2]), inverse)
    reply[0], reply[1] = first, second

    @pl.loop(0, cells // LANES)
    def _(x):
        lanes = pl.ds(pl.multiple_of(x * LANES, LANES), LANES)
        grad = [wide(message[i, pl.ds(x, 1), :]) for i in range(9)]
        matrices = [with_diagonal(grad, wide(reply[step, pl.ds(x, 1), :])) for step in range(2)]

        def body(i, sums):
            start = pl.multiple_of(i * 2 * SUB, 2 * SUB)
            pairs = [noise_rows(lambda a, rows: noise[0, 0, step, a, rows, lanes], start) for step in range(2)]
            for half in range(2):
                rows = pl.ds(start + half * SUB, SUB)
                q = [base[0, 0, a, rows, lanes] for a in range(3)]
                for step in range(2):
                    q = stepped(q, pairs[step][half], matrices[step])
                for a in range(3):
                    new_fields[0, 0, a, rows, lanes] = q[a]
                sums = add_moments(sums, q)
            return sums

        for i, s in enumerate(lax.fori_loop(0, count // (2 * SUB), body, [zero] * 6, unroll=unroll)):
            reply[2 + i, pl.ds(x, 1), :] = column_sum(s)


def call_extra(before, extra_fields, extra_noise, moments, parts):
    depth = extra_fields.shape[-1] // LANES
    return pl.pallas_call(
        functools.partial(extra, 7),
        out_shape=(
            pltpu.VMEM(extra_fields.shape, f32),
            jax.ShapeDtypeStruct((8, depth, LANES), f32),
        ),
        in_specs=[anywhere, vmem, vmem, vmem] + [vmem] * len(parts),
        out_specs=(vmem, vmem),
        scratch_shapes=[pltpu.VMEM(parts[0].shape, f32)],
        compiler_params=pltpu.CompilerParams(vmem_limit_bytes=SMALL),
        cost_estimate=small(32 << 20, 9 << 20),
        name="extra_fields",
    )(before, *near_memory(extra_fields, extra_noise), moments, *parts)


def finish(piece_count, before, block, *refs):
    pieces, (_, new_base, rows, sems) = refs[:piece_count], refs[piece_count:]
    _, depth, tiles, _ = rows.shape
    last = block.shape[0]
    flat = rows.reshape(6 * depth * tiles, LANES)
    copies = [pltpu.make_async_copy(block.at[i], new_base.at[0, 0, tiles - last + i], sems.at[i]) for i in range(last)]
    for copy in copies:
        copy.start()
    tile = 0
    for piece in pieces:
        for place in range(piece.shape[1]):
            for i in range(6):
                flat[pl.ds(i * depth * tiles + tile, depth, stride=tiles), :] = piece[i, place]
            tile += 1
    for copy in copies:
        copy.wait()


def call_finish(before, block, pieces, new_base):
    tiles, cells = new_base.shape[2], new_base.shape[-1]
    return pl.pallas_call(
        functools.partial(finish, len(pieces)),
        out_shape=(
            jax.ShapeDtypeStruct(new_base.shape, f32),
            jax.ShapeDtypeStruct((6, cells // LANES, tiles, LANES), f32),
        ),
        in_specs=[anywhere, vmem] + [vmem] * len(pieces) + [hbm],
        out_specs=(hbm, vmem),
        input_output_aliases={2 + len(pieces): 0},
        scratch_shapes=[pltpu.SemaphoreType.DMA((block.shape[0],))],
        compiler_params=pltpu.CompilerParams(vmem_limit_bytes=4 << 20),
        cost_estimate=small(1 << 10, 1 << 20),
        name="finish",
    )(before, *near_memory(block), *pieces, new_base)


def heavy(helper, base, noise, grad, near, far, ready, old_base, new_base, stress, fields, rows, answer, sems):
    _, _, tiles, _, count, cells = base.shape
    me = lax.axis_index("gy")
    depth = cells // LANES
    flat = rows.reshape(6 * depth * tiles, LANES)

    def store(k, tile):
        return pltpu.make_async_copy(fields.at[k], new_base.at[0, 0, tile], sems.at[k])

    def result(x):
        target = stress.at[0, 0, :, :, pl.ds(x * LANES, LANES)]
        return pltpu.make_async_copy(rows.at[:, x], target, sems.at[HEAVY_MOST + x])

    rows[...] = ready[...]
    places, order = owned_order(tiles, me, helper)
    for k, (h, tile) in enumerate(order):

        @pl.when(k < places)
        def _(k=k, h=h, tile=tile):
            flip = (me ^ h) >> 1
            is_far = ((me ^ h) & 1) == 1
            for i in range(near.shape[1]):
                answer[i] = jnp.where(is_far, far[flip, i], near[flip, i])

            def sums_of(x):
                lanes = pl.ds(x * LANES, LANES)
                g = tile_grad(grad, depth, tile, x)
                matrices = [with_diagonal(g, wide(answer[step, pl.ds(x, 1), :])) for step in range(2)]

                def read(a, part):
                    return base[0, 0, tile, a, part, lanes]

                def write(a, part, value):
                    fields[k, a, part, lanes] = value

                def shock(step, a, part):
                    return noise[0, 0, tile, step, a, part, lanes]

                return tile_sums(read, write, shock, matrices, count, add_moments, 6)

            sums = packed_sums(sums_of, depth)
            store(k, tile).start()
            sums = [s + answer[2 + i] for i, s in enumerate(sums)]
            for i, value in enumerate(stress_rows(sums, 1.0 / ALL_FIELDS)):
                flat[pl.ds(i * depth * tiles + tile, depth, stride=tiles), :] = value

    for x in range(depth):
        result(x).start()
    for k, (_, tile) in enumerate(order):

        @pl.when(k < places)
        def _(k=k, tile=tile):
            store(k, tile).wait()

    for x in range(depth):
        result(x).wait()


def call_heavy(helper_tile, base_fields, base_noise, grad, near, far, ready, new_base):
    _, _, tiles, _, count, cells = base_fields.shape
    depth = cells // LANES
    return pl.pallas_call(
        heavy,
        out_shape=(
            jax.ShapeDtypeStruct(new_base.shape, f32),
            jax.ShapeDtypeStruct((1, 1, 6, tiles, cells), f32),
        ),
        in_specs=[vmem] * 7 + [hbm],
        out_specs=(hbm, hbm),
        input_output_aliases={7: 0},
        scratch_shapes=[
            pltpu.VMEM((HEAVY_MOST, 3, count, cells), f32),
            pltpu.VMEM((6, depth, tiles, LANES), f32),
            pltpu.VMEM(near.shape[1:], f32),
            pltpu.SemaphoreType.DMA((HEAVY_MOST + depth,)),
        ],
        compiler_params=pltpu.CompilerParams(vmem_limit_bytes=SMALL),
        cost_estimate=small(8 << 20, 4 << 20),
        name="heavy_tiles",
    )(helper_tile, *near_memory(base_fields, base_noise), grad, near, far, ready, new_base)


def per_device(
    velocity, wall_cells, tile_counts, helper_tile, base_fields, extra_fields, base_noise, extra_noise
):
    tiles = tile_counts.shape[2]
    pairs = lax.axis_size("gy") // 2
    helper_tile, x_one, x_two, y_one, y_two = call_edges(helper_tile, velocity)
    y_two = swap_across(y_two, "gy")
    x_two = swap_across(x_two, "gx")
    x_one = swap_within(x_one, "gx")
    y_one = swap_within(y_one, "gy")
    halos = (y_two, x_two, x_one, y_one)
    moments = call_heavy_moments(helper_tile, base_fields, base_noise)
    grad, keep, send = call_gradients(tiles, helper_tile, velocity, halos, wall_cells, moments)
    gaps = 3
    new_base, block, pieces, done = None, None, [], 0

    def fill(before, extra_near=None):
        nonlocal new_base, block, done
        here = (tiles - done) // (gaps - len(pieces))
        new_base, block, piece, extra_far = call_ordinary(
            done, here, before, base_fields, base_noise, grad, block, new_base, extra_near
        )
        pieces.append(piece)
        done += here
        return piece, extra_far

    received = swapped(send, 1)
    before, _ = fill(send)
    keep, *sends = call_merge(before, keep, received)
    farthest_first = sorted(range(1, pairs), key=lambda flip: -flip.bit_count())
    parts = [keep] + [swapped(sends[flip - 1], 2 * flip) for flip in farthest_first]
    extra_sums = call_extra_moments(sends[0], extra_fields, extra_noise)
    before, _ = fill(extra_sums)
    extra_near, reply = call_extra(before, extra_fields, extra_noise, extra_sums, parts)
    replies = {flip: swapped(reply, 2 * flip) for flip in farthest_first}
    before, new_extra = fill(reply, extra_near)
    near = call_join(before, [reply] + [replies[flip] for flip in range(1, pairs)])
    far = swapped(near, 1)
    new_base, ready = call_finish(near, block, pieces, new_base)
    new_base, stress = call_heavy(helper_tile, base_fields, base_noise, grad, near, far, ready, new_base)
    return new_base, new_extra, jnp.swapaxes(stress, 2, 3)


def solution(mesh):
    in_specs = (
        P(None, "gx", "gy", None),
        P("gx", "gy", None),
        P("gx", "gy", None),
        P("gx", None),
        P("gx", "gy", None, None, None, None),
        P("gx", "gy", None, None, None),
        P("gx", "gy", None, None, None, None, None),
        P("gx", "gy", None, None, None, None),
    )
    out_specs = (
        P("gx", "gy", None, None, None, None),
        P("gx", "gy", None, None, None),
        P("gx", "gy", None, None, None),
    )
    return jax.shard_map(
        per_device, mesh=mesh, in_specs=in_specs, out_specs=out_specs, check_vma=False
    )
```

```python
import functools

import jax
import jax.numpy as jnp
from jax import lax
from jax.experimental import pallas as pl
from jax.experimental.pallas import tpu as pltpu
from jax.sharding import PartitionSpec as P

ALL_FIELDS = 256
HEAVY_MOST = 4
LANES = 128
SUB = 8
SMALL = 10 << 20

time_step = 0.05
weissenberg = 0.25
max_extension = 50.0
noise_scale = (time_step / weissenberg) ** 0.5
component_pairs = ((0, 0), (1, 1), (2, 2), (0, 1), (0, 2), (1, 2))
moment_of = {(0, 0): 0, (1, 1): 1, (2, 2): 2, (0, 1): 3, (1, 0): 3, (0, 2): 4, (2, 0): 4, (1, 2): 5, (2, 1): 5}
f32 = jnp.float32

vmem = pl.BlockSpec(memory_space=pltpu.VMEM)
hbm = pl.BlockSpec(memory_space=pltpu.HBM)
anywhere = pl.BlockSpec(memory_space=pl.ANY)


def far_memory(*arrays):
    return [pltpu.with_memory_space_constraint(array, pltpu.HBM) for array in arrays]


def near_memory(*arrays):
    return [pltpu.with_memory_space_constraint(array, pltpu.VMEM) for array in arrays]


def column_sum(value):
    return jnp.sum(value, axis=0, keepdims=True)


def interleaved(a, b, bit):
    low = (lax.broadcasted_iota(jnp.int32, (SUB, LANES), 0) & bit) == 0
    return jnp.where(low, a, b) + pltpu.roll(jnp.where(low, b, a), bit, 0)


def packed_sums(values_of, count):
    stack = []
    for x in range(count):
        bit, values = 1, values_of(x)
        while stack and stack[-1][0] == bit:
            values = [interleaved(a, b, bit) for a, b in zip(stack.pop()[1], values)]
            bit *= 2
        stack.append((bit, values))
    return stack[0][1]


def wide(row):
    return jnp.broadcast_to(row, (SUB, LANES))


def turned(value, cell_z):
    sub = lax.broadcasted_iota(jnp.int32, value.shape, 0)
    group = lax.broadcasted_iota(jnp.int32, value.shape, 1) // cell_z
    skewed = pltpu.roll(value, cell_z, 1, stride=cell_z, stride_axis=0)
    mixed = jnp.take_along_axis(skewed, (group + sub) & (SUB - 1), axis=0, mode="promise_in_bounds")
    return pltpu.roll(mixed, 0, 1, stride=cell_z, stride_axis=0)


def relax_of(total, inverse):
    factor = 1.0 / (1.0 - total * inverse / max_extension)
    return 1.0 - (time_step * 0.5 / weissenberg) * factor


def stepped(vectors, noise, matrix):
    return [
        matrix[3 * a] * vectors[0]
        + matrix[3 * a + 1] * vectors[1]
        + matrix[3 * a + 2] * vectors[2]
        + noise_scale * noise[a]
        for a in range(3)
    ]


def with_diagonal(grad, relax):
    return [g + relax if i % 4 == 0 else g for i, g in enumerate(grad)]


def noise_rows(ref, start):
    both = [ref(a, pl.ds(start, 2 * SUB)).astype(f32) for a in range(3)]
    return [[w[:SUB] for w in both], [w[SUB:] for w in both]]


def add_moments(sums, q):
    return [s + q[a] * q[b] for s, (a, b) in zip(sums, component_pairs)]


def product_sums(sums, q, w):
    terms = [q[a] * q[b] for a, b in component_pairs]
    terms += [q[a] * w[b] for a in range(3) for b in range(3)]
    terms += [w[0] * w[0] + w[1] * w[1] + w[2] * w[2]]
    return [s + t for s, t in zip(sums, terms)]


def coefficients(g, m):
    cross = lambda a, b: m[6 + 3 * a + b]
    square = lambda a, b: m[moment_of[a, b]]
    once, twice, kick = 0.0, 0.0, 0.0
    for a in range(3):
        for b in range(3):
            once += g[3 * a + b] * square(a, b)
            kick += g[3 * a + b] * cross(b, a)
            inner = 0.0
            for c in range(3):
                inner += g[3 * a + c] * square(b, c)
            twice += g[3 * a + b] * inner
    return [
        twice + (2 * noise_scale) * kick + noise_scale**2 * m[15],
        2.0 * once + (2 * noise_scale) * (cross(0, 0) + cross(1, 1) + cross(2, 2)),
        m[0] + m[1] + m[2],
    ]


def owned_slots(tiles, me, helper):
    found = []
    row = helper[...]
    for h in range(helper.shape[1]):
        tile = row[0, h] - me * tiles
        found.append((h, (tile >= 0) & (tile < tiles), tile))
    return found


def owned_order(tiles, me, helper):
    places = jnp.int32(0)
    order = [jnp.int32(0)] * HEAVY_MOST
    for h, owned, tile in owned_slots(tiles, me, helper):
        entry = h * tiles + tile
        order = [jnp.where(owned & (places == k), entry, kept) for k, kept in enumerate(order)]
        places = places + owned.astype(jnp.int32)
    return places, [(entry // tiles, entry % tiles) for entry in order]


def small(flops, traffic):
    return pl.CostEstimate(flops=flops, bytes_accessed=traffic, transcendentals=0)


def is_even(axis):
    return (lax.axis_index(axis) & 1) == 0


def edges(helper, velocity, helper_near, x_one, x_two, y_one, y_two):
    depth, width = velocity.shape[1:3]
    helper_near[...] = helper[...]
    even = is_even("gx")
    for a in range(3):
        first, last = velocity[a, 0], velocity[a, depth - 1]
        x_one[a] = jnp.where(even, last, first)
        x_two[a] = jnp.where(even, first, last)
    even = is_even("gy")
    for a in range(3):
        for x in range(depth):
            first, last = velocity[a, x, pl.ds(0, 1), :], velocity[a, x, pl.ds(width - 1, 1), :]
            y_one[a, pl.ds(x, 1), :] = jnp.where(even, last, first)
            y_two[a, pl.ds(x, 1), :] = jnp.where(even, first, last)


def call_edges(helper_tile, velocity):
    _, depth, width, length = velocity.shape
    along_x = jax.ShapeDtypeStruct((3, width, length), f32)
    along_y = jax.ShapeDtypeStruct((3, depth, length), f32)
    return pl.pallas_call(
        edges,
        out_shape=(jax.ShapeDtypeStruct(helper_tile.shape, jnp.int32), along_x, along_x, along_y, along_y),
        in_specs=[vmem, vmem],
        out_specs=(vmem,) * 5,
        compiler_params=pltpu.CompilerParams(vmem_limit_bytes=4 << 20),
        cost_estimate=small(1 << 10, 1 << 17),
        name="edges",
    )(*far_memory(helper_tile, velocity))


def swap_within(block, axis):
    return lax.ppermute(block, axis, [(i, i ^ 1) for i in range(lax.axis_size(axis))])


def swap_across(block, along_rows):
    rows, columns = lax.axis_size("gx"), lax.axis_size("gy")
    size = rows if along_rows else columns

    def partner(row, column):
        place = row if along_rows else column
        if place in (0, size - 1):
            row, column = (row, column ^ 1) if along_rows else (row ^ 1, column)
        else:
            place += 1 if place & 1 else -1
            row, column = (place, column) if along_rows else (row, place)
        return row * columns + column

    places = [(row, column) for row in range(rows) for column in range(columns)]
    return lax.ppermute(block, ("gx", "gy"), [(i, partner(*place)) for i, place in enumerate(places)])


def low_and_high(axis, one, two, a):
    even, place = is_even(axis), lax.axis_index(axis)
    low = jnp.where(even, two[a], one[a])
    high = jnp.where(even, one[a], two[a])
    return jnp.where(place == 0, 0.0, low), jnp.where(place == lax.axis_size(axis) - 1, 0.0, high)


def heavy_moments(helper, base, noise, out, fields, shocks, sems):
    _, _, count, cells = fields.shape
    tiles = base.shape[2]
    me = lax.axis_index("gy")

    def loads(k, tile):
        return (
            pltpu.make_async_copy(base.at[0, 0, tile], fields.at[k], sems.at[0, k]),
            pltpu.make_async_copy(noise.at[0, 0, tile, 0], shocks.at[k], sems.at[1, k]),
        )

    places, order = owned_order(tiles, me, helper)
    for k, (_, tile) in enumerate(order):

        @pl.when(k < places)
        def _(k=k, tile=tile):
            for copy in loads(k, tile):
                copy.start()

    for k, (h, tile) in enumerate(order):

        @pl.when(k < places)
        def _(k=k, h=h, tile=tile):
            for copy in loads(k, tile):
                copy.wait()

            def sums_of(x):
                lanes = pl.ds(x * LANES, LANES)
                sums = [jnp.zeros((SUB, LANES), f32)] * 16
                for group in range(count // (2 * SUB)):
                    pair = noise_rows(lambda a, rows: shocks[k, a, rows, lanes], group * 2 * SUB)
                    for half in range(2):
                        rows = pl.ds((2 * group + half) * SUB, SUB)
                        sums = product_sums(sums, [fields[k, a, rows, lanes] for a in range(3)], pair[half])
                return sums

            for i, value in enumerate(packed_sums(sums_of, cells // LANES)):
                out[h, i] = value


def call_heavy_moments(helper_tile, base_fields, base_noise):
    slots = helper_tile.shape[1]
    count, cells = base_fields.shape[-2:]
    return pl.pallas_call(
        heavy_moments,
        out_shape=jax.ShapeDtypeStruct((slots, 16, cells // LANES, LANES), f32),
        in_specs=[vmem, hbm, hbm],
        out_specs=vmem,
        scratch_shapes=[
            pltpu.VMEM((HEAVY_MOST, 3, count, cells), f32),
            pltpu.VMEM((HEAVY_MOST, 3, count, cells), jnp.bfloat16),
            pltpu.SemaphoreType.DMA((2, HEAVY_MOST)),
        ],
        compiler_params=pltpu.CompilerParams(vmem_limit_bytes=SMALL),
        cost_estimate=small(8 << 20, 3 << 20),
        name="heavy_moments",
    )(helper_tile, *far_memory(base_fields, base_noise))


def extra_moments(unroll, before, base, noise, out):
    _, _, _, count, cells = base.shape
    zero = jnp.zeros((SUB, LANES), f32)

    @pl.loop(0, cells // LANES)
    def _(x):
        lanes = pl.ds(pl.multiple_of(x * LANES, LANES), LANES)

        def body(i, sums):
            start = pl.multiple_of(i * 2 * SUB, 2 * SUB)
            pair = noise_rows(lambda a, rows: noise[0, 0, 0, a, rows, lanes], start)
            for half in range(2):
                rows = pl.ds(start + half * SUB, SUB)
                sums = product_sums(sums, [base[0, 0, a, rows, lanes] for a in range(3)], pair[half])
            return sums

        for i, s in enumerate(lax.fori_loop(0, count // (2 * SUB), body, [zero] * 16, unroll=unroll)):
            out[i, pl.ds(x, 1), :] = column_sum(s)


def call_extra_moments(before, extra_fields, extra_noise):
    cells = extra_fields.shape[-1]
    return pl.pallas_call(
        functools.partial(extra_moments, 7),
        out_shape=jax.ShapeDtypeStruct((16, cells // LANES, LANES), f32),
        in_specs=[anywhere, vmem, vmem],
        out_specs=vmem,
        compiler_params=pltpu.CompilerParams(vmem_limit_bytes=SMALL),
        cost_estimate=small(8 << 20, 5 << 20),
        name="extra_moments",
    )(before, *near_memory(extra_fields, extra_noise))


def gradients(tiles, helper, velocity, y_two, x_two, x_one, y_one, wall, moments, grad, keep, send):
    me = lax.axis_index("gy")
    depth = velocity.shape[1]
    cell_z = velocity.shape[3] // tiles
    sub = lax.broadcasted_iota(jnp.int32, (SUB, LANES), 0)
    lane = lax.broadcasted_iota(jnp.int32, (SUB, LANES), 1)
    z = lane % cell_z
    scales = [turned(jnp.where(wall[x] == 0, 0.5 * time_step, 0.0).astype(f32), cell_z) for x in range(depth)]
    for a in range(3):
        x_low, x_high = low_and_high("gx", x_one, x_two, a)
        y_low, y_high = low_and_high("gy", y_one, y_two, a)
        rows = [x_low] + [velocity[a, x] for x in range(depth)] + [x_high]
        rows = [turned(row, cell_z) for row in rows]
        low, high = turned(y_low, cell_z), turned(y_high, cell_z)
        for x in range(depth):
            here = rows[x + 1]
            above = high if x == depth - 1 else pltpu.roll(high, LANES - cell_z * (x + 1), 1)
            below = low if x == 0 else pltpu.roll(low, LANES - cell_z * x, 1)
            y_up = jnp.where(lane < LANES - cell_z, pltpu.roll(here, LANES - cell_z, 1), above)
            y_down = jnp.where(lane >= cell_z, pltpu.roll(here, cell_z, 1), below)
            next_tile = pltpu.roll(pltpu.roll(here, cell_z - 1, 1), 1, 0)
            last_tile = pltpu.roll(pltpu.roll(here, LANES - cell_z + 1, 1), SUB - 1, 0)
            next_tile = jnp.where(sub == 0, 0.0, next_tile)
            last_tile = jnp.where(sub == SUB - 1, 0.0, last_tile)
            z_up = jnp.where(z == cell_z - 1, next_tile, pltpu.roll(here, LANES - 1, 1))
            z_down = jnp.where(z == 0, last_tile, pltpu.roll(here, 1, 1))
            for b, difference in enumerate((rows[x + 2] - rows[x], y_up - y_down, z_up - z_down)):
                grad[pl.ds(((3 * a + b) * depth + x) * SUB, SUB), :] = difference * scales[x]
    keep[...] = jnp.zeros(keep.shape, f32)
    send[...] = jnp.zeros(send.shape, f32)
    for h, owned, tile in owned_slots(tiles, me, helper):

        @pl.when(owned)
        def _(h=h, tile=tile):
            g = [grad[pl.ds(i * depth * SUB + SUB - 1 - tile, depth, stride=SUB), :] for i in range(9)]
            rows = g + coefficients(g, [moments[h, i] for i in range(16)])
            stays = (me & 1) == (h & 1)

            @pl.when(stays)
            def _():
                for i, row in enumerate(rows):
                    keep[h >> 1, i] = row

            @pl.when(jnp.logical_not(stays))
            def _():
                for i, row in enumerate(rows):
                    send[h >> 1, i] = row


def call_gradients(tiles, helper_tile, velocity, halos, wall_cells, moments):
    slots = helper_tile.shape[1]
    depth = velocity.shape[1]
    half = jax.ShapeDtypeStruct((slots // 2, 12, depth, LANES), f32)
    return pl.pallas_call(
        functools.partial(gradients, tiles),
        out_shape=(jax.ShapeDtypeStruct((9 * depth * SUB, LANES), f32), half, half),
        in_specs=[vmem] * 8,
        out_specs=(vmem,) * 3,
        compiler_params=pltpu.CompilerParams(vmem_limit_bytes=8 << 20),
        cost_estimate=small(4 << 20, 1 << 20),
        name="gradients",
    )(helper_tile, velocity, *halos, wall_cells, moments)


def swapped(block, flip):
    size = lax.axis_size("gy")
    return lax.ppermute(block, "gy", [(i, i ^ flip) for i in range(size)])


def merge(before, kept, received, keep, *sends):
    pair = lax.axis_index("gy") >> 1
    for flip, out in enumerate((keep,) + sends):
        out[...] = kept[pair ^ flip] + received[pair ^ flip]


def call_merge(before, kept, received):
    one = jax.ShapeDtypeStruct(kept.shape[1:], f32)
    return pl.pallas_call(
        merge,
        out_shape=(one,) * kept.shape[0],
        in_specs=[anywhere, vmem, vmem],
        out_specs=(vmem,) * kept.shape[0],
        compiler_params=pltpu.CompilerParams(vmem_limit_bytes=4 << 20),
        cost_estimate=small(1 << 10, 1 << 18),
        name="merge",
    )(before, kept, received)


def join(before, *refs):
    for i, ref in enumerate(refs[:-1]):
        refs[-1][i] = ref[...]


def call_join(before, blocks):
    return pl.pallas_call(
        join,
        out_shape=jax.ShapeDtypeStruct((len(blocks),) + blocks[0].shape, f32),
        in_specs=[anywhere] + [vmem] * len(blocks),
        out_specs=vmem,
        compiler_params=pltpu.CompilerParams(vmem_limit_bytes=4 << 20),
        cost_estimate=small(1 << 10, 1 << 18),
        name="join",
    )(before, *blocks)


def stress_rows(sums, inverse):
    second = [s * inverse for s in sums]
    stretch = 1.0 / (1.0 - (second[0] + second[1] + second[2]) / max_extension)
    return [(stretch * s - (1.0 if i < 3 else 0.0)) * (1.0 / weissenberg) for i, s in enumerate(second)]


def tile_grad(grad, depth, tile, x):
    return [wide(grad[pl.ds((i * depth + x + 1) * SUB - 1 - tile, 1), :]) for i in range(9)]


def tile_sums(read, write, noise, matrices, count, add, many):
    sums = [jnp.zeros((SUB, LANES), f32)] * many
    for group in range(count // (2 * SUB)):
        pairs = [noise_rows(functools.partial(noise, step), group * 2 * SUB) for step in range(len(matrices))]
        for half in range(2):
            rows = pl.ds((2 * group + half) * SUB, SUB)
            q = [read(a, rows) for a in range(3)]
            for step, matrix in enumerate(matrices):
                q = stepped(q, pairs[step][half], matrix)
            for a in range(3):
                write(a, rows, q[a])
            sums = add(sums, q)
    return sums


def add_square(sums, q):
    return [sums[0] + (q[0] * q[0] + q[1] * q[1] + q[2] * q[2])]


def ordinary(first, direct, has_block, has_base, has_extra, *refs):
    refs = list(refs)
    before, base, noise, grad = refs[:4]
    del refs[:4]
    block = refs.pop(0) if has_block else None
    if has_base:
        refs.pop(0)
    extra_near = refs.pop(0) if has_extra else None
    new_base = refs.pop(0) if has_block or direct else None
    new_extra = refs.pop(0) if has_extra else None
    fields, stress, early, halfway, relaxes, sems = refs
    _, _, count, cells = fields.shape
    here = direct + fields.shape[0]
    depth = cells // LANES
    inverse = 1.0 / count
    copies = []
    if has_block:
        last = block.shape[0]
        copies += [
            pltpu.make_async_copy(block.at[i], new_base.at[0, 0, first - last + i], sems.at[i]) for i in range(last)
        ]
    if has_extra:
        copies += [
            pltpu.make_async_copy(extra_near.at[0, 0, a], new_extra.at[0, 0, a], sems.at[len(copies) + a])
            for a in range(3)
        ]
    for copy in copies:
        copy.start()
    for place in range(here):
        tile = first + place

        def squares(x):
            total = jnp.zeros((SUB, LANES), f32)
            for group in range(count // SUB):
                for a in range(3):
                    q = base[0, 0, tile, a, pl.ds(group * SUB, SUB), pl.ds(x * LANES, LANES)]
                    total = total + q * q
            return [total]

        sums = packed_sums(squares, depth)
        for step in range(2):
            relaxes[place, step] = relax_of(sums[0], inverse)

            def sums_of(x):
                lanes = pl.ds(x * LANES, LANES)
                matrix = with_diagonal(tile_grad(grad, depth, tile, x), wide(relaxes[place, step, pl.ds(x, 1), :]))

                def read(a, rows):
                    return base[0, 0, tile, a, rows, lanes] if step == 0 else halfway[place, a, rows, lanes]

                def write(a, rows, value):
                    if step == 0:
                        halfway[place, a, rows, lanes] = value
                    elif place < direct:
                        early[place, a, rows, lanes] = value
                    else:
                        fields[place - direct, a, rows, lanes] = value

                def shock(_, a, rows):
                    return noise[0, 0, tile, step, a, rows, lanes]

                if step == 0:
                    return tile_sums(read, write, shock, [matrix], count, add_square, 1)
                return tile_sums(read, write, shock, [matrix], count, add_moments, 6)

            sums = packed_sums(sums_of, depth)
        if place < direct:
            copies.append(pltpu.make_async_copy(early.at[place], new_base.at[0, 0, tile], sems.at[len(copies)]))
            copies[-1].start()
        for i, row in enumerate(stress_rows(sums, inverse)):
            stress[i, place] = row
    for copy in copies:
        copy.wait()


def call_ordinary(first, here, direct, before, base_fields, base_noise, grad, block, new_base, new_extra):
    count, cells = base_fields.shape[-2:]
    depth = cells // LANES
    has_block, has_base, has_extra = block is not None, new_base is not None, new_extra is not None
    operands = [before, *near_memory(base_fields, base_noise), grad]
    specs = [anywhere, vmem, vmem, vmem]
    shapes, out_specs, aliases = [], [], {}
    copies = 0
    if has_block:
        operands += near_memory(block)
        specs.append(vmem)
        copies += block.shape[0]
    if has_block or direct:
        copies += direct
        shapes.append(jax.ShapeDtypeStruct(base_fields.shape, f32))
        out_specs.append(hbm)
    if has_base:
        aliases[len(operands)] = 0
        operands.append(new_base)
        specs.append(hbm)
    if has_extra:
        operands += near_memory(new_extra)
        specs.append(vmem)
        shapes.append(jax.ShapeDtypeStruct(new_extra.shape, f32))
        out_specs.append(hbm)
        copies += 3
    shapes += [
        pltpu.VMEM((here - direct, 3, count, cells), f32),
        jax.ShapeDtypeStruct((6, here, depth, LANES), f32),
    ]
    out_specs += [vmem, vmem]
    results = pl.pallas_call(
        functools.partial(ordinary, first, direct, has_block, has_base, has_extra),
        out_shape=tuple(shapes),
        in_specs=specs,
        out_specs=tuple(out_specs),
        input_output_aliases=aliases,
        scratch_shapes=[
            pltpu.VMEM((max(direct, 1), 3, count, cells), f32),
            pltpu.VMEM((here, 3, count, cells), f32),
            pltpu.VMEM((here, 2, depth, LANES), f32),
            pltpu.SemaphoreType.DMA((max(copies, 1),)),
        ],
        compiler_params=pltpu.CompilerParams(vmem_limit_bytes=SMALL),
        cost_estimate=small(8 << 20, 3 << 20),
        name="ordinary_tiles",
    )(*operands)
    results = list(results)
    piece, block = results.pop(), results.pop()
    new_base = results.pop(0) if has_block or direct else None
    return new_base, block, piece, (results[0] if has_extra else None)


def extra(unroll, before, base, noise, moments, *refs):
    *parts, new_fields, reply, message = refs
    _, _, _, count, cells = base.shape
    inverse = 1.0 / float(ALL_FIELDS)
    zero = jnp.zeros((SUB, LANES), f32)
    message[...] = sum(part[...] for part in parts)
    own = coefficients([message[i] for i in range(9)], [moments[i] for i in range(16)])
    both = [message[9 + i] + own[i] for i in range(3)]
    first = relax_of(both[2], inverse)
    second = relax_of(both[0] + first * (both[1] + first * both[2]), inverse)
    reply[0], reply[1] = first, second

    @pl.loop(0, cells // LANES)
    def _(x):
        lanes = pl.ds(pl.multiple_of(x * LANES, LANES), LANES)
        grad = [wide(message[i, pl.ds(x, 1), :]) for i in range(9)]
        matrices = [with_diagonal(grad, wide(reply[step, pl.ds(x, 1), :])) for step in range(2)]

        def body(i, sums):
            start = pl.multiple_of(i * 2 * SUB, 2 * SUB)
            pairs = [noise_rows(lambda a, rows: noise[0, 0, step, a, rows, lanes], start) for step in range(2)]
            for half in range(2):
                rows = pl.ds(start + half * SUB, SUB)
                q = [base[0, 0, a, rows, lanes] for a in range(3)]
                for step in range(2):
                    q = stepped(q, pairs[step][half], matrices[step])
                for a in range(3):
                    new_fields[0, 0, a, rows, lanes] = q[a]
                sums = add_moments(sums, q)
            return sums

        for i, s in enumerate(lax.fori_loop(0, count // (2 * SUB), body, [zero] * 6, unroll=unroll)):
            reply[2 + i, pl.ds(x, 1), :] = column_sum(s)


def call_extra(before, extra_fields, extra_noise, moments, parts):
    depth = extra_fields.shape[-1] // LANES
    return pl.pallas_call(
        functools.partial(extra, 7),
        out_shape=(
            pltpu.VMEM(extra_fields.shape, f32),
            jax.ShapeDtypeStruct((8, depth, LANES), f32),
        ),
        in_specs=[anywhere, vmem, vmem, vmem] + [vmem] * len(parts),
        out_specs=(vmem, vmem),
        scratch_shapes=[pltpu.VMEM(parts[0].shape, f32)],
        compiler_params=pltpu.CompilerParams(vmem_limit_bytes=SMALL),
        cost_estimate=small(32 << 20, 9 << 20),
        name="extra_fields",
    )(before, *near_memory(extra_fields, extra_noise), moments, *parts)


def finish(piece_count, before, block, *refs):
    pieces, (_, new_base, rows, sems) = refs[:piece_count], refs[piece_count:]
    _, depth, tiles, _ = rows.shape
    last = block.shape[0]
    flat = rows.reshape(6 * depth * tiles, LANES)
    copies = [pltpu.make_async_copy(block.at[i], new_base.at[0, 0, tiles - last + i], sems.at[i]) for i in range(last)]
    for copy in copies:
        copy.start()
    tile = 0
    for piece in pieces:
        for place in range(piece.shape[1]):
            for i in range(6):
                flat[pl.ds(i * depth * tiles + tile, depth, stride=tiles), :] = piece[i, place]
            tile += 1
    for copy in copies:
        copy.wait()


def call_finish(before, block, pieces, new_base):
    tiles, cells = new_base.shape[2], new_base.shape[-1]
    return pl.pallas_call(
        functools.partial(finish, len(pieces)),
        out_shape=(
            jax.ShapeDtypeStruct(new_base.shape, f32),
            jax.ShapeDtypeStruct((6, cells // LANES, tiles, LANES), f32),
        ),
        in_specs=[anywhere, vmem] + [vmem] * len(pieces) + [hbm],
        out_specs=(hbm, vmem),
        input_output_aliases={2 + len(pieces): 0},
        scratch_shapes=[pltpu.SemaphoreType.DMA((block.shape[0],))],
        compiler_params=pltpu.CompilerParams(vmem_limit_bytes=4 << 20),
        cost_estimate=small(1 << 10, 1 << 20),
        name="finish",
    )(before, *near_memory(block), *pieces, new_base)


def heavy(helper, base, noise, grad, near, far, ready, old_base, new_base, stress, fields, rows, answer, sems):
    _, _, tiles, _, count, cells = base.shape
    me = lax.axis_index("gy")
    depth = cells // LANES
    flat = rows.reshape(6 * depth * tiles, LANES)

    def store(k, tile):
        return pltpu.make_async_copy(fields.at[k], new_base.at[0, 0, tile], sems.at[k])

    def result(x):
        target = stress.at[0, 0, :, :, pl.ds(x * LANES, LANES)]
        return pltpu.make_async_copy(rows.at[:, x], target, sems.at[HEAVY_MOST + x])

    rows[...] = ready[...]
    places, order = owned_order(tiles, me, helper)
    for k, (h, tile) in enumerate(order):

        @pl.when(k < places)
        def _(k=k, h=h, tile=tile):
            flip = (me ^ h) >> 1
            is_far = ((me ^ h) & 1) == 1
            for i in range(near.shape[1]):
                answer[i] = jnp.where(is_far, far[flip, i], near[flip, i])

            def sums_of(x):
                lanes = pl.ds(x * LANES, LANES)
                g = tile_grad(grad, depth, tile, x)
                matrices = [with_diagonal(g, wide(answer[step, pl.ds(x, 1), :])) for step in range(2)]

                def read(a, part):
                    return base[0, 0, tile, a, part, lanes]

                def write(a, part, value):
                    fields[k, a, part, lanes] = value

                def shock(step, a, part):
                    return noise[0, 0, tile, step, a, part, lanes]

                return tile_sums(read, write, shock, matrices, count, add_moments, 6)

            sums = packed_sums(sums_of, depth)
            store(k, tile).start()
            sums = [s + answer[2 + i] for i, s in enumerate(sums)]
            for i, value in enumerate(stress_rows(sums, 1.0 / ALL_FIELDS)):
                flat[pl.ds(i * depth * tiles + tile, depth, stride=tiles), :] = value

    for x in range(depth):
        result(x).start()
    for k, (_, tile) in enumerate(order):

        @pl.when(k < places)
        def _(k=k, tile=tile):
            store(k, tile).wait()

    for x in range(depth):
        result(x).wait()


def call_heavy(helper_tile, base_fields, base_noise, grad, near, far, ready, new_base):
    _, _, tiles, _, count, cells = base_fields.shape
    depth = cells // LANES
    return pl.pallas_call(
        heavy,
        out_shape=(
            jax.ShapeDtypeStruct(new_base.shape, f32),
            jax.ShapeDtypeStruct((1, 1, 6, tiles, cells), f32),
        ),
        in_specs=[vmem] * 7 + [hbm],
        out_specs=(hbm, hbm),
        input_output_aliases={7: 0},
        scratch_shapes=[
            pltpu.VMEM((HEAVY_MOST, 3, count, cells), f32),
            pltpu.VMEM((6, depth, tiles, LANES), f32),
            pltpu.VMEM(near.shape[1:], f32),
            pltpu.SemaphoreType.DMA((HEAVY_MOST + depth,)),
        ],
        compiler_params=pltpu.CompilerParams(vmem_limit_bytes=SMALL),
        cost_estimate=small(8 << 20, 4 << 20),
        name="heavy_tiles",
    )(helper_tile, *near_memory(base_fields, base_noise), grad, near, far, ready, new_base)


def per_device(
    velocity, wall_cells, tile_counts, helper_tile, base_fields, extra_fields, base_noise, extra_noise
):
    tiles = tile_counts.shape[2]
    pairs = lax.axis_size("gy") // 2
    helper_tile, x_one, x_two, y_one, y_two = call_edges(helper_tile, velocity)
    y_two = swap_across(y_two, False)
    x_two = swap_across(x_two, True)
    x_one = swap_within(x_one, "gx")
    y_one = swap_within(y_one, "gy")
    halos = (y_two, x_two, x_one, y_one)
    moments = call_heavy_moments(helper_tile, base_fields, base_noise)
    grad, keep, send = call_gradients(tiles, helper_tile, velocity, halos, wall_cells, moments)
    some = tiles // 4
    ordinary_fields = (base_fields, base_noise, grad)
    received = swapped(send, 1)
    _, block, begun, _ = call_ordinary(0, some, 0, send, *ordinary_fields, None, None, None)
    before = begun
    keep, *sends = call_merge(before, keep, received)
    farthest_first = sorted(range(1, pairs), key=lambda flip: -flip.bit_count())
    parts = [keep] + [swapped(sends[flip - 1], 2 * flip) for flip in farthest_first]
    extra_sums = call_extra_moments(sends[0], extra_fields, extra_noise)
    extra_near, reply = call_extra(extra_sums, extra_fields, extra_noise, extra_sums, parts)
    replies = {flip: swapped(reply, 2 * flip) for flip in farthest_first}
    new_base, block, ended, new_extra = call_ordinary(
        some, tiles - some, tiles - 2 * some, reply, *ordinary_fields, block, None, extra_near
    )
    near = call_join(ended, [reply] + [replies[flip] for flip in range(1, pairs)])
    far = swapped(near, 1)
    new_base, ready = call_finish(near, block, (begun, ended), new_base)
    new_base, stress = call_heavy(helper_tile, base_fields, base_noise, grad, near, far, ready, new_base)
    return new_base, new_extra, jnp.swapaxes(stress, 2, 3)


def solution(mesh):
    in_specs = (
        P(None, "gx", "gy", None),
        P("gx", "gy", None),
        P("gx", "gy", None),
        P("gx", None),
        P("gx", "gy", None, None, None, None),
        P("gx", "gy", None, None, None),
        P("gx", "gy", None, None, None, None, None),
        P("gx", "gy", None, None, None, None),
    )
    out_specs = (
        P("gx", "gy", None, None, None, None),
        P("gx", "gy", None, None, None),
        P("gx", "gy", None, None, None),
    )
    return jax.shard_map(
        per_device, mesh=mesh, in_specs=in_specs, out_specs=out_specs, check_vma=False
    )
```

```python
import functools

import jax
import jax.numpy as jnp
from jax import lax
from jax.experimental import pallas as pl
from jax.experimental.pallas import tpu as pltpu
from jax.sharding import PartitionSpec as P

ALL_FIELDS = 256
HEAVY_MOST = 4
LANES = 128
SUB = 8
SMALL = 10 << 20

time_step = 0.05
weissenberg = 0.25
max_extension = 50.0
noise_scale = (time_step / weissenberg) ** 0.5
component_pairs = ((0, 0), (1, 1), (2, 2), (0, 1), (0, 2), (1, 2))
moment_of = {(0, 0): 0, (1, 1): 1, (2, 2): 2, (0, 1): 3, (1, 0): 3, (0, 2): 4, (2, 0): 4, (1, 2): 5, (2, 1): 5}
f32 = jnp.float32

vmem = pl.BlockSpec(memory_space=pltpu.VMEM)
hbm = pl.BlockSpec(memory_space=pltpu.HBM)
anywhere = pl.BlockSpec(memory_space=pl.ANY)


def far_memory(*arrays):
    return [pltpu.with_memory_space_constraint(array, pltpu.HBM) for array in arrays]


def near_memory(*arrays):
    return [pltpu.with_memory_space_constraint(array, pltpu.VMEM) for array in arrays]


def column_sum(value):
    return jnp.sum(value, axis=0, keepdims=True)


def interleaved(a, b, bit):
    low = (lax.broadcasted_iota(jnp.int32, (SUB, LANES), 0) & bit) == 0
    return jnp.where(low, a, b) + pltpu.roll(jnp.where(low, b, a), bit, 0)


def packed_sums(values_of, count):
    stack = []
    for x in range(count):
        bit, values = 1, values_of(x)
        while stack and stack[-1][0] == bit:
            values = [interleaved(a, b, bit) for a, b in zip(stack.pop()[1], values)]
            bit *= 2
        stack.append((bit, values))
    return stack[0][1]


def wide(row):
    return jnp.broadcast_to(row, (SUB, LANES))


def turned(value, cell_z):
    sub = lax.broadcasted_iota(jnp.int32, value.shape, 0)
    group = lax.broadcasted_iota(jnp.int32, value.shape, 1) // cell_z
    skewed = pltpu.roll(value, cell_z, 1, stride=cell_z, stride_axis=0)
    mixed = jnp.take_along_axis(skewed, (group + sub) & (SUB - 1), axis=0, mode="promise_in_bounds")
    return pltpu.roll(mixed, 0, 1, stride=cell_z, stride_axis=0)


def relax_of(total, inverse):
    factor = 1.0 / (1.0 - total * inverse / max_extension)
    return 1.0 - (time_step * 0.5 / weissenberg) * factor


def stepped(vectors, noise, matrix):
    return [
        matrix[3 * a] * vectors[0]
        + matrix[3 * a + 1] * vectors[1]
        + matrix[3 * a + 2] * vectors[2]
        + noise_scale * noise[a]
        for a in range(3)
    ]


def with_diagonal(grad, relax):
    return [g + relax if i % 4 == 0 else g for i, g in enumerate(grad)]


def noise_rows(ref, start):
    both = [ref(a, pl.ds(start, 2 * SUB)).astype(f32) for a in range(3)]
    return [[w[:SUB] for w in both], [w[SUB:] for w in both]]


def add_moments(sums, q):
    return [s + q[a] * q[b] for s, (a, b) in zip(sums, component_pairs)]


def product_sums(sums, q, w):
    terms = [q[a] * q[b] for a, b in component_pairs]
    terms += [q[a] * w[b] for a in range(3) for b in range(3)]
    terms += [w[0] * w[0] + w[1] * w[1] + w[2] * w[2]]
    return [s + t for s, t in zip(sums, terms)]


def coefficients(g, m):
    cross = lambda a, b: m[6 + 3 * a + b]
    square = lambda a, b: m[moment_of[a, b]]
    once, twice, kick = 0.0, 0.0, 0.0
    for a in range(3):
        for b in range(3):
            once += g[3 * a + b] * square(a, b)
            kick += g[3 * a + b] * cross(b, a)
            inner = 0.0
            for c in range(3):
                inner += g[3 * a + c] * square(b, c)
            twice += g[3 * a + b] * inner
    return [
        twice + (2 * noise_scale) * kick + noise_scale**2 * m[15],
        2.0 * once + (2 * noise_scale) * (cross(0, 0) + cross(1, 1) + cross(2, 2)),
        m[0] + m[1] + m[2],
    ]


def owned_slots(tiles, me, helper):
    found = []
    row = helper[...]
    for h in range(helper.shape[1]):
        tile = row[0, h] - me * tiles
        found.append((h, (tile >= 0) & (tile < tiles), tile))
    return found


def owned_order(tiles, me, helper, parities=(0, 1)):
    places = jnp.int32(0)
    order = [jnp.int32(0)] * HEAVY_MOST
    for h, owned, tile in owned_slots(tiles, me, helper):
        if len(parities) == 1:
            owned = owned & (((me ^ h) & 1) == parities[0])
        entry = h * tiles + tile
        order = [jnp.where(owned & (places == k), entry, kept) for k, kept in enumerate(order)]
        places = places + owned.astype(jnp.int32)
    return places, [(entry // tiles, entry % tiles) for entry in order]


def small(flops, traffic):
    return pl.CostEstimate(flops=flops, bytes_accessed=traffic, transcendentals=0)


def is_even(axis):
    return (lax.axis_index(axis) & 1) == 0


def edges(helper, velocity, helper_near, x_one, x_two, y_one, y_two):
    depth, width = velocity.shape[1:3]
    helper_near[...] = helper[...]
    even = is_even("gx")
    for a in range(3):
        first, last = velocity[a, 0], velocity[a, depth - 1]
        x_one[a] = jnp.where(even, last, first)
        x_two[a] = jnp.where(even, first, last)
    even = is_even("gy")
    for a in range(3):
        for x in range(depth):
            first, last = velocity[a, x, pl.ds(0, 1), :], velocity[a, x, pl.ds(width - 1, 1), :]
            y_one[a, pl.ds(x, 1), :] = jnp.where(even, last, first)
            y_two[a, pl.ds(x, 1), :] = jnp.where(even, first, last)


def call_edges(helper_tile, velocity):
    _, depth, width, length = velocity.shape
    along_x = jax.ShapeDtypeStruct((3, width, length), f32)
    along_y = jax.ShapeDtypeStruct((3, depth, length), f32)
    return pl.pallas_call(
        edges,
        out_shape=(jax.ShapeDtypeStruct(helper_tile.shape, jnp.int32), along_x, along_x, along_y, along_y),
        in_specs=[vmem, vmem],
        out_specs=(vmem,) * 5,
        compiler_params=pltpu.CompilerParams(vmem_limit_bytes=4 << 20),
        cost_estimate=small(1 << 10, 1 << 17),
        name="edges",
    )(*far_memory(helper_tile, velocity))


def swap_within(block, axis):
    return lax.ppermute(block, axis, [(i, i ^ 1) for i in range(lax.axis_size(axis))])


def swap_across(block, along_rows):
    rows, columns = lax.axis_size("gx"), lax.axis_size("gy")
    size = rows if along_rows else columns

    def partner(row, column):
        place = row if along_rows else column
        if place in (0, size - 1):
            row, column = (row, column ^ 1) if along_rows else (row ^ 1, column)
        else:
            place += 1 if place & 1 else -1
            row, column = (place, column) if along_rows else (row, place)
        return row * columns + column

    places = [(row, column) for row in range(rows) for column in range(columns)]
    return lax.ppermute(block, ("gx", "gy"), [(i, partner(*place)) for i, place in enumerate(places)])


def low_and_high(axis, one, two, a):
    even, place = is_even(axis), lax.axis_index(axis)
    low = jnp.where(even, two[a], one[a])
    high = jnp.where(even, one[a], two[a])
    return jnp.where(place == 0, 0.0, low), jnp.where(place == lax.axis_size(axis) - 1, 0.0, high)


def heavy_moments(helper, base, noise, out, fields, shocks, sems):
    _, _, count, cells = fields.shape
    tiles = base.shape[2]
    me = lax.axis_index("gy")

    def loads(k, tile):
        return (
            pltpu.make_async_copy(base.at[0, 0, tile], fields.at[k], sems.at[0, k]),
            pltpu.make_async_copy(noise.at[0, 0, tile, 0], shocks.at[k], sems.at[1, k]),
        )

    places, order = owned_order(tiles, me, helper)
    for k, (_, tile) in enumerate(order):

        @pl.when(k < places)
        def _(k=k, tile=tile):
            for copy in loads(k, tile):
                copy.start()

    for k, (h, tile) in enumerate(order):

        @pl.when(k < places)
        def _(k=k, h=h, tile=tile):
            for copy in loads(k, tile):
                copy.wait()

            def sums_of(x):
                lanes = pl.ds(x * LANES, LANES)
                sums = [jnp.zeros((SUB, LANES), f32)] * 16
                for group in range(count // (2 * SUB)):
                    pair = noise_rows(lambda a, rows: shocks[k, a, rows, lanes], group * 2 * SUB)
                    for half in range(2):
                        rows = pl.ds((2 * group + half) * SUB, SUB)
                        sums = product_sums(sums, [fields[k, a, rows, lanes] for a in range(3)], pair[half])
                return sums

            for i, value in enumerate(packed_sums(sums_of, cells // LANES)):
                out[h, i] = value


def call_heavy_moments(helper_tile, base_fields, base_noise):
    slots = helper_tile.shape[1]
    count, cells = base_fields.shape[-2:]
    return pl.pallas_call(
        heavy_moments,
        out_shape=jax.ShapeDtypeStruct((slots, 16, cells // LANES, LANES), f32),
        in_specs=[vmem, hbm, hbm],
        out_specs=vmem,
        scratch_shapes=[
            pltpu.VMEM((HEAVY_MOST, 3, count, cells), f32),
            pltpu.VMEM((HEAVY_MOST, 3, count, cells), jnp.bfloat16),
            pltpu.SemaphoreType.DMA((2, HEAVY_MOST)),
        ],
        compiler_params=pltpu.CompilerParams(vmem_limit_bytes=SMALL),
        cost_estimate=small(8 << 20, 3 << 20),
        name="heavy_moments",
    )(helper_tile, *far_memory(base_fields, base_noise))


def extra_moments(unroll, before, base, noise, out, partial):
    _, _, _, count, cells = base.shape
    zero = jnp.zeros((SUB, LANES), f32)

    @pl.loop(0, cells // LANES)
    def _(x):
        lanes = pl.ds(pl.multiple_of(x * LANES, LANES), LANES)

        def body(i, sums):
            start = pl.multiple_of(i * 2 * SUB, 2 * SUB)
            pair = noise_rows(lambda a, rows: noise[0, 0, 0, a, rows, lanes], start)
            for half in range(2):
                rows = pl.ds(start + half * SUB, SUB)
                sums = product_sums(sums, [base[0, 0, a, rows, lanes] for a in range(3)], pair[half])
            return sums

        for i, s in enumerate(lax.fori_loop(0, count // (2 * SUB), body, [zero] * 16, unroll=unroll)):
            partial[i, x] = s

    for i, s in enumerate(packed_sums(lambda x: [partial[i, x] for i in range(16)], cells // LANES)):
        out[i] = s


def call_extra_moments(before, extra_fields, extra_noise):
    cells = extra_fields.shape[-1]
    return pl.pallas_call(
        functools.partial(extra_moments, 7),
        out_shape=jax.ShapeDtypeStruct((16, cells // LANES, LANES), f32),
        in_specs=[anywhere, vmem, vmem],
        out_specs=vmem,
        scratch_shapes=[pltpu.VMEM((16, cells // LANES, SUB, LANES), f32)],
        compiler_params=pltpu.CompilerParams(vmem_limit_bytes=SMALL),
        cost_estimate=small(8 << 20, 5 << 20),
        name="extra_moments",
    )(before, *near_memory(extra_fields, extra_noise))


def gradients(tiles, helper, velocity, y_two, x_two, x_one, y_one, wall, moments, grad, keep, send):
    me = lax.axis_index("gy")
    depth = velocity.shape[1]
    cell_z = velocity.shape[3] // tiles
    sub = lax.broadcasted_iota(jnp.int32, (SUB, LANES), 0)
    lane = lax.broadcasted_iota(jnp.int32, (SUB, LANES), 1)
    z = lane % cell_z
    scales = [turned(jnp.where(wall[x] == 0, 0.5 * time_step, 0.0).astype(f32), cell_z) for x in range(depth)]
    for a in range(3):
        x_low, x_high = low_and_high("gx", x_one, x_two, a)
        y_low, y_high = low_and_high("gy", y_one, y_two, a)
        rows = [x_low] + [velocity[a, x] for x in range(depth)] + [x_high]
        rows = [turned(row, cell_z) for row in rows]
        low, high = turned(y_low, cell_z), turned(y_high, cell_z)
        for x in range(depth):
            here = rows[x + 1]
            above = high if x == depth - 1 else pltpu.roll(high, LANES - cell_z * (x + 1), 1)
            below = low if x == 0 else pltpu.roll(low, LANES - cell_z * x, 1)
            y_up = jnp.where(lane < LANES - cell_z, pltpu.roll(here, LANES - cell_z, 1), above)
            y_down = jnp.where(lane >= cell_z, pltpu.roll(here, cell_z, 1), below)
            next_tile = pltpu.roll(pltpu.roll(here, cell_z - 1, 1), 1, 0)
            last_tile = pltpu.roll(pltpu.roll(here, LANES - cell_z + 1, 1), SUB - 1, 0)
            next_tile = jnp.where(sub == 0, 0.0, next_tile)
            last_tile = jnp.where(sub == SUB - 1, 0.0, last_tile)
            z_up = jnp.where(z == cell_z - 1, next_tile, pltpu.roll(here, LANES - 1, 1))
            z_down = jnp.where(z == 0, last_tile, pltpu.roll(here, 1, 1))
            for b, difference in enumerate((rows[x + 2] - rows[x], y_up - y_down, z_up - z_down)):
                grad[pl.ds(((3 * a + b) * depth + x) * SUB, SUB), :] = difference * scales[x]
    keep[...] = jnp.zeros(keep.shape, f32)
    send[...] = jnp.zeros(send.shape, f32)
    for h, owned, tile in owned_slots(tiles, me, helper):

        @pl.when(owned)
        def _(h=h, tile=tile):
            g = [grad[pl.ds(i * depth * SUB + SUB - 1 - tile, depth, stride=SUB), :] for i in range(9)]
            rows = g + coefficients(g, [moments[h, i] for i in range(16)])
            stays = (me & 1) == (h & 1)

            @pl.when(stays)
            def _():
                for i, row in enumerate(rows):
                    keep[h >> 1, i] = row

            @pl.when(jnp.logical_not(stays))
            def _():
                for i, row in enumerate(rows):
                    send[h >> 1, i] = row


def call_gradients(tiles, helper_tile, velocity, halos, wall_cells, moments):
    slots = helper_tile.shape[1]
    depth = velocity.shape[1]
    half = jax.ShapeDtypeStruct((slots // 2, 12, depth, LANES), f32)
    return pl.pallas_call(
        functools.partial(gradients, tiles),
        out_shape=(jax.ShapeDtypeStruct((9 * depth * SUB, LANES), f32), half, half),
        in_specs=[vmem] * 8,
        out_specs=(vmem,) * 3,
        compiler_params=pltpu.CompilerParams(vmem_limit_bytes=8 << 20),
        cost_estimate=small(4 << 20, 1 << 20),
        name="gradients",
    )(helper_tile, velocity, *halos, wall_cells, moments)


def swapped(block, flip):
    size = lax.axis_size("gy")
    return lax.ppermute(block, "gy", [(i, i ^ flip) for i in range(size)])


def merge(before, kept, received, keep, *sends):
    pair = lax.axis_index("gy") >> 1
    for flip, out in enumerate((keep,) + sends):
        out[...] = kept[pair ^ flip] + received[pair ^ flip]


def call_merge(before, kept, received):
    one = jax.ShapeDtypeStruct(kept.shape[1:], f32)
    return pl.pallas_call(
        merge,
        out_shape=(one,) * kept.shape[0],
        in_specs=[anywhere, vmem, vmem],
        out_specs=(vmem,) * kept.shape[0],
        compiler_params=pltpu.CompilerParams(vmem_limit_bytes=4 << 20),
        cost_estimate=small(1 << 10, 1 << 18),
        name="merge",
    )(before, kept, received)


def join(before, *refs):
    for i, ref in enumerate(refs[:-1]):
        refs[-1][i] = ref[...]


def call_join(before, blocks):
    return pl.pallas_call(
        join,
        out_shape=jax.ShapeDtypeStruct((len(blocks),) + blocks[0].shape, f32),
        in_specs=[anywhere] + [vmem] * len(blocks),
        out_specs=vmem,
        compiler_params=pltpu.CompilerParams(vmem_limit_bytes=4 << 20),
        cost_estimate=small(1 << 10, 1 << 18),
        name="join",
    )(before, *blocks)


def stress_rows(sums, inverse):
    second = [s * inverse for s in sums]
    stretch = 1.0 / (1.0 - (second[0] + second[1] + second[2]) / max_extension)
    return [(stretch * s - (1.0 if i < 3 else 0.0)) * (1.0 / weissenberg) for i, s in enumerate(second)]


def tile_grad(grad, depth, tile, x):
    return [wide(grad[pl.ds((i * depth + x + 1) * SUB - 1 - tile, 1), :]) for i in range(9)]


def tile_sums(read, write, noise, matrices, count, add, many):
    sums = [jnp.zeros((SUB, LANES), f32)] * many
    for group in range(count // (2 * SUB)):
        pairs = [noise_rows(functools.partial(noise, step), group * 2 * SUB) for step in range(len(matrices))]
        for half in range(2):
            rows = pl.ds((2 * group + half) * SUB, SUB)
            q = [read(a, rows) for a in range(3)]
            for step, matrix in enumerate(matrices):
                q = stepped(q, pairs[step][half], matrix)
            for a in range(3):
                write(a, rows, q[a])
            sums = add(sums, q)
    return sums


def add_square(sums, q):
    return [sums[0] + (q[0] * q[0] + q[1] * q[1] + q[2] * q[2])]


def ordinary(first, direct, has_block, has_base, has_extra, *refs):
    refs = list(refs)
    before, base, noise, grad = refs[:4]
    del refs[:4]
    block = refs.pop(0) if has_block else None
    if has_base:
        refs.pop(0)
    extra_near = refs.pop(0) if has_extra else None
    new_base = refs.pop(0) if has_block or direct else None
    new_extra = refs.pop(0) if has_extra else None
    fields, stress, early, halfway, relaxes, sems = refs
    _, _, count, cells = fields.shape
    here = direct + fields.shape[0]
    depth = cells // LANES
    inverse = 1.0 / count
    copies = []
    if has_block:
        last = block.shape[0]
        copies += [
            pltpu.make_async_copy(block.at[i], new_base.at[0, 0, first - last + i], sems.at[i]) for i in range(last)
        ]
    if has_extra:
        copies += [
            pltpu.make_async_copy(extra_near.at[0, 0, a], new_extra.at[0, 0, a], sems.at[len(copies) + a])
            for a in range(3)
        ]
    for copy in copies:
        copy.start()
    for place in range(here):
        tile = first + place

        def squares(x):
            total = jnp.zeros((SUB, LANES), f32)
            for group in range(count // SUB):
                for a in range(3):
                    q = base[0, 0, tile, a, pl.ds(group * SUB, SUB), pl.ds(x * LANES, LANES)]
                    total = total + q * q
            return [total]

        sums = packed_sums(squares, depth)
        for step in range(2):
            relaxes[place, step] = relax_of(sums[0], inverse)

            def sums_of(x):
                lanes = pl.ds(x * LANES, LANES)
                matrix = with_diagonal(tile_grad(grad, depth, tile, x), wide(relaxes[place, step, pl.ds(x, 1), :]))

                def read(a, rows):
                    return base[0, 0, tile, a, rows, lanes] if step == 0 else halfway[place, a, rows, lanes]

                def write(a, rows, value):
                    if step == 0:
                        halfway[place, a, rows, lanes] = value
                    elif place < direct:
                        early[place, a, rows, lanes] = value
                    else:
                        fields[place - direct, a, rows, lanes] = value

                def shock(_, a, rows):
                    return noise[0, 0, tile, step, a, rows, lanes]

                if step == 0:
                    return tile_sums(read, write, shock, [matrix], count, add_square, 1)
                return tile_sums(read, write, shock, [matrix], count, add_moments, 6)

            sums = packed_sums(sums_of, depth)
        if place < direct:
            copies.append(pltpu.make_async_copy(early.at[place], new_base.at[0, 0, tile], sems.at[len(copies)]))
            copies[-1].start()
        for i, row in enumerate(stress_rows(sums, inverse)):
            stress[i, place] = row
    for copy in copies:
        copy.wait()


def call_ordinary(first, here, direct, before, base_fields, base_noise, grad, block, new_base, new_extra):
    count, cells = base_fields.shape[-2:]
    depth = cells // LANES
    has_block, has_base, has_extra = block is not None, new_base is not None, new_extra is not None
    operands = [before, *near_memory(base_fields, base_noise), grad]
    specs = [anywhere, vmem, vmem, vmem]
    shapes, out_specs, aliases = [], [], {}
    copies = 0
    if has_block:
        operands += near_memory(block)
        specs.append(vmem)
        copies += block.shape[0]
    if has_block or direct:
        copies += direct
        shapes.append(jax.ShapeDtypeStruct(base_fields.shape, f32))
        out_specs.append(hbm)
    if has_base:
        aliases[len(operands)] = 0
        operands.append(new_base)
        specs.append(hbm)
    if has_extra:
        operands += near_memory(new_extra)
        specs.append(vmem)
        shapes.append(jax.ShapeDtypeStruct(new_extra.shape, f32))
        out_specs.append(hbm)
        copies += 3
    shapes += [
        pltpu.VMEM((here - direct, 3, count, cells), f32),
        jax.ShapeDtypeStruct((6, here, depth, LANES), f32),
    ]
    out_specs += [vmem, vmem]
    results = pl.pallas_call(
        functools.partial(ordinary, first, direct, has_block, has_base, has_extra),
        out_shape=tuple(shapes),
        in_specs=specs,
        out_specs=tuple(out_specs),
        input_output_aliases=aliases,
        scratch_shapes=[
            pltpu.VMEM((max(direct, 1), 3, count, cells), f32),
            pltpu.VMEM((here, 3, count, cells), f32),
            pltpu.VMEM((here, 2, depth, LANES), f32),
            pltpu.SemaphoreType.DMA((max(copies, 1),)),
        ],
        compiler_params=pltpu.CompilerParams(vmem_limit_bytes=SMALL),
        cost_estimate=small(8 << 20, 3 << 20),
        name="ordinary_tiles",
    )(*operands)
    results = list(results)
    piece, block = results.pop(), results.pop()
    new_base = results.pop(0) if has_block or direct else None
    return new_base, block, piece, (results[0] if has_extra else None)


def extra(unroll, before, base, noise, moments, *refs):
    *parts, new_fields, reply, message, partial = refs
    _, _, _, count, cells = base.shape
    inverse = 1.0 / float(ALL_FIELDS)
    zero = jnp.zeros((SUB, LANES), f32)
    message[...] = sum(part[...] for part in parts)
    own = coefficients([message[i] for i in range(9)], [moments[i] for i in range(16)])
    both = [message[9 + i] + own[i] for i in range(3)]
    first = relax_of(both[2], inverse)
    second = relax_of(both[0] + first * (both[1] + first * both[2]), inverse)
    reply[0], reply[1] = first, second

    @pl.loop(0, cells // LANES)
    def _(x):
        lanes = pl.ds(pl.multiple_of(x * LANES, LANES), LANES)
        grad = [wide(message[i, pl.ds(x, 1), :]) for i in range(9)]
        matrices = [with_diagonal(grad, wide(reply[step, pl.ds(x, 1), :])) for step in range(2)]

        def body(i, sums):
            start = pl.multiple_of(i * 2 * SUB, 2 * SUB)
            pairs = [noise_rows(lambda a, rows: noise[0, 0, step, a, rows, lanes], start) for step in range(2)]
            for half in range(2):
                rows = pl.ds(start + half * SUB, SUB)
                q = [base[0, 0, a, rows, lanes] for a in range(3)]
                for step in range(2):
                    q = stepped(q, pairs[step][half], matrices[step])
                for a in range(3):
                    new_fields[0, 0, a, rows, lanes] = q[a]
                sums = add_moments(sums, q)
            return sums

        for i, s in enumerate(lax.fori_loop(0, count // (2 * SUB), body, [zero] * 6, unroll=unroll)):
            partial[i, x] = s

    for i, s in enumerate(packed_sums(lambda x: [partial[i, x] for i in range(6)], cells // LANES)):
        reply[2 + i] = s


def call_extra(before, extra_fields, extra_noise, moments, parts):
    depth = extra_fields.shape[-1] // LANES
    return pl.pallas_call(
        functools.partial(extra, 7),
        out_shape=(
            pltpu.VMEM(extra_fields.shape, f32),
            jax.ShapeDtypeStruct((8, depth, LANES), f32),
        ),
        in_specs=[anywhere, vmem, vmem, vmem] + [vmem] * len(parts),
        out_specs=(vmem, vmem),
        scratch_shapes=[pltpu.VMEM(parts[0].shape, f32), pltpu.VMEM((6, depth, SUB, LANES), f32)],
        compiler_params=pltpu.CompilerParams(vmem_limit_bytes=SMALL),
        cost_estimate=small(32 << 20, 9 << 20),
        name="extra_fields",
    )(before, *near_memory(extra_fields, extra_noise), moments, *parts)


def heavy(parity, helper, base, noise, grad, replies, new_base, rows, fields, answer, sems):
    _, _, tiles, _, count, cells = base.shape
    me = lax.axis_index("gy")
    depth = cells // LANES
    flat = rows.reshape(6 * depth * tiles, LANES)

    def store(k, tile):
        return pltpu.make_async_copy(fields.at[k], new_base.at[0, 0, tile], sems.at[k])

    places, order = owned_order(tiles, me, helper, (parity,))
    for k, (h, tile) in enumerate(order):

        @pl.when(k < places)
        def _(k=k, h=h, tile=tile):
            answer[...] = replies[(me ^ h) >> 1]

            def sums_of(x):
                lanes = pl.ds(x * LANES, LANES)
                g = tile_grad(grad, depth, tile, x)
                matrices = [with_diagonal(g, wide(answer[step, pl.ds(x, 1), :])) for step in range(2)]

                def read(a, part):
                    return base[0, 0, tile, a, part, lanes]

                def write(a, part, value):
                    fields[k, a, part, lanes] = value

                def shock(step, a, part):
                    return noise[0, 0, tile, step, a, part, lanes]

                return tile_sums(read, write, shock, matrices, count, add_moments, 6)

            sums = packed_sums(sums_of, depth)
            store(k, tile).start()
            sums = [s + answer[2 + i] for i, s in enumerate(sums)]
            for i, value in enumerate(stress_rows(sums, 1.0 / ALL_FIELDS)):
                flat[pl.ds(i * depth * tiles + tile, depth, stride=tiles), :] = value

    def wait():
        for k, (_, tile) in enumerate(order):

            @pl.when(k < places)
            def _(k=k, tile=tile):
                store(k, tile).wait()

    return wait


def heavy_scratch(near, held):
    return [pltpu.VMEM((HEAVY_MOST,) + held, f32), pltpu.VMEM(near.shape[1:], f32)]


def finish(piece_count, helper, base, noise, grad, near, block, *refs):
    pieces, (_, new_base, rows, fields, answer, sems) = refs[:piece_count], refs[piece_count:]
    _, depth, tiles, _ = rows.shape
    last = block.shape[0]
    flat = rows.reshape(6 * depth * tiles, LANES)
    me = lax.axis_index("gy")
    named = [jnp.bool_(False)] * last
    for _, owned, tile in owned_slots(tiles, me, helper):
        named = [n | (owned & (tile == tiles - last + i)) for i, n in enumerate(named)]
    copies = [
        pltpu.make_async_copy(block.at[i], new_base.at[0, 0, tiles - last + i], sems.at[HEAVY_MOST + i])
        for i in range(last)
    ]
    for copy, is_heavy in zip(copies, named):
        pl.when(jnp.logical_not(is_heavy))(copy.start)
    tile = 0
    for piece in pieces:
        for place in range(piece.shape[1]):
            for i in range(6):
                flat[pl.ds(i * depth * tiles + tile, depth, stride=tiles), :] = piece[i, place]
            tile += 1
    wait = heavy(0, helper, base, noise, grad, near, new_base, rows, fields, answer, sems)
    wait()
    for copy, is_heavy in zip(copies, named):
        pl.when(jnp.logical_not(is_heavy))(copy.wait)


def call_finish(helper_tile, base_fields, base_noise, grad, near, block, pieces, new_base):
    tiles, cells = new_base.shape[2], new_base.shape[-1]
    return pl.pallas_call(
        functools.partial(finish, len(pieces)),
        out_shape=(
            jax.ShapeDtypeStruct(new_base.shape, f32),
            jax.ShapeDtypeStruct((6, cells // LANES, tiles, LANES), f32),
        ),
        in_specs=[vmem] * (6 + len(pieces)) + [hbm],
        out_specs=(hbm, vmem),
        input_output_aliases={6 + len(pieces): 0},
        scratch_shapes=heavy_scratch(near, block.shape[1:])
        + [pltpu.SemaphoreType.DMA((HEAVY_MOST + block.shape[0],))],
        compiler_params=pltpu.CompilerParams(vmem_limit_bytes=SMALL),
        cost_estimate=small(1 << 10, 1 << 20),
        name="finish",
    )(helper_tile, *near_memory(base_fields, base_noise), grad, near, *near_memory(block), *pieces, new_base)


def final(helper, base, noise, grad, far, ready, old_base, new_base, stress, rows, fields, answer, sems):
    depth = rows.shape[1]

    def result(x):
        target = stress.at[0, 0, :, :, pl.ds(x * LANES, LANES)]
        return pltpu.make_async_copy(rows.at[:, x], target, sems.at[HEAVY_MOST + x])

    rows[...] = ready[...]
    wait = heavy(1, helper, base, noise, grad, far, new_base, rows, fields, answer, sems)
    for x in range(depth):
        result(x).start()
    wait()
    for x in range(depth):
        result(x).wait()


def call_final(helper_tile, base_fields, base_noise, grad, far, ready, new_base):
    _, _, tiles, _, count, cells = base_fields.shape
    depth = cells // LANES
    return pl.pallas_call(
        final,
        out_shape=(
            jax.ShapeDtypeStruct(new_base.shape, f32),
            jax.ShapeDtypeStruct((1, 1, 6, tiles, cells), f32),
        ),
        in_specs=[vmem] * 6 + [hbm],
        out_specs=(hbm, hbm),
        input_output_aliases={6: 0},
        scratch_shapes=[pltpu.VMEM((6, depth, tiles, LANES), f32)]
        + heavy_scratch(far, (3, count, cells))
        + [pltpu.SemaphoreType.DMA((HEAVY_MOST + depth,))],
        compiler_params=pltpu.CompilerParams(vmem_limit_bytes=SMALL),
        cost_estimate=small(8 << 20, 4 << 20),
        name="heavy_tiles",
    )(helper_tile, *near_memory(base_fields, base_noise), grad, far, ready, new_base)


def per_device(
    velocity, wall_cells, tile_counts, helper_tile, base_fields, extra_fields, base_noise, extra_noise
):
    tiles = tile_counts.shape[2]
    pairs = lax.axis_size("gy") // 2
    helper_tile, x_one, x_two, y_one, y_two = call_edges(helper_tile, velocity)
    y_two = swap_across(y_two, False)
    x_two = swap_across(x_two, True)
    x_one = swap_within(x_one, "gx")
    y_one = swap_within(y_one, "gy")
    halos = (y_two, x_two, x_one, y_one)
    moments = call_heavy_moments(helper_tile, base_fields, base_noise)
    grad, keep, send = call_gradients(tiles, helper_tile, velocity, halos, wall_cells, moments)
    some = tiles // 4
    ordinary_fields = (base_fields, base_noise, grad)
    received = swapped(send, 1)
    _, block, begun, _ = call_ordinary(0, some, 0, send, *ordinary_fields, None, None, None)
    before = begun
    keep, *sends = call_merge(before, keep, received)
    farthest_first = sorted(range(1, pairs), key=lambda flip: -flip.bit_count())
    parts = [keep] + [swapped(sends[flip - 1], 2 * flip) for flip in farthest_first]
    extra_sums = call_extra_moments(sends[0], extra_fields, extra_noise)
    extra_near, reply = call_extra(extra_sums, extra_fields, extra_noise, extra_sums, parts)
    replies = {flip: swapped(reply, 2 * flip) for flip in farthest_first}
    new_base, block, ended, new_extra = call_ordinary(
        some, tiles - some, tiles - 2 * some, reply, *ordinary_fields, block, None, extra_near
    )
    near = call_join(ended, [reply] + [replies[flip] for flip in range(1, pairs)])
    far = swapped(near, 1)
    given = (helper_tile, base_fields, base_noise, grad)
    new_base, ready = call_finish(*given, near, block, (begun, ended), new_base)
    new_base, stress = call_final(*given, far, ready, new_base)
    return new_base, new_extra, jnp.swapaxes(stress, 2, 3)


def solution(mesh):
    in_specs = (
        P(None, "gx", "gy", None),
        P("gx", "gy", None),
        P("gx", "gy", None),
        P("gx", None),
        P("gx", "gy", None, None, None, None),
        P("gx", "gy", None, None, None),
        P("gx", "gy", None, None, None, None, None),
        P("gx", "gy", None, None, None, None),
    )
    out_specs = (
        P("gx", "gy", None, None, None, None),
        P("gx", "gy", None, None, None),
        P("gx", "gy", None, None, None),
    )
    return jax.shard_map(
        per_device, mesh=mesh, in_specs=in_specs, out_specs=out_specs, check_vma=False
    )
```

```python
import functools

import jax
import jax.numpy as jnp
from jax import lax
from jax.experimental import pallas as pl
from jax.experimental.pallas import tpu as pltpu
from jax.sharding import PartitionSpec as P

ALL_FIELDS = 256
HEAVY_MOST = 4
LANES = 128
SUB = 8
SMALL = 12 << 20

time_step = 0.05
weissenberg = 0.25
max_extension = 50.0
noise_scale = (time_step / weissenberg) ** 0.5
component_pairs = ((0, 0), (1, 1), (2, 2), (0, 1), (0, 2), (1, 2))
moment_of = {(0, 0): 0, (1, 1): 1, (2, 2): 2, (0, 1): 3, (1, 0): 3, (0, 2): 4, (2, 0): 4, (1, 2): 5, (2, 1): 5}
f32 = jnp.float32

vmem = pl.BlockSpec(memory_space=pltpu.VMEM)
hbm = pl.BlockSpec(memory_space=pltpu.HBM)
anywhere = pl.BlockSpec(memory_space=pl.ANY)


def far_memory(*arrays):
    return [pltpu.with_memory_space_constraint(array, pltpu.HBM) for array in arrays]


def near_memory(*arrays):
    return [pltpu.with_memory_space_constraint(array, pltpu.VMEM) for array in arrays]


def column_sum(value):
    return jnp.sum(value, axis=0, keepdims=True)


def interleaved(a, b, bit):
    low = (lax.broadcasted_iota(jnp.int32, (SUB, LANES), 0) & bit) == 0
    return jnp.where(low, a, b) + pltpu.roll(jnp.where(low, b, a), bit, 0)


def packed_sums(values_of, count):
    stack = []
    for x in range(count):
        bit, values = 1, values_of(x)
        while stack and stack[-1][0] == bit:
            values = [interleaved(a, b, bit) for a, b in zip(stack.pop()[1], values)]
            bit *= 2
        stack.append((bit, values))
    return stack[0][1]


def wide(row):
    return jnp.broadcast_to(row, (SUB, LANES))


def turned(value, cell_z):
    sub = lax.broadcasted_iota(jnp.int32, value.shape, 0)
    group = lax.broadcasted_iota(jnp.int32, value.shape, 1) // cell_z
    skewed = pltpu.roll(value, cell_z, 1, stride=cell_z, stride_axis=0)
    mixed = jnp.take_along_axis(skewed, (group + sub) & (SUB - 1), axis=0, mode="promise_in_bounds")
    return pltpu.roll(mixed, 0, 1, stride=cell_z, stride_axis=0)


def relax_of(total, inverse):
    factor = 1.0 / (1.0 - total * inverse / max_extension)
    return 1.0 - (time_step * 0.5 / weissenberg) * factor


def stepped(vectors, noise, matrix):
    return [
        matrix[3 * a] * vectors[0]
        + matrix[3 * a + 1] * vectors[1]
        + matrix[3 * a + 2] * vectors[2]
        + noise_scale * noise[a]
        for a in range(3)
    ]


def with_diagonal(grad, relax):
    return [g + relax if i % 4 == 0 else g for i, g in enumerate(grad)]


def noise_rows(ref, start):
    both = [ref(a, pl.ds(start, 2 * SUB)).astype(f32) for a in range(3)]
    return [[w[:SUB] for w in both], [w[SUB:] for w in both]]


def add_moments(sums, q):
    return [s + q[a] * q[b] for s, (a, b) in zip(sums, component_pairs)]


def product_sums(sums, q, w):
    terms = [q[a] * q[b] for a, b in component_pairs]
    terms += [q[a] * w[b] for a in range(3) for b in range(3)]
    terms += [w[0] * w[0] + w[1] * w[1] + w[2] * w[2]]
    return [s + t for s, t in zip(sums, terms)]


def coefficients(g, m):
    cross = lambda a, b: m[6 + 3 * a + b]
    square = lambda a, b: m[moment_of[a, b]]
    once, twice, kick = 0.0, 0.0, 0.0
    for a in range(3):
        for b in range(3):
            once += g[3 * a + b] * square(a, b)
            kick += g[3 * a + b] * cross(b, a)
            inner = 0.0
            for c in range(3):
                inner += g[3 * a + c] * square(b, c)
            twice += g[3 * a + b] * inner
    return [
        twice + (2 * noise_scale) * kick + noise_scale**2 * m[15],
        2.0 * once + (2 * noise_scale) * (cross(0, 0) + cross(1, 1) + cross(2, 2)),
        m[0] + m[1] + m[2],
    ]


def owned_slots(tiles, me, helper):
    found = []
    row = helper[...]
    for h in range(helper.shape[1]):
        tile = row[0, h] - me * tiles
        found.append((h, (tile >= 0) & (tile < tiles), tile))
    return found


def owned_order(tiles, me, helper, parities=(0, 1)):
    places = jnp.int32(0)
    order = [jnp.int32(0)] * HEAVY_MOST
    for h, owned, tile in owned_slots(tiles, me, helper):
        if len(parities) == 1:
            owned = owned & (((me ^ h) & 1) == parities[0])
        entry = h * tiles + tile
        order = [jnp.where(owned & (places == k), entry, kept) for k, kept in enumerate(order)]
        places = places + owned.astype(jnp.int32)
    return places, [(entry // tiles, entry % tiles) for entry in order]


def small(flops, traffic):
    return pl.CostEstimate(flops=flops, bytes_accessed=traffic, transcendentals=0)


def is_even(axis):
    return (lax.axis_index(axis) & 1) == 0


def edges(helper, velocity, helper_near, x_one, x_two, y_one, y_two):
    depth, width = velocity.shape[1:3]
    helper_near[...] = helper[...]
    even = is_even("gx")
    for a in range(3):
        first, last = velocity[a, 0], velocity[a, depth - 1]
        x_one[a] = jnp.where(even, last, first)
        x_two[a] = jnp.where(even, first, last)
    even = is_even("gy")
    for a in range(3):
        for x in range(depth):
            first, last = velocity[a, x, pl.ds(0, 1), :], velocity[a, x, pl.ds(width - 1, 1), :]
            y_one[a, pl.ds(x, 1), :] = jnp.where(even, last, first)
            y_two[a, pl.ds(x, 1), :] = jnp.where(even, first, last)


def call_edges(helper_tile, velocity):
    _, depth, width, length = velocity.shape
    along_x = jax.ShapeDtypeStruct((3, width, length), f32)
    along_y = jax.ShapeDtypeStruct((3, depth, length), f32)
    return pl.pallas_call(
        edges,
        out_shape=(jax.ShapeDtypeStruct(helper_tile.shape, jnp.int32), along_x, along_x, along_y, along_y),
        in_specs=[vmem, vmem],
        out_specs=(vmem,) * 5,
        compiler_params=pltpu.CompilerParams(vmem_limit_bytes=4 << 20),
        cost_estimate=small(1 << 10, 1 << 17),
        name="edges",
    )(*far_memory(helper_tile, velocity))


def swap_within(block, axis):
    return lax.ppermute(block, axis, [(i, i ^ 1) for i in range(lax.axis_size(axis))])


def swap_across(block, along_rows):
    rows, columns = lax.axis_size("gx"), lax.axis_size("gy")
    size = rows if along_rows else columns

    def partner(row, column):
        place = row if along_rows else column
        if place in (0, size - 1):
            row, column = (row, column ^ 1) if along_rows else (row ^ 1, column)
        else:
            place += 1 if place & 1 else -1
            row, column = (place, column) if along_rows else (row, place)
        return row * columns + column

    places = [(row, column) for row in range(rows) for column in range(columns)]
    return lax.ppermute(block, ("gx", "gy"), [(i, partner(*place)) for i, place in enumerate(places)])


def low_and_high(axis, one, two, a):
    even, place = is_even(axis), lax.axis_index(axis)
    low = jnp.where(even, two[a], one[a])
    high = jnp.where(even, one[a], two[a])
    return jnp.where(place == 0, 0.0, low), jnp.where(place == lax.axis_size(axis) - 1, 0.0, high)


def heavy_moments(helper, base, noise, out, fields, shocks, sems):
    _, _, count, cells = fields.shape
    tiles = base.shape[2]
    me = lax.axis_index("gy")

    def loads(k, tile):
        return (
            pltpu.make_async_copy(base.at[0, 0, tile], fields.at[k], sems.at[0, k]),
            pltpu.make_async_copy(noise.at[0, 0, tile, 0], shocks.at[k], sems.at[1, k]),
        )

    places, order = owned_order(tiles, me, helper)
    for k, (_, tile) in enumerate(order):

        @pl.when(k < places)
        def _(k=k, tile=tile):
            for copy in loads(k, tile):
                copy.start()

    for k, (h, tile) in enumerate(order):

        @pl.when(k < places)
        def _(k=k, h=h, tile=tile):
            for copy in loads(k, tile):
                copy.wait()

            def sums_of(x):
                lanes = pl.ds(x * LANES, LANES)
                sums = [jnp.zeros((SUB, LANES), f32)] * 16
                for group in range(count // (2 * SUB)):
                    pair = noise_rows(lambda a, rows: shocks[k, a, rows, lanes], group * 2 * SUB)
                    for half in range(2):
                        rows = pl.ds((2 * group + half) * SUB, SUB)
                        sums = product_sums(sums, [fields[k, a, rows, lanes] for a in range(3)], pair[half])
                return sums

            for i, value in enumerate(packed_sums(sums_of, cells // LANES)):
                out[h, i] = value


def call_heavy_moments(helper_tile, base_fields, base_noise):
    slots = helper_tile.shape[1]
    count, cells = base_fields.shape[-2:]
    return pl.pallas_call(
        heavy_moments,
        out_shape=jax.ShapeDtypeStruct((slots, 16, cells // LANES, LANES), f32),
        in_specs=[vmem, hbm, hbm],
        out_specs=vmem,
        scratch_shapes=[
            pltpu.VMEM((HEAVY_MOST, 3, count, cells), f32),
            pltpu.VMEM((HEAVY_MOST, 3, count, cells), jnp.bfloat16),
            pltpu.SemaphoreType.DMA((2, HEAVY_MOST)),
        ],
        compiler_params=pltpu.CompilerParams(vmem_limit_bytes=SMALL),
        cost_estimate=small(8 << 20, 3 << 20),
        name="heavy_moments",
    )(helper_tile, *far_memory(base_fields, base_noise))


def outer_sums(sums, left, right):
    return [s + left[a] * right[b] for s, (a, b) in zip(sums, [(a, b) for a in range(3) for b in range(3)])]


def extra_moments(unroll, before, base, noise, out, partial):
    _, _, _, count, cells = base.shape
    zero = jnp.zeros((SUB, LANES), f32)

    @pl.loop(0, cells // LANES)
    def _(x):
        lanes = pl.ds(pl.multiple_of(x * LANES, LANES), LANES)

        def body(steps, i, sums):
            start = pl.multiple_of(i * 2 * SUB, 2 * SUB)
            pairs = [noise_rows(lambda a, rows: noise[0, 0, step, a, rows, lanes], start) for step in range(steps)]
            for half in range(2):
                q = [base[0, 0, a, pl.ds(start + half * SUB, SUB), lanes] for a in range(3)]
                w = [pair[half] for pair in pairs]
                if steps == 1:
                    sums = add_moments(sums[:6], q) + outer_sums(sums[6:15], q, w[0]) + add_moments(sums[15:], w[0])
                else:
                    sums = outer_sums(sums[:9], q, w[1]) + outer_sums(sums[9:18], *w) + add_moments(sums[18:], w[1])
            return sums

        at = 0
        for steps, many in ((1, 21), (2, 24)):
            loop = functools.partial(body, steps)
            for i, s in enumerate(lax.fori_loop(0, count // (2 * SUB), loop, [zero] * many, unroll=unroll)):
                partial[at + i, x] = s
            at += many

    for i in range(45):
        out[i] = packed_sums(lambda x: [partial[i, x]], cells // LANES)[0]


def call_extra_moments(before, extra_fields, extra_noise):
    cells = extra_fields.shape[-1]
    return pl.pallas_call(
        functools.partial(extra_moments, 7),
        out_shape=jax.ShapeDtypeStruct((45, cells // LANES, LANES), f32),
        in_specs=[anywhere, vmem, vmem],
        out_specs=vmem,
        scratch_shapes=[pltpu.VMEM((45, cells // LANES, SUB, LANES), f32)],
        compiler_params=pltpu.CompilerParams(vmem_limit_bytes=SMALL),
        cost_estimate=small(8 << 20, 5 << 20),
        name="extra_moments",
    )(before, *near_memory(extra_fields, extra_noise))


def gradients(tiles, helper, velocity, y_two, x_two, x_one, y_one, wall, moments, grad, keep, send):
    me = lax.axis_index("gy")
    depth = velocity.shape[1]
    cell_z = velocity.shape[3] // tiles
    sub = lax.broadcasted_iota(jnp.int32, (SUB, LANES), 0)
    lane = lax.broadcasted_iota(jnp.int32, (SUB, LANES), 1)
    z = lane % cell_z
    scales = [turned(jnp.where(wall[x] == 0, 0.5 * time_step, 0.0).astype(f32), cell_z) for x in range(depth)]
    for a in range(3):
        x_low, x_high = low_and_high("gx", x_one, x_two, a)
        y_low, y_high = low_and_high("gy", y_one, y_two, a)
        rows = [x_low] + [velocity[a, x] for x in range(depth)] + [x_high]
        rows = [turned(row, cell_z) for row in rows]
        low, high = turned(y_low, cell_z), turned(y_high, cell_z)
        for x in range(depth):
            here = rows[x + 1]
            above = high if x == depth - 1 else pltpu.roll(high, LANES - cell_z * (x + 1), 1)
            below = low if x == 0 else pltpu.roll(low, LANES - cell_z * x, 1)
            y_up = jnp.where(lane < LANES - cell_z, pltpu.roll(here, LANES - cell_z, 1), above)
            y_down = jnp.where(lane >= cell_z, pltpu.roll(here, cell_z, 1), below)
            next_tile = pltpu.roll(pltpu.roll(here, cell_z - 1, 1), 1, 0)
            last_tile = pltpu.roll(pltpu.roll(here, LANES - cell_z + 1, 1), SUB - 1, 0)
            next_tile = jnp.where(sub == 0, 0.0, next_tile)
            last_tile = jnp.where(sub == SUB - 1, 0.0, last_tile)
            z_up = jnp.where(z == cell_z - 1, next_tile, pltpu.roll(here, LANES - 1, 1))
            z_down = jnp.where(z == 0, last_tile, pltpu.roll(here, 1, 1))
            for b, difference in enumerate((rows[x + 2] - rows[x], y_up - y_down, z_up - z_down)):
                grad[pl.ds(((3 * a + b) * depth + x) * SUB, SUB), :] = difference * scales[x]
    keep[...] = jnp.zeros(keep.shape, f32)
    send[...] = jnp.zeros(send.shape, f32)
    for h, owned, tile in owned_slots(tiles, me, helper):

        @pl.when(owned)
        def _(h=h, tile=tile):
            g = [grad[pl.ds(i * depth * SUB + SUB - 1 - tile, depth, stride=SUB), :] for i in range(9)]
            rows = g + coefficients(g, [moments[h, i] for i in range(16)])
            stays = (me & 1) == (h & 1)

            @pl.when(stays)
            def _():
                for i, row in enumerate(rows):
                    keep[h >> 1, i] = row

            @pl.when(jnp.logical_not(stays))
            def _():
                for i, row in enumerate(rows):
                    send[h >> 1, i] = row


def call_gradients(tiles, helper_tile, velocity, halos, wall_cells, moments):
    slots = helper_tile.shape[1]
    depth = velocity.shape[1]
    half = jax.ShapeDtypeStruct((slots // 2, 12, depth, LANES), f32)
    return pl.pallas_call(
        functools.partial(gradients, tiles),
        out_shape=(jax.ShapeDtypeStruct((9 * depth * SUB, LANES), f32), half, half),
        in_specs=[vmem] * 8,
        out_specs=(vmem,) * 3,
        compiler_params=pltpu.CompilerParams(vmem_limit_bytes=8 << 20),
        cost_estimate=small(4 << 20, 1 << 20),
        name="gradients",
    )(helper_tile, velocity, *halos, wall_cells, moments)


def swapped(block, flip):
    size = lax.axis_size("gy")
    return lax.ppermute(block, "gy", [(i, i ^ flip) for i in range(size)])


def merge(before, kept, received, keep, *sends):
    pair = lax.axis_index("gy") >> 1
    for flip, out in enumerate((keep,) + sends):
        out[...] = kept[pair ^ flip] + received[pair ^ flip]


def call_merge(before, kept, received):
    one = jax.ShapeDtypeStruct(kept.shape[1:], f32)
    return pl.pallas_call(
        merge,
        out_shape=(one,) * kept.shape[0],
        in_specs=[anywhere, vmem, vmem],
        out_specs=(vmem,) * kept.shape[0],
        compiler_params=pltpu.CompilerParams(vmem_limit_bytes=4 << 20),
        cost_estimate=small(1 << 10, 1 << 18),
        name="merge",
    )(before, kept, received)


def join(before, *refs):
    for i, ref in enumerate(refs[:-1]):
        refs[-1][i] = ref[...]


def call_join(before, blocks):
    return pl.pallas_call(
        join,
        out_shape=jax.ShapeDtypeStruct((len(blocks),) + blocks[0].shape, f32),
        in_specs=[anywhere] + [vmem] * len(blocks),
        out_specs=vmem,
        compiler_params=pltpu.CompilerParams(vmem_limit_bytes=4 << 20),
        cost_estimate=small(1 << 10, 1 << 18),
        name="join",
    )(before, *blocks)


def stress_rows(sums, inverse):
    second = [s * inverse for s in sums]
    stretch = 1.0 / (1.0 - (second[0] + second[1] + second[2]) / max_extension)
    return [(stretch * s - (1.0 if i < 3 else 0.0)) * (1.0 / weissenberg) for i, s in enumerate(second)]


def tile_grad(grad, depth, tile, x):
    return [wide(grad[pl.ds((i * depth + x + 1) * SUB - 1 - tile, 1), :]) for i in range(9)]


def tile_sums(read, write, noise, matrices, count, add, many):
    sums = [jnp.zeros((SUB, LANES), f32)] * many
    for group in range(count // (2 * SUB)):
        pairs = [noise_rows(functools.partial(noise, step), group * 2 * SUB) for step in range(len(matrices))]
        for half in range(2):
            rows = pl.ds((2 * group + half) * SUB, SUB)
            q = [read(a, rows) for a in range(3)]
            for step, matrix in enumerate(matrices):
                q = stepped(q, pairs[step][half], matrix)
            for a in range(3):
                write(a, rows, q[a])
            sums = add(sums, q)
    return sums


def add_square(sums, q):
    return [sums[0] + (q[0] * q[0] + q[1] * q[1] + q[2] * q[2])]


def ordinary(first, direct, has_block, has_base, has_extra, *refs):
    refs = list(refs)
    before, base, noise, grad = refs[:4]
    del refs[:4]
    block = refs.pop(0) if has_block else None
    if has_base:
        refs.pop(0)
    extra, extra_noise, drive = [refs.pop(0) for _ in range(3)] if has_extra else [None] * 3
    new_base = refs.pop(0) if has_block or direct else None
    new_extra = refs.pop(0) if has_extra else None
    fields, stress, early, halfway, relaxes, advanced, sems = refs
    _, _, count, cells = fields.shape
    here = direct + fields.shape[0]
    depth = cells // LANES
    inverse = 1.0 / count
    copies = []
    if has_block:
        last = block.shape[0]
        copies += [
            pltpu.make_async_copy(block.at[i], new_base.at[0, 0, first - last + i], sems.at[i]) for i in range(last)
        ]
    for copy in copies:
        copy.start()
    if has_extra:
        at = len(copies)

        def leave(x):
            lanes = pl.ds(x * LANES, LANES)
            return pltpu.make_async_copy(advanced.at[:, :, lanes], new_extra.at[0, 0, :, :, lanes], sems.at[at + x])

        @pl.loop(0, depth)
        def _(x):
            lanes = pl.ds(pl.multiple_of(x * LANES, LANES), LANES)
            rows_of = [wide(drive[i, pl.ds(x, 1), :]) for i in range(11)]
            matrices = [with_diagonal(rows_of[:9], rows_of[9 + step]) for step in range(2)]

            def body(i, carry):
                start = pl.multiple_of(i * 2 * SUB, 2 * SUB)
                pairs = [
                    noise_rows(lambda a, rows: extra_noise[0, 0, step, a, rows, lanes], start) for step in range(2)
                ]
                for half in range(2):
                    rows = pl.ds(start + half * SUB, SUB)
                    q = [extra[0, 0, a, rows, lanes] for a in range(3)]
                    for step in range(2):
                        q = stepped(q, pairs[step][half], matrices[step])
                    for a in range(3):
                        advanced[a, rows, lanes] = q[a]
                return carry

            lax.fori_loop(0, extra.shape[3] // (2 * SUB), body, 0, unroll=7)
            leave(x).start()

        copies += [leave(x) for x in range(depth)]
    for place in range(here):
        tile = first + place

        def squares(x):
            total = jnp.zeros((SUB, LANES), f32)
            for group in range(count // SUB):
                for a in range(3):
                    q = base[0, 0, tile, a, pl.ds(group * SUB, SUB), pl.ds(x * LANES, LANES)]
                    total = total + q * q
            return [total]

        sums = packed_sums(squares, depth)
        for step in range(2):
            relaxes[place, step] = relax_of(sums[0], inverse)

            def sums_of(x):
                lanes = pl.ds(x * LANES, LANES)
                matrix = with_diagonal(tile_grad(grad, depth, tile, x), wide(relaxes[place, step, pl.ds(x, 1), :]))

                def read(a, rows):
                    return base[0, 0, tile, a, rows, lanes] if step == 0 else halfway[place, a, rows, lanes]

                def write(a, rows, value):
                    if step == 0:
                        halfway[place, a, rows, lanes] = value
                    elif place < direct:
                        early[place, a, rows, lanes] = value
                    else:
                        fields[place - direct, a, rows, lanes] = value

                def shock(_, a, rows):
                    return noise[0, 0, tile, step, a, rows, lanes]

                if step == 0:
                    return tile_sums(read, write, shock, [matrix], count, add_square, 1)
                return tile_sums(read, write, shock, [matrix], count, add_moments, 6)

            sums = packed_sums(sums_of, depth)
        if place < direct:
            copies.append(pltpu.make_async_copy(early.at[place], new_base.at[0, 0, tile], sems.at[len(copies)]))
            copies[-1].start()
        for i, row in enumerate(stress_rows(sums, inverse)):
            stress[i, place] = row
    for copy in copies:
        copy.wait()


def call_ordinary(first, here, direct, before, base_fields, base_noise, grad, block, new_base, extra):
    count, cells = base_fields.shape[-2:]
    depth = cells // LANES
    has_block, has_base, has_extra = block is not None, new_base is not None, extra is not None
    operands = [before, *near_memory(base_fields, base_noise), grad]
    specs = [anywhere, vmem, vmem, vmem]
    shapes, out_specs, aliases = [], [], {}
    copies = 0
    if has_block:
        operands += near_memory(block)
        specs.append(vmem)
        copies += block.shape[0]
    if has_block or direct:
        copies += direct
        shapes.append(jax.ShapeDtypeStruct(base_fields.shape, f32))
        out_specs.append(hbm)
    if has_base:
        aliases[len(operands)] = 0
        operands.append(new_base)
        specs.append(hbm)
    if has_extra:
        operands += near_memory(*extra[:2]) + [extra[2]]
        specs += [vmem] * 3
        shapes.append(jax.ShapeDtypeStruct(extra[0].shape, f32))
        out_specs.append(hbm)
        copies += depth
    shapes += [
        pltpu.VMEM((here - direct, 3, count, cells), f32),
        jax.ShapeDtypeStruct((6, here, depth, LANES), f32),
    ]
    out_specs += [vmem, vmem]
    results = pl.pallas_call(
        functools.partial(ordinary, first, direct, has_block, has_base, has_extra),
        out_shape=tuple(shapes),
        in_specs=specs,
        out_specs=tuple(out_specs),
        input_output_aliases=aliases,
        scratch_shapes=[
            pltpu.VMEM((max(direct, 1), 3, count, cells), f32),
            pltpu.VMEM((here, 3, count, cells), f32),
            pltpu.VMEM((here, 2, depth, LANES), f32),
            pltpu.VMEM(extra[0].shape[2:] if has_extra else (SUB, LANES), f32),
            pltpu.SemaphoreType.DMA((max(copies, 1),)),
        ],
        compiler_params=pltpu.CompilerParams(vmem_limit_bytes=SMALL),
        cost_estimate=small(8 << 20, 3 << 20),
        name="ordinary_tiles",
    )(*operands)
    results = list(results)
    piece, block = results.pop(), results.pop()
    new_base = results.pop(0) if has_block or direct else None
    return new_base, block, piece, (results[0] if has_extra else None)


def moments_after(g, first, second, m):
    one, two = with_diagonal(g, first), with_diagonal(g, second)
    both = [[sum(two[3 * a + k] * one[3 * k + b] for k in range(3)) for b in range(3)] for a in range(3)]
    kick = [[noise_scale * two[3 * a + b] for b in range(3)] for a in range(3)]

    def mixed(of_q, of_w):
        return [
            [sum(both[a][i] * of_q(i, j) for i in range(3)) + sum(kick[a][i] * of_w(i, j) for i in range(3)) for j in range(3)]
            for a in range(3)
        ]

    with_q = mixed(lambda i, j: m[moment_of[i, j]], lambda i, j: m[6 + 3 * j + i])
    with_one = mixed(lambda i, j: m[6 + 3 * i + j], lambda i, j: m[15 + moment_of[i, j]])
    with_two = mixed(lambda i, j: m[21 + 3 * i + j], lambda i, j: m[30 + 3 * i + j])
    return [
        sum(with_q[a][j] * both[b][j] + with_one[a][j] * kick[b][j] for j in range(3))
        + noise_scale * (with_two[a][b] + with_two[b][a])
        + noise_scale**2 * m[39 + i]
        for i, (a, b) in enumerate(component_pairs)
    ]


def answering(moments, *refs):
    *parts, reply, drive = refs
    inverse = 1.0 / float(ALL_FIELDS)
    message = [sum(part[i] for part in parts) for i in range(12)]
    grad, m = message[:9], [moments[i] for i in range(45)]
    own = coefficients(grad, m[:15] + [m[15] + m[16] + m[17]])
    both = [message[9 + i] + own[i] for i in range(3)]
    first = relax_of(both[2], inverse)
    second = relax_of(both[0] + first * (both[1] + first * both[2]), inverse)
    for i, value in enumerate([first, second] + moments_after(grad, first, second, m)):
        reply[i] = value
    for i, value in enumerate(grad + [first, second]):
        drive[i] = value


def call_answering(moments, parts):
    depth = moments.shape[1]
    return pl.pallas_call(
        answering,
        out_shape=(
            jax.ShapeDtypeStruct((8, depth, LANES), f32),
            jax.ShapeDtypeStruct((11, depth, LANES), f32),
        ),
        in_specs=[vmem] * (1 + len(parts)),
        out_specs=(vmem, vmem),
        compiler_params=pltpu.CompilerParams(vmem_limit_bytes=4 << 20),
        cost_estimate=small(1 << 20, 1 << 19),
        name="answering",
    )(moments, *parts)


def heavy(parity, helper, base, noise, grad, replies, new_base, rows, fields, answer, sems):
    _, _, tiles, _, count, cells = base.shape
    me = lax.axis_index("gy")
    depth = cells // LANES
    flat = rows.reshape(6 * depth * tiles, LANES)

    def store(k, tile):
        return pltpu.make_async_copy(fields.at[k], new_base.at[0, 0, tile], sems.at[k])

    places, order = owned_order(tiles, me, helper, (parity,))
    for k, (h, tile) in enumerate(order):

        @pl.when(k < places)
        def _(k=k, h=h, tile=tile):
            answer[...] = replies[(me ^ h) >> 1]

            def sums_of(x):
                lanes = pl.ds(x * LANES, LANES)
                g = tile_grad(grad, depth, tile, x)
                matrices = [with_diagonal(g, wide(answer[step, pl.ds(x, 1), :])) for step in range(2)]

                def read(a, part):
                    return base[0, 0, tile, a, part, lanes]

                def write(a, part, value):
                    fields[k, a, part, lanes] = value

                def shock(step, a, part):
                    return noise[0, 0, tile, step, a, part, lanes]

                return tile_sums(read, write, shock, matrices, count, add_moments, 6)

            sums = packed_sums(sums_of, depth)
            store(k, tile).start()
            sums = [s + answer[2 + i] for i, s in enumerate(sums)]
            for i, value in enumerate(stress_rows(sums, 1.0 / ALL_FIELDS)):
                flat[pl.ds(i * depth * tiles + tile, depth, stride=tiles), :] = value

    def wait():
        for k, (_, tile) in enumerate(order):

            @pl.when(k < places)
            def _(k=k, tile=tile):
                store(k, tile).wait()

    return wait


def heavy_scratch(near, held):
    return [pltpu.VMEM((HEAVY_MOST,) + held, f32), pltpu.VMEM(near.shape[1:], f32)]


def finish(piece_count, helper, base, noise, grad, near, block, *refs):
    pieces, (_, new_base, rows, fields, answer, sems) = refs[:piece_count], refs[piece_count:]
    _, depth, tiles, _ = rows.shape
    last = block.shape[0]
    flat = rows.reshape(6 * depth * tiles, LANES)
    me = lax.axis_index("gy")
    named = [jnp.bool_(False)] * last
    for _, owned, tile in owned_slots(tiles, me, helper):
        named = [n | (owned & (tile == tiles - last + i)) for i, n in enumerate(named)]
    copies = [
        pltpu.make_async_copy(block.at[i], new_base.at[0, 0, tiles - last + i], sems.at[HEAVY_MOST + i])
        for i in range(last)
    ]
    for copy, is_heavy in zip(copies, named):
        pl.when(jnp.logical_not(is_heavy))(copy.start)
    tile = 0
    for piece in pieces:
        for place in range(piece.shape[1]):
            for i in range(6):
                flat[pl.ds(i * depth * tiles + tile, depth, stride=tiles), :] = piece[i, place]
            tile += 1
    wait = heavy(0, helper, base, noise, grad, near, new_base, rows, fields, answer, sems)
    wait()
    for copy, is_heavy in zip(copies, named):
        pl.when(jnp.logical_not(is_heavy))(copy.wait)


def call_finish(helper_tile, base_fields, base_noise, grad, near, block, pieces, new_base):
    tiles, cells = new_base.shape[2], new_base.shape[-1]
    return pl.pallas_call(
        functools.partial(finish, len(pieces)),
        out_shape=(
            jax.ShapeDtypeStruct(new_base.shape, f32),
            jax.ShapeDtypeStruct((6, cells // LANES, tiles, LANES), f32),
        ),
        in_specs=[vmem] * (6 + len(pieces)) + [hbm],
        out_specs=(hbm, vmem),
        input_output_aliases={6 + len(pieces): 0},
        scratch_shapes=heavy_scratch(near, block.shape[1:])
        + [pltpu.SemaphoreType.DMA((HEAVY_MOST + block.shape[0],))],
        compiler_params=pltpu.CompilerParams(vmem_limit_bytes=SMALL),
        cost_estimate=small(1 << 10, 1 << 20),
        name="finish",
    )(helper_tile, *near_memory(base_fields, base_noise), grad, near, *near_memory(block), *pieces, new_base)


def final(helper, base, noise, grad, far, ready, old_base, new_base, stress, rows, fields, answer, sems):
    depth = rows.shape[1]

    def result(x):
        target = stress.at[0, 0, :, :, pl.ds(x * LANES, LANES)]
        return pltpu.make_async_copy(rows.at[:, x], target, sems.at[HEAVY_MOST + x])

    rows[...] = ready[...]
    wait = heavy(1, helper, base, noise, grad, far, new_base, rows, fields, answer, sems)
    for x in range(depth):
        result(x).start()
    wait()
    for x in range(depth):
        result(x).wait()


def call_final(helper_tile, base_fields, base_noise, grad, far, ready, new_base):
    _, _, tiles, _, count, cells = base_fields.shape
    depth = cells // LANES
    return pl.pallas_call(
        final,
        out_shape=(
            jax.ShapeDtypeStruct(new_base.shape, f32),
            jax.ShapeDtypeStruct((1, 1, 6, tiles, cells), f32),
        ),
        in_specs=[vmem] * 6 + [hbm],
        out_specs=(hbm, hbm),
        input_output_aliases={6: 0},
        scratch_shapes=[pltpu.VMEM((6, depth, tiles, LANES), f32)]
        + heavy_scratch(far, (3, count, cells))
        + [pltpu.SemaphoreType.DMA((HEAVY_MOST + depth,))],
        compiler_params=pltpu.CompilerParams(vmem_limit_bytes=SMALL),
        cost_estimate=small(8 << 20, 4 << 20),
        name="heavy_tiles",
    )(helper_tile, *near_memory(base_fields, base_noise), grad, far, ready, new_base)


def per_device(
    velocity, wall_cells, tile_counts, helper_tile, base_fields, extra_fields, base_noise, extra_noise
):
    tiles = tile_counts.shape[2]
    pairs = lax.axis_size("gy") // 2
    helper_tile, x_one, x_two, y_one, y_two = call_edges(helper_tile, velocity)
    y_two = swap_across(y_two, False)
    x_two = swap_across(x_two, True)
    x_one = swap_within(x_one, "gx")
    y_one = swap_within(y_one, "gy")
    halos = (y_two, x_two, x_one, y_one)
    moments = call_heavy_moments(helper_tile, base_fields, base_noise)
    grad, keep, send = call_gradients(tiles, helper_tile, velocity, halos, wall_cells, moments)
    some = 3 * tiles // 8
    ordinary_fields = (base_fields, base_noise, grad)
    received = swapped(send, 1)
    _, block, begun, _ = call_ordinary(0, some, 0, send, *ordinary_fields, None, None, None)
    keep, *sends = call_merge(begun, keep, received)
    farthest_first = sorted(range(1, pairs), key=lambda flip: -flip.bit_count())
    parts = [keep] + [swapped(sends[flip - 1], 2 * flip) for flip in farthest_first]
    extra_sums = call_extra_moments(sends[0], extra_fields, extra_noise)
    reply, drive = call_answering(extra_sums, parts)
    replies = {flip: swapped(reply, 2 * flip) for flip in farthest_first}
    new_base, block, ended, new_extra = call_ordinary(
        some, tiles - some, tiles - some - 2, reply, *ordinary_fields, block, None, (extra_fields, extra_noise, drive)
    )
    near = call_join(ended, [reply] + [replies[flip] for flip in range(1, pairs)])
    far = swapped(near, 1)
    given = (helper_tile, base_fields, base_noise, grad)
    new_base, ready = call_finish(*given, near, block, (begun, ended), new_base)
    new_base, stress = call_final(*given, far, ready, new_base)
    return new_base, new_extra, jnp.swapaxes(stress, 2, 3)


def solution(mesh):
    in_specs = (
        P(None, "gx", "gy", None),
        P("gx", "gy", None),
        P("gx", "gy", None),
        P("gx", None),
        P("gx", "gy", None, None, None, None),
        P("gx", "gy", None, None, None),
        P("gx", "gy", None, None, None, None, None),
        P("gx", "gy", None, None, None, None),
    )
    out_specs = (
        P("gx", "gy", None, None, None, None),
        P("gx", "gy", None, None, None),
        P("gx", "gy", None, None, None),
    )
    return jax.shard_map(
        per_device, mesh=mesh, in_specs=in_specs, out_specs=out_specs, check_vma=False
    )
```

```python
import functools

import jax
import jax.numpy as jnp
from jax import lax
from jax.experimental import pallas as pl
from jax.experimental.pallas import tpu as pltpu
from jax.sharding import PartitionSpec as P

ALL_FIELDS = 256
HEAVY_MOST = 4
LANES = 128
SUB = 8
SMALL = 12 << 20

time_step = 0.05
weissenberg = 0.25
max_extension = 50.0
noise_scale = (time_step / weissenberg) ** 0.5
component_pairs = ((0, 0), (1, 1), (2, 2), (0, 1), (0, 2), (1, 2))
moment_of = {(0, 0): 0, (1, 1): 1, (2, 2): 2, (0, 1): 3, (1, 0): 3, (0, 2): 4, (2, 0): 4, (1, 2): 5, (2, 1): 5}
f32 = jnp.float32

vmem = pl.BlockSpec(memory_space=pltpu.VMEM)
hbm = pl.BlockSpec(memory_space=pltpu.HBM)
anywhere = pl.BlockSpec(memory_space=pl.ANY)


def far_memory(*arrays):
    return [pltpu.with_memory_space_constraint(array, pltpu.HBM) for array in arrays]


def near_memory(*arrays):
    return [pltpu.with_memory_space_constraint(array, pltpu.VMEM) for array in arrays]


def column_sum(value):
    return jnp.sum(value, axis=0, keepdims=True)


def interleaved(a, b, bit):
    low = (lax.broadcasted_iota(jnp.int32, (SUB, LANES), 0) & bit) == 0
    return jnp.where(low, a, b) + pltpu.roll(jnp.where(low, b, a), bit, 0)


def packed_sums(values_of, count):
    stack = []
    for x in range(count):
        bit, values = 1, values_of(x)
        while stack and stack[-1][0] == bit:
            values = [interleaved(a, b, bit) for a, b in zip(stack.pop()[1], values)]
            bit *= 2
        stack.append((bit, values))
    return stack[0][1]


def wide(row):
    return jnp.broadcast_to(row, (SUB, LANES))


def turned(value, cell_z):
    sub = lax.broadcasted_iota(jnp.int32, value.shape, 0)
    group = lax.broadcasted_iota(jnp.int32, value.shape, 1) // cell_z
    skewed = pltpu.roll(value, cell_z, 1, stride=cell_z, stride_axis=0)
    mixed = jnp.take_along_axis(skewed, (group + sub) & (SUB - 1), axis=0, mode="promise_in_bounds")
    return pltpu.roll(mixed, 0, 1, stride=cell_z, stride_axis=0)


def relax_of(total, inverse):
    factor = 1.0 / (1.0 - total * inverse / max_extension)
    return 1.0 - (time_step * 0.5 / weissenberg) * factor


def stepped(vectors, noise, matrix):
    return [
        matrix[3 * a] * vectors[0]
        + matrix[3 * a + 1] * vectors[1]
        + matrix[3 * a + 2] * vectors[2]
        + noise_scale * noise[a]
        for a in range(3)
    ]


def with_diagonal(grad, relax):
    return [g + relax if i % 4 == 0 else g for i, g in enumerate(grad)]


def noise_rows(ref, start):
    both = [ref(a, pl.ds(start, 2 * SUB)).astype(f32) for a in range(3)]
    return [[w[:SUB] for w in both], [w[SUB:] for w in both]]


def add_moments(sums, q):
    return [s + q[a] * q[b] for s, (a, b) in zip(sums, component_pairs)]


def product_sums(sums, q, w):
    terms = [q[a] * q[b] for a, b in component_pairs]
    terms += [q[a] * w[b] for a in range(3) for b in range(3)]
    terms += [w[0] * w[0] + w[1] * w[1] + w[2] * w[2]]
    return [s + t for s, t in zip(sums, terms)]


def coefficients(g, m):
    cross = lambda a, b: m[6 + 3 * a + b]
    square = lambda a, b: m[moment_of[a, b]]
    once, twice, kick = 0.0, 0.0, 0.0
    for a in range(3):
        for b in range(3):
            once += g[3 * a + b] * square(a, b)
            kick += g[3 * a + b] * cross(b, a)
            inner = 0.0
            for c in range(3):
                inner += g[3 * a + c] * square(b, c)
            twice += g[3 * a + b] * inner
    return [
        twice + (2 * noise_scale) * kick + noise_scale**2 * m[15],
        2.0 * once + (2 * noise_scale) * (cross(0, 0) + cross(1, 1) + cross(2, 2)),
        m[0] + m[1] + m[2],
    ]


def owned_slots(tiles, me, helper):
    found = []
    row = helper[...]
    for h in range(helper.shape[1]):
        tile = row[0, h] - me * tiles
        found.append((h, (tile >= 0) & (tile < tiles), tile))
    return found


def owned_order(tiles, me, helper, parities=(0, 1)):
    places = jnp.int32(0)
    order = [jnp.int32(0)] * HEAVY_MOST
    for h, owned, tile in owned_slots(tiles, me, helper):
        if len(parities) == 1:
            owned = owned & (((me ^ h) & 1) == parities[0])
        entry = h * tiles + tile
        order = [jnp.where(owned & (places == k), entry, kept) for k, kept in enumerate(order)]
        places = places + owned.astype(jnp.int32)
    return places, [(entry // tiles, entry % tiles) for entry in order]


def small(flops, traffic):
    return pl.CostEstimate(flops=flops, bytes_accessed=traffic, transcendentals=0)


def is_even(axis):
    return (lax.axis_index(axis) & 1) == 0


def edges(helper, velocity, helper_near, x_one, x_two, y_one, y_two):
    depth, width = velocity.shape[1:3]
    helper_near[...] = helper[...]
    even = is_even("gx")
    for a in range(3):
        first, last = velocity[a, 0], velocity[a, depth - 1]
        x_one[a] = jnp.where(even, last, first)
        x_two[a] = jnp.where(even, first, last)
    even = is_even("gy")
    for a in range(3):
        for x in range(depth):
            first, last = velocity[a, x, pl.ds(0, 1), :], velocity[a, x, pl.ds(width - 1, 1), :]
            y_one[a, pl.ds(x, 1), :] = jnp.where(even, last, first)
            y_two[a, pl.ds(x, 1), :] = jnp.where(even, first, last)


def call_edges(helper_tile, velocity):
    _, depth, width, length = velocity.shape
    along_x = jax.ShapeDtypeStruct((3, width, length), f32)
    along_y = jax.ShapeDtypeStruct((3, depth, length), f32)
    return pl.pallas_call(
        edges,
        out_shape=(jax.ShapeDtypeStruct(helper_tile.shape, jnp.int32), along_x, along_x, along_y, along_y),
        in_specs=[vmem, vmem],
        out_specs=(vmem,) * 5,
        compiler_params=pltpu.CompilerParams(vmem_limit_bytes=4 << 20),
        cost_estimate=small(1 << 10, 1 << 17),
        name="edges",
    )(*far_memory(helper_tile, velocity))


def swap_within(block, axis):
    return lax.ppermute(block, axis, [(i, i ^ 1) for i in range(lax.axis_size(axis))])


def swap_across(block, along_rows):
    rows, columns = lax.axis_size("gx"), lax.axis_size("gy")
    size = rows if along_rows else columns

    def partner(row, column):
        place = row if along_rows else column
        if place in (0, size - 1):
            row, column = (row, column ^ 1) if along_rows else (row ^ 1, column)
        else:
            place += 1 if place & 1 else -1
            row, column = (place, column) if along_rows else (row, place)
        return row * columns + column

    places = [(row, column) for row in range(rows) for column in range(columns)]
    return lax.ppermute(block, ("gx", "gy"), [(i, partner(*place)) for i, place in enumerate(places)])


def low_and_high(axis, one, two, a):
    even, place = is_even(axis), lax.axis_index(axis)
    low = jnp.where(even, two[a], one[a])
    high = jnp.where(even, one[a], two[a])
    return jnp.where(place == 0, 0.0, low), jnp.where(place == lax.axis_size(axis) - 1, 0.0, high)


def heavy_moments(helper, base, noise, out, fields, shocks, sems):
    _, _, count, cells = fields.shape
    tiles = base.shape[2]
    me = lax.axis_index("gy")

    def loads(k, tile):
        return (
            pltpu.make_async_copy(base.at[0, 0, tile], fields.at[k], sems.at[0, k]),
            pltpu.make_async_copy(noise.at[0, 0, tile, 0], shocks.at[k], sems.at[1, k]),
        )

    places, order = owned_order(tiles, me, helper)
    for k, (_, tile) in enumerate(order):

        @pl.when(k < places)
        def _(k=k, tile=tile):
            for copy in loads(k, tile):
                copy.start()

    for k, (h, tile) in enumerate(order):

        @pl.when(k < places)
        def _(k=k, h=h, tile=tile):
            for copy in loads(k, tile):
                copy.wait()

            def sums_of(x):
                lanes = pl.ds(x * LANES, LANES)
                sums = [jnp.zeros((SUB, LANES), f32)] * 16
                for group in range(count // (2 * SUB)):
                    pair = noise_rows(lambda a, rows: shocks[k, a, rows, lanes], group * 2 * SUB)
                    for half in range(2):
                        rows = pl.ds((2 * group + half) * SUB, SUB)
                        sums = product_sums(sums, [fields[k, a, rows, lanes] for a in range(3)], pair[half])
                return sums

            for i, value in enumerate(packed_sums(sums_of, cells // LANES)):
                out[h, i] = value


def call_heavy_moments(helper_tile, base_fields, base_noise):
    slots = helper_tile.shape[1]
    count, cells = base_fields.shape[-2:]
    return pl.pallas_call(
        heavy_moments,
        out_shape=jax.ShapeDtypeStruct((slots, 16, cells // LANES, LANES), f32),
        in_specs=[vmem, hbm, hbm],
        out_specs=vmem,
        scratch_shapes=[
            pltpu.VMEM((HEAVY_MOST, 3, count, cells), f32),
            pltpu.VMEM((HEAVY_MOST, 3, count, cells), jnp.bfloat16),
            pltpu.SemaphoreType.DMA((2, HEAVY_MOST)),
        ],
        compiler_params=pltpu.CompilerParams(vmem_limit_bytes=SMALL),
        cost_estimate=small(8 << 20, 3 << 20),
        name="heavy_moments",
    )(helper_tile, *far_memory(base_fields, base_noise))


def outer_sums(sums, left, right):
    return [s + left[a] * right[b] for s, (a, b) in zip(sums, [(a, b) for a in range(3) for b in range(3)])]


def extra_moments(steps, unroll, before, base, noise, out, partial):
    _, _, _, count, cells = base.shape
    many = out.shape[0]

    @pl.loop(0, cells // LANES)
    def _(x):
        lanes = pl.ds(pl.multiple_of(x * LANES, LANES), LANES)

        def body(i, sums):
            start = pl.multiple_of(i * 2 * SUB, 2 * SUB)
            pairs = [noise_rows(lambda a, rows: noise[0, 0, step, a, rows, lanes], start) for step in range(steps)]
            for half in range(2):
                q = [base[0, 0, a, pl.ds(start + half * SUB, SUB), lanes] for a in range(3)]
                w = [pair[half] for pair in pairs]
                if steps == 1:
                    sums = add_moments(sums[:6], q) + outer_sums(sums[6:15], q, w[0]) + add_moments(sums[15:], w[0])
                else:
                    sums = outer_sums(sums[:9], q, w[1]) + outer_sums(sums[9:18], *w) + add_moments(sums[18:], w[1])
            return sums

        zero = jnp.zeros((SUB, LANES), f32)
        for i, s in enumerate(lax.fori_loop(0, count // (2 * SUB), body, [zero] * many, unroll=unroll)):
            partial[i, x] = s

    for i in range(many):
        out[i] = packed_sums(lambda x: [partial[i, x]], cells // LANES)[0]


def call_extra_moments(steps, before, extra_fields, extra_noise):
    cells = extra_fields.shape[-1]
    many = 21 if steps == 1 else 24
    return pl.pallas_call(
        functools.partial(extra_moments, steps, 7),
        out_shape=jax.ShapeDtypeStruct((many, cells // LANES, LANES), f32),
        in_specs=[anywhere, vmem, vmem],
        out_specs=vmem,
        scratch_shapes=[pltpu.VMEM((many, cells // LANES, SUB, LANES), f32)],
        compiler_params=pltpu.CompilerParams(vmem_limit_bytes=SMALL),
        cost_estimate=small(8 << 20, 5 << 20),
        name="extra_moments",
    )(before, *near_memory(extra_fields, extra_noise))


def gradients(tiles, before, helper, velocity, y_two, x_two, x_one, y_one, wall, moments, grad, keep, send):
    me = lax.axis_index("gy")
    depth = velocity.shape[1]
    cell_z = velocity.shape[3] // tiles
    sub = lax.broadcasted_iota(jnp.int32, (SUB, LANES), 0)
    lane = lax.broadcasted_iota(jnp.int32, (SUB, LANES), 1)
    z = lane % cell_z
    scales = [turned(jnp.where(wall[x] == 0, 0.5 * time_step, 0.0).astype(f32), cell_z) for x in range(depth)]
    for a in range(3):
        x_low, x_high = low_and_high("gx", x_one, x_two, a)
        y_low, y_high = low_and_high("gy", y_one, y_two, a)
        rows = [x_low] + [velocity[a, x] for x in range(depth)] + [x_high]
        rows = [turned(row, cell_z) for row in rows]
        low, high = turned(y_low, cell_z), turned(y_high, cell_z)
        for x in range(depth):
            here = rows[x + 1]
            above = high if x == depth - 1 else pltpu.roll(high, LANES - cell_z * (x + 1), 1)
            below = low if x == 0 else pltpu.roll(low, LANES - cell_z * x, 1)
            y_up = jnp.where(lane < LANES - cell_z, pltpu.roll(here, LANES - cell_z, 1), above)
            y_down = jnp.where(lane >= cell_z, pltpu.roll(here, cell_z, 1), below)
            next_tile = pltpu.roll(pltpu.roll(here, cell_z - 1, 1), 1, 0)
            last_tile = pltpu.roll(pltpu.roll(here, LANES - cell_z + 1, 1), SUB - 1, 0)
            next_tile = jnp.where(sub == 0, 0.0, next_tile)
            last_tile = jnp.where(sub == SUB - 1, 0.0, last_tile)
            z_up = jnp.where(z == cell_z - 1, next_tile, pltpu.roll(here, LANES - 1, 1))
            z_down = jnp.where(z == 0, last_tile, pltpu.roll(here, 1, 1))
            for b, difference in enumerate((rows[x + 2] - rows[x], y_up - y_down, z_up - z_down)):
                grad[pl.ds(((3 * a + b) * depth + x) * SUB, SUB), :] = difference * scales[x]
    keep[...] = jnp.zeros(keep.shape, f32)
    send[...] = jnp.zeros(send.shape, f32)
    for h, owned, tile in owned_slots(tiles, me, helper):

        @pl.when(owned)
        def _(h=h, tile=tile):
            g = [grad[pl.ds(i * depth * SUB + SUB - 1 - tile, depth, stride=SUB), :] for i in range(9)]
            rows = g + coefficients(g, [moments[h, i] for i in range(16)])
            stays = (me & 1) == (h & 1)

            @pl.when(stays)
            def _():
                for i, row in enumerate(rows):
                    keep[h >> 1, i] = row

            @pl.when(jnp.logical_not(stays))
            def _():
                for i, row in enumerate(rows):
                    send[h >> 1, i] = row


def call_gradients(tiles, before, helper_tile, velocity, halos, wall_cells, moments):
    slots = helper_tile.shape[1]
    depth = velocity.shape[1]
    half = jax.ShapeDtypeStruct((slots // 2, 12, depth, LANES), f32)
    return pl.pallas_call(
        functools.partial(gradients, tiles),
        out_shape=(jax.ShapeDtypeStruct((9 * depth * SUB, LANES), f32), half, half),
        in_specs=[anywhere] + [vmem] * 8,
        out_specs=(vmem,) * 3,
        compiler_params=pltpu.CompilerParams(vmem_limit_bytes=8 << 20),
        cost_estimate=small(4 << 20, 1 << 20),
        name="gradients",
    )(before, helper_tile, velocity, *halos, wall_cells, moments)


def swapped(block, flip):
    size = lax.axis_size("gy")
    return lax.ppermute(block, "gy", [(i, i ^ flip) for i in range(size)])


def merge(before, kept, received, keep, *sends):
    pair = lax.axis_index("gy") >> 1
    for flip, out in enumerate((keep,) + sends):
        out[...] = kept[pair ^ flip] + received[pair ^ flip]


def call_merge(before, kept, received):
    one = jax.ShapeDtypeStruct(kept.shape[1:], f32)
    return pl.pallas_call(
        merge,
        out_shape=(one,) * kept.shape[0],
        in_specs=[anywhere, vmem, vmem],
        out_specs=(vmem,) * kept.shape[0],
        compiler_params=pltpu.CompilerParams(vmem_limit_bytes=4 << 20),
        cost_estimate=small(1 << 10, 1 << 18),
        name="merge",
    )(before, kept, received)


def join(before, *refs):
    for i, ref in enumerate(refs[:-1]):
        refs[-1][i] = ref[...]


def call_join(before, blocks):
    return pl.pallas_call(
        join,
        out_shape=jax.ShapeDtypeStruct((len(blocks),) + blocks[0].shape, f32),
        in_specs=[anywhere] + [vmem] * len(blocks),
        out_specs=vmem,
        compiler_params=pltpu.CompilerParams(vmem_limit_bytes=4 << 20),
        cost_estimate=small(1 << 10, 1 << 18),
        name="join",
    )(before, *blocks)


def stress_rows(sums, inverse):
    second = [s * inverse for s in sums]
    stretch = 1.0 / (1.0 - (second[0] + second[1] + second[2]) / max_extension)
    return [(stretch * s - (1.0 if i < 3 else 0.0)) * (1.0 / weissenberg) for i, s in enumerate(second)]


def tile_grad(grad, depth, tile, x):
    return [wide(grad[pl.ds((i * depth + x + 1) * SUB - 1 - tile, 1), :]) for i in range(9)]


def tile_sums(read, write, noise, matrices, count, add, many):
    sums = [jnp.zeros((SUB, LANES), f32)] * many
    for group in range(count // (2 * SUB)):
        pairs = [noise_rows(functools.partial(noise, step), group * 2 * SUB) for step in range(len(matrices))]
        for half in range(2):
            rows = pl.ds((2 * group + half) * SUB, SUB)
            q = [read(a, rows) for a in range(3)]
            for step, matrix in enumerate(matrices):
                q = stepped(q, pairs[step][half], matrix)
            for a in range(3):
                write(a, rows, q[a])
            sums = add(sums, q)
    return sums


def add_square(sums, q):
    return [sums[0] + (q[0] * q[0] + q[1] * q[1] + q[2] * q[2])]


def ordinary(first, direct, has_block, has_base, has_extra, *refs):
    refs = list(refs)
    before, base, noise, grad = refs[:4]
    del refs[:4]
    block = refs.pop(0) if has_block else None
    if has_base:
        refs.pop(0)
    extra, extra_noise, drive = [refs.pop(0) for _ in range(3)] if has_extra else [None] * 3
    new_base = refs.pop(0) if has_block or direct else None
    new_extra = refs.pop(0) if has_extra else None
    fields, stress, early, halfway, relaxes, advanced, sems = refs
    _, _, count, cells = fields.shape
    here = direct + fields.shape[0]
    depth = cells // LANES
    inverse = 1.0 / count
    copies = []
    if has_block:
        last = block.shape[0]
        copies += [
            pltpu.make_async_copy(block.at[i], new_base.at[0, 0, first - last + i], sems.at[i]) for i in range(last)
        ]
    for copy in copies:
        copy.start()
    if has_extra:
        at = len(copies)

        def leave(x):
            lanes = pl.ds(x * LANES, LANES)
            return pltpu.make_async_copy(advanced.at[:, :, lanes], new_extra.at[0, 0, :, :, lanes], sems.at[at + x])

        @pl.loop(0, depth)
        def _(x):
            lanes = pl.ds(pl.multiple_of(x * LANES, LANES), LANES)
            rows_of = [wide(drive[i, pl.ds(x, 1), :]) for i in range(11)]
            matrices = [with_diagonal(rows_of[:9], rows_of[9 + step]) for step in range(2)]

            def body(i, carry):
                start = pl.multiple_of(i * 2 * SUB, 2 * SUB)
                pairs = [
                    noise_rows(lambda a, rows: extra_noise[0, 0, step, a, rows, lanes], start) for step in range(2)
                ]
                for half in range(2):
                    rows = pl.ds(start + half * SUB, SUB)
                    q = [extra[0, 0, a, rows, lanes] for a in range(3)]
                    for step in range(2):
                        q = stepped(q, pairs[step][half], matrices[step])
                    for a in range(3):
                        advanced[a, rows, lanes] = q[a]
                return carry

            lax.fori_loop(0, extra.shape[3] // (2 * SUB), body, 0, unroll=7)
            leave(x).start()

        copies += [leave(x) for x in range(depth)]
    for place in range(here):
        tile = first + place

        def squares(x):
            total = jnp.zeros((SUB, LANES), f32)
            for group in range(count // SUB):
                for a in range(3):
                    q = base[0, 0, tile, a, pl.ds(group * SUB, SUB), pl.ds(x * LANES, LANES)]
                    total = total + q * q
            return [total]

        sums = packed_sums(squares, depth)
        for step in range(2):
            relaxes[place, step] = relax_of(sums[0], inverse)

            def sums_of(x):
                lanes = pl.ds(x * LANES, LANES)
                matrix = with_diagonal(tile_grad(grad, depth, tile, x), wide(relaxes[place, step, pl.ds(x, 1), :]))

                def read(a, rows):
                    return base[0, 0, tile, a, rows, lanes] if step == 0 else halfway[place, a, rows, lanes]

                def write(a, rows, value):
                    if step == 0:
                        halfway[place, a, rows, lanes] = value
                    elif place < direct:
                        early[place, a, rows, lanes] = value
                    else:
                        fields[place - direct, a, rows, lanes] = value

                def shock(_, a, rows):
                    return noise[0, 0, tile, step, a, rows, lanes]

                if step == 0:
                    return tile_sums(read, write, shock, [matrix], count, add_square, 1)
                return tile_sums(read, write, shock, [matrix], count, add_moments, 6)

            sums = packed_sums(sums_of, depth)
        if place < direct:
            copies.append(pltpu.make_async_copy(early.at[place], new_base.at[0, 0, tile], sems.at[len(copies)]))
            copies[-1].start()
        for i, row in enumerate(stress_rows(sums, inverse)):
            stress[i, place] = row
    for copy in copies:
        copy.wait()


def call_ordinary(first, here, direct, before, base_fields, base_noise, grad, block, new_base, extra):
    count, cells = base_fields.shape[-2:]
    depth = cells // LANES
    has_block, has_base, has_extra = block is not None, new_base is not None, extra is not None
    operands = [before, *near_memory(base_fields, base_noise), grad]
    specs = [anywhere, vmem, vmem, vmem]
    shapes, out_specs, aliases = [], [], {}
    copies = 0
    if has_block:
        operands += near_memory(block)
        specs.append(vmem)
        copies += block.shape[0]
    if has_block or direct:
        copies += direct
        shapes.append(jax.ShapeDtypeStruct(base_fields.shape, f32))
        out_specs.append(hbm)
    if has_base:
        aliases[len(operands)] = 0
        operands.append(new_base)
        specs.append(hbm)
    if has_extra:
        operands += near_memory(*extra[:2]) + [extra[2]]
        specs += [vmem] * 3
        shapes.append(jax.ShapeDtypeStruct(extra[0].shape, f32))
        out_specs.append(hbm)
        copies += depth
    shapes += [
        pltpu.VMEM((here - direct, 3, count, cells), f32),
        jax.ShapeDtypeStruct((6, here, depth, LANES), f32),
    ]
    out_specs += [vmem, vmem]
    results = pl.pallas_call(
        functools.partial(ordinary, first, direct, has_block, has_base, has_extra),
        out_shape=tuple(shapes),
        in_specs=specs,
        out_specs=tuple(out_specs),
        input_output_aliases=aliases,
        scratch_shapes=[
            pltpu.VMEM((max(direct, 1), 3, count, cells), f32),
            pltpu.VMEM((here, 3, count, cells), f32),
            pltpu.VMEM((here, 2, depth, LANES), f32),
            pltpu.VMEM(extra[0].shape[2:] if has_extra else (SUB, LANES), f32),
            pltpu.SemaphoreType.DMA((max(copies, 1),)),
        ],
        compiler_params=pltpu.CompilerParams(vmem_limit_bytes=SMALL),
        cost_estimate=small(8 << 20, 3 << 20),
        name="ordinary_tiles",
    )(*operands)
    results = list(results)
    piece, block = results.pop(), results.pop()
    new_base = results.pop(0) if has_block or direct else None
    return new_base, block, piece, (results[0] if has_extra else None)


def moments_after(g, first, second, m):
    one, two = with_diagonal(g, first), with_diagonal(g, second)
    both = [[sum(two[3 * a + k] * one[3 * k + b] for k in range(3)) for b in range(3)] for a in range(3)]
    kick = [[noise_scale * two[3 * a + b] for b in range(3)] for a in range(3)]

    def mixed(of_q, of_w):
        return [
            [sum(both[a][i] * of_q(i, j) for i in range(3)) + sum(kick[a][i] * of_w(i, j) for i in range(3)) for j in range(3)]
            for a in range(3)
        ]

    with_q = mixed(lambda i, j: m[moment_of[i, j]], lambda i, j: m[6 + 3 * j + i])
    with_one = mixed(lambda i, j: m[6 + 3 * i + j], lambda i, j: m[15 + moment_of[i, j]])
    with_two = mixed(lambda i, j: m[21 + 3 * i + j], lambda i, j: m[30 + 3 * i + j])
    return [
        sum(with_q[a][j] * both[b][j] + with_one[a][j] * kick[b][j] for j in range(3))
        + noise_scale * (with_two[a][b] + with_two[b][a])
        + noise_scale**2 * m[39 + i]
        for i, (a, b) in enumerate(component_pairs)
    ]


def answering(before, moments, later, *refs):
    *parts, reply, drive = refs
    inverse = 1.0 / float(ALL_FIELDS)
    message = [sum(part[i] for part in parts) for i in range(12)]
    grad, m = message[:9], [moments[i] for i in range(21)] + [later[i] for i in range(24)]
    own = coefficients(grad, m[:15] + [m[15] + m[16] + m[17]])
    both = [message[9 + i] + own[i] for i in range(3)]
    first = relax_of(both[2], inverse)
    second = relax_of(both[0] + first * (both[1] + first * both[2]), inverse)
    for i, value in enumerate([first, second] + moments_after(grad, first, second, m)):
        reply[i] = value
    for i, value in enumerate(grad + [first, second]):
        drive[i] = value


def call_answering(before, moments, later, parts):
    depth = moments.shape[1]
    return pl.pallas_call(
        answering,
        out_shape=(
            jax.ShapeDtypeStruct((8, depth, LANES), f32),
            jax.ShapeDtypeStruct((11, depth, LANES), f32),
        ),
        in_specs=[anywhere] + [vmem] * (2 + len(parts)),
        out_specs=(vmem, vmem),
        compiler_params=pltpu.CompilerParams(vmem_limit_bytes=4 << 20),
        cost_estimate=small(1 << 20, 1 << 19),
        name="answering",
    )(before, moments, later, *parts)


def heavy(parity, helper, base, noise, grad, replies, new_base, rows, fields, answer, sems):
    _, _, tiles, _, count, cells = base.shape
    me = lax.axis_index("gy")
    depth = cells // LANES
    flat = rows.reshape(6 * depth * tiles, LANES)

    def store(k, tile):
        return pltpu.make_async_copy(fields.at[k], new_base.at[0, 0, tile], sems.at[k])

    places, order = owned_order(tiles, me, helper, (parity,))
    for k, (h, tile) in enumerate(order):

        @pl.when(k < places)
        def _(k=k, h=h, tile=tile):
            answer[...] = replies[(me ^ h) >> 1]

            def sums_of(x):
                lanes = pl.ds(x * LANES, LANES)
                g = tile_grad(grad, depth, tile, x)
                matrices = [with_diagonal(g, wide(answer[step, pl.ds(x, 1), :])) for step in range(2)]

                def read(a, part):
                    return base[0, 0, tile, a, part, lanes]

                def write(a, part, value):
                    fields[k, a, part, lanes] = value

                def shock(step, a, part):
                    return noise[0, 0, tile, step, a, part, lanes]

                return tile_sums(read, write, shock, matrices, count, add_moments, 6)

            sums = packed_sums(sums_of, depth)
            store(k, tile).start()
            sums = [s + answer[2 + i] for i, s in enumerate(sums)]
            for i, value in enumerate(stress_rows(sums, 1.0 / ALL_FIELDS)):
                flat[pl.ds(i * depth * tiles + tile, depth, stride=tiles), :] = value

    def wait():
        for k, (_, tile) in enumerate(order):

            @pl.when(k < places)
            def _(k=k, tile=tile):
                store(k, tile).wait()

    return wait


def heavy_scratch(near, held):
    return [pltpu.VMEM((HEAVY_MOST,) + held, f32), pltpu.VMEM(near.shape[1:], f32)]


def finish(piece_count, helper, base, noise, grad, near, block, *refs):
    pieces, (_, new_base, rows, fields, answer, sems) = refs[:piece_count], refs[piece_count:]
    _, depth, tiles, _ = rows.shape
    last = block.shape[0]
    flat = rows.reshape(6 * depth * tiles, LANES)
    me = lax.axis_index("gy")
    named = [jnp.bool_(False)] * last
    for _, owned, tile in owned_slots(tiles, me, helper):
        named = [n | (owned & (tile == tiles - last + i)) for i, n in enumerate(named)]
    copies = [
        pltpu.make_async_copy(block.at[i], new_base.at[0, 0, tiles - last + i], sems.at[HEAVY_MOST + i])
        for i in range(last)
    ]
    for copy, is_heavy in zip(copies, named):
        pl.when(jnp.logical_not(is_heavy))(copy.start)
    tile = 0
    for piece in pieces:
        for place in range(piece.shape[1]):
            for i in range(6):
                flat[pl.ds(i * depth * tiles + tile, depth, stride=tiles), :] = piece[i, place]
            tile += 1
    wait = heavy(0, helper, base, noise, grad, near, new_base, rows, fields, answer, sems)
    wait()
    for copy, is_heavy in zip(copies, named):
        pl.when(jnp.logical_not(is_heavy))(copy.wait)


def call_finish(helper_tile, base_fields, base_noise, grad, near, block, pieces, new_base):
    tiles, cells = new_base.shape[2], new_base.shape[-1]
    return pl.pallas_call(
        functools.partial(finish, len(pieces)),
        out_shape=(
            jax.ShapeDtypeStruct(new_base.shape, f32),
            jax.ShapeDtypeStruct((6, cells // LANES, tiles, LANES), f32),
        ),
        in_specs=[vmem] * (6 + len(pieces)) + [hbm],
        out_specs=(hbm, vmem),
        input_output_aliases={6 + len(pieces): 0},
        scratch_shapes=heavy_scratch(near, block.shape[1:])
        + [pltpu.SemaphoreType.DMA((HEAVY_MOST + block.shape[0],))],
        compiler_params=pltpu.CompilerParams(vmem_limit_bytes=SMALL),
        cost_estimate=small(1 << 10, 1 << 20),
        name="finish",
    )(helper_tile, *near_memory(base_fields, base_noise), grad, near, *near_memory(block), *pieces, new_base)


def final(helper, base, noise, grad, far, ready, old_base, new_base, stress, rows, fields, answer, sems):
    depth = rows.shape[1]

    def result(x):
        target = stress.at[0, 0, :, :, pl.ds(x * LANES, LANES)]
        return pltpu.make_async_copy(rows.at[:, x], target, sems.at[HEAVY_MOST + x])

    rows[...] = ready[...]
    wait = heavy(1, helper, base, noise, grad, far, new_base, rows, fields, answer, sems)
    for x in range(depth):
        result(x).start()
    wait()
    for x in range(depth):
        result(x).wait()


def call_final(helper_tile, base_fields, base_noise, grad, far, ready, new_base):
    _, _, tiles, _, count, cells = base_fields.shape
    depth = cells // LANES
    return pl.pallas_call(
        final,
        out_shape=(
            jax.ShapeDtypeStruct(new_base.shape, f32),
            jax.ShapeDtypeStruct((1, 1, 6, tiles, cells), f32),
        ),
        in_specs=[vmem] * 6 + [hbm],
        out_specs=(hbm, hbm),
        input_output_aliases={6: 0},
        scratch_shapes=[pltpu.VMEM((6, depth, tiles, LANES), f32)]
        + heavy_scratch(far, (3, count, cells))
        + [pltpu.SemaphoreType.DMA((HEAVY_MOST + depth,))],
        compiler_params=pltpu.CompilerParams(vmem_limit_bytes=SMALL),
        cost_estimate=small(8 << 20, 4 << 20),
        name="heavy_tiles",
    )(helper_tile, *near_memory(base_fields, base_noise), grad, far, ready, new_base)


def per_device(
    velocity, wall_cells, tile_counts, helper_tile, base_fields, extra_fields, base_noise, extra_noise
):
    tiles = tile_counts.shape[2]
    pairs = lax.axis_size("gy") // 2
    helper_tile, x_one, x_two, y_one, y_two = call_edges(helper_tile, velocity)
    y_two = swap_across(y_two, False)
    x_two = swap_across(x_two, True)
    x_one = swap_within(x_one, "gx")
    y_one = swap_within(y_one, "gy")
    halos = (y_two, x_two, x_one, y_one)
    moments = call_heavy_moments(helper_tile, base_fields, base_noise)
    later = call_extra_moments(2, moments, extra_fields, extra_noise)
    grad, keep, send = call_gradients(tiles, later, helper_tile, velocity, halos, wall_cells, moments)
    some = 3 * tiles // 8
    ordinary_fields = (base_fields, base_noise, grad)
    received = swapped(send, 1)
    _, block, begun, _ = call_ordinary(0, some, 0, send, *ordinary_fields, None, None, None)
    keep, *sends = call_merge(begun, keep, received)
    farthest_first = sorted(range(1, pairs), key=lambda flip: -flip.bit_count())
    parts = [keep] + [swapped(sends[flip - 1], 2 * flip) for flip in farthest_first]
    extra_sums = call_extra_moments(1, sends[0], extra_fields, extra_noise)
    more = tiles - some - 3
    new_base, block, going, _ = call_ordinary(some, more, 0, extra_sums, *ordinary_fields, block, None, None)
    reply, drive = call_answering(going, extra_sums, later, parts)
    replies = {flip: swapped(reply, 2 * flip) for flip in farthest_first}
    new_base, block, ended, new_extra = call_ordinary(
        tiles - 3, 3, 1, reply, *ordinary_fields, block, new_base, (extra_fields, extra_noise, drive)
    )
    near = call_join(ended, [reply] + [replies[flip] for flip in range(1, pairs)])
    far = swapped(near, 1)
    given = (helper_tile, base_fields, base_noise, grad)
    new_base, ready = call_finish(*given, near, block, (begun, going, ended), new_base)
    new_base, stress = call_final(*given, far, ready, new_base)
    return new_base, new_extra, jnp.swapaxes(stress, 2, 3)


def solution(mesh):
    in_specs = (
        P(None, "gx", "gy", None),
        P("gx", "gy", None),
        P("gx", "gy", None),
        P("gx", None),
        P("gx", "gy", None, None, None, None),
        P("gx", "gy", None, None, None),
        P("gx", "gy", None, None, None, None, None),
        P("gx", "gy", None, None, None, None),
    )
    out_specs = (
        P("gx", "gy", None, None, None, None),
        P("gx", "gy", None, None, None),
        P("gx", "gy", None, None, None),
    )
    return jax.shard_map(
        per_device, mesh=mesh, in_specs=in_specs, out_specs=out_specs, check_vma=False
    )
```

```python
import functools

import jax
import jax.numpy as jnp
from jax import lax
from jax.experimental import pallas as pl
from jax.experimental.pallas import tpu as pltpu
from jax.sharding import PartitionSpec as P

ALL_FIELDS = 256
HEAVY_MOST = 4
LANES = 128
SUB = 8
SMALL = 12 << 20

time_step = 0.05
weissenberg = 0.25
max_extension = 50.0
noise_scale = (time_step / weissenberg) ** 0.5
component_pairs = ((0, 0), (1, 1), (2, 2), (0, 1), (0, 2), (1, 2))
moment_of = {(0, 0): 0, (1, 1): 1, (2, 2): 2, (0, 1): 3, (1, 0): 3, (0, 2): 4, (2, 0): 4, (1, 2): 5, (2, 1): 5}
f32 = jnp.float32

vmem = pl.BlockSpec(memory_space=pltpu.VMEM)
hbm = pl.BlockSpec(memory_space=pltpu.HBM)
anywhere = pl.BlockSpec(memory_space=pl.ANY)


def far_memory(*arrays):
    return [pltpu.with_memory_space_constraint(array, pltpu.HBM) for array in arrays]


def near_memory(*arrays):
    return [pltpu.with_memory_space_constraint(array, pltpu.VMEM) for array in arrays]


def column_sum(value):
    return jnp.sum(value, axis=0, keepdims=True)


def interleaved(a, b, bit):
    low = (lax.broadcasted_iota(jnp.int32, (SUB, LANES), 0) & bit) == 0
    return jnp.where(low, a, b) + pltpu.roll(jnp.where(low, b, a), bit, 0)


def packed_sums(values_of, count):
    stack = []
    for x in range(count):
        bit, values = 1, values_of(x)
        while stack and stack[-1][0] == bit:
            values = [interleaved(a, b, bit) for a, b in zip(stack.pop()[1], values)]
            bit *= 2
        stack.append((bit, values))
    return stack[0][1]


def wide(row):
    return jnp.broadcast_to(row, (SUB, LANES))


def turned(value, cell_z):
    sub = lax.broadcasted_iota(jnp.int32, value.shape, 0)
    group = lax.broadcasted_iota(jnp.int32, value.shape, 1) // cell_z
    skewed = pltpu.roll(value, cell_z, 1, stride=cell_z, stride_axis=0)
    mixed = jnp.take_along_axis(skewed, (group + sub) & (SUB - 1), axis=0, mode="promise_in_bounds")
    return pltpu.roll(mixed, 0, 1, stride=cell_z, stride_axis=0)


def relax_of(total, inverse):
    factor = 1.0 / (1.0 - total * inverse / max_extension)
    return 1.0 - (time_step * 0.5 / weissenberg) * factor


def stepped(vectors, noise, matrix):
    return [
        matrix[3 * a] * vectors[0]
        + matrix[3 * a + 1] * vectors[1]
        + matrix[3 * a + 2] * vectors[2]
        + noise_scale * noise[a]
        for a in range(3)
    ]


def with_diagonal(grad, relax):
    return [g + relax if i % 4 == 0 else g for i, g in enumerate(grad)]


def noise_rows(ref, start):
    both = [ref(a, pl.ds(start, 2 * SUB)).astype(f32) for a in range(3)]
    return [[w[:SUB] for w in both], [w[SUB:] for w in both]]


def add_moments(sums, q):
    return [s + q[a] * q[b] for s, (a, b) in zip(sums, component_pairs)]


def product_sums(sums, q, w):
    terms = [q[a] * q[b] for a, b in component_pairs]
    terms += [q[a] * w[b] for a in range(3) for b in range(3)]
    terms += [w[0] * w[0] + w[1] * w[1] + w[2] * w[2]]
    return [s + t for s, t in zip(sums, terms)]


def coefficients(g, m):
    cross = lambda a, b: m[6 + 3 * a + b]
    square = lambda a, b: m[moment_of[a, b]]
    once, twice, kick = 0.0, 0.0, 0.0
    for a in range(3):
        for b in range(3):
            once += g[3 * a + b] * square(a, b)
            kick += g[3 * a + b] * cross(b, a)
            inner = 0.0
            for c in range(3):
                inner += g[3 * a + c] * square(b, c)
            twice += g[3 * a + b] * inner
    return [
        twice + (2 * noise_scale) * kick + noise_scale**2 * m[15],
        2.0 * once + (2 * noise_scale) * (cross(0, 0) + cross(1, 1) + cross(2, 2)),
        m[0] + m[1] + m[2],
    ]


def owned_slots(tiles, me, helper):
    found = []
    row = helper[...]
    for h in range(helper.shape[1]):
        tile = row[0, h] - me * tiles
        found.append((h, (tile >= 0) & (tile < tiles), tile))
    return found


def owned_order(tiles, me, helper, parities=(0, 1)):
    places = jnp.int32(0)
    order = [jnp.int32(0)] * HEAVY_MOST
    for h, owned, tile in owned_slots(tiles, me, helper):
        if len(parities) == 1:
            owned = owned & (((me ^ h) & 1) == parities[0])
        entry = h * tiles + tile
        order = [jnp.where(owned & (places == k), entry, kept) for k, kept in enumerate(order)]
        places = places + owned.astype(jnp.int32)
    return places, [(entry // tiles, entry % tiles) for entry in order]


def small(flops, traffic):
    return pl.CostEstimate(flops=flops, bytes_accessed=traffic, transcendentals=0)


def is_even(axis):
    return (lax.axis_index(axis) & 1) == 0


def edges(helper, velocity, helper_near, x_one, x_two, y_one, y_two):
    depth, width = velocity.shape[1:3]
    helper_near[...] = helper[...]
    even = is_even("gx")
    for a in range(3):
        first, last = velocity[a, 0], velocity[a, depth - 1]
        x_one[a] = jnp.where(even, last, first)
        x_two[a] = jnp.where(even, first, last)
    even = is_even("gy")
    for a in range(3):
        for x in range(depth):
            first, last = velocity[a, x, pl.ds(0, 1), :], velocity[a, x, pl.ds(width - 1, 1), :]
            y_one[a, pl.ds(x, 1), :] = jnp.where(even, last, first)
            y_two[a, pl.ds(x, 1), :] = jnp.where(even, first, last)


def call_edges(helper_tile, velocity):
    _, depth, width, length = velocity.shape
    along_x = jax.ShapeDtypeStruct((3, width, length), f32)
    along_y = jax.ShapeDtypeStruct((3, depth, length), f32)
    return pl.pallas_call(
        edges,
        out_shape=(jax.ShapeDtypeStruct(helper_tile.shape, jnp.int32), along_x, along_x, along_y, along_y),
        in_specs=[vmem, vmem],
        out_specs=(vmem,) * 5,
        compiler_params=pltpu.CompilerParams(vmem_limit_bytes=4 << 20),
        cost_estimate=small(1 << 10, 1 << 17),
        name="edges",
    )(*far_memory(helper_tile, velocity))


def swap_within(block, axis):
    return lax.ppermute(block, axis, [(i, i ^ 1) for i in range(lax.axis_size(axis))])


def swap_across(block, along_rows):
    rows, columns = lax.axis_size("gx"), lax.axis_size("gy")
    size = rows if along_rows else columns

    def partner(row, column):
        place = row if along_rows else column
        if place in (0, size - 1):
            row, column = (row, column ^ 1) if along_rows else (row ^ 1, column)
        else:
            place += 1 if place & 1 else -1
            row, column = (place, column) if along_rows else (row, place)
        return row * columns + column

    places = [(row, column) for row in range(rows) for column in range(columns)]
    return lax.ppermute(block, ("gx", "gy"), [(i, partner(*place)) for i, place in enumerate(places)])


def low_and_high(axis, one, two, a):
    even, place = is_even(axis), lax.axis_index(axis)
    low = jnp.where(even, two[a], one[a])
    high = jnp.where(even, one[a], two[a])
    return jnp.where(place == 0, 0.0, low), jnp.where(place == lax.axis_size(axis) - 1, 0.0, high)


def later_sums(sums, q, one, two):
    return outer_sums(sums[:9], q, two) + outer_sums(sums[9:18], one, two) + add_moments(sums[18:], two)


def early_sums(helper, base, noise, extra, extra_noise, out, later, fields, shocks, near, near_noise, partial, sems):
    _, _, count, cells = fields.shape
    depth = cells // LANES
    tiles = base.shape[2]
    each = 4 * SUB
    pieces = near.shape[1] // each
    me = lax.axis_index("gy")

    def loads(k, tile):
        return (
            pltpu.make_async_copy(base.at[0, 0, tile], fields.at[k], sems.at[0, k]),
            pltpu.make_async_copy(noise.at[0, 0, tile, 0], shocks.at[k], sems.at[1, k]),
        )

    def piece_loads(r):
        rows = pl.ds(pl.multiple_of(r * each, each), each)
        return (
            pltpu.make_async_copy(extra.at[0, 0, :, rows], near.at[:, rows], sems.at[0, HEAVY_MOST + r]),
            pltpu.make_async_copy(extra_noise.at[0, 0, :, :, rows], near_noise.at[:, :, rows], sems.at[1, HEAVY_MOST + r]),
        )

    places, order = owned_order(tiles, me, helper)
    for k, (_, tile) in enumerate(order):

        @pl.when(k < places)
        def _(k=k, tile=tile):
            for copy in loads(k, tile):
                copy.start()

    for r in range(pieces):
        for copy in piece_loads(r):
            copy.start()
    partial[...] = jnp.zeros(partial.shape, f32)
    for k, (h, tile) in enumerate(order):

        @pl.when(k < places)
        def _(k=k, h=h, tile=tile):
            for copy in loads(k, tile):
                copy.wait()

            def sums_of(x):
                lanes = pl.ds(x * LANES, LANES)
                sums = [jnp.zeros((SUB, LANES), f32)] * 16
                for group in range(count // (2 * SUB)):
                    pair = noise_rows(lambda a, rows: shocks[k, a, rows, lanes], group * 2 * SUB)
                    for half in range(2):
                        rows = pl.ds((2 * group + half) * SUB, SUB)
                        sums = product_sums(sums, [fields[k, a, rows, lanes] for a in range(3)], pair[half])
                return sums

            for i, value in enumerate(packed_sums(sums_of, depth)):
                out[h, i] = value

    @pl.loop(0, pieces)
    def _(r):
        for copy in piece_loads(r):
            copy.wait()

        def at(x):
            lanes = pl.ds(pl.multiple_of(x * LANES, LANES), LANES)
            sums = [partial[i, x] for i in range(24)]
            for group in range(2):
                start = pl.multiple_of(r * each + group * 2 * SUB, 2 * SUB)
                one, two = [
                    noise_rows(lambda a, rows: near_noise[step, a, rows, lanes], start) for step in range(2)
                ]
                for half in range(2):
                    q = [near[a, pl.ds(start + half * SUB, SUB), lanes] for a in range(3)]
                    sums = later_sums(sums, q, one[half], two[half])
            for i, value in enumerate(sums):
                partial[i, x] = value

        @pl.loop(0, depth // 4)
        def _(x):
            for i in range(4):
                at(4 * x + i)

    for i in range(24):
        later[i] = packed_sums(lambda x: [partial[i, x]], depth)[0]


def call_early_sums(helper_tile, base_fields, base_noise, extra_fields, extra_noise):
    slots = helper_tile.shape[1]
    count, cells = base_fields.shape[-2:]
    depth = cells // LANES
    return pl.pallas_call(
        early_sums,
        out_shape=(
            jax.ShapeDtypeStruct((slots, 16, depth, LANES), f32),
            jax.ShapeDtypeStruct((24, depth, LANES), f32),
        ),
        in_specs=[vmem, hbm, hbm, hbm, hbm],
        out_specs=(vmem, vmem),
        scratch_shapes=[
            pltpu.VMEM((HEAVY_MOST, 3, count, cells), f32),
            pltpu.VMEM((HEAVY_MOST, 3, count, cells), jnp.bfloat16),
            pltpu.VMEM(extra_fields.shape[2:], f32),
            pltpu.VMEM(extra_noise.shape[2:], jnp.bfloat16),
            pltpu.VMEM((24, depth, SUB, LANES), f32),
            pltpu.SemaphoreType.DMA((2, HEAVY_MOST + extra_fields.shape[3] // (4 * SUB))),
        ],
        compiler_params=pltpu.CompilerParams(vmem_limit_bytes=SMALL),
        cost_estimate=small(8 << 20, 3 << 20),
        name="early_sums",
    )(helper_tile, *far_memory(base_fields, base_noise, extra_fields, extra_noise))


def outer_sums(sums, left, right):
    return [s + left[a] * right[b] for s, (a, b) in zip(sums, [(a, b) for a in range(3) for b in range(3)])]


def extra_moments(steps, unroll, before, base, noise, out, partial):
    _, _, _, count, cells = base.shape
    many = out.shape[0]

    @pl.loop(0, cells // LANES)
    def _(x):
        lanes = pl.ds(pl.multiple_of(x * LANES, LANES), LANES)

        def body(i, sums):
            start = pl.multiple_of(i * 2 * SUB, 2 * SUB)
            pairs = [noise_rows(lambda a, rows: noise[0, 0, step, a, rows, lanes], start) for step in range(steps)]
            for half in range(2):
                q = [base[0, 0, a, pl.ds(start + half * SUB, SUB), lanes] for a in range(3)]
                w = [pair[half] for pair in pairs]
                if steps == 1:
                    sums = add_moments(sums[:6], q) + outer_sums(sums[6:15], q, w[0]) + add_moments(sums[15:], w[0])
                else:
                    sums = outer_sums(sums[:9], q, w[1]) + outer_sums(sums[9:18], *w) + add_moments(sums[18:], w[1])
            return sums

        zero = jnp.zeros((SUB, LANES), f32)
        for i, s in enumerate(lax.fori_loop(0, count // (2 * SUB), body, [zero] * many, unroll=unroll)):
            partial[i, x] = s

    for i in range(many):
        out[i] = packed_sums(lambda x: [partial[i, x]], cells // LANES)[0]


def call_extra_moments(steps, before, extra_fields, extra_noise):
    cells = extra_fields.shape[-1]
    many = 21 if steps == 1 else 24
    return pl.pallas_call(
        functools.partial(extra_moments, steps, 7),
        out_shape=jax.ShapeDtypeStruct((many, cells // LANES, LANES), f32),
        in_specs=[anywhere, vmem, vmem],
        out_specs=vmem,
        scratch_shapes=[pltpu.VMEM((many, cells // LANES, SUB, LANES), f32)],
        compiler_params=pltpu.CompilerParams(vmem_limit_bytes=SMALL),
        cost_estimate=small(8 << 20, 5 << 20),
        name="extra_moments",
    )(before, *near_memory(extra_fields, extra_noise))


def gradients(tiles, before, helper, velocity, y_two, x_two, x_one, y_one, wall, moments, grad, keep, send):
    me = lax.axis_index("gy")
    depth = velocity.shape[1]
    cell_z = velocity.shape[3] // tiles
    sub = lax.broadcasted_iota(jnp.int32, (SUB, LANES), 0)
    lane = lax.broadcasted_iota(jnp.int32, (SUB, LANES), 1)
    z = lane % cell_z
    scales = [turned(jnp.where(wall[x] == 0, 0.5 * time_step, 0.0).astype(f32), cell_z) for x in range(depth)]
    for a in range(3):
        x_low, x_high = low_and_high("gx", x_one, x_two, a)
        y_low, y_high = low_and_high("gy", y_one, y_two, a)
        rows = [x_low] + [velocity[a, x] for x in range(depth)] + [x_high]
        rows = [turned(row, cell_z) for row in rows]
        low, high = turned(y_low, cell_z), turned(y_high, cell_z)
        for x in range(depth):
            here = rows[x + 1]
            above = high if x == depth - 1 else pltpu.roll(high, LANES - cell_z * (x + 1), 1)
            below = low if x == 0 else pltpu.roll(low, LANES - cell_z * x, 1)
            y_up = jnp.where(lane < LANES - cell_z, pltpu.roll(here, LANES - cell_z, 1), above)
            y_down = jnp.where(lane >= cell_z, pltpu.roll(here, cell_z, 1), below)
            next_tile = pltpu.roll(pltpu.roll(here, cell_z - 1, 1), 1, 0)
            last_tile = pltpu.roll(pltpu.roll(here, LANES - cell_z + 1, 1), SUB - 1, 0)
            next_tile = jnp.where(sub == 0, 0.0, next_tile)
            last_tile = jnp.where(sub == SUB - 1, 0.0, last_tile)
            z_up = jnp.where(z == cell_z - 1, next_tile, pltpu.roll(here, LANES - 1, 1))
            z_down = jnp.where(z == 0, last_tile, pltpu.roll(here, 1, 1))
            for b, difference in enumerate((rows[x + 2] - rows[x], y_up - y_down, z_up - z_down)):
                grad[pl.ds(((3 * a + b) * depth + x) * SUB, SUB), :] = difference * scales[x]
    keep[...] = jnp.zeros(keep.shape, f32)
    send[...] = jnp.zeros(send.shape, f32)
    for h, owned, tile in owned_slots(tiles, me, helper):

        @pl.when(owned)
        def _(h=h, tile=tile):
            g = [grad[pl.ds(i * depth * SUB + SUB - 1 - tile, depth, stride=SUB), :] for i in range(9)]
            rows = g + coefficients(g, [moments[h, i] for i in range(16)])
            stays = (me & 1) == (h & 1)

            @pl.when(stays)
            def _():
                for i, row in enumerate(rows):
                    keep[h >> 1, i] = row

            @pl.when(jnp.logical_not(stays))
            def _():
                for i, row in enumerate(rows):
                    send[h >> 1, i] = row


def call_gradients(tiles, before, helper_tile, velocity, halos, wall_cells, moments):
    slots = helper_tile.shape[1]
    depth = velocity.shape[1]
    half = jax.ShapeDtypeStruct((slots // 2, 12, depth, LANES), f32)
    return pl.pallas_call(
        functools.partial(gradients, tiles),
        out_shape=(jax.ShapeDtypeStruct((9 * depth * SUB, LANES), f32), half, half),
        in_specs=[anywhere] + [vmem] * 8,
        out_specs=(vmem,) * 3,
        compiler_params=pltpu.CompilerParams(vmem_limit_bytes=8 << 20),
        cost_estimate=small(4 << 20, 1 << 20),
        name="gradients",
    )(before, helper_tile, velocity, *halos, wall_cells, moments)


def swapped(block, flip):
    size = lax.axis_size("gy")
    return lax.ppermute(block, "gy", [(i, i ^ flip) for i in range(size)])


def merge(before, kept, received, keep, *sends):
    pair = lax.axis_index("gy") >> 1
    for flip, out in enumerate((keep,) + sends):
        out[...] = kept[pair ^ flip] + received[pair ^ flip]


def call_merge(before, kept, received):
    one = jax.ShapeDtypeStruct(kept.shape[1:], f32)
    return pl.pallas_call(
        merge,
        out_shape=(one,) * kept.shape[0],
        in_specs=[anywhere, vmem, vmem],
        out_specs=(vmem,) * kept.shape[0],
        compiler_params=pltpu.CompilerParams(vmem_limit_bytes=4 << 20),
        cost_estimate=small(1 << 10, 1 << 18),
        name="merge",
    )(before, kept, received)


def join(before, *refs):
    for i, ref in enumerate(refs[:-1]):
        refs[-1][i] = ref[...]


def call_join(before, blocks):
    return pl.pallas_call(
        join,
        out_shape=jax.ShapeDtypeStruct((len(blocks),) + blocks[0].shape, f32),
        in_specs=[anywhere] + [vmem] * len(blocks),
        out_specs=vmem,
        compiler_params=pltpu.CompilerParams(vmem_limit_bytes=4 << 20),
        cost_estimate=small(1 << 10, 1 << 18),
        name="join",
    )(before, *blocks)


def stress_rows(sums, inverse):
    second = [s * inverse for s in sums]
    stretch = 1.0 / (1.0 - (second[0] + second[1] + second[2]) / max_extension)
    return [(stretch * s - (1.0 if i < 3 else 0.0)) * (1.0 / weissenberg) for i, s in enumerate(second)]


def tile_grad(grad, depth, tile, x):
    return [wide(grad[pl.ds((i * depth + x + 1) * SUB - 1 - tile, 1), :]) for i in range(9)]


def tile_sums(read, write, noise, matrices, count, add, many):
    sums = [jnp.zeros((SUB, LANES), f32)] * many
    for group in range(count // (2 * SUB)):
        pairs = [noise_rows(functools.partial(noise, step), group * 2 * SUB) for step in range(len(matrices))]
        for half in range(2):
            rows = pl.ds((2 * group + half) * SUB, SUB)
            q = [read(a, rows) for a in range(3)]
            for step, matrix in enumerate(matrices):
                q = stepped(q, pairs[step][half], matrix)
            for a in range(3):
                write(a, rows, q[a])
            sums = add(sums, q)
    return sums


def add_square(sums, q):
    return [sums[0] + (q[0] * q[0] + q[1] * q[1] + q[2] * q[2])]


def ordinary(first, direct, has_block, has_base, has_extra, *refs):
    refs = list(refs)
    before, base, noise, grad = refs[:4]
    del refs[:4]
    block = refs.pop(0) if has_block else None
    if has_base:
        refs.pop(0)
    extra, extra_noise, drive = [refs.pop(0) for _ in range(3)] if has_extra else [None] * 3
    new_base = refs.pop(0) if has_block or direct else None
    new_extra = refs.pop(0) if has_extra else None
    fields, stress, early, halfway, relaxes, advanced, sems = refs
    _, _, count, cells = fields.shape
    here = direct + fields.shape[0]
    depth = cells // LANES
    inverse = 1.0 / count
    copies = []
    if has_block:
        last = block.shape[0]
        copies += [
            pltpu.make_async_copy(block.at[i], new_base.at[0, 0, first - last + i], sems.at[i]) for i in range(last)
        ]
    for copy in copies:
        copy.start()
    if has_extra:
        at = len(copies)

        def leave(x):
            lanes = pl.ds(x * LANES, LANES)
            return pltpu.make_async_copy(advanced.at[:, :, lanes], new_extra.at[0, 0, :, :, lanes], sems.at[at + x])

        @pl.loop(0, depth)
        def _(x):
            lanes = pl.ds(pl.multiple_of(x * LANES, LANES), LANES)
            rows_of = [wide(drive[i, pl.ds(x, 1), :]) for i in range(11)]
            matrices = [with_diagonal(rows_of[:9], rows_of[9 + step]) for step in range(2)]

            def body(i, carry):
                start = pl.multiple_of(i * 2 * SUB, 2 * SUB)
                pairs = [
                    noise_rows(lambda a, rows: extra_noise[0, 0, step, a, rows, lanes], start) for step in range(2)
                ]
                for half in range(2):
                    rows = pl.ds(start + half * SUB, SUB)
                    q = [extra[0, 0, a, rows, lanes] for a in range(3)]
                    for step in range(2):
                        q = stepped(q, pairs[step][half], matrices[step])
                    for a in range(3):
                        advanced[a, rows, lanes] = q[a]
                return carry

            lax.fori_loop(0, extra.shape[3] // (2 * SUB), body, 0, unroll=7)
            leave(x).start()

        copies += [leave(x) for x in range(depth)]
    for place in range(here):
        tile = first + place

        def squares(x):
            total = jnp.zeros((SUB, LANES), f32)
            for group in range(count // SUB):
                for a in range(3):
                    q = base[0, 0, tile, a, pl.ds(group * SUB, SUB), pl.ds(x * LANES, LANES)]
                    total = total + q * q
            return [total]

        sums = packed_sums(squares, depth)
        for step in range(2):
            relaxes[place, step] = relax_of(sums[0], inverse)

            def sums_of(x):
                lanes = pl.ds(x * LANES, LANES)
                matrix = with_diagonal(tile_grad(grad, depth, tile, x), wide(relaxes[place, step, pl.ds(x, 1), :]))

                def read(a, rows):
                    return base[0, 0, tile, a, rows, lanes] if step == 0 else halfway[place, a, rows, lanes]

                def write(a, rows, value):
                    if step == 0:
                        halfway[place, a, rows, lanes] = value
                    elif place < direct:
                        early[place, a, rows, lanes] = value
                    else:
                        fields[place - direct, a, rows, lanes] = value

                def shock(_, a, rows):
                    return noise[0, 0, tile, step, a, rows, lanes]

                if step == 0:
                    return tile_sums(read, write, shock, [matrix], count, add_square, 1)
                return tile_sums(read, write, shock, [matrix], count, add_moments, 6)

            sums = packed_sums(sums_of, depth)
        if place < direct:
            copies.append(pltpu.make_async_copy(early.at[place], new_base.at[0, 0, tile], sems.at[len(copies)]))
            copies[-1].start()
        for i, row in enumerate(stress_rows(sums, inverse)):
            stress[i, place] = row
    for copy in copies:
        copy.wait()


def call_ordinary(first, here, direct, before, base_fields, base_noise, grad, block, new_base, extra):
    count, cells = base_fields.shape[-2:]
    depth = cells // LANES
    has_block, has_base, has_extra = block is not None, new_base is not None, extra is not None
    operands = [before, *near_memory(base_fields, base_noise), grad]
    specs = [anywhere, vmem, vmem, vmem]
    shapes, out_specs, aliases = [], [], {}
    copies = 0
    if has_block:
        operands += near_memory(block)
        specs.append(vmem)
        copies += block.shape[0]
    if has_block or direct:
        copies += direct
        shapes.append(jax.ShapeDtypeStruct(base_fields.shape, f32))
        out_specs.append(hbm)
    if has_base:
        aliases[len(operands)] = 0
        operands.append(new_base)
        specs.append(hbm)
    if has_extra:
        operands += near_memory(*extra[:2]) + [extra[2]]
        specs += [vmem] * 3
        shapes.append(jax.ShapeDtypeStruct(extra[0].shape, f32))
        out_specs.append(hbm)
        copies += depth
    shapes += [
        pltpu.VMEM((here - direct, 3, count, cells), f32),
        jax.ShapeDtypeStruct((6, here, depth, LANES), f32),
    ]
    out_specs += [vmem, vmem]
    results = pl.pallas_call(
        functools.partial(ordinary, first, direct, has_block, has_base, has_extra),
        out_shape=tuple(shapes),
        in_specs=specs,
        out_specs=tuple(out_specs),
        input_output_aliases=aliases,
        scratch_shapes=[
            pltpu.VMEM((max(direct, 1), 3, count, cells), f32),
            pltpu.VMEM((here, 3, count, cells), f32),
            pltpu.VMEM((here, 2, depth, LANES), f32),
            pltpu.VMEM(extra[0].shape[2:] if has_extra else (SUB, LANES), f32),
            pltpu.SemaphoreType.DMA((max(copies, 1),)),
        ],
        compiler_params=pltpu.CompilerParams(vmem_limit_bytes=SMALL),
        cost_estimate=small(8 << 20, 3 << 20),
        name="ordinary_tiles",
    )(*operands)
    results = list(results)
    piece, block = results.pop(), results.pop()
    new_base = results.pop(0) if has_block or direct else None
    return new_base, block, piece, (results[0] if has_extra else None)


def moments_after(g, first, second, m):
    one, two = with_diagonal(g, first), with_diagonal(g, second)
    both = [[sum(two[3 * a + k] * one[3 * k + b] for k in range(3)) for b in range(3)] for a in range(3)]
    kick = [[noise_scale * two[3 * a + b] for b in range(3)] for a in range(3)]

    def mixed(of_q, of_w):
        return [
            [sum(both[a][i] * of_q(i, j) for i in range(3)) + sum(kick[a][i] * of_w(i, j) for i in range(3)) for j in range(3)]
            for a in range(3)
        ]

    with_q = mixed(lambda i, j: m[moment_of[i, j]], lambda i, j: m[6 + 3 * j + i])
    with_one = mixed(lambda i, j: m[6 + 3 * i + j], lambda i, j: m[15 + moment_of[i, j]])
    with_two = mixed(lambda i, j: m[21 + 3 * i + j], lambda i, j: m[30 + 3 * i + j])
    return [
        sum(with_q[a][j] * both[b][j] + with_one[a][j] * kick[b][j] for j in range(3))
        + noise_scale * (with_two[a][b] + with_two[b][a])
        + noise_scale**2 * m[39 + i]
        for i, (a, b) in enumerate(component_pairs)
    ]


def answering(before, moments, later, *refs):
    *parts, reply, drive = refs
    inverse = 1.0 / float(ALL_FIELDS)
    message = [sum(part[i] for part in parts) for i in range(12)]
    grad, m = message[:9], [moments[i] for i in range(21)] + [later[i] for i in range(24)]
    own = coefficients(grad, m[:15] + [m[15] + m[16] + m[17]])
    both = [message[9 + i] + own[i] for i in range(3)]
    first = relax_of(both[2], inverse)
    second = relax_of(both[0] + first * (both[1] + first * both[2]), inverse)
    for i, value in enumerate([first, second] + moments_after(grad, first, second, m)):
        reply[i] = value
    for i, value in enumerate(grad + [first, second]):
        drive[i] = value


def call_answering(before, moments, later, parts):
    depth = moments.shape[1]
    return pl.pallas_call(
        answering,
        out_shape=(
            jax.ShapeDtypeStruct((8, depth, LANES), f32),
            jax.ShapeDtypeStruct((11, depth, LANES), f32),
        ),
        in_specs=[anywhere] + [vmem] * (2 + len(parts)),
        out_specs=(vmem, vmem),
        compiler_params=pltpu.CompilerParams(vmem_limit_bytes=4 << 20),
        cost_estimate=small(1 << 20, 1 << 19),
        name="answering",
    )(before, moments, later, *parts)


def heavy(parity, helper, base, noise, grad, replies, new_base, rows, fields, answer, sems):
    _, _, tiles, _, count, cells = base.shape
    me = lax.axis_index("gy")
    depth = cells // LANES
    flat = rows.reshape(6 * depth * tiles, LANES)

    def store(k, tile):
        return pltpu.make_async_copy(fields.at[k], new_base.at[0, 0, tile], sems.at[k])

    places, order = owned_order(tiles, me, helper, (parity,))
    for k, (h, tile) in enumerate(order):

        @pl.when(k < places)
        def _(k=k, h=h, tile=tile):
            answer[...] = replies[(me ^ h) >> 1]

            def sums_of(x):
                lanes = pl.ds(x * LANES, LANES)
                g = tile_grad(grad, depth, tile, x)
                matrices = [with_diagonal(g, wide(answer[step, pl.ds(x, 1), :])) for step in range(2)]

                def read(a, part):
                    return base[0, 0, tile, a, part, lanes]

                def write(a, part, value):
                    fields[k, a, part, lanes] = value

                def shock(step, a, part):
                    return noise[0, 0, tile, step, a, part, lanes]

                return tile_sums(read, write, shock, matrices, count, add_moments, 6)

            sums = packed_sums(sums_of, depth)
            store(k, tile).start()
            sums = [s + answer[2 + i] for i, s in enumerate(sums)]
            for i, value in enumerate(stress_rows(sums, 1.0 / ALL_FIELDS)):
                flat[pl.ds(i * depth * tiles + tile, depth, stride=tiles), :] = value

    def wait():
        for k, (_, tile) in enumerate(order):

            @pl.when(k < places)
            def _(k=k, tile=tile):
                store(k, tile).wait()

    return wait


def heavy_scratch(near, held):
    return [pltpu.VMEM((HEAVY_MOST,) + held, f32), pltpu.VMEM(near.shape[1:], f32)]


def finish(piece_count, helper, base, noise, grad, near, block, *refs):
    pieces, (_, new_base, rows, fields, answer, sems) = refs[:piece_count], refs[piece_count:]
    _, depth, tiles, _ = rows.shape
    last = block.shape[0]
    flat = rows.reshape(6 * depth * tiles, LANES)
    me = lax.axis_index("gy")
    named = [jnp.bool_(False)] * last
    for _, owned, tile in owned_slots(tiles, me, helper):
        named = [n | (owned & (tile == tiles - last + i)) for i, n in enumerate(named)]
    copies = [
        pltpu.make_async_copy(block.at[i], new_base.at[0, 0, tiles - last + i], sems.at[HEAVY_MOST + i])
        for i in range(last)
    ]
    for copy, is_heavy in zip(copies, named):
        pl.when(jnp.logical_not(is_heavy))(copy.start)
    tile = 0
    for piece in pieces:
        for place in range(piece.shape[1]):
            for i in range(6):
                flat[pl.ds(i * depth * tiles + tile, depth, stride=tiles), :] = piece[i, place]
            tile += 1
    wait = heavy(0, helper, base, noise, grad, near, new_base, rows, fields, answer, sems)
    wait()
    for copy, is_heavy in zip(copies, named):
        pl.when(jnp.logical_not(is_heavy))(copy.wait)


def call_finish(helper_tile, base_fields, base_noise, grad, near, block, pieces, new_base):
    tiles, cells = new_base.shape[2], new_base.shape[-1]
    return pl.pallas_call(
        functools.partial(finish, len(pieces)),
        out_shape=(
            jax.ShapeDtypeStruct(new_base.shape, f32),
            jax.ShapeDtypeStruct((6, cells // LANES, tiles, LANES), f32),
        ),
        in_specs=[vmem] * (6 + len(pieces)) + [hbm],
        out_specs=(hbm, vmem),
        input_output_aliases={6 + len(pieces): 0},
        scratch_shapes=heavy_scratch(near, block.shape[1:])
        + [pltpu.SemaphoreType.DMA((HEAVY_MOST + block.shape[0],))],
        compiler_params=pltpu.CompilerParams(vmem_limit_bytes=SMALL),
        cost_estimate=small(1 << 10, 1 << 20),
        name="finish",
    )(helper_tile, *near_memory(base_fields, base_noise), grad, near, *near_memory(block), *pieces, new_base)


def final(helper, base, noise, grad, far, ready, old_base, new_base, stress, rows, fields, answer, sems):
    depth = rows.shape[1]

    def result(x):
        target = stress.at[0, 0, :, :, pl.ds(x * LANES, LANES)]
        return pltpu.make_async_copy(rows.at[:, x], target, sems.at[HEAVY_MOST + x])

    rows[...] = ready[...]
    wait = heavy(1, helper, base, noise, grad, far, new_base, rows, fields, answer, sems)
    for x in range(depth):
        result(x).start()
    wait()
    for x in range(depth):
        result(x).wait()


def call_final(helper_tile, base_fields, base_noise, grad, far, ready, new_base):
    _, _, tiles, _, count, cells = base_fields.shape
    depth = cells // LANES
    return pl.pallas_call(
        final,
        out_shape=(
            jax.ShapeDtypeStruct(new_base.shape, f32),
            jax.ShapeDtypeStruct((1, 1, 6, tiles, cells), f32),
        ),
        in_specs=[vmem] * 6 + [hbm],
        out_specs=(hbm, hbm),
        input_output_aliases={6: 0},
        scratch_shapes=[pltpu.VMEM((6, depth, tiles, LANES), f32)]
        + heavy_scratch(far, (3, count, cells))
        + [pltpu.SemaphoreType.DMA((HEAVY_MOST + depth,))],
        compiler_params=pltpu.CompilerParams(vmem_limit_bytes=SMALL),
        cost_estimate=small(8 << 20, 4 << 20),
        name="heavy_tiles",
    )(helper_tile, *near_memory(base_fields, base_noise), grad, far, ready, new_base)


def per_device(
    velocity, wall_cells, tile_counts, helper_tile, base_fields, extra_fields, base_noise, extra_noise
):
    tiles = tile_counts.shape[2]
    pairs = lax.axis_size("gy") // 2
    helper_tile, x_one, x_two, y_one, y_two = call_edges(helper_tile, velocity)
    y_two = swap_across(y_two, False)
    x_two = swap_across(x_two, True)
    x_one = swap_within(x_one, "gx")
    y_one = swap_within(y_one, "gy")
    halos = (y_two, x_two, x_one, y_one)
    moments, later = call_early_sums(helper_tile, base_fields, base_noise, extra_fields, extra_noise)
    grad, keep, send = call_gradients(tiles, later, helper_tile, velocity, halos, wall_cells, moments)
    some = 3 * tiles // 8
    ordinary_fields = (base_fields, base_noise, grad)
    received = swapped(send, 1)
    _, block, begun, _ = call_ordinary(0, some, 0, send, *ordinary_fields, None, None, None)
    keep, *sends = call_merge(begun, keep, received)
    farthest_first = sorted(range(1, pairs), key=lambda flip: -flip.bit_count())
    parts = [keep] + [swapped(sends[flip - 1], 2 * flip) for flip in farthest_first]
    extra_sums = call_extra_moments(1, sends[0], extra_fields, extra_noise)
    more = tiles - some - 3
    new_base, block, going, _ = call_ordinary(some, more, 0, extra_sums, *ordinary_fields, block, None, None)
    reply, drive = call_answering(going, extra_sums, later, parts)
    replies = {flip: swapped(reply, 2 * flip) for flip in farthest_first}
    new_base, block, ended, new_extra = call_ordinary(
        tiles - 3, 3, 1, reply, *ordinary_fields, block, new_base, (extra_fields, extra_noise, drive)
    )
    near = call_join(ended, [reply] + [replies[flip] for flip in range(1, pairs)])
    far = swapped(near, 1)
    given = (helper_tile, base_fields, base_noise, grad)
    new_base, ready = call_finish(*given, near, block, (begun, going, ended), new_base)
    new_base, stress = call_final(*given, far, ready, new_base)
    return new_base, new_extra, jnp.swapaxes(stress, 2, 3)


def solution(mesh):
    in_specs = (
        P(None, "gx", "gy", None),
        P("gx", "gy", None),
        P("gx", "gy", None),
        P("gx", None),
        P("gx", "gy", None, None, None, None),
        P("gx", "gy", None, None, None),
        P("gx", "gy", None, None, None, None, None),
        P("gx", "gy", None, None, None, None),
    )
    out_specs = (
        P("gx", "gy", None, None, None, None),
        P("gx", "gy", None, None, None),
        P("gx", "gy", None, None, None),
    )
    return jax.shard_map(
        per_device, mesh=mesh, in_specs=in_specs, out_specs=out_specs, check_vma=False
    )
```

```python
import functools

import jax
import jax.numpy as jnp
from jax import lax
from jax.experimental import pallas as pl
from jax.experimental.pallas import tpu as pltpu
from jax.sharding import PartitionSpec as P

ALL_FIELDS = 256
HEAVY_MOST = 4
LANES = 128
SUB = 8
SMALL = 12 << 20

time_step = 0.05
weissenberg = 0.25
max_extension = 50.0
noise_scale = (time_step / weissenberg) ** 0.5
component_pairs = ((0, 0), (1, 1), (2, 2), (0, 1), (0, 2), (1, 2))
moment_of = {(0, 0): 0, (1, 1): 1, (2, 2): 2, (0, 1): 3, (1, 0): 3, (0, 2): 4, (2, 0): 4, (1, 2): 5, (2, 1): 5}
f32 = jnp.float32

vmem = pl.BlockSpec(memory_space=pltpu.VMEM)
hbm = pl.BlockSpec(memory_space=pltpu.HBM)
anywhere = pl.BlockSpec(memory_space=pl.ANY)


def far_memory(*arrays):
    return [pltpu.with_memory_space_constraint(array, pltpu.HBM) for array in arrays]


def near_memory(*arrays):
    return [pltpu.with_memory_space_constraint(array, pltpu.VMEM) for array in arrays]


def column_sum(value):
    return jnp.sum(value, axis=0, keepdims=True)


def interleaved(a, b, bit):
    low = (lax.broadcasted_iota(jnp.int32, (SUB, LANES), 0) & bit) == 0
    return jnp.where(low, a, b) + pltpu.roll(jnp.where(low, b, a), bit, 0)


def packed_sums(values_of, count):
    stack = []
    for x in range(count):
        bit, values = 1, values_of(x)
        while stack and stack[-1][0] == bit:
            values = [interleaved(a, b, bit) for a, b in zip(stack.pop()[1], values)]
            bit *= 2
        stack.append((bit, values))
    return stack[0][1]


def wide(row):
    return jnp.broadcast_to(row, (SUB, LANES))


def turned(value, cell_z):
    sub = lax.broadcasted_iota(jnp.int32, value.shape, 0)
    group = lax.broadcasted_iota(jnp.int32, value.shape, 1) // cell_z
    skewed = pltpu.roll(value, cell_z, 1, stride=cell_z, stride_axis=0)
    mixed = jnp.take_along_axis(skewed, (group + sub) & (SUB - 1), axis=0, mode="promise_in_bounds")
    return pltpu.roll(mixed, 0, 1, stride=cell_z, stride_axis=0)


def relax_of(total, inverse):
    factor = 1.0 / (1.0 - total * inverse / max_extension)
    return 1.0 - (time_step * 0.5 / weissenberg) * factor


def stepped(vectors, noise, matrix):
    return [
        matrix[3 * a] * vectors[0]
        + matrix[3 * a + 1] * vectors[1]
        + matrix[3 * a + 2] * vectors[2]
        + noise_scale * noise[a]
        for a in range(3)
    ]


def with_diagonal(grad, relax):
    return [g + relax if i % 4 == 0 else g for i, g in enumerate(grad)]


def noise_rows(ref, start):
    both = [ref(a, pl.ds(start, 2 * SUB)).astype(f32) for a in range(3)]
    return [[w[:SUB] for w in both], [w[SUB:] for w in both]]


def add_moments(sums, q):
    return [s + q[a] * q[b] for s, (a, b) in zip(sums, component_pairs)]


def product_sums(sums, q, w):
    terms = [q[a] * q[b] for a, b in component_pairs]
    terms += [q[a] * w[b] for a in range(3) for b in range(3)]
    terms += [w[0] * w[0] + w[1] * w[1] + w[2] * w[2]]
    return [s + t for s, t in zip(sums, terms)]


def coefficients(g, m):
    cross = lambda a, b: m[6 + 3 * a + b]
    square = lambda a, b: m[moment_of[a, b]]
    once, twice, kick = 0.0, 0.0, 0.0
    for a in range(3):
        for b in range(3):
            once += g[3 * a + b] * square(a, b)
            kick += g[3 * a + b] * cross(b, a)
            inner = 0.0
            for c in range(3):
                inner += g[3 * a + c] * square(b, c)
            twice += g[3 * a + b] * inner
    return [
        twice + (2 * noise_scale) * kick + noise_scale**2 * m[15],
        2.0 * once + (2 * noise_scale) * (cross(0, 0) + cross(1, 1) + cross(2, 2)),
        m[0] + m[1] + m[2],
    ]


def owned_slots(tiles, me, helper):
    found = []
    row = helper[...]
    for h in range(helper.shape[1]):
        tile = row[0, h] - me * tiles
        found.append((h, (tile >= 0) & (tile < tiles), tile))
    return found


def owned_order(tiles, me, helper, parities=(0, 1)):
    places = jnp.int32(0)
    order = [jnp.int32(0)] * HEAVY_MOST
    for h, owned, tile in owned_slots(tiles, me, helper):
        if len(parities) == 1:
            owned = owned & (((me ^ h) & 1) == parities[0])
        entry = h * tiles + tile
        order = [jnp.where(owned & (places == k), entry, kept) for k, kept in enumerate(order)]
        places = places + owned.astype(jnp.int32)
    return places, [(entry // tiles, entry % tiles) for entry in order]


def small(flops, traffic):
    return pl.CostEstimate(flops=flops, bytes_accessed=traffic, transcendentals=0)


def is_even(axis):
    return (lax.axis_index(axis) & 1) == 0


def edges(helper, velocity, helper_near, x_one, x_two, y_one, y_two):
    depth, width = velocity.shape[1:3]
    helper_near[...] = helper[...]
    even = is_even("gx")
    for a in range(3):
        first, last = velocity[a, 0], velocity[a, depth - 1]
        x_one[a] = jnp.where(even, last, first)
        x_two[a] = jnp.where(even, first, last)
    even = is_even("gy")
    for a in range(3):
        for x in range(depth):
            first, last = velocity[a, x, pl.ds(0, 1), :], velocity[a, x, pl.ds(width - 1, 1), :]
            y_one[a, pl.ds(x, 1), :] = jnp.where(even, last, first)
            y_two[a, pl.ds(x, 1), :] = jnp.where(even, first, last)


def call_edges(helper_tile, velocity):
    _, depth, width, length = velocity.shape
    along_x = jax.ShapeDtypeStruct((3, width, length), f32)
    along_y = jax.ShapeDtypeStruct((3, depth, length), f32)
    return pl.pallas_call(
        edges,
        out_shape=(jax.ShapeDtypeStruct(helper_tile.shape, jnp.int32), along_x, along_x, along_y, along_y),
        in_specs=[vmem, vmem],
        out_specs=(vmem,) * 5,
        compiler_params=pltpu.CompilerParams(vmem_limit_bytes=4 << 20),
        cost_estimate=small(1 << 10, 1 << 17),
        name="edges",
    )(*far_memory(helper_tile, velocity))


def swap_within(block, axis):
    return lax.ppermute(block, axis, [(i, i ^ 1) for i in range(lax.axis_size(axis))])


def swap_across(block, along_rows):
    rows, columns = lax.axis_size("gx"), lax.axis_size("gy")
    size = rows if along_rows else columns

    def partner(row, column):
        place = row if along_rows else column
        if place in (0, size - 1):
            row, column = (row, column ^ 1) if along_rows else (row ^ 1, column)
        else:
            place += 1 if place & 1 else -1
            row, column = (place, column) if along_rows else (row, place)
        return row * columns + column

    places = [(row, column) for row in range(rows) for column in range(columns)]
    return lax.ppermute(block, ("gx", "gy"), [(i, partner(*place)) for i, place in enumerate(places)])


def low_and_high(axis, one, two, a):
    even, place = is_even(axis), lax.axis_index(axis)
    low = jnp.where(even, two[a], one[a])
    high = jnp.where(even, one[a], two[a])
    return jnp.where(place == 0, 0.0, low), jnp.where(place == lax.axis_size(axis) - 1, 0.0, high)


def heavy_moments(helper, base, noise, out, fields, shocks, sems):
    _, _, count, cells = fields.shape
    tiles = base.shape[2]
    me = lax.axis_index("gy")

    def loads(k, tile):
        return (
            pltpu.make_async_copy(base.at[0, 0, tile], fields.at[k], sems.at[0, k]),
            pltpu.make_async_copy(noise.at[0, 0, tile, 0], shocks.at[k], sems.at[1, k]),
        )

    places, order = owned_order(tiles, me, helper)
    for k, (_, tile) in enumerate(order):

        @pl.when(k < places)
        def _(k=k, tile=tile):
            for copy in loads(k, tile):
                copy.start()

    for k, (h, tile) in enumerate(order):

        @pl.when(k < places)
        def _(k=k, h=h, tile=tile):
            for copy in loads(k, tile):
                copy.wait()

            def sums_of(x):
                lanes = pl.ds(x * LANES, LANES)
                sums = [jnp.zeros((SUB, LANES), f32)] * 16
                for group in range(count // (2 * SUB)):
                    pair = noise_rows(lambda a, rows: shocks[k, a, rows, lanes], group * 2 * SUB)
                    for half in range(2):
                        rows = pl.ds((2 * group + half) * SUB, SUB)
                        sums = product_sums(sums, [fields[k, a, rows, lanes] for a in range(3)], pair[half])
                return sums

            for i, value in enumerate(packed_sums(sums_of, cells // LANES)):
                out[h, i] = value


def call_heavy_moments(helper_tile, base_fields, base_noise):
    slots = helper_tile.shape[1]
    count, cells = base_fields.shape[-2:]
    return pl.pallas_call(
        heavy_moments,
        out_shape=jax.ShapeDtypeStruct((slots, 16, cells // LANES, LANES), f32),
        in_specs=[vmem, hbm, hbm],
        out_specs=vmem,
        scratch_shapes=[
            pltpu.VMEM((HEAVY_MOST, 3, count, cells), f32),
            pltpu.VMEM((HEAVY_MOST, 3, count, cells), jnp.bfloat16),
            pltpu.SemaphoreType.DMA((2, HEAVY_MOST)),
        ],
        compiler_params=pltpu.CompilerParams(vmem_limit_bytes=SMALL),
        cost_estimate=small(8 << 20, 3 << 20),
        name="heavy_moments",
    )(helper_tile, *far_memory(base_fields, base_noise))


def outer_sums(sums, left, right):
    return [s + left[a] * right[b] for s, (a, b) in zip(sums, [(a, b) for a in range(3) for b in range(3)])]


def extra_moments(unroll, before, base, noise, out, partial):
    _, _, _, count, cells = base.shape
    zero = jnp.zeros((SUB, LANES), f32)

    @pl.loop(0, cells // LANES)
    def _(x):
        lanes = pl.ds(pl.multiple_of(x * LANES, LANES), LANES)

        def body(steps, i, sums):
            start = pl.multiple_of(i * 2 * SUB, 2 * SUB)
            pairs = [noise_rows(lambda a, rows: noise[0, 0, step, a, rows, lanes], start) for step in range(steps)]
            for half in range(2):
                q = [base[0, 0, a, pl.ds(start + half * SUB, SUB), lanes] for a in range(3)]
                w = [pair[half] for pair in pairs]
                if steps == 1:
                    sums = add_moments(sums[:6], q) + outer_sums(sums[6:15], q, w[0]) + add_moments(sums[15:], w[0])
                else:
                    sums = outer_sums(sums[:9], q, w[1]) + outer_sums(sums[9:18], *w) + add_moments(sums[18:], w[1])
            return sums

        at = 0
        for steps, many in ((1, 21), (2, 24)):
            loop = functools.partial(body, steps)
            for i, s in enumerate(lax.fori_loop(0, count // (2 * SUB), loop, [zero] * many, unroll=unroll)):
                partial[at + i, x] = s
            at += many

    for i in range(45):
        out[i] = packed_sums(lambda x: [partial[i, x]], cells // LANES)[0]


def call_extra_moments(before, extra_fields, extra_noise):
    cells = extra_fields.shape[-1]
    return pl.pallas_call(
        functools.partial(extra_moments, 7),
        out_shape=jax.ShapeDtypeStruct((45, cells // LANES, LANES), f32),
        in_specs=[anywhere, vmem, vmem],
        out_specs=vmem,
        scratch_shapes=[pltpu.VMEM((45, cells // LANES, SUB, LANES), f32)],
        compiler_params=pltpu.CompilerParams(vmem_limit_bytes=SMALL),
        cost_estimate=small(8 << 20, 5 << 20),
        name="extra_moments",
    )(before, *near_memory(extra_fields, extra_noise))


def gradients(tiles, helper, velocity, y_two, x_two, x_one, y_one, wall, moments, grad, keep, send):
    me = lax.axis_index("gy")
    depth = velocity.shape[1]
    cell_z = velocity.shape[3] // tiles
    sub = lax.broadcasted_iota(jnp.int32, (SUB, LANES), 0)
    lane = lax.broadcasted_iota(jnp.int32, (SUB, LANES), 1)
    z = lane % cell_z
    scales = [turned(jnp.where(wall[x] == 0, 0.5 * time_step, 0.0).astype(f32), cell_z) for x in range(depth)]
    for a in range(3):
        x_low, x_high = low_and_high("gx", x_one, x_two, a)
        y_low, y_high = low_and_high("gy", y_one, y_two, a)
        rows = [x_low] + [velocity[a, x] for x in range(depth)] + [x_high]
        rows = [turned(row, cell_z) for row in rows]
        low, high = turned(y_low, cell_z), turned(y_high, cell_z)
        for x in range(depth):
            here = rows[x + 1]
            above = high if x == depth - 1 else pltpu.roll(high, LANES - cell_z * (x + 1), 1)
            below = low if x == 0 else pltpu.roll(low, LANES - cell_z * x, 1)
            y_up = jnp.where(lane < LANES - cell_z, pltpu.roll(here, LANES - cell_z, 1), above)
            y_down = jnp.where(lane >= cell_z, pltpu.roll(here, cell_z, 1), below)
            next_tile = pltpu.roll(pltpu.roll(here, cell_z - 1, 1), 1, 0)
            last_tile = pltpu.roll(pltpu.roll(here, LANES - cell_z + 1, 1), SUB - 1, 0)
            next_tile = jnp.where(sub == 0, 0.0, next_tile)
            last_tile = jnp.where(sub == SUB - 1, 0.0, last_tile)
            z_up = jnp.where(z == cell_z - 1, next_tile, pltpu.roll(here, LANES - 1, 1))
            z_down = jnp.where(z == 0, last_tile, pltpu.roll(here, 1, 1))
            for b, difference in enumerate((rows[x + 2] - rows[x], y_up - y_down, z_up - z_down)):
                grad[pl.ds(((3 * a + b) * depth + x) * SUB, SUB), :] = difference * scales[x]
    keep[...] = jnp.zeros(keep.shape, f32)
    send[...] = jnp.zeros(send.shape, f32)
    for h, owned, tile in owned_slots(tiles, me, helper):

        @pl.when(owned)
        def _(h=h, tile=tile):
            g = [grad[pl.ds(i * depth * SUB + SUB - 1 - tile, depth, stride=SUB), :] for i in range(9)]
            rows = g + coefficients(g, [moments[h, i] for i in range(16)])
            stays = (me & 1) == (h & 1)

            @pl.when(stays)
            def _():
                for i, row in enumerate(rows):
                    keep[h >> 1, i] = row

            @pl.when(jnp.logical_not(stays))
            def _():
                for i, row in enumerate(rows):
                    send[h >> 1, i] = row


def call_gradients(tiles, helper_tile, velocity, halos, wall_cells, moments):
    slots = helper_tile.shape[1]
    depth = velocity.shape[1]
    half = jax.ShapeDtypeStruct((slots // 2, 12, depth, LANES), f32)
    return pl.pallas_call(
        functools.partial(gradients, tiles),
        out_shape=(jax.ShapeDtypeStruct((9 * depth * SUB, LANES), f32), half, half),
        in_specs=[vmem] * 8,
        out_specs=(vmem,) * 3,
        compiler_params=pltpu.CompilerParams(vmem_limit_bytes=8 << 20),
        cost_estimate=small(4 << 20, 1 << 20),
        name="gradients",
    )(helper_tile, velocity, *halos, wall_cells, moments)


def swapped(block, flip):
    size = lax.axis_size("gy")
    return lax.ppermute(block, "gy", [(i, i ^ flip) for i in range(size)])


def merge(before, kept, received, keep, *sends):
    pair = lax.axis_index("gy") >> 1
    for flip, out in enumerate((keep,) + sends):
        out[...] = kept[pair ^ flip] + received[pair ^ flip]


def call_merge(before, kept, received):
    one = jax.ShapeDtypeStruct(kept.shape[1:], f32)
    return pl.pallas_call(
        merge,
        out_shape=(one,) * kept.shape[0],
        in_specs=[anywhere, vmem, vmem],
        out_specs=(vmem,) * kept.shape[0],
        compiler_params=pltpu.CompilerParams(vmem_limit_bytes=4 << 20),
        cost_estimate=small(1 << 10, 1 << 18),
        name="merge",
    )(before, kept, received)


def join(before, *refs):
    for i, ref in enumerate(refs[:-1]):
        refs[-1][i] = ref[...]


def call_join(before, blocks):
    return pl.pallas_call(
        join,
        out_shape=jax.ShapeDtypeStruct((len(blocks),) + blocks[0].shape, f32),
        in_specs=[anywhere] + [vmem] * len(blocks),
        out_specs=vmem,
        compiler_params=pltpu.CompilerParams(vmem_limit_bytes=4 << 20),
        cost_estimate=small(1 << 10, 1 << 18),
        name="join",
    )(before, *blocks)


def stress_rows(sums, inverse):
    second = [s * inverse for s in sums]
    stretch = 1.0 / (1.0 - (second[0] + second[1] + second[2]) / max_extension)
    return [(stretch * s - (1.0 if i < 3 else 0.0)) * (1.0 / weissenberg) for i, s in enumerate(second)]


def tile_grad(grad, depth, tile, x):
    return [wide(grad[pl.ds((i * depth + x + 1) * SUB - 1 - tile, 1), :]) for i in range(9)]


def tile_sums(read, write, noise, matrices, count, add, many):
    sums = [jnp.zeros((SUB, LANES), f32)] * many
    for group in range(count // (2 * SUB)):
        pairs = [noise_rows(functools.partial(noise, step), group * 2 * SUB) for step in range(len(matrices))]
        for half in range(2):
            rows = pl.ds((2 * group + half) * SUB, SUB)
            q = [read(a, rows) for a in range(3)]
            for step, matrix in enumerate(matrices):
                q = stepped(q, pairs[step][half], matrix)
            for a in range(3):
                write(a, rows, q[a])
            sums = add(sums, q)
    return sums


def add_square(sums, q):
    return [sums[0] + (q[0] * q[0] + q[1] * q[1] + q[2] * q[2])]


def ordinary(first, direct, has_block, has_base, has_extra, *refs):
    refs = list(refs)
    before, base, noise, grad = refs[:4]
    del refs[:4]
    block = refs.pop(0) if has_block else None
    if has_base:
        refs.pop(0)
    extra, extra_noise, drive = [refs.pop(0) for _ in range(3)] if has_extra else [None] * 3
    new_base = refs.pop(0) if has_block or direct else None
    new_extra = refs.pop(0) if has_extra else None
    fields, stress, early, halfway, relaxes, advanced, sems = refs
    _, _, count, cells = fields.shape
    here = direct + fields.shape[0]
    depth = cells // LANES
    inverse = 1.0 / count
    copies = []
    if has_block:
        last = block.shape[0]
        copies += [
            pltpu.make_async_copy(block.at[i], new_base.at[0, 0, first - last + i], sems.at[i]) for i in range(last)
        ]
    for copy in copies:
        copy.start()
    if has_extra:
        at = len(copies)

        def leave(x):
            lanes = pl.ds(x * LANES, LANES)
            return pltpu.make_async_copy(advanced.at[:, :, lanes], new_extra.at[0, 0, :, :, lanes], sems.at[at + x])

        @pl.loop(0, depth)
        def _(x):
            lanes = pl.ds(pl.multiple_of(x * LANES, LANES), LANES)
            rows_of = [wide(drive[i, pl.ds(x, 1), :]) for i in range(11)]
            matrices = [with_diagonal(rows_of[:9], rows_of[9 + step]) for step in range(2)]

            def body(i, carry):
                start = pl.multiple_of(i * 2 * SUB, 2 * SUB)
                pairs = [
                    noise_rows(lambda a, rows: extra_noise[0, 0, step, a, rows, lanes], start) for step in range(2)
                ]
                for half in range(2):
                    rows = pl.ds(start + half * SUB, SUB)
                    q = [extra[0, 0, a, rows, lanes] for a in range(3)]
                    for step in range(2):
                        q = stepped(q, pairs[step][half], matrices[step])
                    for a in range(3):
                        advanced[a, rows, lanes] = q[a]
                return carry

            lax.fori_loop(0, extra.shape[3] // (2 * SUB), body, 0, unroll=7)
            leave(x).start()

        copies += [leave(x) for x in range(depth)]
    for place in range(here):
        tile = first + place

        def squares(x):
            total = jnp.zeros((SUB, LANES), f32)
            for group in range(count // SUB):
                for a in range(3):
                    q = base[0, 0, tile, a, pl.ds(group * SUB, SUB), pl.ds(x * LANES, LANES)]
                    total = total + q * q
            return [total]

        sums = packed_sums(squares, depth)
        for step in range(2):
            relaxes[place, step] = relax_of(sums[0], inverse)

            def sums_of(x):
                lanes = pl.ds(x * LANES, LANES)
                matrix = with_diagonal(tile_grad(grad, depth, tile, x), wide(relaxes[place, step, pl.ds(x, 1), :]))

                def read(a, rows):
                    return base[0, 0, tile, a, rows, lanes] if step == 0 else halfway[place, a, rows, lanes]

                def write(a, rows, value):
                    if step == 0:
                        halfway[place, a, rows, lanes] = value
                    elif place < direct:
                        early[place, a, rows, lanes] = value
                    else:
                        fields[place - direct, a, rows, lanes] = value

                def shock(_, a, rows):
                    return noise[0, 0, tile, step, a, rows, lanes]

                if step == 0:
                    return tile_sums(read, write, shock, [matrix], count, add_square, 1)
                return tile_sums(read, write, shock, [matrix], count, add_moments, 6)

            sums = packed_sums(sums_of, depth)
        if place < direct:
            copies.append(pltpu.make_async_copy(early.at[place], new_base.at[0, 0, tile], sems.at[len(copies)]))
            copies[-1].start()
        for i, row in enumerate(stress_rows(sums, inverse)):
            stress[i, place] = row
    for copy in copies:
        copy.wait()


def call_ordinary(first, here, direct, before, base_fields, base_noise, grad, block, new_base, extra):
    count, cells = base_fields.shape[-2:]
    depth = cells // LANES
    has_block, has_base, has_extra = block is not None, new_base is not None, extra is not None
    operands = [before, *near_memory(base_fields, base_noise), grad]
    specs = [anywhere, vmem, vmem, vmem]
    shapes, out_specs, aliases = [], [], {}
    copies = 0
    if has_block:
        operands += near_memory(block)
        specs.append(vmem)
        copies += block.shape[0]
    if has_block or direct:
        copies += direct
        shapes.append(jax.ShapeDtypeStruct(base_fields.shape, f32))
        out_specs.append(hbm)
    if has_base:
        aliases[len(operands)] = 0
        operands.append(new_base)
        specs.append(hbm)
    if has_extra:
        operands += near_memory(*extra[:2]) + [extra[2]]
        specs += [vmem] * 3
        shapes.append(jax.ShapeDtypeStruct(extra[0].shape, f32))
        out_specs.append(hbm)
        copies += depth
    shapes += [
        pltpu.VMEM((here - direct, 3, count, cells), f32),
        jax.ShapeDtypeStruct((6, here, depth, LANES), f32),
    ]
    out_specs += [vmem, vmem]
    results = pl.pallas_call(
        functools.partial(ordinary, first, direct, has_block, has_base, has_extra),
        out_shape=tuple(shapes),
        in_specs=specs,
        out_specs=tuple(out_specs),
        input_output_aliases=aliases,
        scratch_shapes=[
            pltpu.VMEM((max(direct, 1), 3, count, cells), f32),
            pltpu.VMEM((here, 3, count, cells), f32),
            pltpu.VMEM((here, 2, depth, LANES), f32),
            pltpu.VMEM(extra[0].shape[2:] if has_extra else (SUB, LANES), f32),
            pltpu.SemaphoreType.DMA((max(copies, 1),)),
        ],
        compiler_params=pltpu.CompilerParams(vmem_limit_bytes=SMALL),
        cost_estimate=small(8 << 20, 3 << 20),
        name="ordinary_tiles",
    )(*operands)
    results = list(results)
    piece, block = results.pop(), results.pop()
    new_base = results.pop(0) if has_block or direct else None
    return new_base, block, piece, (results[0] if has_extra else None)


def moments_after(g, first, second, m):
    one, two = with_diagonal(g, first), with_diagonal(g, second)
    both = [[sum(two[3 * a + k] * one[3 * k + b] for k in range(3)) for b in range(3)] for a in range(3)]
    kick = [[noise_scale * two[3 * a + b] for b in range(3)] for a in range(3)]

    def mixed(of_q, of_w):
        return [
            [sum(both[a][i] * of_q(i, j) for i in range(3)) + sum(kick[a][i] * of_w(i, j) for i in range(3)) for j in range(3)]
            for a in range(3)
        ]

    with_q = mixed(lambda i, j: m[moment_of[i, j]], lambda i, j: m[6 + 3 * j + i])
    with_one = mixed(lambda i, j: m[6 + 3 * i + j], lambda i, j: m[15 + moment_of[i, j]])
    with_two = mixed(lambda i, j: m[21 + 3 * i + j], lambda i, j: m[30 + 3 * i + j])
    return [
        sum(with_q[a][j] * both[b][j] + with_one[a][j] * kick[b][j] for j in range(3))
        + noise_scale * (with_two[a][b] + with_two[b][a])
        + noise_scale**2 * m[39 + i]
        for i, (a, b) in enumerate(component_pairs)
    ]


def answering(moments, *refs):
    *parts, reply, drive = refs
    inverse = 1.0 / float(ALL_FIELDS)
    message = [sum(part[i] for part in parts) for i in range(12)]
    grad, m = message[:9], [moments[i] for i in range(45)]
    own = coefficients(grad, m[:15] + [m[15] + m[16] + m[17]])
    both = [message[9 + i] + own[i] for i in range(3)]
    first = relax_of(both[2], inverse)
    second = relax_of(both[0] + first * (both[1] + first * both[2]), inverse)
    for i, value in enumerate([first, second] + moments_after(grad, first, second, m)):
        reply[i] = value
    for i, value in enumerate(grad + [first, second]):
        drive[i] = value


def call_answering(moments, parts):
    depth = moments.shape[1]
    return pl.pallas_call(
        answering,
        out_shape=(
            jax.ShapeDtypeStruct((8, depth, LANES), f32),
            jax.ShapeDtypeStruct((11, depth, LANES), f32),
        ),
        in_specs=[vmem] * (1 + len(parts)),
        out_specs=(vmem, vmem),
        compiler_params=pltpu.CompilerParams(vmem_limit_bytes=4 << 20),
        cost_estimate=small(1 << 20, 1 << 19),
        name="answering",
    )(moments, *parts)


def heavy(parity, helper, base, noise, grad, replies, new_base, rows, fields, answer, sems):
    _, _, tiles, _, count, cells = base.shape
    me = lax.axis_index("gy")
    depth = cells // LANES
    flat = rows.reshape(6 * depth * tiles, LANES)

    def store(k, tile):
        return pltpu.make_async_copy(fields.at[k], new_base.at[0, 0, tile], sems.at[k])

    places, order = owned_order(tiles, me, helper, (parity,))
    for k, (h, tile) in enumerate(order):

        @pl.when(k < places)
        def _(k=k, h=h, tile=tile):
            answer[...] = replies[(me ^ h) >> 1]

            def sums_of(x):
                lanes = pl.ds(x * LANES, LANES)
                g = tile_grad(grad, depth, tile, x)
                matrices = [with_diagonal(g, wide(answer[step, pl.ds(x, 1), :])) for step in range(2)]

                def read(a, part):
                    return base[0, 0, tile, a, part, lanes]

                def write(a, part, value):
                    fields[k, a, part, lanes] = value

                def shock(step, a, part):
                    return noise[0, 0, tile, step, a, part, lanes]

                return tile_sums(read, write, shock, matrices, count, add_moments, 6)

            sums = packed_sums(sums_of, depth)
            store(k, tile).start()
            sums = [s + answer[2 + i] for i, s in enumerate(sums)]
            for i, value in enumerate(stress_rows(sums, 1.0 / ALL_FIELDS)):
                flat[pl.ds(i * depth * tiles + tile, depth, stride=tiles), :] = value

    def wait():
        for k, (_, tile) in enumerate(order):

            @pl.when(k < places)
            def _(k=k, tile=tile):
                store(k, tile).wait()

    return wait


def heavy_scratch(near, held):
    return [pltpu.VMEM((HEAVY_MOST,) + held, f32), pltpu.VMEM(near.shape[1:], f32)]


def finish(piece_count, helper, base, noise, grad, near, block, *refs):
    pieces, (_, new_base, rows, fields, answer, sems) = refs[:piece_count], refs[piece_count:]
    _, depth, tiles, _ = rows.shape
    last = block.shape[0]
    flat = rows.reshape(6 * depth * tiles, LANES)
    me = lax.axis_index("gy")
    named = [jnp.bool_(False)] * last
    for _, owned, tile in owned_slots(tiles, me, helper):
        named = [n | (owned & (tile == tiles - last + i)) for i, n in enumerate(named)]
    copies = [
        pltpu.make_async_copy(block.at[i], new_base.at[0, 0, tiles - last + i], sems.at[HEAVY_MOST + i])
        for i in range(last)
    ]
    for copy, is_heavy in zip(copies, named):
        pl.when(jnp.logical_not(is_heavy))(copy.start)
    tile = 0
    for piece in pieces:
        for place in range(piece.shape[1]):
            for i in range(6):
                flat[pl.ds(i * depth * tiles + tile, depth, stride=tiles), :] = piece[i, place]
            tile += 1
    wait = heavy(0, helper, base, noise, grad, near, new_base, rows, fields, answer, sems)
    wait()
    for copy, is_heavy in zip(copies, named):
        pl.when(jnp.logical_not(is_heavy))(copy.wait)


def call_finish(helper_tile, base_fields, base_noise, grad, near, block, pieces, new_base):
    tiles, cells = new_base.shape[2], new_base.shape[-1]
    return pl.pallas_call(
        functools.partial(finish, len(pieces)),
        out_shape=(
            jax.ShapeDtypeStruct(new_base.shape, f32),
            jax.ShapeDtypeStruct((6, cells // LANES, tiles, LANES), f32),
        ),
        in_specs=[vmem] * (6 + len(pieces)) + [hbm],
        out_specs=(hbm, vmem),
        input_output_aliases={6 + len(pieces): 0},
        scratch_shapes=heavy_scratch(near, block.shape[1:])
        + [pltpu.SemaphoreType.DMA((HEAVY_MOST + block.shape[0],))],
        compiler_params=pltpu.CompilerParams(vmem_limit_bytes=SMALL),
        cost_estimate=small(1 << 10, 1 << 20),
        name="finish",
    )(helper_tile, *near_memory(base_fields, base_noise), grad, near, *near_memory(block), *pieces, new_base)


def final(helper, base, noise, grad, far, ready, old_base, new_base, stress, rows, fields, answer, sems):
    depth = rows.shape[1]

    def result(x):
        target = stress.at[0, 0, :, :, pl.ds(x * LANES, LANES)]
        return pltpu.make_async_copy(rows.at[:, x], target, sems.at[HEAVY_MOST + x])

    rows[...] = ready[...]
    wait = heavy(1, helper, base, noise, grad, far, new_base, rows, fields, answer, sems)
    for x in range(depth):
        result(x).start()
    wait()
    for x in range(depth):
        result(x).wait()


def call_final(helper_tile, base_fields, base_noise, grad, far, ready, new_base):
    _, _, tiles, _, count, cells = base_fields.shape
    depth = cells // LANES
    return pl.pallas_call(
        final,
        out_shape=(
            jax.ShapeDtypeStruct(new_base.shape, f32),
            jax.ShapeDtypeStruct((1, 1, 6, tiles, cells), f32),
        ),
        in_specs=[vmem] * 6 + [hbm],
        out_specs=(hbm, hbm),
        input_output_aliases={6: 0},
        scratch_shapes=[pltpu.VMEM((6, depth, tiles, LANES), f32)]
        + heavy_scratch(far, (3, count, cells))
        + [pltpu.SemaphoreType.DMA((HEAVY_MOST + depth,))],
        compiler_params=pltpu.CompilerParams(vmem_limit_bytes=SMALL),
        cost_estimate=small(8 << 20, 4 << 20),
        name="heavy_tiles",
    )(helper_tile, *near_memory(base_fields, base_noise), grad, far, ready, new_base)


def per_device(
    velocity, wall_cells, tile_counts, helper_tile, base_fields, extra_fields, base_noise, extra_noise
):
    tiles = tile_counts.shape[2]
    pairs = lax.axis_size("gy") // 2
    helper_tile, x_one, x_two, y_one, y_two = call_edges(helper_tile, velocity)
    y_two = swap_across(y_two, False)
    x_two = swap_across(x_two, True)
    x_one = swap_within(x_one, "gx")
    y_one = swap_within(y_one, "gy")
    halos = (y_two, x_two, x_one, y_one)
    moments = call_heavy_moments(helper_tile, base_fields, base_noise)
    grad, keep, send = call_gradients(tiles, helper_tile, velocity, halos, wall_cells, moments)
    some = tiles // 2
    ordinary_fields = (base_fields, base_noise, grad)
    received = swapped(send, 1)
    _, block, begun, _ = call_ordinary(0, some, 0, send, *ordinary_fields, None, None, None)
    keep, *sends = call_merge(begun, keep, received)
    farthest_first = sorted(range(1, pairs), key=lambda flip: -flip.bit_count())
    parts = [keep] + [swapped(sends[flip - 1], 2 * flip) for flip in farthest_first]
    extra_sums = call_extra_moments(sends[0], extra_fields, extra_noise)
    reply, drive = call_answering(extra_sums, parts)
    replies = {flip: swapped(reply, 2 * flip) for flip in farthest_first}
    new_base, block, ended, new_extra = call_ordinary(
        some, tiles - some, tiles - some - 2, reply, *ordinary_fields, block, None, (extra_fields, extra_noise, drive)
    )
    near = call_join(ended, [reply] + [replies[flip] for flip in range(1, pairs)])
    far = swapped(near, 1)
    given = (helper_tile, base_fields, base_noise, grad)
    new_base, ready = call_finish(*given, near, block, (begun, ended), new_base)
    new_base, stress = call_final(*given, far, ready, new_base)
    return new_base, new_extra, jnp.swapaxes(stress, 2, 3)


def solution(mesh):
    in_specs = (
        P(None, "gx", "gy", None),
        P("gx", "gy", None),
        P("gx", "gy", None),
        P("gx", None),
        P("gx", "gy", None, None, None, None),
        P("gx", "gy", None, None, None),
        P("gx", "gy", None, None, None, None, None),
        P("gx", "gy", None, None, None, None),
    )
    out_specs = (
        P("gx", "gy", None, None, None, None),
        P("gx", "gy", None, None, None),
        P("gx", "gy", None, None, None),
    )
    return jax.shard_map(
        per_device, mesh=mesh, in_specs=in_specs, out_specs=out_specs, check_vma=False
    )
```
